32 devices in a mesh: seq: 16 (over z, x, core), batch: 2 (over y).
Axes of the slice: x: 2, y: 2, z: 4, core: 2. Of those that a mesh axis runs over, the one named last changes fastest.
Arguments:
- states: float32 [2, 2048, 1024], P('batch', 'seq'), may hold values from -6 to 6
- lengths: int32 [2, 4], P('batch'), may hold values from 0 to 2048, as said below
- w_query: bfloat16 [1024, 1024], P(None, 'seq'), may hold values from -0.1875 to 0.1875
- w_key: bfloat16 [1024, 1024], P(None, 'seq'), may hold values from -0.1875 to 0.1875
- w_value: bfloat16 [1024, 1024], P(None, 'seq'), may hold values from -0.1875 to 0.1875
- w_out: bfloat16 [1024, 1024], P('seq'), may hold values from -0.1875 to 0.1875
- w_up: bfloat16 [1024, 4096], P(None, 'seq'), may hold values from -0.1875 to 0.1875
- w_gate: bfloat16 [1024, 4096], P(None, 'seq'), may hold values from -0.1875 to 0.1875
- w_down: bfloat16 [4096, 1024], P('seq'), may hold values from -0.1875 to 0.1875
- qk_scale: float32 [1024], replicated, may hold values from 0.8 to 1.6
- up_scale: float32 [4096], replicated, may hold values from 0.5 to 1.5
- gate_scale: float32 [4096], replicated, may hold values from 0.5 to 1.5
- alpha_attn: float32 [1024], replicated, may hold values from 0.15 to 0.6
- alpha_mlp: float32 [1024], replicated, may hold values from 0.15 to 0.6
- d_out: float32 [2, 2048, 1024], P('batch', 'seq'), may hold values from -6 to 6
Outputs:
- output: float32 [2, 2048, 1024], P('batch', 'seq')
- d_states: float32 [2, 2048, 1024], P('batch', 'seq')
- g_query: float32 [1024, 1024], P(None, 'seq')
- g_key: float32 [1024, 1024], P(None, 'seq')
- g_value: float32 [1024, 1024], P(None, 'seq')
- g_out: float32 [1024, 1024], P('seq')
- g_up: float32 [1024, 4096], P(None, 'seq')
- g_gate: float32 [1024, 4096], P(None, 'seq')
- g_down: float32 [4096, 1024], P('seq')
- g_qk_scale: float32 [1024], replicated
- g_up_scale: float32 [4096], replicated
- g_gate_scale: float32 [4096], replicated
- g_alpha_attn: float32 [1024], replicated
- g_alpha_mlp: float32 [1024], replicated
The draws below stay inside these ranges and needn't reach their ends.
Inputs may be any that keep to these rules, and one draw needn't show every extreme that they name: Each row's 4 lengths sum to 2048, and documents may be empty; among the 1 row of each index of batch, one row holds a single document of 2048 tokens.
All inputs are finite; a program needn't handle non-finite values.
Results may differ from the reference program's by a relative error of at most 0.025.
Values may be sent and summed in bfloat16 or wider, within the bound.
A program may use at most 192 MiB of HBM per device.

```python
import jax
import jax.numpy as jnp
from jax import lax

D = 1024
HEADS = 16
HEAD = 64
FF = 4096
ROWS_DEV = 1
DOCS = 4
BATCHES = 2
SEQLEN = 2048


def draw_lengths(key, part):
    key = jax.random.fold_in(key, 11)
    cut_key = jax.random.fold_in(key, 1)
    pick_key = jax.random.fold_in(key, 2)
    cuts = jax.random.randint(cut_key, (BATCHES, DOCS - 1), 0, SEQLEN + 1).astype(jnp.int32)
    cuts = jnp.sort(cuts, axis=1)
    edges = jnp.concatenate([jnp.zeros((BATCHES, 1), jnp.int32), cuts, jnp.full((BATCHES, 1), SEQLEN, jnp.int32)], axis=1)
    ragged = (edges[:, 1:] - edges[:, :-1]).astype(jnp.int32)
    groups = BATCHES // ROWS_DEV
    picked = jax.random.randint(pick_key, (groups,), 0, ROWS_DEV).astype(jnp.int32)
    row_place = (jnp.arange(BATCHES, dtype=jnp.int32) % ROWS_DEV).astype(jnp.int32)
    chosen = row_place == jnp.repeat(picked, ROWS_DEV)
    single = jnp.concatenate([jnp.full((1,), SEQLEN, jnp.int32), jnp.zeros((DOCS - 1,), jnp.int32)])
    return jnp.where(chosen[:, None], single[None, :], ragged).astype(jnp.int32)


def level_of(own_key, dims, split, low, largest):
    loudness = 1.0
    for dim, blocks in split:
        heights = jax.random.uniform(jax.random.fold_in(jax.random.fold_in(own_key, 6), dim), (blocks,), jnp.float32, low / len(split), largest / len(split))
        loudness = loudness * jnp.repeat(jnp.exp(heights), dims[dim] // blocks).reshape((-1,) + (1,) * (len(dims) - 1 - dim))
    return loudness


def gaussian(rng, extent, spread, most, cuts=(), held_as=jnp.bfloat16):
    drawn = spread * jax.random.normal(rng, extent, jnp.float32)
    if cuts:
        drawn = drawn * level_of(rng, extent, cuts, -0.22, 0.18)
    return jnp.clip(drawn, -most, most).astype(held_as)


def setup_inputs(seed: int = 0) -> dict:
    seeds = jax.random.split(jax.random.key(seed), 16)
    states = gaussian(seeds[0], (BATCHES, SEQLEN, D), 1.0, 6.0, ((0, 2), (1, 16)), jnp.float32)
    lengths = draw_lengths(jax.random.fold_in(seeds[15], 71), 0)
    w_query = gaussian(seeds[2], (D, D), D ** -0.5, 0.1875, ((1, 16),))
    w_key = gaussian(seeds[3], (D, D), D ** -0.5, 0.1875, ((1, 16),))
    w_value = gaussian(seeds[4], (D, D), D ** -0.5, 0.1875, ((1, 16),))
    w_out = gaussian(seeds[5], (D, D), D ** -0.5, 0.1875, ((0, 16),))
    w_up = gaussian(seeds[6], (D, FF), D ** -0.5, 0.1875, ((1, 16),))
    w_gate = gaussian(seeds[7], (D, FF), D ** -0.5, 0.1875, ((1, 16),))
    w_down = gaussian(seeds[8], (FF, D), D ** -0.5, 0.1875, ((0, 16),))
    qk_scale = jnp.clip(jax.random.uniform(seeds[9], (D,), jnp.float32, 0.8, 1.6), 0.8, 1.6)
    up_scale = jnp.clip(jax.random.uniform(seeds[10], (FF,), jnp.float32, 0.5, 1.5), 0.5, 1.5)
    gate_scale = jnp.clip(jax.random.uniform(seeds[11], (FF,), jnp.float32, 0.5, 1.5), 0.5, 1.5)
    alpha_attn = jnp.clip(jax.random.uniform(seeds[12], (D,), jnp.float32, 0.15, 0.6), 0.15, 0.6)
    alpha_mlp = jnp.clip(jax.random.uniform(seeds[13], (D,), jnp.float32, 0.15, 0.6), 0.15, 0.6)
    d_out = gaussian(seeds[14], (BATCHES, SEQLEN, D), 1.0, 6.0, ((0, 2), (1, 16)), jnp.float32)
    return dict(states=states, lengths=lengths, w_query=w_query, w_key=w_key, w_value=w_value, w_out=w_out, w_up=w_up, w_gate=w_gate, w_down=w_down, qk_scale=qk_scale, up_scale=up_scale, gate_scale=gate_scale, alpha_attn=alpha_attn, alpha_mlp=alpha_mlp, d_out=d_out)


@jax.custom_vjp
def low(v):
    return lax.optimization_barrier(v.astype(jnp.bfloat16)).astype(jnp.float32)

@jax.custom_vjp
def low_back(v):
    return v

def low_keep(v):
    return (low(v), None)

def low_pass(kept, grad):
    return (grad,)

def back_keep(v):
    return (v, None)

def back_low(kept, grad):
    return (low(grad),)
low.defvjp(low_keep, low_pass)
low_back.defvjp(back_keep, back_low)
EPS = 1e-06
HIGH = lax.Precision.HIGHEST

def normalized(weight, axis):
    return weight * lax.rsqrt(lax.optimization_barrier(jnp.sum(weight * weight, axis=axis, keepdims=True)) + EPS)

def rms(values):
    return values * lax.rsqrt(lax.optimization_barrier(jnp.mean(values * values, axis=-1, keepdims=True)) + EPS)

def doc_layout(len_row, tok_index):
    ends = jnp.cumsum(len_row).astype(jnp.int32)
    starts = (ends - len_row).astype(jnp.int32)
    started = starts[None, :] <= tok_index[:, None]
    doc_ids = (lax.optimization_barrier(jnp.sum(started.astype(jnp.int32), axis=1)) - 1).astype(jnp.int32)
    first_tok = lax.optimization_barrier(jnp.max(jnp.where(started, starts[None, :], 0), axis=1)).astype(jnp.int32)
    return (doc_ids, (tok_index - first_tok).astype(jnp.int32))

def rope(values, position):
    half = values.shape[-1] // 2
    freqs = 10000.0 ** (-jnp.arange(half, dtype=jnp.float32) / half)
    angle = position.astype(jnp.float32)[:, None] * freqs[None, :]
    cosine = jnp.cos(angle)[:, None, :]
    sine = jnp.sin(angle)[:, None, :]
    first = values[..., :half]
    second = values[..., half:]
    return jnp.concatenate([first * cosine - second * sine, first * sine + second * cosine], axis=-1)

def prepare(linear, position, gain):
    count = linear.shape[0]
    shaped = linear.reshape(count, HEADS, HEAD)
    turned = rms(rope(shaped, position)) * gain.reshape(HEADS, HEAD)
    return turned.reshape(count, HEADS * HEAD)

def residual_mix(state, branch, alpha):
    return rms(state + alpha * (rms(branch) - state))

def gating(up_lin, gate_lin, up_scale, gate_scale):
    return up_scale * up_lin * jax.nn.silu(gate_scale * gate_lin)

def row_layer(x_row, len_row, units, qk_scale, up_scale, gate_scale, alpha_attn, alpha_mlp):
    u_query, u_key, u_value, u_out, u_up, u_gate, u_down = units
    count = x_row.shape[0]
    tok_index = jnp.arange(count, dtype=jnp.int32)
    doc_ids, position = doc_layout(len_row, tok_index)
    x_low = low(x_row)
    query_lin = low_back(jnp.dot(x_low, u_query, precision=HIGH))
    key_lin = low_back(jnp.dot(x_low, u_key, precision=HIGH))
    value_lin = low_back(jnp.dot(x_low, u_value, precision=HIGH))
    query_h = low(prepare(query_lin, position, qk_scale)).reshape(count, HEADS, HEAD)
    key_h = low(prepare(key_lin, position, qk_scale)).reshape(count, HEADS, HEAD)
    value_h = low(value_lin).reshape(count, HEADS, HEAD)
    block_rows = min(512, count)
    blocks = count // block_rows
    score_scale = HEAD ** (-0.5)

    def attend_block(args):
        query_blk, doc_blk, index_blk = args
        scores = low_back(score_scale * jnp.einsum('qhd,khd->qhk', query_blk, key_h, precision=HIGH))
        allowed = (doc_blk[:, None] == doc_ids[None, :]) & (tok_index[None, :] <= index_blk[:, None])
        scores = jnp.where(allowed[:, None, :], scores, -1e+30)
        weights = low(jax.nn.softmax(scores, axis=-1))
        return jnp.einsum('qhk,khd->qhd', weights, value_h, precision=HIGH)
    attended = lax.map(jax.checkpoint(attend_block), (query_h.reshape(blocks, block_rows, HEADS, HEAD), doc_ids.reshape(blocks, block_rows), tok_index.reshape(blocks, block_rows)))
    attended = attended.reshape(count, HEADS * HEAD)
    attended_low = low(low_back(attended))
    attn_branch = low_back(jnp.dot(attended_low, u_out, precision=HIGH))
    state_mid = residual_mix(x_row, attn_branch, alpha_attn)
    mid_low = low(state_mid)
    up_lin = low_back(jnp.dot(mid_low, u_up, precision=HIGH))
    gate_lin = low_back(jnp.dot(mid_low, u_gate, precision=HIGH))
    gated_low = low(gating(up_lin, gate_lin, up_scale, gate_scale))
    mlp_branch = low_back(jnp.dot(gated_low, u_down, precision=HIGH))
    return residual_mix(state_mid, mlp_branch, alpha_mlp)

def reference(states, lengths, w_query, w_key, w_value, w_out, w_up, w_gate, w_down, qk_scale, up_scale, gate_scale, alpha_attn, alpha_mlp, d_out):

    def forward(x_all, wq_f, wk_f, wv_f, wo_f, wu_f, wg_f, wd_f, qk_f, up_f, gate_f, attn_f, mlp_f):
        units = (low(normalized(wq_f, 0)), low(normalized(wk_f, 0)), low(normalized(wv_f, 0)), low(normalized(wo_f, 1)), low(normalized(wu_f, 0)), low(normalized(wg_f, 0)), low(normalized(wd_f, 1)))

        def one_row(row):
            return row_layer(row[0], row[1], units, qk_f, up_f, gate_f, attn_f, mlp_f)
        return lax.map(one_row, (x_all, lengths))
    output, pullback = jax.vjp(forward, states.astype(jnp.float32), w_query.astype(jnp.float32), w_key.astype(jnp.float32), w_value.astype(jnp.float32), w_out.astype(jnp.float32), w_up.astype(jnp.float32), w_gate.astype(jnp.float32), w_down.astype(jnp.float32), qk_scale.astype(jnp.float32), up_scale.astype(jnp.float32), gate_scale.astype(jnp.float32), alpha_attn.astype(jnp.float32), alpha_mlp.astype(jnp.float32))
    grads = pullback(d_out.astype(jnp.float32))
    return (output, grads[0], grads[1], grads[2], grads[3], grads[4], grads[5], grads[6], grads[7], grads[8], grads[9], grads[10], grads[11], grads[12])
```

```python
import jax
import jax.numpy as jnp
import numpy as np
from jax import lax
from jax.experimental import pallas as pl
from jax.experimental.pallas import tpu as pltpu
from jax.sharding import PartitionSpec as P

HEADS = 16
HEAD = 64


EPS = 1e-06


def shifted(value, axis, steps):
    count = lax.axis_size(axis)
    first, last = (max(0, -steps), min(count, count - steps))
    return lax.ppermute(value, axis, [(source, source + steps) for source in range(first, last)])


def shifted_2(block, axis, distance):
    devices = range(lax.axis_size(axis))
    route = [((i - distance) % len(devices), i) for i in devices]
    return lax.ppermute(block, axis, route)


def normalized(weight, axis):
    wide = weight.astype(jnp.float32)
    return wide * lax.rsqrt(jnp.sum(wide * wide, axis=axis, keepdims=True) + EPS)


def rms(values):
    return values * lax.rsqrt(jnp.mean(values * values, axis=-1, keepdims=True) + EPS)


def doc_layout(len_row, tok_index):
    docs = jnp.arange(len_row.shape[0])
    starts = jnp.sum(jnp.where(docs[:, None] < docs[None, :], len_row[:, None], 0), axis=0)
    started = starts[None, :] <= tok_index[:, None]
    doc_ids = jnp.sum(started.astype(jnp.int32), axis=1) - 1
    first_tok = jnp.max(jnp.where(started, starts[None, :], 0), axis=1)
    return (doc_ids, tok_index - first_tok)


def rope(values, position):
    half = values.shape[-1] // 2
    freqs = 10000.0 ** (-jnp.arange(half, dtype=jnp.float32) / half)
    angle = position.astype(jnp.float32)[:, None] * freqs[None, :]
    cosine = jnp.cos(angle)[:, None, :]
    sine = jnp.sin(angle)[:, None, :]
    first = values[..., :half]
    second = values[..., half:]
    return jnp.concatenate(
        [first * cosine - second * sine, first * sine + second * cosine], axis=-1
    )


def prepare(linear, position, gain):
    count = linear.shape[0]
    shaped = linear.reshape(count, HEADS, HEAD)
    turned = rms(rope(shaped, position)) * gain.reshape(HEADS, HEAD)
    return turned.reshape(count, HEADS * HEAD)


def residual_mix(state, branch, alpha):
    return rms(state + alpha * (rms(branch) - state))


def gating(up_lin, gate_lin, up_scale, gate_scale):
    return up_scale * up_lin * jax.nn.silu(gate_scale * gate_lin)


def unit_back(raw_shard, grad_shard, axis):
    primal, pullback = jax.vjp(
        lambda weight: normalized(weight, axis), raw_shard.astype(jnp.float32)
    )
    return pullback(grad_shard)[0]


def on_device_general(
    states,
    lengths,
    w_query,
    w_key,
    w_value,
    w_out,
    w_up,
    w_gate,
    w_down,
    qk_scale,
    up_scale,
    gate_scale,
    alpha_attn,
    alpha_mlp,
    d_out,
):
    seq_count = lax.axis_size("seq")
    my_index = lax.axis_index("seq")
    rows = states.shape[0]
    tok = states.shape[1]
    width = states.shape[2]
    flat = rows * tok
    score_scale = HEAD ** (-0.5)
    row_layout = jax.vmap(doc_layout, in_axes=(0, None))
    unit_query = normalized(w_query, 0).astype(jnp.bfloat16)
    unit_key = normalized(w_key, 0).astype(jnp.bfloat16)
    unit_value = normalized(w_value, 0).astype(jnp.bfloat16)
    unit_out = normalized(w_out, 1).astype(jnp.bfloat16)
    unit_up = normalized(w_up, 0).astype(jnp.bfloat16)
    unit_gate = normalized(w_gate, 0).astype(jnp.bfloat16)
    unit_down = normalized(w_down, 1).astype(jnp.bfloat16)
    full_weights = (
        lax.all_gather(unit_query, "seq", axis=1, tiled=True),
        lax.all_gather(unit_key, "seq", axis=1, tiled=True),
        lax.all_gather(unit_value, "seq", axis=1, tiled=True),
        lax.all_gather(unit_out, "seq", axis=0, tiled=True),
        lax.all_gather(unit_up, "seq", axis=1, tiled=True),
        lax.all_gather(unit_gate, "seq", axis=1, tiled=True),
        lax.all_gather(unit_down, "seq", axis=0, tiled=True),
    )
    full_query, full_key, full_value, full_out, full_up, full_gate, full_down = full_weights
    tok_index = my_index * tok + jnp.arange(tok, dtype=jnp.int32)
    doc_ids, position = row_layout(lengths, tok_index)
    flat_pos = position.reshape(flat)
    state_in = states.reshape(flat, width)
    x_low = state_in.astype(jnp.bfloat16)
    query_lin = jnp.dot(x_low, full_query, preferred_element_type=jnp.float32)
    key_lin = jnp.dot(x_low, full_key, preferred_element_type=jnp.float32)
    value_lin = jnp.dot(x_low, full_value, preferred_element_type=jnp.float32)

    def front(query_part, key_part, gain):
        return (prepare(query_part, flat_pos, gain), prepare(key_part, flat_pos, gain))

    query_f, key_f = front(query_lin, key_lin, qk_scale)
    query_h = query_f.astype(jnp.bfloat16).reshape(rows, tok, HEADS, HEAD)
    key_h = key_f.astype(jnp.bfloat16).reshape(rows, tok, HEADS, HEAD)
    value_h = value_lin.astype(jnp.bfloat16).reshape(rows, tok, HEADS, HEAD)

    def block_scores(key_blk, source):
        key_index = source * tok + jnp.arange(tok, dtype=jnp.int32)
        key_docs, key_pos = row_layout(lengths, key_index)
        scores = (
            jnp.einsum("bqhd,bkhd->bqhk", query_h, key_blk, preferred_element_type=jnp.float32)
            * score_scale
        )
        allowed = (doc_ids[:, :, None] == key_docs[:, None, :]) & (
            key_index[None, None, :] <= tok_index[None, :, None]
        )
        return (scores, allowed[:, :, None, :])

    def is_active(source):
        last_key = jnp.reshape(source * tok + tok - 1, (1,))
        last_doc, last_pos = row_layout(lengths, last_key)
        return (source <= my_index) & jnp.any(last_doc[:, 0] >= doc_ids[:, 0])

    def attend(running, key_blk, value_blk, source):

        def compute(carried):
            best, denom_sum, accum = carried
            scores, allowed = block_scores(key_blk, source)
            new_best = jnp.maximum(best, jnp.max(jnp.where(allowed, scores, -1e30), axis=3))
            weights = jnp.where(allowed, jnp.exp(scores - new_best[:, :, :, None]), 0.0)
            shrink = jnp.exp(best - new_best)
            denom_sum = denom_sum * shrink + jnp.sum(weights, axis=3)
            accum = accum * shrink[:, :, :, None] + jnp.einsum(
                "bqhk,bkhd->bqhd",
                weights.astype(jnp.bfloat16),
                value_blk,
                preferred_element_type=jnp.float32,
            )
            return (new_best, denom_sum, accum)

        return lax.cond(is_active(source), compute, lambda carried: carried, running)

    reach = seq_count - 1
    start_state = (
        jnp.full((rows, tok, HEADS), -1e30, jnp.float32),
        jnp.zeros((rows, tok, HEADS), jnp.float32),
        jnp.zeros((rows, tok, HEADS, HEAD), jnp.float32),
    )
    first_state = attend(start_state, key_h, value_h, my_index)

    def cycle_step(step, loop_carry):
        running, key_blk, value_blk = loop_carry
        key_blk, value_blk = shifted((key_blk, value_blk), "seq", 1)
        source = (my_index - step) % seq_count
        return (attend(running, key_blk, value_blk, source), key_blk, value_blk)

    final_state, spent_key, spent_value = lax.fori_loop(
        1, reach + 1, cycle_step, (first_state, key_h, value_h)
    )
    best, denom_sum, accum = final_state
    attended = accum / denom_sum[:, :, :, None]
    log_sum = best + jnp.log(denom_sum)
    attended_low = attended.astype(jnp.bfloat16).reshape(flat, width)
    attn_branch = jnp.dot(attended_low, full_out, preferred_element_type=jnp.float32)
    state_mid = residual_mix(state_in, attn_branch, alpha_attn)
    mid_low = state_mid.astype(jnp.bfloat16)
    up_lin = jnp.dot(mid_low, full_up, preferred_element_type=jnp.float32)
    gate_lin = jnp.dot(mid_low, full_gate, preferred_element_type=jnp.float32)
    gated_low = gating(up_lin, gate_lin, up_scale, gate_scale).astype(jnp.bfloat16)
    mlp_branch = jnp.dot(gated_low, full_down, preferred_element_type=jnp.float32)
    output = residual_mix(state_mid, mlp_branch, alpha_mlp)
    back_weights = (
        lax.all_gather(unit_query, "seq", axis=1, tiled=True),
        lax.all_gather(unit_key, "seq", axis=1, tiled=True),
        lax.all_gather(unit_value, "seq", axis=1, tiled=True),
        lax.all_gather(unit_out, "seq", axis=0, tiled=True),
        lax.all_gather(unit_up, "seq", axis=1, tiled=True),
        lax.all_gather(unit_gate, "seq", axis=1, tiled=True),
        lax.all_gather(unit_down, "seq", axis=0, tiled=True),
    )
    back_query, back_key, back_value, back_out, back_up, back_gate, back_down = back_weights
    primal, pull_mlp = jax.vjp(residual_mix, state_mid, mlp_branch, alpha_mlp)
    d_mid, d_mlp, g_alpha_mlp = pull_mlp(d_out.reshape(flat, width))
    d_mlp_low = d_mlp.astype(jnp.bfloat16)
    grad_down = jnp.einsum("tf,td->fd", gated_low, d_mlp_low, preferred_element_type=jnp.float32)
    d_gated = jnp.einsum("td,fd->tf", d_mlp_low, back_down, preferred_element_type=jnp.float32)
    primal, pull_gate = jax.vjp(gating, up_lin, gate_lin, up_scale, gate_scale)
    d_up, d_gate, g_up_scale, g_gate_scale = pull_gate(d_gated)
    d_up_low = d_up.astype(jnp.bfloat16)
    d_gate_low = d_gate.astype(jnp.bfloat16)
    grad_up = jnp.einsum("tc,tf->cf", mid_low, d_up_low, preferred_element_type=jnp.float32)
    grad_gate = jnp.einsum("tc,tf->cf", mid_low, d_gate_low, preferred_element_type=jnp.float32)
    d_mid = d_mid + jnp.einsum("tf,cf->tc", d_up_low, back_up, preferred_element_type=jnp.float32)
    d_mid = d_mid + jnp.einsum(
        "tf,cf->tc", d_gate_low, back_gate, preferred_element_type=jnp.float32
    )
    primal, pull_attn = jax.vjp(residual_mix, state_in, attn_branch, alpha_attn)
    d_state, d_attn, g_alpha_attn = pull_attn(d_mid)
    d_attn_low = d_attn.astype(jnp.bfloat16)
    grad_out = jnp.einsum("tc,td->cd", attended_low, d_attn_low, preferred_element_type=jnp.float32)
    d_attended = jnp.einsum("td,cd->tc", d_attn_low, back_out, preferred_element_type=jnp.float32)
    d_att_low = d_attended.astype(jnp.bfloat16).reshape(rows, tok, HEADS, HEAD)
    delta = jnp.sum(d_att_low.astype(jnp.float32) * attended, axis=3)

    def attend_back(d_query, key_blk, value_blk, d_key, d_value, source):

        def compute(carried):
            d_query, d_key, d_value = carried
            scores, allowed = block_scores(key_blk, source)
            probs = jnp.where(allowed, jnp.exp(scores - log_sum[:, :, :, None]), 0.0)
            d_probs = jnp.einsum(
                "bqhd,bkhd->bqhk", d_att_low, value_blk, preferred_element_type=jnp.float32
            )
            d_scores = (probs * (d_probs - delta[:, :, :, None])).astype(jnp.bfloat16)
            d_query = d_query + jnp.einsum(
                "bqhk,bkhd->bqhd", d_scores, key_blk, preferred_element_type=jnp.float32
            )
            d_key = d_key + jnp.einsum(
                "bqhk,bqhd->bkhd", d_scores, query_h, preferred_element_type=jnp.float32
            )
            d_value = d_value + jnp.einsum(
                "bqhk,bqhd->bkhd",
                probs.astype(jnp.bfloat16),
                d_att_low,
                preferred_element_type=jnp.float32,
            )
            return (d_query, d_key, d_value)

        return lax.cond(
            is_active(source), compute, lambda carried: carried, (d_query, d_key, d_value)
        )

    def back_step(step, loop_carry):
        d_query, key_blk, value_blk, d_key, d_value = loop_carry
        source = (my_index - step) % seq_count
        d_query, d_key, d_value = attend_back(d_query, key_blk, value_blk, d_key, d_value, source)
        d_key, d_value = (
            shifted_2(d_key.astype(jnp.bfloat16), "seq", 1).astype(d_key.dtype),
            shifted_2(d_value.astype(jnp.bfloat16), "seq", 1).astype(d_value.dtype),
        )
        key_blk, value_blk = shifted((key_blk, value_blk), "seq", 1)
        return (d_query, key_blk, value_blk, d_key, d_value)

    zero_heads = jnp.zeros((rows, tok, HEADS, HEAD), jnp.float32)
    d_query_h, last_key_blk, last_value_blk, d_key_h, d_value_h = lax.fori_loop(
        0, reach, back_step, (zero_heads, key_h, value_h, zero_heads, zero_heads)
    )
    d_query_h, d_key_h, d_value_h = attend_back(
        d_query_h, last_key_blk, last_value_blk, d_key_h, d_value_h, (my_index - reach) % seq_count
    )
    d_key_h, d_value_h = (
        shifted_2(d_key_h.astype(jnp.bfloat16), "seq", -reach).astype(d_key_h.dtype),
        shifted_2(d_value_h.astype(jnp.bfloat16), "seq", -reach).astype(d_value_h.dtype),
    )
    primal, pull_front = jax.vjp(front, query_lin, key_lin, qk_scale)
    d_query_lin, d_key_lin, g_qk_scale = pull_front(
        (d_query_h.reshape(flat, width) * score_scale, d_key_h.reshape(flat, width) * score_scale)
    )
    d_query_low = d_query_lin.astype(jnp.bfloat16)
    d_key_low = d_key_lin.astype(jnp.bfloat16)
    d_value_low = d_value_h.reshape(flat, width).astype(jnp.bfloat16)
    grad_query = jnp.einsum("tc,tj->cj", x_low, d_query_low, preferred_element_type=jnp.float32)
    grad_key = jnp.einsum("tc,tj->cj", x_low, d_key_low, preferred_element_type=jnp.float32)
    grad_value = jnp.einsum("tc,tj->cj", x_low, d_value_low, preferred_element_type=jnp.float32)
    d_state = d_state + jnp.einsum(
        "tj,cj->tc", d_query_low, back_query, preferred_element_type=jnp.float32
    )
    d_state = d_state + jnp.einsum(
        "tj,cj->tc", d_key_low, back_key, preferred_element_type=jnp.float32
    )
    d_state = d_state + jnp.einsum(
        "tj,cj->tc", d_value_low, back_value, preferred_element_type=jnp.float32
    )
    shards = (
        lax.psum_scatter(
            grad_query.astype(jnp.bfloat16), "seq", scatter_dimension=1, tiled=True
        ).astype(jnp.float32),
        lax.psum_scatter(
            grad_key.astype(jnp.bfloat16), "seq", scatter_dimension=1, tiled=True
        ).astype(jnp.float32),
        lax.psum_scatter(
            grad_value.astype(jnp.bfloat16), "seq", scatter_dimension=1, tiled=True
        ).astype(jnp.float32),
        lax.psum_scatter(
            grad_out.astype(jnp.bfloat16), "seq", scatter_dimension=0, tiled=True
        ).astype(jnp.float32),
        lax.psum_scatter(
            grad_up.astype(jnp.bfloat16), "seq", scatter_dimension=1, tiled=True
        ).astype(jnp.float32),
        lax.psum_scatter(
            grad_gate.astype(jnp.bfloat16), "seq", scatter_dimension=1, tiled=True
        ).astype(jnp.float32),
        lax.psum_scatter(
            grad_down.astype(jnp.bfloat16), "seq", scatter_dimension=0, tiled=True
        ).astype(jnp.float32),
    )
    summed = (
        lax.psum(shards[0].astype(jnp.bfloat16), "batch").astype(jnp.float32),
        lax.psum(shards[1].astype(jnp.bfloat16), "batch").astype(jnp.float32),
        lax.psum(shards[2].astype(jnp.bfloat16), "batch").astype(jnp.float32),
        lax.psum(shards[3].astype(jnp.bfloat16), "batch").astype(jnp.float32),
        lax.psum(shards[4].astype(jnp.bfloat16), "batch").astype(jnp.float32),
        lax.psum(shards[5].astype(jnp.bfloat16), "batch").astype(jnp.float32),
        lax.psum(shards[6].astype(jnp.bfloat16), "batch").astype(jnp.float32),
    )
    gain_grads = lax.psum(
        (g_qk_scale, g_up_scale, g_gate_scale, g_alpha_attn, g_alpha_mlp), ("seq", "batch")
    )
    g_query = unit_back(w_query, summed[0], 0)
    g_key = unit_back(w_key, summed[1], 0)
    g_value = unit_back(w_value, summed[2], 0)
    g_out = unit_back(w_out, summed[3], 1)
    g_up = unit_back(w_up, summed[4], 0)
    g_gate = unit_back(w_gate, summed[5], 0)
    g_down = unit_back(w_down, summed[6], 1)
    return (
        output.reshape(rows, tok, width),
        d_state.reshape(rows, tok, width),
        g_query,
        g_key,
        g_value,
        g_out,
        g_up,
        g_gate,
        g_down,
        gain_grads[0],
        gain_grads[1],
        gain_grads[2],
        gain_grads[3],
        gain_grads[4],
    )


BF16 = jnp.bfloat16
F32 = jnp.float32
LANES = 128
MIB = 1 << 20
NT = (((1,), (1,)), ((), ()))
TN = (((0,), (0,)), ((), ()))


def place():
    s = lax.axis_index("seq")
    return s // 4, (s // 2) % 2, s % 2, lax.axis_index("batch")


def dev(z, x, c, y):
    return (z * 4 + x * 2 + c, y)


def remote(src, dst, send, recv, device):
    return pltpu.make_async_remote_copy(
        src_ref=src,
        dst_ref=dst,
        send_sem=send,
        recv_sem=recv,
        device_id=device,
        device_id_type=pl.DeviceIdType.MESH,
    )


def greet(fixed, line=True):
    z, x, c, y = place()
    bar = pltpu.get_barrier_semaphore()
    for device in fixed:
        pl.semaphore_signal(bar, inc=1, device_id=device, device_id_type=pl.DeviceIdType.MESH)
    count = len(fixed)
    if line:
        for step in (-1, 1):

            @pl.when((z + step >= 0) & (z + step < 4))
            def _():
                pl.semaphore_signal(
                    bar,
                    inc=1,
                    device_id=dev(z + step, x, c, y),
                    device_id_type=pl.DeviceIdType.MESH,
                )

        count = count + jnp.where((z == 0) | (z == 3), 1, 2)
    pl.semaphore_wait(bar, count)


def dot(a, b):
    return jnp.dot(a, b, preferred_element_type=F32)


def dot_nt(a, b):
    return lax.dot_general(a, b, NT, preferred_element_type=F32)


def dot_tn(a, b):
    return lax.dot_general(a, b, TN, preferred_element_type=F32)


def row_gather_body(buf, recv, zsend, xsend, csend, visit):
    z, x, c, y = place()

    def slot(zz, xx, cc):
        return zz * 4 + xx * 2 + cc

    def forward_z(zz, step):
        b = slot(zz, x, c)
        return remote(
            buf.at[b], buf.at[b], zsend.at[zz, (step + 1) // 2], recv.at[b], dev(z + step, x, c, y)
        )

    def forward_x(zz):
        b = slot(zz, x, c)
        return remote(buf.at[b], buf.at[b], xsend.at[zz], recv.at[b], dev(z, 1 - x, c, y))

    def forward_c(zz, xx):
        b = slot(zz, xx, c)
        return remote(buf.at[b], buf.at[b], csend.at[zz, xx], recv.at[b], dev(z, x, 1 - c, y))

    def arrived(zz, xx, cc):
        b = slot(zz, xx, cc)
        remote(buf.at[b], buf.at[b], csend.at[0, 0], recv.at[b], dev(z, x, 1 - c, y)).wait_recv()

    def inside(v):
        return (v >= 0) & (v < 4)

    for step in (-1, 1):

        @pl.when(inside(z + step))
        def _():
            forward_z(z, step).start()

    forward_x(z).start()
    forward_c(z, x).start()
    visit(slot(z, x, c))
    for k in range(0, 4):
        for way in (-1, 1):
            if k > 0:
                zz = z - way * k

                @pl.when(inside(zz))
                def _():
                    arrived(zz, x, c)

                    @pl.when(inside(z + way))
                    def _():
                        forward_z(zz, way).start()

                    forward_x(zz).start()
                    forward_c(zz, x).start()
                    visit(slot(zz, x, c))

        for way in (-1, 1) if k > 0 else (1,):
            zz = z - way * k

            @pl.when(inside(zz))
            def _():
                arrived(zz, 1 - x, c)
                forward_c(zz, 1 - x).start()
                visit(slot(zz, 1 - x, c))

                arrived(zz, x, 1 - c)
                visit(slot(zz, x, 1 - c))

                arrived(zz, 1 - x, 1 - c)
                visit(slot(zz, 1 - x, 1 - c))

    for zz in range(4):
        for step in (-1, 1):
            own_or_passing = (zz <= z) if step > 0 else (zz >= z)

            @pl.when(own_or_passing & inside(z + step))
            def _():
                forward_z(zz, step).wait_send()

        forward_x(zz).wait_send()
        for xx in range(2):
            forward_c(zz, xx).wait_send()


ROW_GATHER_SEMS = [
    pltpu.SemaphoreType.DMA((16,)),
    pltpu.SemaphoreType.DMA((4, 2)),
    pltpu.SemaphoreType.DMA((4,)),
    pltpu.SemaphoreType.DMA((4, 2)),
]


def greet_row_near():
    z, x, c, y = place()
    greet([dev(z, 1 - x, c, y), dev(z, x, 1 - c, y)])


def row_gather_kernel(x_ref, out_ref, copy_sem, *sems):
    z, x, c, y = place()
    own = pltpu.make_async_copy(x_ref, out_ref.at[z * 4 + x * 2 + c], copy_sem)
    own.start()
    greet_row_near()
    own.wait()
    row_gather_body(out_ref, *sems, lambda slot: None)


def row_gather(value, cid):
    return pl.pallas_call(
        row_gather_kernel,
        name="row_gather",
        out_shape=jax.ShapeDtypeStruct((16,) + value.shape, value.dtype),
        in_specs=[pl.BlockSpec(memory_space=pl.ANY)],
        out_specs=pl.BlockSpec(memory_space=pl.ANY),
        scratch_shapes=[pltpu.SemaphoreType.DMA] + ROW_GATHER_SEMS,
        compiler_params=pltpu.CompilerParams(collective_id=cid, has_side_effects=True),
    )(value)


def line_gather_body(buf, recv, zsend, visit):
    z, x, c, y = place()

    def inside(v):
        return (v >= 0) & (v < 4)

    def forward(zz, step):
        return remote(
            buf.at[zz], buf.at[zz], zsend.at[zz, (step + 1) // 2], recv.at[zz], dev(z + step, x, c, y)
        )

    for step in (-1, 1):

        @pl.when(inside(z + step))
        def _():
            forward(z, step).start()

    visit(z)
    for k in range(1, 4):
        for way in (-1, 1):
            zz = z - way * k

            @pl.when(inside(zz))
            def _():
                remote(
                    buf.at[zz], buf.at[zz], zsend.at[0, 0], recv.at[zz], dev(z - way, x, c, y)
                ).wait_recv()

                @pl.when(inside(z + way))
                def _():
                    forward(zz, way).start()

                visit(zz)

    for zz in range(4):
        for step in (-1, 1):
            own_or_passing = (zz <= z) if step > 0 else (zz >= z)

            @pl.when(own_or_passing & inside(z + step))
            def _():
                forward(zz, step).wait_send()


LINE_SEMS = [pltpu.SemaphoreType.DMA((4,)), pltpu.SemaphoreType.DMA((4, 2))]


def line_gather_kernel(x_ref, out_ref, *sems):
    z, x, c, y = place()
    greet([])
    out_ref[z] = x_ref[...]
    line_gather_body(out_ref, *sems, lambda zz: None)


def line_gather(value, cid):
    return pl.pallas_call(
        line_gather_kernel,
        name="line_gather",
        out_shape=jax.ShapeDtypeStruct((4,) + value.shape, value.dtype),
        in_specs=[pl.BlockSpec(memory_space=pltpu.VMEM)],
        out_specs=pl.BlockSpec(memory_space=pltpu.VMEM),
        scratch_shapes=LINE_SEMS,
        compiler_params=pltpu.CompilerParams(
            collective_id=cid, has_side_effects=True, vmem_limit_bytes=16 * MIB
        ),
    )(value)


def line_reduce_kernel(p_ref, out_ref, passing, landed, send, recv):
    z, x, c, y = place()
    greet([])

    def inside(v):
        return (v >= 0) & (v < 4)

    def hop(owner, way):
        d = (way + 1) // 2
        return remote(
            passing.at[owner],
            landed.at[owner, d],
            send.at[owner],
            recv.at[owner, d],
            dev(z + way, x, c, y),
        )

    for k in range(3, 0, -1):
        for way in (-1, 1):
            owner = z + way * k
            d = (way + 1) // 2

            @pl.when(inside(owner))
            def _():
                @pl.when(inside(z - way))
                def _():
                    hop(owner, way).wait_recv()
                    passing[owner] = (
                        p_ref[owner].astype(F32) + landed[owner, d].astype(F32)
                    ).astype(BF16)

                @pl.when(jnp.logical_not(inside(z - way)))
                def _():
                    passing[owner] = p_ref[owner].astype(BF16)

                hop(owner, way).start()

    out_ref[...] = p_ref[z].astype(F32)
    for way in (-1, 1):
        d = (way + 1) // 2

        @pl.when(inside(z - way))
        def _():
            remote(
                passing.at[z], landed.at[z, d], send.at[z], recv.at[z, d], dev(z - way, x, c, y)
            ).wait_recv()
            out_ref[...] += landed[z, d].astype(F32)

    for owner in range(4):

        @pl.when(owner != z)
        def _():
            way = jnp.where(owner > z, 1, -1)
            remote(
                passing.at[owner],
                landed.at[owner, 0],
                send.at[owner],
                recv.at[owner, 0],
                dev(z + way, x, c, y),
            ).wait_send()


def line_reduce(parts, cid):
    shape = parts.shape[1:]
    return pl.pallas_call(
        line_reduce_kernel,
        name="line_reduce",
        out_shape=jax.ShapeDtypeStruct(shape, F32),
        in_specs=[pl.BlockSpec(memory_space=pltpu.VMEM)],
        out_specs=pl.BlockSpec(memory_space=pltpu.VMEM),
        scratch_shapes=[
            pltpu.VMEM((4,) + shape, BF16),
            pltpu.VMEM((4, 2) + shape, BF16),
            pltpu.SemaphoreType.DMA((4,)),
            pltpu.SemaphoreType.DMA((4, 2)),
        ],
        compiler_params=pltpu.CompilerParams(
            collective_id=cid, has_side_effects=True, vmem_limit_bytes=32 * MIB
        ),
    )(parts)


def group_gather_kernel(up_ref, gate_ref, down_ref, ups, gates, downs, copies, xs, cs, rx, rc):
    z, x, c, y = place()
    width = up_ref.shape[1]

    def cols(slot):
        return pl.ds(pl.multiple_of(slot * width, width), width)

    def views(slot):
        return (ups.at[:, cols(slot)], gates.at[:, cols(slot)], downs.at[cols(slot), :])

    mine = 2 * x + c
    local = [
        pltpu.make_async_copy(src, dst, copies.at[i])
        for i, (src, dst) in enumerate(zip((up_ref, gate_ref, down_ref), views(mine)))
    ]
    for copy in local:
        copy.start()
    greet([dev(z, 1 - x, c, y), dev(z, x, 1 - c, y)], False)
    own = (up_ref, gate_ref, down_ref)
    to_x = [
        remote(own[i], views(mine)[i], xs.at[i], rx.at[i], dev(z, 1 - x, c, y)) for i in range(3)
    ]
    to_c = [
        remote(own[i], views(mine)[i], cs.at[i], rc.at[i], dev(z, x, 1 - c, y)) for i in range(3)
    ]
    for copy in to_x + to_c:
        copy.start()
    other = 2 * (1 - x) + c
    from_x = views(other)
    onward = [
        remote(from_x[i], from_x[i], cs.at[3 + i], rc.at[3 + i], dev(z, x, 1 - c, y))
        for i in range(3)
    ]
    for i in range(3):
        remote(own[i], from_x[i], xs.at[i], rx.at[i], dev(z, 1 - x, c, y)).wait_recv()
        onward[i].start()
    for i in range(3):
        to_x[i].wait_send()
        to_c[i].wait()
        onward[i].wait()
        local[i].wait()


def group_gather(up, gate, down, cid):
    depth, width = up.shape
    hbm = pl.BlockSpec(memory_space=pl.ANY)
    return pl.pallas_call(
        group_gather_kernel,
        name="group_gather",
        out_shape=(
            jax.ShapeDtypeStruct((depth, 4 * width), BF16),
            jax.ShapeDtypeStruct((depth, 4 * width), BF16),
            jax.ShapeDtypeStruct((4 * width, depth), BF16),
        ),
        in_specs=[hbm] * 3,
        out_specs=(hbm,) * 3,
        scratch_shapes=[
            pltpu.SemaphoreType.DMA((3,)),
            pltpu.SemaphoreType.DMA((3,)),
            pltpu.SemaphoreType.DMA((6,)),
            pltpu.SemaphoreType.DMA((3,)),
            pltpu.SemaphoreType.DMA((6,)),
        ],
        compiler_params=pltpu.CompilerParams(collective_id=cid, has_side_effects=True),
    )(up, gate, down)


def group_reduce_kernel(gu, gg, gd, ou, og, od, *scratch):
    z, x, c, y = place()
    width = ou.shape[1]
    grads = (gu, gg, gd)
    outs = (ou, og, od)
    land_c, sums, land_x, land_y = scratch[0:3], scratch[3:6], scratch[6:9], scratch[9:12]
    sc, rc, sx, rx, sy, ry = scratch[12:18]

    def part(i, slot):
        window = pl.ds(pl.multiple_of(slot * width, width), width)
        return grads[i].at[window, :] if i == 2 else grads[i].at[:, window]

    greet([dev(z, 1 - x, c, y), dev(z, x, 1 - c, y), dev(z, x, c, 1 - y)], False)
    copies_c = [
        remote(
            part(i, 2 * (1 - x if h == 0 else x) + 1 - c),
            land_c[i].at[h],
            sc.at[i, h],
            rc.at[i, h],
            dev(z, x, 1 - c, y),
        )
        for h in range(2)
        for i in range(3)
    ]
    for copy in copies_c:
        copy.start()
    copies_x = [
        remote(sums[i].at[0], land_x[i], sx.at[i], rx.at[i], dev(z, 1 - x, c, y)) for i in range(3)
    ]
    copies_y = [
        remote(sums[i].at[1], land_y[i], sy.at[i], ry.at[i], dev(z, x, c, 1 - y)) for i in range(3)
    ]
    for h in range(2):
        for i in range(3):
            copies_c[h * 3 + i].wait_recv()
            mine = part(i, 2 * (1 - x if h == 0 else x) + c)
            sums[i][h] = (mine[...].astype(F32) + land_c[i][h].astype(F32)).astype(BF16)
            if h == 0:
                copies_x[i].start()
    for i in range(3):
        copies_x[i].wait_recv()
        sums[i][1] = (sums[i][1].astype(F32) + land_x[i][...].astype(F32)).astype(BF16)
        copies_y[i].start()
    for i in range(3):
        copies_y[i].wait_recv()
        outs[i][...] = sums[i][1].astype(F32) + land_y[i][...].astype(F32)
    for copy in copies_c + copies_x + copies_y:
        copy.wait_send()


def group_reduce(gu, gg, gd, cid):
    depth = gu.shape[0]
    width = gu.shape[1] // 4
    vmem = pl.BlockSpec(memory_space=pltpu.VMEM)
    shapes = ((depth, width), (depth, width), (width, depth))
    return pl.pallas_call(
        group_reduce_kernel,
        name="group_reduce",
        out_shape=tuple(jax.ShapeDtypeStruct(shape, F32) for shape in shapes),
        in_specs=[vmem] * 3,
        out_specs=(vmem,) * 3,
        scratch_shapes=[pltpu.VMEM((2,) + shape, BF16) for shape in shapes]
        + [pltpu.VMEM((2,) + shape, BF16) for shape in shapes]
        + [pltpu.VMEM(shape, BF16) for shape in shapes]
        + [pltpu.VMEM(shape, BF16) for shape in shapes]
        + [pltpu.SemaphoreType.DMA((3, 2))] * 2
        + [pltpu.SemaphoreType.DMA((3,))] * 4,
        compiler_params=pltpu.CompilerParams(
            collective_id=cid, has_side_effects=True, vmem_limit_bytes=56 * MIB
        ),
    )(gu, gg, gd)


def exchange_kernel(x_ref, out_ref, copy_sem, send, recv):
    z, x, c, y = place()
    s = z * 4 + x * 2 + c
    own = pltpu.make_async_copy(x_ref.at[s], out_ref.at[s], copy_sem)
    own.start()
    bar = pltpu.get_barrier_semaphore()

    def turn(k):
        return (s + k) % 16

    @pl.loop(1, 16)
    def _(k):
        pl.semaphore_signal(
            bar, inc=1, device_id=(turn(k), y), device_id_type=pl.DeviceIdType.MESH
        )

    pl.semaphore_wait(bar, 15)

    @pl.loop(1, 16)
    def _(k):
        t = turn(k)
        remote(x_ref.at[t], out_ref.at[s], send.at[t], recv.at[s], (t, y)).start()

    own.wait()

    @pl.loop(1, 16)
    def _(k):
        t = turn(k)
        remote(x_ref.at[t], out_ref.at[t], send.at[t], recv.at[t], (t, y)).wait()


def exchange(value, cid):
    vmem = pl.BlockSpec(memory_space=pltpu.VMEM)
    return pl.pallas_call(
        exchange_kernel,
        name="exchange",
        out_shape=jax.ShapeDtypeStruct(value.shape, value.dtype),
        in_specs=[vmem],
        out_specs=vmem,
        scratch_shapes=[
            pltpu.SemaphoreType.DMA,
            pltpu.SemaphoreType.DMA((16,)),
            pltpu.SemaphoreType.DMA((16,)),
        ],
        compiler_params=pltpu.CompilerParams(
            collective_id=cid, has_side_effects=True, vmem_limit_bytes=8 * MIB
        ),
    )(value)


def pack(heads):
    half = heads.shape[1] // 2
    return jnp.concatenate([heads[:, :half], heads[:, half:]], axis=2)


def unpack(packed):
    return jnp.concatenate([packed[:, :, :HEAD], packed[:, :, HEAD:]], axis=1)


BLOCK = 256


def attend_kernel(q_ref, k_ref, v_ref, out_ref, qe_ref):
    count = q_ref.shape[0]
    row = lax.broadcasted_iota(jnp.int32, (BLOCK, BLOCK), 0)
    col = lax.broadcasted_iota(jnp.int32, (BLOCK, BLOCK), 1)
    causal = row >= col
    lane = lax.broadcasted_iota(jnp.int32, (BLOCK, LANES), 1)
    for i in range(count // BLOCK):
        rows = pl.ds(i * BLOCK, BLOCK)
        q = q_ref[rows, :]
        total = jnp.zeros((BLOCK, LANES), F32)
        for j in range(i + 1):
            keys = pl.ds(j * BLOCK, BLOCK)
            p = jnp.exp(dot_nt(q, k_ref[keys, :]))
            if i == j:
                p = jnp.where(causal, p, 0.0)
            total = total + dot(p.astype(BF16), v_ref[keys, :])
        denom = total[:, HEAD : HEAD + 1]
        out_ref[rows, :] = total / denom
        log = -jnp.log(denom)
        high = log.astype(BF16).astype(F32)
        rest = log - high
        qe_ref[rows, :] = jnp.where(
            lane == HEAD, high, jnp.where(lane == HEAD + 1, rest, q.astype(F32))
        ).astype(BF16)


def attend_heads(q, k, v):
    vmem = pl.BlockSpec(memory_space=pltpu.VMEM)
    return pl.pallas_call(
        attend_kernel,
        name="attend",
        out_shape=(jax.ShapeDtypeStruct(q.shape, F32), jax.ShapeDtypeStruct(q.shape, BF16)),
        in_specs=[vmem] * 3,
        out_specs=(vmem,) * 2,
        compiler_params=pltpu.CompilerParams(vmem_limit_bytes=32 * MIB),
    )(q, k, v)


def attend_back_kernel(q_ref, k_ref, v_ref, do_ref, dq_ref, dk_ref, dv_ref):
    count = q_ref.shape[0]
    row = lax.broadcasted_iota(jnp.int32, (BLOCK, BLOCK), 0)
    col = lax.broadcasted_iota(jnp.int32, (BLOCK, BLOCK), 1)
    causal = row <= col
    blocks = count // BLOCK
    for j in range(blocks):
        keys = pl.ds(j * BLOCK, BLOCK)
        k = k_ref[keys, :]
        v = v_ref[keys, :]
        dk = jnp.zeros((BLOCK, LANES), F32)
        dv = jnp.zeros((BLOCK, LANES), F32)
        for i in range(j, blocks):
            rows = pl.ds(i * BLOCK, BLOCK)
            q = q_ref[rows, :]
            do = do_ref[rows, :]
            p = jnp.exp(dot_nt(k, q))
            if i == j:
                p = jnp.where(causal, p, 0.0)
            ds = (p * dot_nt(v, do)).astype(BF16)
            dv = dv + dot(p.astype(BF16), do)
            dk = dk + dot(ds, q)
            dq = dot_tn(ds, k)
            if j == 0:
                dq_ref[rows, :] = dq
            else:
                dq_ref[rows, :] += dq
        dk_ref[keys, :] = dk
        dv_ref[keys, :] = dv


def attend_back_heads(q, k, v, do):
    vmem = pl.BlockSpec(memory_space=pltpu.VMEM)
    shape = jax.ShapeDtypeStruct(q.shape, F32)
    return pl.pallas_call(
        attend_back_kernel,
        name="attend_back",
        out_shape=(shape,) * 3,
        in_specs=[vmem] * 4,
        out_specs=(vmem,) * 3,
        compiler_params=pltpu.CompilerParams(vmem_limit_bytes=40 * MIB),
    )(q, k, v, do)


def inverse_norm(weight, axis):
    wide = weight.astype(F32)
    return lax.rsqrt(jnp.sum(wide * wide, axis=axis, keepdims=True) + EPS)


def unit_pull(weight, grad, axis):
    inverse = inverse_norm(weight, axis)
    unit = weight.astype(F32) * inverse
    return inverse * (grad - unit * jnp.sum(grad * unit, axis=axis, keepdims=True))


def turn_tables(count):
    half = HEAD // 2
    freqs = (10000.0 ** (-np.arange(half, dtype=np.float32) / half)).astype(np.float32)
    angle = np.arange(count, dtype=np.float32)[:, None] * freqs[None, :]
    cosine = np.cos(angle).astype(np.float32)
    sine = np.sin(angle).astype(np.float32)
    return np.tile(cosine, (1, 4)), np.concatenate([-sine, sine, -sine, sine], axis=1)


def swap_halves(value):
    half = HEAD // 2
    pieces = [value[:, k * half : (k + 1) * half] for k in (1, 0, 3, 2)]
    return jnp.concatenate(pieces, axis=1)


def head_mean(value):
    first = jnp.mean(value[:, :HEAD], axis=1, keepdims=True)
    second = jnp.mean(value[:, HEAD:], axis=1, keepdims=True)
    count = value.shape[0]
    return jnp.concatenate(
        [jnp.broadcast_to(first, (count, HEAD)), jnp.broadcast_to(second, (count, HEAD))], axis=1
    )


def mix(state, branch, alpha):
    inv_b = lax.rsqrt(jnp.mean(branch * branch, axis=-1, keepdims=True) + EPS)
    unit_b = branch * inv_b
    step = unit_b - state
    mixed = state + alpha * step
    inv_m = lax.rsqrt(jnp.mean(mixed * mixed, axis=-1, keepdims=True) + EPS)
    return mixed * inv_m, (unit_b, inv_b, step, inv_m)


def mix_back(grad, out, saved, alpha):
    unit_b, inv_b, step, inv_m = saved
    d_mixed = inv_m * (grad - out * jnp.mean(grad * out, axis=-1, keepdims=True))
    d_alpha = jnp.sum(d_mixed * step, axis=0)
    d_unit = d_mixed * alpha
    d_branch = inv_b * (d_unit - unit_b * jnp.mean(d_unit * unit_b, axis=-1, keepdims=True))
    return d_mixed - d_unit, d_branch, d_alpha


def pad_lanes(value, fill):
    count = value.shape[0]
    extra = jnp.concatenate(fill + [jnp.zeros((count, LANES - HEAD - len(fill)), F32)], axis=1)
    return jnp.concatenate([value.astype(F32), extra], axis=1).astype(BF16)


def on_device_heads(
    states,
    lengths,
    w_query,
    w_key,
    w_value,
    w_out,
    w_up,
    w_gate,
    w_down,
    qk_scale,
    up_scale,
    gate_scale,
    alpha_attn,
    alpha_mlp,
    d_out,
):
    s = lax.axis_index("seq")
    z, x, c, y = place()
    tok, width = states.shape[1:]
    count = 16 * tok
    state_in = states.reshape(tok, width)
    grad_out = d_out.reshape(tok, width)

    unit_qkv = jnp.concatenate(
        [normalized(w, 0).astype(BF16) for w in (w_query, w_key, w_value)], axis=1
    )
    unit_out = normalized(w_out, 1).astype(BF16)
    unit_up = normalized(w_up, 0).astype(BF16)
    unit_gate = normalized(w_gate, 0).astype(BF16)
    unit_down = normalized(w_down, 1).astype(BF16)

    x_all = row_gather(state_in.astype(BF16), 1).reshape(count, width)
    full_out = row_gather(unit_out, 2).reshape(width, width)
    full_qkv = row_gather(unit_qkv.T, 3).reshape(3 * width, width)
    ups, gates, downs = group_gather(unit_up, unit_gate, unit_down, 4)

    linear = dot(x_all, unit_qkv)
    cosine, sine = turn_tables(count)
    gain = lax.dynamic_slice(qk_scale, (s * HEAD,), (HEAD,))
    gains = jnp.concatenate([gain, gain])[None, :]
    turned = linear[:, :LANES] * cosine + swap_halves(linear[:, :LANES]) * sine
    inverse = lax.rsqrt(head_mean(turned * turned) + EPS)
    unit_qk = turned * inverse
    qk = (unit_qk * gains).astype(BF16)
    ones = jnp.ones((count, 1), F32)
    q_ext = pad_lanes(qk[:, :HEAD].astype(F32) * HEAD ** (-0.5), [])
    k_ext = pad_lanes(qk[:, HEAD:], [ones, ones])
    v_ext = pad_lanes(linear[:, LANES:].astype(BF16), [ones, ones])

    attended, q_back = attend_heads(q_ext, k_ext, v_ext)
    attended = attended[:, :HEAD]
    att_in = exchange(pack(attended.astype(BF16).reshape(16, tok, HEAD)), 5)
    att_low = unpack(att_in).transpose(1, 0, 2).reshape(tok, width)

    attn_branch = dot(att_low, full_out)
    state_mid, saved_attn = mix(state_in, attn_branch, alpha_attn)

    mid_all = line_gather(state_mid.astype(BF16), 6).reshape(4 * tok, width)
    units = ups.shape[1]
    up_gain = lax.dynamic_slice(up_scale, (z * units,), (units,))
    gate_gain = lax.dynamic_slice(gate_scale, (z * units,), (units,))
    up_lin = dot(mid_all, ups)
    gate_lin = dot(mid_all, gates) * gate_gain
    up_val = up_lin * up_gain
    sig = 1.0 / (1.0 + jnp.exp(-gate_lin))
    act = gate_lin * sig
    hidden = (up_val * act).astype(BF16)
    mlp_branch = line_reduce(dot(hidden, downs).astype(BF16).reshape(4, tok, width), 7)
    output, saved_mlp = mix(state_mid, mlp_branch, alpha_mlp)

    d_mid, d_mlp, g_alpha_mlp = mix_back(grad_out, output, saved_mlp, alpha_mlp)
    d_mlp_all = line_gather(d_mlp.astype(BF16), 8).reshape(4 * tok, width)
    d_hidden = dot_nt(d_mlp_all, downs)
    d_up_val = d_hidden * act
    d_gate_val = d_hidden * up_val * (sig * (1.0 + gate_lin * (1.0 - sig)))
    g_up_scale = jnp.sum(d_up_val * up_lin, axis=0)
    g_gate_scale = jnp.sum(d_gate_val * gate_lin, axis=0) / gate_gain
    d_up_low = (d_up_val * up_gain).astype(BF16)
    d_gate_low = (d_gate_val * gate_gain).astype(BF16)
    d_mid_part = dot_nt(d_up_low, ups) + dot_nt(d_gate_low, gates)
    d_mid = d_mid + line_reduce(d_mid_part.astype(BF16).reshape(4, tok, width), 9)
    grad_down = dot_tn(hidden, d_mlp_all).astype(BF16)
    grad_up = dot_tn(mid_all, d_up_low).astype(BF16)
    grad_gate = dot_tn(mid_all, d_gate_low).astype(BF16)

    d_state, d_attn, g_alpha_attn = mix_back(d_mid, state_mid, saved_attn, alpha_attn)
    d_attn_low = d_attn.astype(BF16)
    d_att = dot_nt(d_attn_low, full_out).astype(BF16)
    d_att_in = exchange(pack(d_att.reshape(tok, 16, HEAD).transpose(1, 0, 2)), 10)
    d_att_head = unpack(d_att_in).reshape(count, HEAD)
    delta = -jnp.sum(d_att_head.astype(F32) * attended, axis=1, keepdims=True)
    delta_high = delta.astype(BF16).astype(F32)
    do_ext = pad_lanes(d_att_head, [delta_high, delta - delta_high])

    d_q, d_k, d_v = attend_back_heads(q_back, k_ext, v_ext, do_ext)
    g_up_sum, g_gate_sum, g_down_sum = group_reduce(grad_up, grad_gate, grad_down, 11)
    grad_out_w = dot_tn(att_low, d_attn_low).astype(BF16)
    g_out_shard = lax.psum_scatter(grad_out_w, "seq", scatter_dimension=0, tiled=True)

    d_qk = jnp.concatenate([d_q[:, :HEAD] * HEAD ** (-0.5), d_k[:, :HEAD]], axis=1)
    g_qk = jnp.sum(d_qk * unit_qk, axis=0)
    d_unit = d_qk * gains
    d_turned = inverse * (d_unit - unit_qk * head_mean(d_unit * unit_qk))
    d_qk_low = (d_turned * cosine - swap_halves(d_turned) * sine).astype(BF16)
    d_lin = jnp.concatenate([d_qk_low, d_v[:, :HEAD].astype(BF16)], axis=1)
    grad_qkv = dot_tn(x_all, d_lin).astype(BF16)
    d_lin_pad = jnp.concatenate([d_lin, jnp.zeros((count, HEAD), BF16)], axis=1)
    d_lin_in = exchange(d_lin_pad.reshape(16, tok, 4 * HEAD), 12)
    d_lin_own = d_lin_in[:, :, : 3 * HEAD].transpose(1, 0, 2).reshape(tok, 3 * width)
    d_state = d_state + dot(d_lin_own, full_qkv)

    g_small = lax.psum(
        jnp.concatenate([grad_qkv, g_out_shard.reshape(width, HEAD)], axis=1), "batch"
    ).astype(F32)

    place_units = (z * units,)
    gains_full = jnp.concatenate(
        [
            lax.dynamic_update_slice(
                jnp.zeros((width,), F32), g_qk[:HEAD] + g_qk[HEAD:], (s * HEAD,)
            ),
            lax.dynamic_update_slice(jnp.zeros((up_scale.shape[0],), F32), g_up_scale, place_units),
            lax.dynamic_update_slice(jnp.zeros((up_scale.shape[0],), F32), g_gate_scale, place_units),
            g_alpha_attn,
            g_alpha_mlp,
        ]
    )
    gains_full = lax.psum(gains_full, ("seq", "batch"))
    ff = up_scale.shape[0]
    cuts = (0, width, width + ff, width + 2 * ff, 2 * width + 2 * ff, 3 * width + 2 * ff)
    gain_grads = [gains_full[a:b] for a, b in zip(cuts[:-1], cuts[1:])]

    return (
        output.reshape(states.shape),
        d_state.reshape(states.shape),
        unit_pull(w_query, g_small[:, :HEAD], 0),
        unit_pull(w_key, g_small[:, HEAD : 2 * HEAD], 0),
        unit_pull(w_value, g_small[:, 2 * HEAD : 3 * HEAD], 0),
        unit_pull(w_out, g_small[:, 3 * HEAD :].reshape(HEAD, width), 1),
        unit_pull(w_up, g_up_sum, 0),
        unit_pull(w_gate, g_gate_sum, 0),
        unit_pull(w_down, g_down_sum, 1),
        *gain_grads,
    )


def solution(mesh):
    seq, batch = mesh.shape["seq"], mesh.shape["batch"]
    body = on_device_heads if (seq == HEADS and batch == 2) else on_device_general
    return jax.shard_map(
        body,
        mesh=mesh,
        in_specs=(
            P("batch", "seq", None),
            P("batch", None),
            P(None, "seq"),
            P(None, "seq"),
            P(None, "seq"),
            P("seq", None),
            P(None, "seq"),
            P(None, "seq"),
            P("seq", None),
            P(),
            P(),
            P(),
            P(),
            P(),
            P("batch", "seq", None),
        ),
        out_specs=(
            P("batch", "seq", None),
            P("batch", "seq", None),
            P(None, "seq"),
            P(None, "seq"),
            P(None, "seq"),
            P("seq", None),
            P(None, "seq"),
            P(None, "seq"),
            P("seq", None),
            P(),
            P(),
            P(),
            P(),
            P(),
        ),
        check_vma=False,
    )
```

```python
import jax
import jax.numpy as jnp
import numpy as np
from jax import lax
from jax.experimental import pallas as pl
from jax.experimental.pallas import tpu as pltpu
from jax.sharding import PartitionSpec as P

HEADS = 16
HEAD = 64


EPS = 1e-06


def shifted(value, axis, steps):
    count = lax.axis_size(axis)
    first, last = (max(0, -steps), min(count, count - steps))
    return lax.ppermute(value, axis, [(source, source + steps) for source in range(first, last)])


def shifted_2(block, axis, distance):
    devices = range(lax.axis_size(axis))
    route = [((i - distance) % len(devices), i) for i in devices]
    return lax.ppermute(block, axis, route)


def normalized(weight, axis):
    wide = weight.astype(jnp.float32)
    return wide * lax.rsqrt(jnp.sum(wide * wide, axis=axis, keepdims=True) + EPS)


def rms(values):
    return values * lax.rsqrt(jnp.mean(values * values, axis=-1, keepdims=True) + EPS)


def doc_layout(len_row, tok_index):
    docs = jnp.arange(len_row.shape[0])
    starts = jnp.sum(jnp.where(docs[:, None] < docs[None, :], len_row[:, None], 0), axis=0)
    started = starts[None, :] <= tok_index[:, None]
    doc_ids = jnp.sum(started.astype(jnp.int32), axis=1) - 1
    first_tok = jnp.max(jnp.where(started, starts[None, :], 0), axis=1)
    return (doc_ids, tok_index - first_tok)


def rope(values, position):
    half = values.shape[-1] // 2
    freqs = 10000.0 ** (-jnp.arange(half, dtype=jnp.float32) / half)
    angle = position.astype(jnp.float32)[:, None] * freqs[None, :]
    cosine = jnp.cos(angle)[:, None, :]
    sine = jnp.sin(angle)[:, None, :]
    first = values[..., :half]
    second = values[..., half:]
    return jnp.concatenate(
        [first * cosine - second * sine, first * sine + second * cosine], axis=-1
    )


def prepare(linear, position, gain):
    count = linear.shape[0]
    shaped = linear.reshape(count, HEADS, HEAD)
    turned = rms(rope(shaped, position)) * gain.reshape(HEADS, HEAD)
    return turned.reshape(count, HEADS * HEAD)


def residual_mix(state, branch, alpha):
    return rms(state + alpha * (rms(branch) - state))


def gating(up_lin, gate_lin, up_scale, gate_scale):
    return up_scale * up_lin * jax.nn.silu(gate_scale * gate_lin)


def unit_back(raw_shard, grad_shard, axis):
    primal, pullback = jax.vjp(
        lambda weight: normalized(weight, axis), raw_shard.astype(jnp.float32)
    )
    return pullback(grad_shard)[0]


def on_device_general(
    states,
    lengths,
    w_query,
    w_key,
    w_value,
    w_out,
    w_up,
    w_gate,
    w_down,
    qk_scale,
    up_scale,
    gate_scale,
    alpha_attn,
    alpha_mlp,
    d_out,
):
    seq_count = lax.axis_size("seq")
    my_index = lax.axis_index("seq")
    rows = states.shape[0]
    tok = states.shape[1]
    width = states.shape[2]
    flat = rows * tok
    score_scale = HEAD ** (-0.5)
    row_layout = jax.vmap(doc_layout, in_axes=(0, None))
    unit_query = normalized(w_query, 0).astype(jnp.bfloat16)
    unit_key = normalized(w_key, 0).astype(jnp.bfloat16)
    unit_value = normalized(w_value, 0).astype(jnp.bfloat16)
    unit_out = normalized(w_out, 1).astype(jnp.bfloat16)
    unit_up = normalized(w_up, 0).astype(jnp.bfloat16)
    unit_gate = normalized(w_gate, 0).astype(jnp.bfloat16)
    unit_down = normalized(w_down, 1).astype(jnp.bfloat16)
    full_weights = (
        lax.all_gather(unit_query, "seq", axis=1, tiled=True),
        lax.all_gather(unit_key, "seq", axis=1, tiled=True),
        lax.all_gather(unit_value, "seq", axis=1, tiled=True),
        lax.all_gather(unit_out, "seq", axis=0, tiled=True),
        lax.all_gather(unit_up, "seq", axis=1, tiled=True),
        lax.all_gather(unit_gate, "seq", axis=1, tiled=True),
        lax.all_gather(unit_down, "seq", axis=0, tiled=True),
    )
    full_query, full_key, full_value, full_out, full_up, full_gate, full_down = full_weights
    tok_index = my_index * tok + jnp.arange(tok, dtype=jnp.int32)
    doc_ids, position = row_layout(lengths, tok_index)
    flat_pos = position.reshape(flat)
    state_in = states.reshape(flat, width)
    x_low = state_in.astype(jnp.bfloat16)
    query_lin = jnp.dot(x_low, full_query, preferred_element_type=jnp.float32)
    key_lin = jnp.dot(x_low, full_key, preferred_element_type=jnp.float32)
    value_lin = jnp.dot(x_low, full_value, preferred_element_type=jnp.float32)

    def front(query_part, key_part, gain):
        return (prepare(query_part, flat_pos, gain), prepare(key_part, flat_pos, gain))

    query_f, key_f = front(query_lin, key_lin, qk_scale)
    query_h = query_f.astype(jnp.bfloat16).reshape(rows, tok, HEADS, HEAD)
    key_h = key_f.astype(jnp.bfloat16).reshape(rows, tok, HEADS, HEAD)
    value_h = value_lin.astype(jnp.bfloat16).reshape(rows, tok, HEADS, HEAD)

    def block_scores(key_blk, source):
        key_index = source * tok + jnp.arange(tok, dtype=jnp.int32)
        key_docs, key_pos = row_layout(lengths, key_index)
        scores = (
            jnp.einsum("bqhd,bkhd->bqhk", query_h, key_blk, preferred_element_type=jnp.float32)
            * score_scale
        )
        allowed = (doc_ids[:, :, None] == key_docs[:, None, :]) & (
            key_index[None, None, :] <= tok_index[None, :, None]
        )
        return (scores, allowed[:, :, None, :])

    def is_active(source):
        last_key = jnp.reshape(source * tok + tok - 1, (1,))
        last_doc, last_pos = row_layout(lengths, last_key)
        return (source <= my_index) & jnp.any(last_doc[:, 0] >= doc_ids[:, 0])

    def attend(running, key_blk, value_blk, source):

        def compute(carried):
            best, denom_sum, accum = carried
            scores, allowed = block_scores(key_blk, source)
            new_best = jnp.maximum(best, jnp.max(jnp.where(allowed, scores, -1e30), axis=3))
            weights = jnp.where(allowed, jnp.exp(scores - new_best[:, :, :, None]), 0.0)
            shrink = jnp.exp(best - new_best)
            denom_sum = denom_sum * shrink + jnp.sum(weights, axis=3)
            accum = accum * shrink[:, :, :, None] + jnp.einsum(
                "bqhk,bkhd->bqhd",
                weights.astype(jnp.bfloat16),
                value_blk,
                preferred_element_type=jnp.float32,
            )
            return (new_best, denom_sum, accum)

        return lax.cond(is_active(source), compute, lambda carried: carried, running)

    reach = seq_count - 1
    start_state = (
        jnp.full((rows, tok, HEADS), -1e30, jnp.float32),
        jnp.zeros((rows, tok, HEADS), jnp.float32),
        jnp.zeros((rows, tok, HEADS, HEAD), jnp.float32),
    )
    first_state = attend(start_state, key_h, value_h, my_index)

    def cycle_step(step, loop_carry):
        running, key_blk, value_blk = loop_carry
        key_blk, value_blk = shifted((key_blk, value_blk), "seq", 1)
        source = (my_index - step) % seq_count
        return (attend(running, key_blk, value_blk, source), key_blk, value_blk)

    final_state, spent_key, spent_value = lax.fori_loop(
        1, reach + 1, cycle_step, (first_state, key_h, value_h)
    )
    best, denom_sum, accum = final_state
    attended = accum / denom_sum[:, :, :, None]
    log_sum = best + jnp.log(denom_sum)
    attended_low = attended.astype(jnp.bfloat16).reshape(flat, width)
    attn_branch = jnp.dot(attended_low, full_out, preferred_element_type=jnp.float32)
    state_mid = residual_mix(state_in, attn_branch, alpha_attn)
    mid_low = state_mid.astype(jnp.bfloat16)
    up_lin = jnp.dot(mid_low, full_up, preferred_element_type=jnp.float32)
    gate_lin = jnp.dot(mid_low, full_gate, preferred_element_type=jnp.float32)
    gated_low = gating(up_lin, gate_lin, up_scale, gate_scale).astype(jnp.bfloat16)
    mlp_branch = jnp.dot(gated_low, full_down, preferred_element_type=jnp.float32)
    output = residual_mix(state_mid, mlp_branch, alpha_mlp)
    back_weights = (
        lax.all_gather(unit_query, "seq", axis=1, tiled=True),
        lax.all_gather(unit_key, "seq", axis=1, tiled=True),
        lax.all_gather(unit_value, "seq", axis=1, tiled=True),
        lax.all_gather(unit_out, "seq", axis=0, tiled=True),
        lax.all_gather(unit_up, "seq", axis=1, tiled=True),
        lax.all_gather(unit_gate, "seq", axis=1, tiled=True),
        lax.all_gather(unit_down, "seq", axis=0, tiled=True),
    )
    back_query, back_key, back_value, back_out, back_up, back_gate, back_down = back_weights
    primal, pull_mlp = jax.vjp(residual_mix, state_mid, mlp_branch, alpha_mlp)
    d_mid, d_mlp, g_alpha_mlp = pull_mlp(d_out.reshape(flat, width))
    d_mlp_low = d_mlp.astype(jnp.bfloat16)
    grad_down = jnp.einsum("tf,td->fd", gated_low, d_mlp_low, preferred_element_type=jnp.float32)
    d_gated = jnp.einsum("td,fd->tf", d_mlp_low, back_down, preferred_element_type=jnp.float32)
    primal, pull_gate = jax.vjp(gating, up_lin, gate_lin, up_scale, gate_scale)
    d_up, d_gate, g_up_scale, g_gate_scale = pull_gate(d_gated)
    d_up_low = d_up.astype(jnp.bfloat16)
    d_gate_low = d_gate.astype(jnp.bfloat16)
    grad_up = jnp.einsum("tc,tf->cf", mid_low, d_up_low, preferred_element_type=jnp.float32)
    grad_gate = jnp.einsum("tc,tf->cf", mid_low, d_gate_low, preferred_element_type=jnp.float32)
    d_mid = d_mid + jnp.einsum("tf,cf->tc", d_up_low, back_up, preferred_element_type=jnp.float32)
    d_mid = d_mid + jnp.einsum(
        "tf,cf->tc", d_gate_low, back_gate, preferred_element_type=jnp.float32
    )
    primal, pull_attn = jax.vjp(residual_mix, state_in, attn_branch, alpha_attn)
    d_state, d_attn, g_alpha_attn = pull_attn(d_mid)
    d_attn_low = d_attn.astype(jnp.bfloat16)
    grad_out = jnp.einsum("tc,td->cd", attended_low, d_attn_low, preferred_element_type=jnp.float32)
    d_attended = jnp.einsum("td,cd->tc", d_attn_low, back_out, preferred_element_type=jnp.float32)
    d_att_low = d_attended.astype(jnp.bfloat16).reshape(rows, tok, HEADS, HEAD)
    delta = jnp.sum(d_att_low.astype(jnp.float32) * attended, axis=3)

    def attend_back(d_query, key_blk, value_blk, d_key, d_value, source):

        def compute(carried):
            d_query, d_key, d_value = carried
            scores, allowed = block_scores(key_blk, source)
            probs = jnp.where(allowed, jnp.exp(scores - log_sum[:, :, :, None]), 0.0)
            d_probs = jnp.einsum(
                "bqhd,bkhd->bqhk", d_att_low, value_blk, preferred_element_type=jnp.float32
            )
            d_scores = (probs * (d_probs - delta[:, :, :, None])).astype(jnp.bfloat16)
            d_query = d_query + jnp.einsum(
                "bqhk,bkhd->bqhd", d_scores, key_blk, preferred_element_type=jnp.float32
            )
            d_key = d_key + jnp.einsum(
                "bqhk,bqhd->bkhd", d_scores, query_h, preferred_element_type=jnp.float32
            )
            d_value = d_value + jnp.einsum(
                "bqhk,bqhd->bkhd",
                probs.astype(jnp.bfloat16),
                d_att_low,
                preferred_element_type=jnp.float32,
            )
            return (d_query, d_key, d_value)

        return lax.cond(
            is_active(source), compute, lambda carried: carried, (d_query, d_key, d_value)
        )

    def back_step(step, loop_carry):
        d_query, key_blk, value_blk, d_key, d_value = loop_carry
        source = (my_index - step) % seq_count
        d_query, d_key, d_value = attend_back(d_query, key_blk, value_blk, d_key, d_value, source)
        d_key, d_value = (
            shifted_2(d_key.astype(jnp.bfloat16), "seq", 1).astype(d_key.dtype),
            shifted_2(d_value.astype(jnp.bfloat16), "seq", 1).astype(d_value.dtype),
        )
        key_blk, value_blk = shifted((key_blk, value_blk), "seq", 1)
        return (d_query, key_blk, value_blk, d_key, d_value)

    zero_heads = jnp.zeros((rows, tok, HEADS, HEAD), jnp.float32)
    d_query_h, last_key_blk, last_value_blk, d_key_h, d_value_h = lax.fori_loop(
        0, reach, back_step, (zero_heads, key_h, value_h, zero_heads, zero_heads)
    )
    d_query_h, d_key_h, d_value_h = attend_back(
        d_query_h, last_key_blk, last_value_blk, d_key_h, d_value_h, (my_index - reach) % seq_count
    )
    d_key_h, d_value_h = (
        shifted_2(d_key_h.astype(jnp.bfloat16), "seq", -reach).astype(d_key_h.dtype),
        shifted_2(d_value_h.astype(jnp.bfloat16), "seq", -reach).astype(d_value_h.dtype),
    )
    primal, pull_front = jax.vjp(front, query_lin, key_lin, qk_scale)
    d_query_lin, d_key_lin, g_qk_scale = pull_front(
        (d_query_h.reshape(flat, width) * score_scale, d_key_h.reshape(flat, width) * score_scale)
    )
    d_query_low = d_query_lin.astype(jnp.bfloat16)
    d_key_low = d_key_lin.astype(jnp.bfloat16)
    d_value_low = d_value_h.reshape(flat, width).astype(jnp.bfloat16)
    grad_query = jnp.einsum("tc,tj->cj", x_low, d_query_low, preferred_element_type=jnp.float32)
    grad_key = jnp.einsum("tc,tj->cj", x_low, d_key_low, preferred_element_type=jnp.float32)
    grad_value = jnp.einsum("tc,tj->cj", x_low, d_value_low, preferred_element_type=jnp.float32)
    d_state = d_state + jnp.einsum(
        "tj,cj->tc", d_query_low, back_query, preferred_element_type=jnp.float32
    )
    d_state = d_state + jnp.einsum(
        "tj,cj->tc", d_key_low, back_key, preferred_element_type=jnp.float32
    )
    d_state = d_state + jnp.einsum(
        "tj,cj->tc", d_value_low, back_value, preferred_element_type=jnp.float32
    )
    shards = (
        lax.psum_scatter(
            grad_query.astype(jnp.bfloat16), "seq", scatter_dimension=1, tiled=True
        ).astype(jnp.float32),
        lax.psum_scatter(
            grad_key.astype(jnp.bfloat16), "seq", scatter_dimension=1, tiled=True
        ).astype(jnp.float32),
        lax.psum_scatter(
            grad_value.astype(jnp.bfloat16), "seq", scatter_dimension=1, tiled=True
        ).astype(jnp.float32),
        lax.psum_scatter(
            grad_out.astype(jnp.bfloat16), "seq", scatter_dimension=0, tiled=True
        ).astype(jnp.float32),
        lax.psum_scatter(
            grad_up.astype(jnp.bfloat16), "seq", scatter_dimension=1, tiled=True
        ).astype(jnp.float32),
        lax.psum_scatter(
            grad_gate.astype(jnp.bfloat16), "seq", scatter_dimension=1, tiled=True
        ).astype(jnp.float32),
        lax.psum_scatter(
            grad_down.astype(jnp.bfloat16), "seq", scatter_dimension=0, tiled=True
        ).astype(jnp.float32),
    )
    summed = (
        lax.psum(shards[0].astype(jnp.bfloat16), "batch").astype(jnp.float32),
        lax.psum(shards[1].astype(jnp.bfloat16), "batch").astype(jnp.float32),
        lax.psum(shards[2].astype(jnp.bfloat16), "batch").astype(jnp.float32),
        lax.psum(shards[3].astype(jnp.bfloat16), "batch").astype(jnp.float32),
        lax.psum(shards[4].astype(jnp.bfloat16), "batch").astype(jnp.float32),
        lax.psum(shards[5].astype(jnp.bfloat16), "batch").astype(jnp.float32),
        lax.psum(shards[6].astype(jnp.bfloat16), "batch").astype(jnp.float32),
    )
    gain_grads = lax.psum(
        (g_qk_scale, g_up_scale, g_gate_scale, g_alpha_attn, g_alpha_mlp), ("seq", "batch")
    )
    g_query = unit_back(w_query, summed[0], 0)
    g_key = unit_back(w_key, summed[1], 0)
    g_value = unit_back(w_value, summed[2], 0)
    g_out = unit_back(w_out, summed[3], 1)
    g_up = unit_back(w_up, summed[4], 0)
    g_gate = unit_back(w_gate, summed[5], 0)
    g_down = unit_back(w_down, summed[6], 1)
    return (
        output.reshape(rows, tok, width),
        d_state.reshape(rows, tok, width),
        g_query,
        g_key,
        g_value,
        g_out,
        g_up,
        g_gate,
        g_down,
        gain_grads[0],
        gain_grads[1],
        gain_grads[2],
        gain_grads[3],
        gain_grads[4],
    )


BF16 = jnp.bfloat16
F32 = jnp.float32
LANES = 128
MIB = 1 << 20
NT = (((1,), (1,)), ((), ()))
TN = (((0,), (0,)), ((), ()))


def place():
    s = lax.axis_index("seq")
    return s // 4, (s // 2) % 2, s % 2, lax.axis_index("batch")


def dev(z, x, c, y):
    return (z * 4 + x * 2 + c, y)


def remote(src, dst, send, recv, device):
    return pltpu.make_async_remote_copy(
        src_ref=src,
        dst_ref=dst,
        send_sem=send,
        recv_sem=recv,
        device_id=device,
        device_id_type=pl.DeviceIdType.MESH,
    )


def dot(a, b):
    return jnp.dot(a, b, preferred_element_type=F32)


def dot_nt(a, b):
    return lax.dot_general(a, b, NT, preferred_element_type=F32)


def dot_tn(a, b):
    return lax.dot_general(a, b, TN, preferred_element_type=F32)


BLOCK = 256


def inverse_norm(weight, axis):
    wide = weight.astype(F32)
    return lax.rsqrt(jnp.sum(wide * wide, axis=axis, keepdims=True) + EPS)


def unit_pull(weight, grad, axis):
    inverse = inverse_norm(weight, axis)
    unit = weight.astype(F32) * inverse
    return inverse * (grad - unit * jnp.sum(grad * unit, axis=axis, keepdims=True))


def turn_tables(count):
    half = HEAD // 2
    freqs = (10000.0 ** (-np.arange(half, dtype=np.float32) / half)).astype(np.float32)
    angle = np.arange(count, dtype=np.float32)[:, None] * freqs[None, :]
    cosine = np.cos(angle).astype(np.float32)
    sine = np.sin(angle).astype(np.float32)
    return np.tile(cosine, (1, 4)), np.concatenate([-sine, sine, -sine, sine], axis=1)


def mix(state, branch, alpha):
    inv_b = lax.rsqrt(jnp.mean(branch * branch, axis=-1, keepdims=True) + EPS)
    unit_b = branch * inv_b
    step = unit_b - state
    mixed = state + alpha * step
    inv_m = lax.rsqrt(jnp.mean(mixed * mixed, axis=-1, keepdims=True) + EPS)
    return mixed * inv_m, (unit_b, inv_b, step, inv_m)


def mix_back(grad, out, saved, alpha):
    unit_b, inv_b, step, inv_m = saved
    d_mixed = inv_m * (grad - out * jnp.mean(grad * out, axis=-1, keepdims=True))
    d_alpha = jnp.sum(d_mixed * step, axis=0)
    d_unit = d_mixed * alpha
    d_branch = inv_b * (d_unit - unit_b * jnp.mean(d_unit * unit_b, axis=-1, keepdims=True))
    return d_mixed - d_unit, d_branch, d_alpha


def inside(v):
    return (v >= 0) & (v < 4)


def unit_cols(w):
    wide = w.astype(F32)
    return (wide * lax.rsqrt(jnp.sum(wide * wide, axis=0, keepdims=True) + EPS)).astype(BF16)


def unit_rows(w):
    wide = w.astype(F32)
    return (wide * lax.rsqrt(jnp.sum(wide * wide, axis=1, keepdims=True) + EPS)).astype(BF16)


class Line:
    def __init__(self, buf, sems):
        self.buf, (self.send, self.recv) = buf, sems

    def hop(self, zz, way):
        z, x, c, y = place()
        b = self.buf.at[zz]
        return remote(b, b, self.send.at[zz, (way + 1) // 2], self.recv.at[zz], dev(z + way, x, c, y))

    def start(self):
        z = place()[0]
        for way in (-1, 1):

            @pl.when(inside(z + way))
            def _():
                self.hop(z, way).start()

    def arrive(self, k, way):
        z = place()[0]
        zz = z - way * k

        @pl.when(inside(zz))
        def _():
            self.hop(zz, -way).wait_recv()

            @pl.when(inside(z + way))
            def _():
                self.hop(zz, way).start()

    def drain(self):
        z = place()[0]
        for zz in range(4):
            for way in (-1, 1):

                @pl.when(((zz - z) * way <= 0) & inside(z + way))
                def _():
                    self.hop(zz, way).wait_send()


LINE_SEM = [pltpu.SemaphoreType.DMA((4, 2)), pltpu.SemaphoreType.DMA((4,))]


class Row:
    def __init__(self, buf, sems):
        self.buf, (self.zs, self.xs, self.cs, self.recv) = buf, sems

    def hop_z(self, zz, way):
        z, x, c, y = place()
        b = zz * 4 + x * 2 + c
        return remote(
            self.buf.at[b], self.buf.at[b], self.zs.at[zz, (way + 1) // 2], self.recv.at[b],
            dev(z + way, x, c, y),
        )

    def hop_x(self, zz):
        z, x, c, y = place()
        b = zz * 4 + x * 2 + c
        return remote(
            self.buf.at[b], self.buf.at[b], self.xs.at[zz], self.recv.at[b], dev(z, 1 - x, c, y)
        )

    def hop_c(self, zz, xx):
        z, x, c, y = place()
        b = zz * 4 + xx * 2 + c
        return remote(
            self.buf.at[b], self.buf.at[b], self.cs.at[zz, xx], self.recv.at[b], dev(z, x, 1 - c, y)
        )

    def arrived(self, b):
        z, x, c, y = place()
        remote(
            self.buf.at[b], self.buf.at[b], self.xs.at[0], self.recv.at[b], dev(z, x, 1 - c, y)
        ).wait_recv()

    def start(self):
        z, x, c, y = place()
        for way in (-1, 1):

            @pl.when(inside(z + way))
            def _():
                self.hop_z(z, way).start()

        self.hop_x(z).start()
        self.hop_c(z, x).start()

    def arrive(self, k):
        z, x, c, y = place()
        for way in (-1, 1):
            zz = z - way * k

            @pl.when(inside(zz))
            def _():
                self.arrived(zz * 4 + x * 2 + c)

                @pl.when(inside(z + way))
                def _():
                    self.hop_z(zz, way).start()

                self.hop_x(zz).start()
                self.hop_c(zz, x).start()

    def relay_from(self, k):
        z = place()[0]
        for way in (-1, 1):
            zz = z - way * k

            @pl.when(inside(zz))
            def _():
                self.relay(zz)

    def finish(self):
        z, x, c, y = place()

        @pl.loop(0, 4)
        def _(zz):
            self.arrived(zz * 4 + x * 2 + 1 - c)
            self.arrived(zz * 4 + (1 - x) * 2 + 1 - c)
            for way in (-1, 1):

                @pl.when(((zz - z) * way <= 0) & inside(z + way))
                def _():
                    self.hop_z(zz, way).wait_send()

            self.hop_x(zz).wait_send()
            self.hop_c(zz, 0).wait_send()
            self.hop_c(zz, 1).wait_send()

    def relay(self, zz):
        z, x, c, y = place()
        self.arrived(zz * 4 + (1 - x) * 2 + c)
        self.hop_c(zz, 1 - x).start()


ROW_SEM = [
    pltpu.SemaphoreType.DMA((4, 2)),
    pltpu.SemaphoreType.DMA((4,)),
    pltpu.SemaphoreType.DMA((4, 2)),
    pltpu.SemaphoreType.DMA((16,)),
]


def greet_row():
    z, x, c, y = place()
    s = z * 4 + x * 2 + c
    bar = pltpu.get_barrier_semaphore()

    @pl.loop(1, 16)
    def _(k):
        pl.semaphore_signal(
            bar, inc=1, device_id=((s + k) % 16, y), device_id_type=pl.DeviceIdType.MESH
        )

    pl.semaphore_signal(bar, inc=1, device_id=dev(z, x, c, 1 - y), device_id_type=pl.DeviceIdType.MESH)
    pl.semaphore_wait(bar, 16)


def half_swap(value):
    lane = lax.broadcasted_iota(jnp.int32, value.shape, 1)
    return jnp.where(
        lane % HEAD < HEAD // 2, pltpu.roll(value, LANES - HEAD // 2, 1), pltpu.roll(value, HEAD // 2, 1)
    )


def head_means(value):
    lane = lax.broadcasted_iota(jnp.int32, value.shape, 1)
    first = jnp.sum(jnp.where(lane < HEAD, value, 0.0), axis=1, keepdims=True)
    both = jnp.sum(value, axis=1, keepdims=True)
    return jnp.where(lane < HEAD, first, both - first) * (1.0 / HEAD)


def side_by_side(block):
    half = block.shape[0] // 2
    lane = lax.broadcasted_iota(jnp.int32, (half, LANES), 1)
    return jnp.where(lane < HEAD, block[:half], pltpu.roll(block[half:], HEAD, 1))


def peers():
    z, x, c, y = place()
    return ((x, 1 - c), (1 - x, c), (1 - x, 1 - c))


def spread_heads(b, env):
    rows = pl.ds(pl.multiple_of(b * LANES, LANES), LANES)
    lane = lax.broadcasted_iota(jnp.int32, (LANES, LANES), 1)
    one = jnp.where(lane < HEAD + 2, 1.0, 0.0)
    qk = env.heads_in[b, 0:LANES, :].astype(F32)
    env.q_ext[rows, :] = jnp.where(lane < HEAD, qk, 0.0).astype(BF16)
    env.k_ext[rows, :] = jnp.where(lane < HEAD, pltpu.roll(qk, HEAD, 1), one).astype(BF16)
    packed = env.heads_in[b, LANES:, :].astype(F32)
    value = jnp.concatenate([packed, pltpu.roll(packed, HEAD, 1)], axis=0)
    env.v_ext[rows, :] = jnp.where(lane < HEAD, value, one).astype(BF16)


class Reduce:
    def __init__(self, part, passing, landed, send, recv):
        self.part, self.passing, self.landed, self.send, self.recv = part, passing, landed, send, recv

    def hop(self, owner, way):
        z, x, c, y = place()
        spot = jnp.where((owner == z + way) & (way < 0), 4, owner)
        return remote(
            self.passing.at[owner], self.landed.at[spot], self.send.at[owner], self.recv.at[spot],
            dev(z + way, x, c, y),
        )

    def wait_spot(self, spot):
        z, x, c, y = place()
        remote(
            self.passing.at[0], self.landed.at[spot], self.send.at[0], self.recv.at[spot],
            dev(z, x, 1 - c, y),
        ).wait_recv()

    def step(self, k):
        z = place()[0]
        for way in (-1, 1):
            owner = z + way * k

            @pl.when(inside(owner))
            def _():
                @pl.when(inside(z - way))
                def _():
                    self.wait_spot(owner)
                    self.passing[owner] = (
                        self.part(owner) + self.landed[owner].astype(F32)
                    ).astype(BF16)

                @pl.when(jnp.logical_not(inside(z - way)))
                def _():
                    self.passing[owner] = self.part(owner).astype(BF16)

                self.hop(owner, way).start()

    def finish(self, total):
        z = place()[0]
        total[...] = self.part(z)

        @pl.when(z > 0)
        def _():
            self.wait_spot(z)
            total[...] += self.landed[z].astype(F32)

        @pl.when(z < 3)
        def _():
            self.wait_spot(4)
            total[...] += self.landed[4].astype(F32)

        for owner in range(4):

            @pl.when(owner != z)
            def _():
                self.hop(owner, jnp.where(owner > z, 1, -1)).wait_send()


REDUCE_SEM = [pltpu.SemaphoreType.DMA((4,)), pltpu.SemaphoreType.DMA((5,))]


class Env:
    def __init__(self, names, refs):
        for name, ref in zip(names, refs, strict=True):
            setattr(self, name, ref)


def window(start, size):
    return pl.ds(pl.multiple_of(start, size), size)


def qkv_rows(slot):
    return window(slot * LANES, LANES), window(4 * LANES + slot * HEAD, HEAD)


def qkv_copies(env, slot, sems, device):
    (send, recv), spots = sems, qkv_rows(slot)
    return [
        remote(env.u_qkv.at[rows, :], env.u_qkv.at[rows, :], send.at[i], recv.at[i], device)
        for i, rows in enumerate(spots)
    ]


def qkv_groups(env):
    z, x, c, y = place()
    mine, other = 2 * x + c, 2 * (1 - x) + c
    core, side = dev(z, x, 1 - c, y), dev(z, 1 - x, c, y)
    s, r = env.q_send, env.q_recv
    return (
        qkv_copies(env, mine, (s.at[0], r.at[0]), core),
        qkv_copies(env, mine, (s.at[1], r.at[1]), side),
        qkv_copies(env, other, (s.at[2], r.at[2]), core),
    )


def ff_views(env, slot, half=None):
    cols = window(slot * 256, 256)
    if half is None:
        return env.ups.at[:, cols], env.gates.at[:, cols], env.downs.at[cols, :]
    upper = window(half * 512, 512)
    return env.ups.at[upper, cols], env.gates.at[upper, cols], env.downs.at[window(slot * 256 + half * 128, 128), :]


def ff_groups(env):
    z, x, c, y = place()
    mine, other = 2 * x + c, 2 * (1 - x) + c
    core, side, twin = dev(z, x, 1 - c, y), dev(z, 1 - x, c, y), dev(z, x, c, 1 - y)

    def group(g, views, device):
        return [
            remote(v, v, env.w_send.at[g, i], env.w_recv.at[g, i], device) for i, v in enumerate(views)
        ]

    return (
        group(0, ff_views(env, mine), core),
        group(1, ff_views(env, mine, y), side),
        group(2, ff_views(env, other, y), core),
        group(3, ff_views(env, other, y), twin),
        group(4, ff_views(env, other, 1 - y), core),
    )


def each(copies, action):
    for copy in copies:
        getattr(copy, action)()


class Piece:
    def __init__(self, view, land_c, land_x, out, land_y, sems):
        self.view, self.land_c, self.land_x, self.out, self.land_y = view, land_c, land_x, out, land_y
        self.send, self.recv = sems

    def to_core(self, h):
        z, x, c, y = place()
        xx = 1 - x if h == 0 else x
        return remote(
            self.view(2 * xx + 1 - c), self.land_c.at[h], self.send.at[h], self.recv.at[h],
            dev(z, x, 1 - c, y),
        )

    def to_side(self):
        z, x, c, y = place()
        return remote(
            self.view(2 * (1 - x) + c), self.land_x, self.send.at[2], self.recv.at[2], dev(z, 1 - x, c, y)
        )

    def to_twin(self):
        z, x, c, y = place()
        return remote(self.out, self.land_y, self.send.at[3], self.recv.at[3], dev(z, x, c, 1 - y))

    def start(self):
        self.to_core(0).start()
        self.to_core(1).start()

    def pass_side(self):
        z, x, c, y = place()
        self.to_core(0).wait_recv()
        give = self.view(2 * (1 - x) + c)
        give[...] = (give[...].astype(F32) + self.land_c[0].astype(F32)).astype(BF16)
        self.to_side().start()

    def pass_twin(self):
        z, x, c, y = place()
        self.to_core(1).wait_recv()
        self.to_side().wait_recv()
        keep = self.view(2 * x + c)
        self.out[...] = (
            keep[...].astype(F32) + self.land_c[1].astype(F32) + self.land_x[...].astype(F32)
        ).astype(BF16)
        self.to_twin().start()

    def finish(self):
        self.to_twin().wait()
        self.to_core(0).wait_send()
        self.to_core(1).wait_send()
        self.to_side().wait_send()


PIECE_SEM = [pltpu.SemaphoreType.DMA((4,))] * 2


def project_block(zz, env):
    z, x, c, y = place()
    linear = dot_nt(env.x_line[zz], env.u_qkv[...])
    lane = lax.broadcasted_iota(jnp.int32, (LANES, LANES), 1)
    scale = jnp.where(lane < HEAD, HEAD ** (-0.5), 1.0)
    cosine, sine = env.cosine[zz], env.sine[zz]
    for sl in range(4):
        qk = linear[:, sl * LANES : (sl + 1) * LANES]
        turned = qk * cosine + half_swap(qk) * sine
        env.turned[zz, sl] = turned
        unit = turned * lax.rsqrt(head_means(turned * turned) + EPS)
        out = (unit * env.gain[sl : sl + 1, :]).astype(BF16).astype(F32) * scale
        env.heads_out[zz, sl, 0:LANES, :] = out.astype(BF16)
        pair = linear[:, (4 + sl // 2) * LANES : (5 + sl // 2) * LANES]
        if sl % 2:
            pair = pltpu.roll(pair, HEAD, 1)
        env.heads_out[zz, sl, LANES:, :] = side_by_side(pair).astype(BF16)
    b = zz * 4 + x * 2 + c
    env.heads_in[b] = env.heads_out[zz, x * 2 + c]
    for i, (xx, cc) in enumerate(peers()):
        remote(
            env.heads_out.at[zz, xx * 2 + cc], env.heads_in.at[b], env.hs.at[zz, i], env.hr.at[b],
            dev(z, xx, cc, y),
        ).start()


def attend_block(i, env):
    z, x, c, y = place()
    s = z * 4 + x * 2 + c
    row = lax.broadcasted_iota(jnp.int32, (BLOCK, BLOCK), 0)
    col = lax.broadcasted_iota(jnp.int32, (BLOCK, BLOCK), 1)
    lane = lax.broadcasted_iota(jnp.int32, (BLOCK, LANES), 1)
    rows = pl.ds(i * BLOCK, BLOCK)
    q = env.q_ext[rows, :]
    total = jnp.zeros((BLOCK, LANES), F32)
    for j in range(i + 1):
        keys = pl.ds(j * BLOCK, BLOCK)
        p = jnp.exp(dot_nt(q, env.k_ext[keys, :]))
        if i == j:
            p = jnp.where(row >= col, p, 0.0)
        total = total + dot(p.astype(BF16), env.v_ext[keys, :])
    denom = total[:, HEAD : HEAD + 1]
    out = total / denom
    env.attended[rows, :] = out
    log = -jnp.log(denom)
    high = log.astype(BF16).astype(F32)
    env.q_ext[rows, :] = jnp.where(
        lane == HEAD, high, jnp.where(lane == HEAD + 1, log - high, q.astype(F32))
    ).astype(BF16)
    for k in range(2):
        t = 2 * i + k
        env.att_out[t] = side_by_side(out[k * LANES : (k + 1) * LANES]).astype(BF16)
        send_head(t, s, env.att_out, env.att_in, env.as_, env.ar, y)


def send_head(t, s, src, land, send, recv, y):
    @pl.when(t != s)
    def _():
        remote(src.at[t], land.at[s], send.at[t], recv.at[s], (t, y)).start()

    @pl.when(t == s)
    def _():
        land[t] = src[t]


def wait_heads(s, src, land, send, recv, y):
    @pl.loop(0, 16)
    def _(t):
        @pl.when(t != s)
        def _():
            remote(src.at[t], land.at[t], send.at[t], recv.at[t], (t, y)).wait()


def lay_heads(land, dst):
    lane = lax.broadcasted_iota(jnp.int32, (HEAD, LANES), 1)
    for p in range(8):
        first = land[2 * p].astype(F32)
        second = land[2 * p + 1].astype(F32)
        cols = slice(p * LANES, (p + 1) * LANES)
        dst[0:HEAD, cols] = jnp.where(lane < HEAD, first, pltpu.roll(second, HEAD, 1)).astype(BF16)
        dst[HEAD:, cols] = jnp.where(lane < HEAD, pltpu.roll(first, HEAD, 1), second).astype(BF16)


def mlp_forward(h, env):
    z = place()[0]

    @pl.loop(0, 4)
    def _(n):
        cols = window(n * 256, 256)
        mid = env.h_line[h].reshape(256, 1024)
        up = dot(mid, env.ups[:, cols])
        gate = dot(mid, env.gates[:, cols]) * env.gate_scale[pl.ds(z, 1), cols]
        env.up_lin[h, :, cols] = up
        env.gate_val[h, :, cols] = gate
        act = gate * (1.0 / (1.0 + jnp.exp(-gate)))
        env.hidden[h, :, cols] = (up * env.up_scale[pl.ds(z, 1), cols] * act).astype(BF16)

    @pl.loop(0, 4)
    def _(n):
        cols = window(n * 256, 256)
        env.part[h, :, :, cols] = dot(env.hidden[h], env.downs[:, cols]).reshape(4, 64, 256)


def mlp_backward(h, env):
    z = place()[0]

    @pl.loop(0, 4)
    def _(n):
        cols = window(n * 256, 256)
        d_hidden = dot_nt(env.dm_line[h].reshape(256, 1024), env.downs[cols, :])
        up, gate = env.up_lin[h, :, cols], env.gate_val[h, :, cols]
        up_gain, gate_gain = env.up_scale[pl.ds(z, 1), cols], env.gate_scale[pl.ds(z, 1), cols]
        sig = 1.0 / (1.0 + jnp.exp(-gate))
        d_up = d_hidden * (gate * sig)
        d_gate = d_hidden * (up * up_gain) * (sig * (1.0 + gate * (1.0 - sig)))
        env.gains[0:1, cols] += jnp.sum(d_up * up, axis=0, keepdims=True)
        env.gains[1:2, cols] += jnp.sum(d_gate * gate, axis=0, keepdims=True) / gate_gain
        env.d_up[h, :, cols] = (d_up * up_gain).astype(BF16)
        env.d_gate[h, :, cols] = (d_gate * gate_gain).astype(BF16)

    @pl.loop(0, 4)
    def _(n):
        cols = window(n * 256, 256)
        back = dot_nt(env.d_up[h], env.ups[cols, :]) + dot_nt(env.d_gate[h], env.gates[cols, :])
        env.part[h, :, :, cols] = back.reshape(4, 64, 256)


def weight_gradient(left, right, out):
    @pl.loop(0, 4)
    def _(n):
        cols = window(n * 256, 256)
        first = dot_tn(left(0), right(0, cols))
        out[:, cols] = (first + dot_tn(left(1), right(1, cols))).astype(BF16)


def rows_of(h):
    return slice(64 * h, 64 * (h + 1))


def after_forward(h, reduce, env):
    z, rows = place()[0], rows_of(h)
    reduce.finish(env.total)
    alpha = env.alpha_mlp[...]
    out, saved = mix(env.mid[rows, :], env.total[...], alpha)
    env.output[rows, :] = out
    d_mid, d_branch, d_alpha = mix_back(env.d_out[rows, :], out, saved, alpha)
    env.d_mid[rows, :] = d_mid
    env.gains[3:4, :] += d_alpha[None, :]
    env.dm_line[h, z] = d_branch.astype(BF16)


def after_backward(h, reduce, env):
    rows = rows_of(h)
    reduce.finish(env.total)
    alpha = env.alpha_attn[...]
    mid, saved = mix(env.states[rows, :], env.branch[rows, :], alpha)
    d_state, d_branch, d_alpha = mix_back(env.d_mid[rows, :] + env.total[...], mid, saved, alpha)
    env.d_states[rows, :] = d_state
    env.gains[2:3, :] += d_alpha[None, :]
    env.d_branch[rows, :] = d_branch.astype(BF16)


def spread_grads(b, env):
    rows = window(b * LANES, LANES)
    lane = lax.broadcasted_iota(jnp.int32, (LANES, LANES), 1)
    packed = env.datt_in[b].astype(F32)
    value = jnp.where(lane < HEAD, jnp.concatenate([packed, pltpu.roll(packed, HEAD, 1)], axis=0), 0.0)
    delta = -jnp.sum(value * env.attended[rows, :], axis=1, keepdims=True)
    high = delta.astype(BF16).astype(F32)
    env.do_ext[rows, :] = jnp.where(
        lane == HEAD, high, jnp.where(lane == HEAD + 1, delta - high, value)
    ).astype(BF16)


def attend_back_block(i, env, last):
    z, x, c, y = place()
    row = lax.broadcasted_iota(jnp.int32, (BLOCK, BLOCK), 0)
    col = lax.broadcasted_iota(jnp.int32, (BLOCK, BLOCK), 1)
    lane = lax.broadcasted_iota(jnp.int32, (LANES, LANES), 1)
    rows = pl.ds(i * BLOCK, BLOCK)
    q = env.q_ext[rows, :]
    do = env.do_ext[rows, :]
    dq = jnp.zeros((BLOCK, LANES), F32)
    for j in range(i + 1):
        keys = pl.ds(j * BLOCK, BLOCK)
        k = env.k_ext[keys, :]
        p = jnp.exp(dot_nt(k, q))
        if i == j:
            p = jnp.where(row <= col, p, 0.0)
        ds = (p * dot_nt(env.v_ext[keys, :], do)).astype(BF16)
        dv = dot(p.astype(BF16), do)
        dk = dot(ds, q)
        dq = dq + dot_tn(ds, k)
        if i == last:
            env.dk[keys, :] = dk
            env.dv[keys, :] = dv
        else:
            env.dk[keys, :] += dk
            env.dv[keys, :] += dv
    for n in range(2):
        part = slice(n * LANES, (n + 1) * LANES)
        b = 2 * i + n
        zz, sl = b // 4, b % 4
        tok = pl.ds(b * LANES, LANES)
        env.back_out[zz, sl, 0:LANES, :] = jnp.where(
            lane < HEAD, dq[part] * HEAD ** (-0.5), pltpu.roll(env.dk[tok, :], HEAD, 1)
        ).astype(BF16)
        env.back_out[zz, sl, LANES:, :] = side_by_side(env.dv[tok, :]).astype(BF16)
        mine = 2 * x + c

        @pl.when(sl == mine)
        def _():
            env.back_in[zz * 4 + mine] = env.back_out[zz, sl]

        @pl.when(sl != mine)
        def _():
            back_copy(zz, sl, mine, env).start()


def back_copy(zz, sl, source, env):
    z, x, c, y = place()
    return remote(
        env.back_out.at[zz, sl], env.back_in.at[zz * 4 + source], env.bs.at[zz, sl],
        env.br.at[zz * 4 + source], dev(z, sl // 2, sl % 2, y),
    )


def project_back(zz, env):
    z, x, c, y = place()
    mine = 2 * x + c
    cosine, sine = env.cosine[zz], env.sine[zz]
    lane = lax.broadcasted_iota(jnp.int32, (LANES, LANES), 1)
    values = []
    for sl in range(4):

        @pl.when(sl != mine)
        def _():
            back_copy(zz, sl, sl, env).wait()

        grad = env.back_in[zz * 4 + sl, 0:LANES, :].astype(F32)
        turned = env.turned[zz, sl]
        inverse = lax.rsqrt(head_means(turned * turned) + EPS)
        unit = turned * inverse
        env.gain_sum[sl : sl + 1, :] += jnp.sum(grad * unit, axis=0, keepdims=True)
        d_unit = grad * env.gain[sl : sl + 1, :]
        d_turned = inverse * (d_unit - unit * head_means(d_unit * unit))
        d_lin = d_turned * cosine - half_swap(d_turned) * sine
        env.d_lin[zz, :, sl * LANES : (sl + 1) * LANES] = d_lin.astype(BF16)
        packed = env.back_in[zz * 4 + sl, LANES:, :].astype(F32)
        values.append(jnp.concatenate([packed, pltpu.roll(packed, HEAD, 1)], axis=0))
    for p in range(2):
        pair = jnp.where(lane < HEAD, values[2 * p], pltpu.roll(values[2 * p + 1], HEAD, 1))
        env.d_lin[zz, :, (4 + p) * LANES : (5 + p) * LANES] = pair.astype(BF16)
    d_x = dot(env.d_lin[zz], env.u_qkv[...])
    env.part[0, zz] = d_x[:64]
    env.part[1, zz] = d_x[64:]


def layer(env):
    z, x, c, y = place()
    s = z * 4 + x * 2 + c
    mine = 2 * x + c
    env.back_out, env.back_in = env.heads_out, env.heads_in
    env.g_qkv, env.g_out = env.u_qkv, env.u_out
    tables = []
    for zz in range(4):
        b = zz * 4 + 2 * x + c
        tables.append(pltpu.make_async_copy(env.cosines.at[b], env.cosine.at[zz], env.t_sem.at[zz, 0]))
        tables.append(pltpu.make_async_copy(env.sines.at[b], env.sine.at[zz], env.t_sem.at[zz, 1]))
    each(tables, "start")

    env.x_line[z] = env.states[...].astype(BF16)
    qk_rows, v_rows = qkv_rows(mine)
    env.u_qkv[qk_rows, :] = jnp.concatenate(
        [unit_rows(env.w_query[...]), unit_rows(env.w_key[...])], axis=0
    )
    env.u_qkv[v_rows, :] = unit_rows(env.w_value[...])
    greet_row()
    line = Line(env.x_line, (env.x_send, env.x_recv))
    line.start()
    q_core, q_side, q_relay = qkv_groups(env)
    each(q_side, "start")
    each(q_core, "start")

    for sl in range(4):
        scale = env.qk_scale[pl.ds(4 * z + sl, 1), :]
        env.gain[sl : sl + 1, :] = jnp.concatenate([scale, scale], axis=1)
    env.u_out[s] = unit_rows(env.w_out[...])
    own = window(mine * 256, 256)
    env.ups[:, own] = unit_cols(env.w_up[...])
    env.gates[:, own] = unit_cols(env.w_gate[...])
    env.downs[own, :] = unit_rows(env.w_down[...])
    env.gains[...] = jnp.zeros_like(env.gains)
    env.gain_sum[...] = jnp.zeros_like(env.gain_sum)
    ff = ff_groups(env)
    each(ff[0], "start")
    each(tables, "wait")

    for way in (-1, 1):
        line.arrive(1, way)
    each(q_side, "wait_recv")
    each(q_relay, "start")
    each(q_core, "wait_recv")
    each(q_relay, "wait_recv")
    project_block(z, env)

    @pl.loop(1, 4)
    def _(k):
        @pl.when(k < 3)
        def _():
            for way in (-1, 1):
                line.arrive(k + 1, way)

        for way in (-1, 1):

            @pl.when(inside(z - way * k))
            def _():
                project_block(z - way * k, env)

    line.drain()
    for group in (q_side, q_core, q_relay):
        each(group, "wait_send")
    uo = Row(env.u_out, (env.o_z, env.o_x, env.o_c, env.o_r))
    uo.start()

    @pl.loop(0, 4)
    def _(zz):
        for i, (xx, cc) in enumerate(peers()):
            b = zz * 4 + xx * 2 + cc
            remote(
                env.heads_out.at[zz, xx * 2 + cc], env.heads_in.at[b], env.hs.at[zz, i], env.hr.at[b],
                dev(z, xx, cc, y),
            ).wait()

    @pl.loop(0, 16)
    def _(b):
        spread_heads(b, env)

    uo.arrive(1)
    for i in range(4):
        attend_block(i, env)
    uo.relay(z)
    for i in range(4, 6):
        attend_block(i, env)
    uo.arrive(2)
    uo.relay_from(1)
    for i in range(6, 8):
        attend_block(i, env)
    uo.arrive(3)
    each(ff[1], "start")
    uo.relay_from(2)
    uo.relay_from(3)
    wait_heads(s, env.att_out, env.att_in, env.as_, env.ar, y)
    lay_heads(env.att_in, env.att_low)
    uo.finish()

    branch = dot(env.att_low[...], env.u_out[...].reshape(1024, 1024))
    env.branch[...] = branch
    mid, _ = mix(env.states[...], branch, env.alpha_attn[...])
    env.mid[...] = mid
    low = mid.astype(BF16)
    env.h_line[0, z] = low[:64]
    env.h_line[1, z] = low[64:]

    fa = Line(env.h_line.at[0], (env.fa_s, env.fa_r))
    fb = Line(env.h_line.at[1], (env.fb_s, env.fb_r))
    ba = Line(env.dm_line.at[0], (env.ba_s, env.ba_r))
    bb = Line(env.dm_line.at[1], (env.bb_s, env.bb_r))

    def reduce(h, send, recv):
        return Reduce(
            lambda owner: env.part[h, owner], env.passing.at[h], env.landed.at[h], send, recv
        )

    r0, r1 = reduce(0, env.r0_s, env.r0_r), reduce(1, env.r1_s, env.r1_r)

    def arrive(gather, k):
        for way in (-1, 1):
            gather.arrive(k, way)

    fa.start()
    arrive(fa, 1)
    each(ff[1], "wait_recv")
    each(ff[2], "start")
    each(ff[3], "start")
    arrive(fa, 2)
    fb.start()
    each(ff[3], "wait_recv")
    each(ff[4], "start")
    each(ff[0], "wait_recv")
    each(ff[2], "wait_recv")
    each(ff[4], "wait_recv")
    arrive(fa, 3)
    mlp_forward(0, env)
    arrive(fb, 1)
    r0.step(3)
    arrive(fb, 2)
    r0.step(2)
    arrive(fb, 3)
    r0.step(1)
    mlp_forward(1, env)
    r1.step(3)
    after_forward(0, r0, env)
    ba.start()
    r1.step(2)
    arrive(ba, 1)
    r1.step(1)
    arrive(ba, 2)
    after_forward(1, r1, env)
    bb.start()
    arrive(ba, 3)
    mlp_backward(0, env)
    arrive(bb, 1)
    r0.step(3)
    arrive(bb, 2)
    r0.step(2)
    arrive(bb, 3)
    r0.step(1)
    mlp_backward(1, env)
    r1.step(3)
    for gather in (fa, fb, ba, bb):
        gather.drain()
    for group in ff:
        each(group, "wait_send")

    def both(ref):
        return lambda h: ref[h].reshape(256, 1024)

    def cols_of(ref):
        def read(h, cols):
            value = ref[h, :, :, cols] if len(ref.shape) == 4 else ref[h, :, cols]
            return value.reshape(256, 256)

        return read

    gu = Piece(lambda slot: env.g_up.at[:, window(slot * 256, 256)], env.lcu, env.lxu, env.ou, env.yu, (env.us, env.ur))
    gg = Piece(lambda slot: env.g_gate.at[:, window(slot * 256, 256)], env.lcg, env.lxg, env.og, env.yg, (env.gs, env.gr))
    gd = Piece(lambda slot: env.g_down.at[window(slot * 256, 256), :], env.lcd, env.lxd, env.od, env.yd, (env.ds, env.dr))
    weight_gradient(both(env.hidden), cols_of(env.dm_line), env.g_down)
    gd.start()
    r1.step(2)
    after_backward(0, r0, env)
    weight_gradient(both(env.h_line), cols_of(env.d_up), env.g_up)
    gu.start()
    r1.step(1)
    weight_gradient(both(env.h_line), cols_of(env.d_gate), env.g_gate)
    gg.start()
    gd.pass_side()
    after_backward(1, r1, env)

    lane = lax.broadcasted_iota(jnp.int32, (LANES, LANES), 1)
    for p in range(4):
        d_att = dot_nt(env.d_branch[...], env.u_out[4 * p : 4 * p + 4].reshape(256, 1024))
        for k in range(4):
            value = d_att[:, (k // 2) * LANES : (k // 2 + 1) * LANES]
            if k % 2:
                value = pltpu.roll(value, HEAD, 1)
            t = 4 * p + k
            env.datt_out[t] = side_by_side(value).astype(BF16)
            send_head(t, s, env.datt_out, env.datt_in, env.das, env.dar, y)

    @pl.loop(0, 4)
    def _(n):
        cols = window(n * 256, 256)
        grad = dot_tn(env.att_low[...], env.d_branch[:, cols])
        env.g_out[:, :, cols] = grad.reshape(16, 64, 256).astype(BF16)

    out_reduce = RowReduce(env)
    out_reduce.start()
    wait_heads(s, env.datt_out, env.datt_in, env.das, env.dar, y)

    @pl.loop(0, 16)
    def _(b):
        spread_grads(b, env)

    attend_back_block(7, env, 7)
    out_reduce.pass_side()
    attend_back_block(6, env, 7)
    gu.pass_side()
    attend_back_block(5, env, 7)
    gg.pass_side()
    attend_back_block(4, env, 7)
    out_reduce.pass_line()
    for i in range(3, -1, -1):
        attend_back_block(i, env, 7)
    out_reduce.step(3)
    project_back(3, env)
    out_reduce.step(2)
    project_back(2, env)
    out_reduce.step(1)
    project_back(1, env)
    gd.pass_twin()
    project_back(0, env)
    for h in range(2):
        (r0, r1)[h].step(3)

    @pl.loop(0, 4)
    def _(n):
        cols = window(n * 256, 256)
        total = dot_tn(env.d_lin[...].reshape(512, 768), env.x_line[:, :, cols].reshape(512, 256))
        env.g_qkv[:, cols] = total.astype(BF16)

    gq = Piece(lambda slot: env.g_qkv.at[qkv_rows(slot)[0], :], env.lcq, env.lxq, env.oq, env.yq, (env.qqs, env.qqr))
    gv = Piece(lambda slot: env.g_qkv.at[qkv_rows(slot)[1], :], env.lcv, env.lxv, env.ov, env.yv, (env.vvs, env.vvr))
    gq.start()
    gv.start()
    r0.step(2)
    r1.step(2)
    for sl in range(4):
        both_parts = env.gain_sum[sl : sl + 1, 0:HEAD] + env.gain_sum[sl : sl + 1, HEAD:]
        env.gains[4 + sl : 5 + sl, 0:HEAD] = both_parts
    small = [
        remote(env.gains, env.gain_land.at[i], env.sm_s.at[i], env.sm_r.at[i], device)
        for i, device in enumerate((dev(z, x, 1 - c, y), dev(z, 1 - x, c, y), dev(z, x, c, 1 - y)))
    ]
    small[0].start()
    gq.pass_side()
    gv.pass_side()
    r0.step(1)
    r1.step(1)
    small[0].wait()
    env.gains[...] += env.gain_land[0]
    small[1].start()
    out_reduce.to_twin()
    gu.pass_twin()
    small[1].wait()
    env.gains[...] += env.gain_land[1]
    small[2].start()
    gg.pass_twin()
    small[2].wait()
    env.gain_line[z] = env.gains[...] + env.gain_land[2]

    def tell(k):
        t = (z + k) % 4
        return remote(
            env.gain_line.at[z], env.gain_line.at[z], env.gl_s.at[k], env.gl_r.at[z], dev(t, x, c, y)
        )

    for k in range(1, 4):
        tell(k).start()
    r0.finish(env.total)
    env.d_states[0:64, :] += env.total[...]
    r1.finish(env.total)
    env.d_states[64:, :] += env.total[...]
    gq.pass_twin()
    gv.pass_twin()
    for k in range(1, 4):
        tell(k).wait_send()
        t = (z + k) % 4
        remote(
            env.gain_line.at[t], env.gain_line.at[t], env.gl_s.at[k], env.gl_r.at[t], dev(t, x, c, y)
        ).wait_recv()

    for piece in (gd, gu, gg, gq, gv):
        piece.finish()
    out_reduce.finish()


class RowReduce:
    def __init__(self, env):
        self.env = env
        self.line = Reduce(self.part, env.o_pass, env.o_land, env.ol_s, env.ol_r)

    def part(self, owner):
        z, x, c, y = place()
        return self.env.g_out[owner * 4 + 2 * x + c].astype(F32)

    def to_core(self, zz, xx):
        z, x, c, y = place()
        e = self.env
        return remote(
            e.g_out.at[zz * 4 + 2 * xx + 1 - c], e.o_c_land.at[zz, xx], e.oc_s.at[zz, xx], e.oc_r.at[zz, xx],
            dev(z, x, 1 - c, y),
        )

    def to_side(self, zz):
        z, x, c, y = place()
        e = self.env
        return remote(
            e.g_out.at[zz * 4 + 2 * (1 - x) + c], e.o_x_land.at[zz], e.ox_s.at[zz], e.ox_r.at[zz],
            dev(z, 1 - x, c, y),
        )

    def twin(self):
        z, x, c, y = place()
        e = self.env
        return remote(e.oo, e.yo, e.oy_s, e.oy_r, dev(z, x, c, 1 - y))

    def start(self):
        z, x, c, y = place()

        @pl.loop(0, 4)
        def _(zz):
            self.to_core(zz, 1 - x).start()
            self.to_core(zz, x).start()

    def pass_side(self):
        z, x, c, y = place()
        e = self.env

        @pl.loop(0, 4)
        def _(zz):
            self.to_core(zz, 1 - x).wait_recv()
            b = zz * 4 + 2 * (1 - x) + c
            e.g_out[b] = (e.g_out[b].astype(F32) + e.o_c_land[zz, 1 - x].astype(F32)).astype(BF16)
            self.to_side(zz).start()

    def pass_line(self):
        z, x, c, y = place()
        e = self.env

        @pl.loop(0, 4)
        def _(zz):
            self.to_core(zz, x).wait_recv()
            self.to_side(zz).wait_recv()
            b = zz * 4 + 2 * x + c
            e.g_out[b] = (
                e.g_out[b].astype(F32) + e.o_c_land[zz, x].astype(F32) + e.o_x_land[zz].astype(F32)
            ).astype(BF16)

    def step(self, k):
        self.line.step(k)

    def to_twin(self):
        e = self.env
        self.line.finish(e.total)
        e.oo[...] = e.total[...].astype(BF16)
        self.twin().start()

    def finish(self):
        z, x, c, y = place()
        self.twin().wait()

        @pl.loop(0, 4)
        def _(zz):
            self.to_core(zz, 0).wait_send()
            self.to_core(zz, 1).wait_send()
            self.to_side(zz).wait_send()


DMA = pltpu.SemaphoreType.DMA


def v(shape, dtype=BF16):
    return pltpu.VMEM(shape, dtype)


LAYER_IN = tuple(
    dict(
        states=None,
        w_query=None,
        w_key=None,
        w_value=None,
        w_out=None,
        w_up=None,
        w_gate=None,
        w_down=None,
        qk_scale=None,
        up_scale=None,
        gate_scale=None,
        alpha_attn=None,
        alpha_mlp=None,
        d_out=None,
        cosines=None,
        sines=None,
    )
)
LAYER_OUT = dict(
    output=((128, 1024), F32), d_states=((128, 1024), F32),
    ou=((1024, 256), BF16), yu=((1024, 256), BF16), og=((1024, 256), BF16), yg=((1024, 256), BF16),
    od=((256, 1024), BF16), yd=((256, 1024), BF16), oq=((128, 1024), BF16), yq=((128, 1024), BF16),
    ov=((64, 1024), BF16), yv=((64, 1024), BF16), oo=((64, 1024), BF16), yo=((64, 1024), BF16),
    gain_line=((4, 8, 1024), F32),
)
LAYER_TMP = dict(
    x_line=v((4, 128, 1024)), u_qkv=v((768, 1024)), u_out=v((16, 64, 1024)),
    turned=v((4, 4, 128, 128), F32), cosine=v((4, 128, 128), F32), sine=v((4, 128, 128), F32),
    gain=v((4, 128), F32), gain_sum=v((4, 128), F32), gains=v((8, 1024), F32),
    gain_land=v((3, 8, 1024), F32),
    heads_out=v((4, 4, 192, 128)), heads_in=v((16, 192, 128)),
    q_ext=v((2048, 128)), k_ext=v((2048, 128)), v_ext=v((2048, 128)), attended=v((2048, 128), F32),
    att_out=v((16, 64, 128)), att_in=v((16, 64, 128)), att_low=v((128, 1024)),
    ups=v((1024, 1024)), gates=v((1024, 1024)), downs=v((1024, 1024)),
    branch=v((128, 1024), F32), mid=v((128, 1024), F32), d_mid=v((128, 1024), F32),
    total=v((64, 1024), F32), d_branch=v((128, 1024)),
    h_line=v((2, 4, 64, 1024)), dm_line=v((2, 4, 64, 1024)),
    up_lin=v((2, 256, 1024), F32), gate_val=v((2, 256, 1024), F32), hidden=v((2, 256, 1024)),
    d_up=v((2, 256, 1024)), d_gate=v((2, 256, 1024)),
    part=v((2, 4, 64, 1024), F32), passing=v((2, 4, 64, 1024)), landed=v((2, 5, 64, 1024)),
    g_up=v((1024, 1024)), g_gate=v((1024, 1024)), g_down=v((1024, 1024)),
    lcu=v((2, 1024, 256)), lcg=v((2, 1024, 256)), lcd=v((2, 256, 1024)), lcq=v((2, 128, 1024)),
    lcv=v((2, 64, 1024)),
    lxu=v((1024, 256)), lxg=v((1024, 256)), lxd=v((256, 1024)), lxq=v((128, 1024)), lxv=v((64, 1024)),
    o_c_land=v((4, 2, 64, 1024)), o_x_land=v((4, 64, 1024)), o_pass=v((4, 64, 1024)),
    o_land=v((5, 64, 1024)),
    datt_out=v((16, 64, 128)), datt_in=v((16, 64, 128)), do_ext=v((2048, 128)),
    dk=v((2048, 128), F32), dv=v((2048, 128), F32),
    d_lin=v((4, 128, 768)),
    t_sem=DMA((4, 2)), x_send=DMA((4, 2)), x_recv=DMA((4,)), q_send=DMA((3, 2)), q_recv=DMA((3, 2)),
    w_send=DMA((5, 3)), w_recv=DMA((5, 3)), hs=DMA((4, 3)), hr=DMA((16,)),
    o_z=DMA((4, 2)), o_x=DMA((4,)), o_c=DMA((4, 2)), o_r=DMA((16,)),
    as_=DMA((16,)), ar=DMA((16,)), das=DMA((16,)), dar=DMA((16,)),
    fa_s=DMA((4, 2)), fa_r=DMA((4,)), fb_s=DMA((4, 2)), fb_r=DMA((4,)),
    ba_s=DMA((4, 2)), ba_r=DMA((4,)), bb_s=DMA((4, 2)), bb_r=DMA((4,)),
    r0_s=DMA((4,)), r0_r=DMA((5,)), r1_s=DMA((4,)), r1_r=DMA((5,)),
    us=DMA((4,)), ur=DMA((4,)), gs=DMA((4,)), gr=DMA((4,)), ds=DMA((4,)), dr=DMA((4,)),
    qqs=DMA((4,)), qqr=DMA((4,)), vvs=DMA((4,)), vvr=DMA((4,)),
    oc_s=DMA((4, 2)), oc_r=DMA((4, 2)), ox_s=DMA((4,)), ox_r=DMA((4,)),
    ol_s=DMA((4,)), ol_r=DMA((5,)), oy_s=DMA, oy_r=DMA,
    bs=DMA((4, 4)), br=DMA((16,)), sm_s=DMA((3,)), sm_r=DMA((3,)), gl_s=DMA((4,)), gl_r=DMA((4,)),
)


def run_layer(*args):
    vmem = pl.BlockSpec(memory_space=pltpu.VMEM)
    names = LAYER_IN + tuple(LAYER_OUT) + tuple(LAYER_TMP)

    def kernel(*refs):
        layer(Env(names, refs))

    outs = pl.pallas_call(
        kernel,
        name="layer",
        out_shape=tuple(jax.ShapeDtypeStruct(*o) for o in LAYER_OUT.values()),
        in_specs=[vmem] * (len(LAYER_IN) - 2) + [pl.BlockSpec(memory_space=pl.ANY)] * 2,
        out_specs=(vmem,) * len(LAYER_OUT),
        scratch_shapes=list(LAYER_TMP.values()),
        compiler_params=pltpu.CompilerParams(
            collective_id=1, has_side_effects=True, vmem_limit_bytes=62 * MIB
        ),
    )(*args)
    return dict(zip(LAYER_OUT, outs))


def on_device_heads(
    states,
    lengths,
    w_query,
    w_key,
    w_value,
    w_out,
    w_up,
    w_gate,
    w_down,
    qk_scale,
    up_scale,
    gate_scale,
    alpha_attn,
    alpha_mlp,
    d_out,
):
    tok, width = states.shape[1:]
    cosine, sine = turn_tables(16 * tok)
    got = run_layer(
        states.reshape(tok, width), w_query.T, w_key.T, w_value.T, w_out, w_up, w_gate, w_down,
        qk_scale.reshape(HEADS, HEAD), up_scale.reshape(4, -1), gate_scale.reshape(4, -1),
        alpha_attn.reshape(1, -1), alpha_mlp.reshape(1, -1), d_out.reshape(tok, width),
        jnp.asarray(cosine.reshape(16, tok, LANES)), jnp.asarray(sine.reshape(16, tok, LANES)),
    )

    def summed(own, other):
        return got[own].astype(F32) + got[other].astype(F32)

    qk_sum, v_sum = summed("oq", "yq"), summed("ov", "yv")
    line = got["gain_line"]
    alphas = line[0] + line[1] + line[2] + line[3]
    return (
        got["output"].reshape(states.shape),
        got["d_states"].reshape(states.shape),
        unit_pull(w_query.T, qk_sum[:HEAD], 1).T,
        unit_pull(w_key.T, qk_sum[HEAD:], 1).T,
        unit_pull(w_value.T, v_sum, 1).T,
        unit_pull(w_out, summed("oo", "yo"), 1),
        unit_pull(w_up, summed("ou", "yu"), 0),
        unit_pull(w_gate, summed("og", "yg"), 0),
        unit_pull(w_down, summed("od", "yd"), 1),
        line[:, 4:8, :HEAD].reshape(-1),
        line[:, 0, :].reshape(-1),
        line[:, 1, :].reshape(-1),
        alphas[2],
        alphas[3],
    )


def solution(mesh):
    seq, batch = mesh.shape["seq"], mesh.shape["batch"]
    body = on_device_heads if (seq == HEADS and batch == 2) else on_device_general
    return jax.shard_map(
        body,
        mesh=mesh,
        in_specs=(
            P("batch", "seq", None),
            P("batch", None),
            P(None, "seq"),
            P(None, "seq"),
            P(None, "seq"),
            P("seq", None),
            P(None, "seq"),
            P(None, "seq"),
            P("seq", None),
            P(),
            P(),
            P(),
            P(),
            P(),
            P("batch", "seq", None),
        ),
        out_specs=(
            P("batch", "seq", None),
            P("batch", "seq", None),
            P(None, "seq"),
            P(None, "seq"),
            P(None, "seq"),
            P("seq", None),
            P(None, "seq"),
            P(None, "seq"),
            P("seq", None),
            P(),
            P(),
            P(),
            P(),
            P(),
        ),
        check_vma=False,
    )
```

```python
import jax
import jax.numpy as jnp
import numpy as np
from jax import lax
from jax.experimental import pallas as pl
from jax.experimental.pallas import tpu as pltpu
from jax.sharding import PartitionSpec as P

HEADS = 16
HEAD = 64


EPS = 1e-06


def shifted(value, axis, steps):
    count = lax.axis_size(axis)
    first, last = (max(0, -steps), min(count, count - steps))
    return lax.ppermute(value, axis, [(source, source + steps) for source in range(first, last)])


def shifted_2(block, axis, distance):
    devices = range(lax.axis_size(axis))
    route = [((i - distance) % len(devices), i) for i in devices]
    return lax.ppermute(block, axis, route)


def normalized(weight, axis):
    wide = weight.astype(jnp.float32)
    return wide * lax.rsqrt(jnp.sum(wide * wide, axis=axis, keepdims=True) + EPS)


def rms(values):
    return values * lax.rsqrt(jnp.mean(values * values, axis=-1, keepdims=True) + EPS)


def doc_layout(len_row, tok_index):
    docs = jnp.arange(len_row.shape[0])
    starts = jnp.sum(jnp.where(docs[:, None] < docs[None, :], len_row[:, None], 0), axis=0)
    started = starts[None, :] <= tok_index[:, None]
    doc_ids = jnp.sum(started.astype(jnp.int32), axis=1) - 1
    first_tok = jnp.max(jnp.where(started, starts[None, :], 0), axis=1)
    return (doc_ids, tok_index - first_tok)


def rope(values, position):
    half = values.shape[-1] // 2
    freqs = 10000.0 ** (-jnp.arange(half, dtype=jnp.float32) / half)
    angle = position.astype(jnp.float32)[:, None] * freqs[None, :]
    cosine = jnp.cos(angle)[:, None, :]
    sine = jnp.sin(angle)[:, None, :]
    first = values[..., :half]
    second = values[..., half:]
    return jnp.concatenate(
        [first * cosine - second * sine, first * sine + second * cosine], axis=-1
    )


def prepare(linear, position, gain):
    count = linear.shape[0]
    shaped = linear.reshape(count, HEADS, HEAD)
    turned = rms(rope(shaped, position)) * gain.reshape(HEADS, HEAD)
    return turned.reshape(count, HEADS * HEAD)


def residual_mix(state, branch, alpha):
    return rms(state + alpha * (rms(branch) - state))


def gating(up_lin, gate_lin, up_scale, gate_scale):
    return up_scale * up_lin * jax.nn.silu(gate_scale * gate_lin)


def unit_back(raw_shard, grad_shard, axis):
    primal, pullback = jax.vjp(
        lambda weight: normalized(weight, axis), raw_shard.astype(jnp.float32)
    )
    return pullback(grad_shard)[0]


def on_device_general(
    states,
    lengths,
    w_query,
    w_key,
    w_value,
    w_out,
    w_up,
    w_gate,
    w_down,
    qk_scale,
    up_scale,
    gate_scale,
    alpha_attn,
    alpha_mlp,
    d_out,
):
    seq_count = lax.axis_size("seq")
    my_index = lax.axis_index("seq")
    rows = states.shape[0]
    tok = states.shape[1]
    width = states.shape[2]
    flat = rows * tok
    score_scale = HEAD ** (-0.5)
    row_layout = jax.vmap(doc_layout, in_axes=(0, None))
    unit_query = normalized(w_query, 0).astype(jnp.bfloat16)
    unit_key = normalized(w_key, 0).astype(jnp.bfloat16)
    unit_value = normalized(w_value, 0).astype(jnp.bfloat16)
    unit_out = normalized(w_out, 1).astype(jnp.bfloat16)
    unit_up = normalized(w_up, 0).astype(jnp.bfloat16)
    unit_gate = normalized(w_gate, 0).astype(jnp.bfloat16)
    unit_down = normalized(w_down, 1).astype(jnp.bfloat16)
    full_weights = (
        lax.all_gather(unit_query, "seq", axis=1, tiled=True),
        lax.all_gather(unit_key, "seq", axis=1, tiled=True),
        lax.all_gather(unit_value, "seq", axis=1, tiled=True),
        lax.all_gather(unit_out, "seq", axis=0, tiled=True),
        lax.all_gather(unit_up, "seq", axis=1, tiled=True),
        lax.all_gather(unit_gate, "seq", axis=1, tiled=True),
        lax.all_gather(unit_down, "seq", axis=0, tiled=True),
    )
    full_query, full_key, full_value, full_out, full_up, full_gate, full_down = full_weights
    tok_index = my_index * tok + jnp.arange(tok, dtype=jnp.int32)
    doc_ids, position = row_layout(lengths, tok_index)
    flat_pos = position.reshape(flat)
    state_in = states.reshape(flat, width)
    x_low = state_in.astype(jnp.bfloat16)
    query_lin = jnp.dot(x_low, full_query, preferred_element_type=jnp.float32)
    key_lin = jnp.dot(x_low, full_key, preferred_element_type=jnp.float32)
    value_lin = jnp.dot(x_low, full_value, preferred_element_type=jnp.float32)

    def front(query_part, key_part, gain):
        return (prepare(query_part, flat_pos, gain), prepare(key_part, flat_pos, gain))

    query_f, key_f = front(query_lin, key_lin, qk_scale)
    query_h = query_f.astype(jnp.bfloat16).reshape(rows, tok, HEADS, HEAD)
    key_h = key_f.astype(jnp.bfloat16).reshape(rows, tok, HEADS, HEAD)
    value_h = value_lin.astype(jnp.bfloat16).reshape(rows, tok, HEADS, HEAD)

    def block_scores(key_blk, source):
        key_index = source * tok + jnp.arange(tok, dtype=jnp.int32)
        key_docs, key_pos = row_layout(lengths, key_index)
        scores = (
            jnp.einsum("bqhd,bkhd->bqhk", query_h, key_blk, preferred_element_type=jnp.float32)
            * score_scale
        )
        allowed = (doc_ids[:, :, None] == key_docs[:, None, :]) & (
            key_index[None, None, :] <= tok_index[None, :, None]
        )
        return (scores, allowed[:, :, None, :])

    def is_active(source):
        last_key = jnp.reshape(source * tok + tok - 1, (1,))
        last_doc, last_pos = row_layout(lengths, last_key)
        return (source <= my_index) & jnp.any(last_doc[:, 0] >= doc_ids[:, 0])

    def attend(running, key_blk, value_blk, source):

        def compute(carried):
            best, denom_sum, accum = carried
            scores, allowed = block_scores(key_blk, source)
            new_best = jnp.maximum(best, jnp.max(jnp.where(allowed, scores, -1e30), axis=3))
            weights = jnp.where(allowed, jnp.exp(scores - new_best[:, :, :, None]), 0.0)
            shrink = jnp.exp(best - new_best)
            denom_sum = denom_sum * shrink + jnp.sum(weights, axis=3)
            accum = accum * shrink[:, :, :, None] + jnp.einsum(
                "bqhk,bkhd->bqhd",
                weights.astype(jnp.bfloat16),
                value_blk,
                preferred_element_type=jnp.float32,
            )
            return (new_best, denom_sum, accum)

        return lax.cond(is_active(source), compute, lambda carried: carried, running)

    reach = seq_count - 1
    start_state = (
        jnp.full((rows, tok, HEADS), -1e30, jnp.float32),
        jnp.zeros((rows, tok, HEADS), jnp.float32),
        jnp.zeros((rows, tok, HEADS, HEAD), jnp.float32),
    )
    first_state = attend(start_state, key_h, value_h, my_index)

    def cycle_step(step, loop_carry):
        running, key_blk, value_blk = loop_carry
        key_blk, value_blk = shifted((key_blk, value_blk), "seq", 1)
        source = (my_index - step) % seq_count
        return (attend(running, key_blk, value_blk, source), key_blk, value_blk)

    final_state, spent_key, spent_value = lax.fori_loop(
        1, reach + 1, cycle_step, (first_state, key_h, value_h)
    )
    best, denom_sum, accum = final_state
    attended = accum / denom_sum[:, :, :, None]
    log_sum = best + jnp.log(denom_sum)
    attended_low = attended.astype(jnp.bfloat16).reshape(flat, width)
    attn_branch = jnp.dot(attended_low, full_out, preferred_element_type=jnp.float32)
    state_mid = residual_mix(state_in, attn_branch, alpha_attn)
    mid_low = state_mid.astype(jnp.bfloat16)
    up_lin = jnp.dot(mid_low, full_up, preferred_element_type=jnp.float32)
    gate_lin = jnp.dot(mid_low, full_gate, preferred_element_type=jnp.float32)
    gated_low = gating(up_lin, gate_lin, up_scale, gate_scale).astype(jnp.bfloat16)
    mlp_branch = jnp.dot(gated_low, full_down, preferred_element_type=jnp.float32)
    output = residual_mix(state_mid, mlp_branch, alpha_mlp)
    back_weights = (
        lax.all_gather(unit_query, "seq", axis=1, tiled=True),
        lax.all_gather(unit_key, "seq", axis=1, tiled=True),
        lax.all_gather(unit_value, "seq", axis=1, tiled=True),
        lax.all_gather(unit_out, "seq", axis=0, tiled=True),
        lax.all_gather(unit_up, "seq", axis=1, tiled=True),
        lax.all_gather(unit_gate, "seq", axis=1, tiled=True),
        lax.all_gather(unit_down, "seq", axis=0, tiled=True),
    )
    back_query, back_key, back_value, back_out, back_up, back_gate, back_down = back_weights
    primal, pull_mlp = jax.vjp(residual_mix, state_mid, mlp_branch, alpha_mlp)
    d_mid, d_mlp, g_alpha_mlp = pull_mlp(d_out.reshape(flat, width))
    d_mlp_low = d_mlp.astype(jnp.bfloat16)
    grad_down = jnp.einsum("tf,td->fd", gated_low, d_mlp_low, preferred_element_type=jnp.float32)
    d_gated = jnp.einsum("td,fd->tf", d_mlp_low, back_down, preferred_element_type=jnp.float32)
    primal, pull_gate = jax.vjp(gating, up_lin, gate_lin, up_scale, gate_scale)
    d_up, d_gate, g_up_scale, g_gate_scale = pull_gate(d_gated)
    d_up_low = d_up.astype(jnp.bfloat16)
    d_gate_low = d_gate.astype(jnp.bfloat16)
    grad_up = jnp.einsum("tc,tf->cf", mid_low, d_up_low, preferred_element_type=jnp.float32)
    grad_gate = jnp.einsum("tc,tf->cf", mid_low, d_gate_low, preferred_element_type=jnp.float32)
    d_mid = d_mid + jnp.einsum("tf,cf->tc", d_up_low, back_up, preferred_element_type=jnp.float32)
    d_mid = d_mid + jnp.einsum(
        "tf,cf->tc", d_gate_low, back_gate, preferred_element_type=jnp.float32
    )
    primal, pull_attn = jax.vjp(residual_mix, state_in, attn_branch, alpha_attn)
    d_state, d_attn, g_alpha_attn = pull_attn(d_mid)
    d_attn_low = d_attn.astype(jnp.bfloat16)
    grad_out = jnp.einsum("tc,td->cd", attended_low, d_attn_low, preferred_element_type=jnp.float32)
    d_attended = jnp.einsum("td,cd->tc", d_attn_low, back_out, preferred_element_type=jnp.float32)
    d_att_low = d_attended.astype(jnp.bfloat16).reshape(rows, tok, HEADS, HEAD)
    delta = jnp.sum(d_att_low.astype(jnp.float32) * attended, axis=3)

    def attend_back(d_query, key_blk, value_blk, d_key, d_value, source):

        def compute(carried):
            d_query, d_key, d_value = carried
            scores, allowed = block_scores(key_blk, source)
            probs = jnp.where(allowed, jnp.exp(scores - log_sum[:, :, :, None]), 0.0)
            d_probs = jnp.einsum(
                "bqhd,bkhd->bqhk", d_att_low, value_blk, preferred_element_type=jnp.float32
            )
            d_scores = (probs * (d_probs - delta[:, :, :, None])).astype(jnp.bfloat16)
            d_query = d_query + jnp.einsum(
                "bqhk,bkhd->bqhd", d_scores, key_blk, preferred_element_type=jnp.float32
            )
            d_key = d_key + jnp.einsum(
                "bqhk,bqhd->bkhd", d_scores, query_h, preferred_element_type=jnp.float32
            )
            d_value = d_value + jnp.einsum(
                "bqhk,bqhd->bkhd",
                probs.astype(jnp.bfloat16),
                d_att_low,
                preferred_element_type=jnp.float32,
            )
            return (d_query, d_key, d_value)

        return lax.cond(
            is_active(source), compute, lambda carried: carried, (d_query, d_key, d_value)
        )

    def back_step(step, loop_carry):
        d_query, key_blk, value_blk, d_key, d_value = loop_carry
        source = (my_index - step) % seq_count
        d_query, d_key, d_value = attend_back(d_query, key_blk, value_blk, d_key, d_value, source)
        d_key, d_value = (
            shifted_2(d_key.astype(jnp.bfloat16), "seq", 1).astype(d_key.dtype),
            shifted_2(d_value.astype(jnp.bfloat16), "seq", 1).astype(d_value.dtype),
        )
        key_blk, value_blk = shifted((key_blk, value_blk), "seq", 1)
        return (d_query, key_blk, value_blk, d_key, d_value)

    zero_heads = jnp.zeros((rows, tok, HEADS, HEAD), jnp.float32)
    d_query_h, last_key_blk, last_value_blk, d_key_h, d_value_h = lax.fori_loop(
        0, reach, back_step, (zero_heads, key_h, value_h, zero_heads, zero_heads)
    )
    d_query_h, d_key_h, d_value_h = attend_back(
        d_query_h, last_key_blk, last_value_blk, d_key_h, d_value_h, (my_index - reach) % seq_count
    )
    d_key_h, d_value_h = (
        shifted_2(d_key_h.astype(jnp.bfloat16), "seq", -reach).astype(d_key_h.dtype),
        shifted_2(d_value_h.astype(jnp.bfloat16), "seq", -reach).astype(d_value_h.dtype),
    )
    primal, pull_front = jax.vjp(front, query_lin, key_lin, qk_scale)
    d_query_lin, d_key_lin, g_qk_scale = pull_front(
        (d_query_h.reshape(flat, width) * score_scale, d_key_h.reshape(flat, width) * score_scale)
    )
    d_query_low = d_query_lin.astype(jnp.bfloat16)
    d_key_low = d_key_lin.astype(jnp.bfloat16)
    d_value_low = d_value_h.reshape(flat, width).astype(jnp.bfloat16)
    grad_query = jnp.einsum("tc,tj->cj", x_low, d_query_low, preferred_element_type=jnp.float32)
    grad_key = jnp.einsum("tc,tj->cj", x_low, d_key_low, preferred_element_type=jnp.float32)
    grad_value = jnp.einsum("tc,tj->cj", x_low, d_value_low, preferred_element_type=jnp.float32)
    d_state = d_state + jnp.einsum(
        "tj,cj->tc", d_query_low, back_query, preferred_element_type=jnp.float32
    )
    d_state = d_state + jnp.einsum(
        "tj,cj->tc", d_key_low, back_key, preferred_element_type=jnp.float32
    )
    d_state = d_state + jnp.einsum(
        "tj,cj->tc", d_value_low, back_value, preferred_element_type=jnp.float32
    )
    shards = (
        lax.psum_scatter(
            grad_query.astype(jnp.bfloat16), "seq", scatter_dimension=1, tiled=True
        ).astype(jnp.float32),
        lax.psum_scatter(
            grad_key.astype(jnp.bfloat16), "seq", scatter_dimension=1, tiled=True
        ).astype(jnp.float32),
        lax.psum_scatter(
            grad_value.astype(jnp.bfloat16), "seq", scatter_dimension=1, tiled=True
        ).astype(jnp.float32),
        lax.psum_scatter(
            grad_out.astype(jnp.bfloat16), "seq", scatter_dimension=0, tiled=True
        ).astype(jnp.float32),
        lax.psum_scatter(
            grad_up.astype(jnp.bfloat16), "seq", scatter_dimension=1, tiled=True
        ).astype(jnp.float32),
        lax.psum_scatter(
            grad_gate.astype(jnp.bfloat16), "seq", scatter_dimension=1, tiled=True
        ).astype(jnp.float32),
        lax.psum_scatter(
            grad_down.astype(jnp.bfloat16), "seq", scatter_dimension=0, tiled=True
        ).astype(jnp.float32),
    )
    summed = (
        lax.psum(shards[0].astype(jnp.bfloat16), "batch").astype(jnp.float32),
        lax.psum(shards[1].astype(jnp.bfloat16), "batch").astype(jnp.float32),
        lax.psum(shards[2].astype(jnp.bfloat16), "batch").astype(jnp.float32),
        lax.psum(shards[3].astype(jnp.bfloat16), "batch").astype(jnp.float32),
        lax.psum(shards[4].astype(jnp.bfloat16), "batch").astype(jnp.float32),
        lax.psum(shards[5].astype(jnp.bfloat16), "batch").astype(jnp.float32),
        lax.psum(shards[6].astype(jnp.bfloat16), "batch").astype(jnp.float32),
    )
    gain_grads = lax.psum(
        (g_qk_scale, g_up_scale, g_gate_scale, g_alpha_attn, g_alpha_mlp), ("seq", "batch")
    )
    g_query = unit_back(w_query, summed[0], 0)
    g_key = unit_back(w_key, summed[1], 0)
    g_value = unit_back(w_value, summed[2], 0)
    g_out = unit_back(w_out, summed[3], 1)
    g_up = unit_back(w_up, summed[4], 0)
    g_gate = unit_back(w_gate, summed[5], 0)
    g_down = unit_back(w_down, summed[6], 1)
    return (
        output.reshape(rows, tok, width),
        d_state.reshape(rows, tok, width),
        g_query,
        g_key,
        g_value,
        g_out,
        g_up,
        g_gate,
        g_down,
        gain_grads[0],
        gain_grads[1],
        gain_grads[2],
        gain_grads[3],
        gain_grads[4],
    )


BF16 = jnp.bfloat16
F32 = jnp.float32
LANES = 128
MIB = 1 << 20
NT = (((1,), (1,)), ((), ()))
TN = (((0,), (0,)), ((), ()))


def place():
    s = lax.axis_index("seq")
    return s // 4, (s // 2) % 2, s % 2, lax.axis_index("batch")


def dev(z, x, c, y):
    return (z * 4 + x * 2 + c, y)


def remote(src, dst, send, recv, device):
    return pltpu.make_async_remote_copy(
        src_ref=src,
        dst_ref=dst,
        send_sem=send,
        recv_sem=recv,
        device_id=device,
        device_id_type=pl.DeviceIdType.MESH,
    )


def dot(a, b):
    return jnp.dot(a, b, preferred_element_type=F32)


def dot_nt(a, b):
    return lax.dot_general(a, b, NT, preferred_element_type=F32)


def dot_tn(a, b):
    return lax.dot_general(a, b, TN, preferred_element_type=F32)


BLOCK = 256


def inverse_norm(weight, axis):
    wide = weight.astype(F32)
    return lax.rsqrt(jnp.sum(wide * wide, axis=axis, keepdims=True) + EPS)


def unit_pull(weight, grad, axis):
    inverse = inverse_norm(weight, axis)
    unit = weight.astype(F32) * inverse
    return inverse * (grad - unit * jnp.sum(grad * unit, axis=axis, keepdims=True))


def turn_tables(count):
    half = HEAD // 2
    freqs = (10000.0 ** (-np.arange(half, dtype=np.float32) / half)).astype(np.float32)
    angle = np.arange(count, dtype=np.float32)[:, None] * freqs[None, :]
    cosine = np.cos(angle).astype(np.float32)
    sine = np.sin(angle).astype(np.float32)
    return np.tile(cosine, (1, 4)), np.concatenate([-sine, sine, -sine, sine], axis=1)


def mix(state, branch, alpha):
    inv_b = lax.rsqrt(jnp.mean(branch * branch, axis=-1, keepdims=True) + EPS)
    unit_b = branch * inv_b
    step = unit_b - state
    mixed = state + alpha * step
    inv_m = lax.rsqrt(jnp.mean(mixed * mixed, axis=-1, keepdims=True) + EPS)
    return mixed * inv_m, (unit_b, inv_b, step, inv_m)


def mix_back(grad, out, saved, alpha):
    unit_b, inv_b, step, inv_m = saved
    d_mixed = inv_m * (grad - out * jnp.mean(grad * out, axis=-1, keepdims=True))
    d_alpha = jnp.sum(d_mixed * step, axis=0)
    d_unit = d_mixed * alpha
    d_branch = inv_b * (d_unit - unit_b * jnp.mean(d_unit * unit_b, axis=-1, keepdims=True))
    return d_mixed - d_unit, d_branch, d_alpha


def inside(v):
    return (v >= 0) & (v < 4)


def unit_cols(w):
    wide = w.astype(F32)
    return (wide * lax.rsqrt(jnp.sum(wide * wide, axis=0, keepdims=True) + EPS)).astype(BF16)


def unit_rows(w):
    wide = w.astype(F32)
    return (wide * lax.rsqrt(jnp.sum(wide * wide, axis=1, keepdims=True) + EPS)).astype(BF16)


class Line:
    def __init__(self, buf, sems):
        self.buf, (self.send, self.recv) = buf, sems

    def hop(self, zz, way):
        z, x, c, y = place()
        b = self.buf.at[zz]
        return remote(b, b, self.send.at[zz, (way + 1) // 2], self.recv.at[zz], dev(z + way, x, c, y))

    def start(self):
        z = place()[0]
        for way in (-1, 1):

            @pl.when(inside(z + way))
            def _():
                self.hop(z, way).start()

    def arrive(self, k, way):
        z = place()[0]
        zz = z - way * k

        @pl.when(inside(zz))
        def _():
            self.hop(zz, -way).wait_recv()

            @pl.when(inside(z + way))
            def _():
                self.hop(zz, way).start()

    def drain(self):
        z = place()[0]
        for zz in range(4):
            for way in (-1, 1):

                @pl.when(((zz - z) * way <= 0) & inside(z + way))
                def _():
                    self.hop(zz, way).wait_send()


LINE_SEM = [pltpu.SemaphoreType.DMA((4, 2)), pltpu.SemaphoreType.DMA((4,))]


class Row:
    def __init__(self, buf, sems):
        self.buf, (self.zs, self.xs, self.cs, self.recv) = buf, sems

    def hop_z(self, zz, way):
        z, x, c, y = place()
        b = zz * 4 + x * 2 + c
        return remote(
            self.buf.at[b], self.buf.at[b], self.zs.at[zz, (way + 1) // 2], self.recv.at[b],
            dev(z + way, x, c, y),
        )

    def hop_x(self, zz):
        z, x, c, y = place()
        b = zz * 4 + x * 2 + c
        return remote(
            self.buf.at[b], self.buf.at[b], self.xs.at[zz], self.recv.at[b], dev(z, 1 - x, c, y)
        )

    def hop_c(self, zz, xx):
        z, x, c, y = place()
        b = zz * 4 + xx * 2 + c
        return remote(
            self.buf.at[b], self.buf.at[b], self.cs.at[zz, xx], self.recv.at[b], dev(z, x, 1 - c, y)
        )

    def arrived(self, b):
        z, x, c, y = place()
        remote(
            self.buf.at[b], self.buf.at[b], self.xs.at[0], self.recv.at[b], dev(z, x, 1 - c, y)
        ).wait_recv()

    def start(self):
        z, x, c, y = place()
        for way in (-1, 1):

            @pl.when(inside(z + way))
            def _():
                self.hop_z(z, way).start()

        self.hop_x(z).start()
        self.hop_c(z, x).start()

    def arrive(self, k):
        z, x, c, y = place()
        for way in (-1, 1):
            zz = z - way * k

            @pl.when(inside(zz))
            def _():
                self.arrived(zz * 4 + x * 2 + c)

                @pl.when(inside(z + way))
                def _():
                    self.hop_z(zz, way).start()

                self.hop_x(zz).start()
                self.hop_c(zz, x).start()

    def relay_from(self, k):
        z = place()[0]
        for way in (-1, 1):
            zz = z - way * k

            @pl.when(inside(zz))
            def _():
                self.relay(zz)

    def finish(self):
        z, x, c, y = place()

        @pl.loop(0, 4)
        def _(zz):
            self.arrived(zz * 4 + x * 2 + 1 - c)
            self.arrived(zz * 4 + (1 - x) * 2 + 1 - c)
            for way in (-1, 1):

                @pl.when(((zz - z) * way <= 0) & inside(z + way))
                def _():
                    self.hop_z(zz, way).wait_send()

            self.hop_x(zz).wait_send()
            self.hop_c(zz, 0).wait_send()
            self.hop_c(zz, 1).wait_send()

    def relay(self, zz):
        z, x, c, y = place()
        self.arrived(zz * 4 + (1 - x) * 2 + c)
        self.hop_c(zz, 1 - x).start()


ROW_SEM = [
    pltpu.SemaphoreType.DMA((4, 2)),
    pltpu.SemaphoreType.DMA((4,)),
    pltpu.SemaphoreType.DMA((4, 2)),
    pltpu.SemaphoreType.DMA((16,)),
]


def greet_row():
    z, x, c, y = place()
    s = z * 4 + x * 2 + c
    bar = pltpu.get_barrier_semaphore()

    @pl.loop(1, 16)
    def _(k):
        pl.semaphore_signal(
            bar, inc=1, device_id=((s + k) % 16, y), device_id_type=pl.DeviceIdType.MESH
        )

    pl.semaphore_signal(bar, inc=1, device_id=dev(z, x, c, 1 - y), device_id_type=pl.DeviceIdType.MESH)
    pl.semaphore_wait(bar, 16)


def half_swap(value):
    lane = lax.broadcasted_iota(jnp.int32, value.shape, 1)
    return jnp.where(
        lane % HEAD < HEAD // 2, pltpu.roll(value, LANES - HEAD // 2, 1), pltpu.roll(value, HEAD // 2, 1)
    )


def head_means(value):
    lane = lax.broadcasted_iota(jnp.int32, value.shape, 1)
    first = jnp.sum(jnp.where(lane < HEAD, value, 0.0), axis=1, keepdims=True)
    both = jnp.sum(value, axis=1, keepdims=True)
    return jnp.where(lane < HEAD, first, both - first) * (1.0 / HEAD)


def side_by_side(block):
    half = block.shape[0] // 2
    lane = lax.broadcasted_iota(jnp.int32, (half, LANES), 1)
    return jnp.where(lane < HEAD, block[:half], pltpu.roll(block[half:], HEAD, 1))


def peers():
    z, x, c, y = place()
    return ((x, 1 - c), (1 - x, c), (1 - x, 1 - c))


def spread_heads(b, env):
    rows = pl.ds(pl.multiple_of(b * LANES, LANES), LANES)
    lane = lax.broadcasted_iota(jnp.int32, (LANES, LANES), 1)
    one = jnp.where(lane < HEAD + 2, 1.0, 0.0)
    qk = env.heads_in[b, 0:LANES, :].astype(F32)
    env.q_ext[rows, :] = jnp.where(lane < HEAD, qk, 0.0).astype(BF16)
    env.k_ext[rows, :] = jnp.where(lane < HEAD, pltpu.roll(qk, HEAD, 1), one).astype(BF16)
    packed = env.heads_in[b, LANES:, :].astype(F32)
    value = jnp.concatenate([packed, pltpu.roll(packed, HEAD, 1)], axis=0)
    env.v_ext[rows, :] = jnp.where(lane < HEAD, value, one).astype(BF16)


class Reduce:
    def __init__(self, part, passing, landed, send, recv):
        self.part, self.passing, self.landed, self.send, self.recv = part, passing, landed, send, recv

    def hop(self, owner, way):
        z, x, c, y = place()
        spot = jnp.where((owner == z + way) & (way < 0), 4, owner)
        return remote(
            self.passing.at[owner], self.landed.at[spot], self.send.at[owner], self.recv.at[spot],
            dev(z + way, x, c, y),
        )

    def wait_spot(self, spot):
        z, x, c, y = place()
        remote(
            self.passing.at[0], self.landed.at[spot], self.send.at[0], self.recv.at[spot],
            dev(z, x, 1 - c, y),
        ).wait_recv()

    def step(self, k):
        z = place()[0]
        for way in (-1, 1):
            owner = z + way * k

            @pl.when(inside(owner))
            def _():
                @pl.when(inside(z - way))
                def _():
                    self.wait_spot(owner)
                    self.passing[owner] = (
                        self.part(owner) + self.landed[owner].astype(F32)
                    ).astype(BF16)

                @pl.when(jnp.logical_not(inside(z - way)))
                def _():
                    self.passing[owner] = self.part(owner).astype(BF16)

                self.hop(owner, way).start()

    def finish(self, total):
        z = place()[0]
        total[...] = self.part(z)

        @pl.when(z > 0)
        def _():
            self.wait_spot(z)
            total[...] += self.landed[z].astype(F32)

        @pl.when(z < 3)
        def _():
            self.wait_spot(4)
            total[...] += self.landed[4].astype(F32)

        for owner in range(4):

            @pl.when(owner != z)
            def _():
                self.hop(owner, jnp.where(owner > z, 1, -1)).wait_send()


REDUCE_SEM = [pltpu.SemaphoreType.DMA((4,)), pltpu.SemaphoreType.DMA((5,))]


class Env:
    def __init__(self, names, refs):
        for name, ref in zip(names, refs, strict=True):
            setattr(self, name, ref)


def window(start, size):
    return pl.ds(pl.multiple_of(start, size), size)


def qkv_rows(slot):
    return window(slot * LANES, LANES), window(4 * LANES + slot * HEAD, HEAD)


def qkv_copies(env, slot, sems, device):
    (send, recv), spots = sems, qkv_rows(slot)
    return [
        remote(env.u_qkv.at[rows, :], env.u_qkv.at[rows, :], send.at[i], recv.at[i], device)
        for i, rows in enumerate(spots)
    ]


def qkv_groups(env):
    z, x, c, y = place()
    mine, other = 2 * x + c, 2 * (1 - x) + c
    core, side = dev(z, x, 1 - c, y), dev(z, 1 - x, c, y)
    s, r = env.q_send, env.q_recv
    return (
        qkv_copies(env, mine, (s.at[0], r.at[0]), core),
        qkv_copies(env, mine, (s.at[1], r.at[1]), side),
        qkv_copies(env, other, (s.at[2], r.at[2]), core),
    )


def ff_views(env, slot, half=None):
    if half is None:
        return env.ups.at[slot], env.gates.at[slot], env.downs.at[slot]
    upper, lower = window(half * 512, 512), window(half * 128, 128)
    return env.ups.at[slot, upper, :], env.gates.at[slot, upper, :], env.downs.at[slot, lower, :]


def ff_groups(env):
    z, x, c, y = place()
    mine, other = 2 * x + c, 2 * (1 - x) + c
    core, side, twin = dev(z, x, 1 - c, y), dev(z, 1 - x, c, y), dev(z, x, c, 1 - y)

    def group(g, views, device):
        return [
            remote(v, v, env.w_send.at[g, i], env.w_recv.at[g, i], device) for i, v in enumerate(views)
        ]

    return (
        group(0, ff_views(env, mine), core),
        group(1, ff_views(env, mine, y), side),
        group(2, ff_views(env, other, y), core),
        group(3, ff_views(env, other, y), twin),
        group(4, ff_views(env, other, 1 - y), core),
    )


def each(copies, action):
    for copy in copies:
        getattr(copy, action)()


class Piece:
    def __init__(self, view, land_c, land_y, land_x, out, sems):
        self.view, self.land_c, self.land_y, self.land_x, self.out = view, land_c, land_y, land_x, out
        self.send, self.recv = sems

    def slot(self, h):
        z, x, c, y = place()
        return 2 * (1 - x if h == 0 else x) + c

    def to_core(self, h):
        z, x, c, y = place()
        xx = 1 - x if h == 0 else x
        return remote(
            self.view(2 * xx + 1 - c, None), self.land_c.at[h], self.send.at[h], self.recv.at[h],
            dev(z, x, 1 - c, y),
        )

    def to_twin(self, h):
        z, x, c, y = place()
        return remote(
            self.view(self.slot(h), 1 - y), self.land_y.at[h], self.send.at[2 + h], self.recv.at[2 + h],
            dev(z, x, c, 1 - y),
        )

    def to_side(self):
        z, x, c, y = place()
        return remote(
            self.view(self.slot(0), y), self.land_x, self.send.at[4], self.recv.at[4], dev(z, 1 - x, c, y)
        )

    def swap(self):
        z, x, c, y = place()
        return remote(self.out(y), self.out(y), self.send.at[5], self.recv.at[5], dev(z, x, c, 1 - y))

    def start(self):
        self.to_core(0).start()
        self.to_core(1).start()

    def pass_twin(self):
        for h in range(2):
            self.to_core(h).wait_recv()
            both = self.view(self.slot(h), None)
            both[...] = (both[...].astype(F32) + self.land_c[h].astype(F32)).astype(BF16)
            self.to_twin(h).start()

    def pass_side(self):
        y = place()[3]
        self.to_twin(0).wait_recv()
        give = self.view(self.slot(0), y)
        give[...] = (give[...].astype(F32) + self.land_y[0].astype(F32)).astype(BF16)
        self.to_side().start()

    def pass_back(self):
        y = place()[3]
        self.to_twin(1).wait_recv()
        self.to_side().wait_recv()
        keep = self.view(self.slot(1), y)
        self.out(y)[...] = (
            keep[...].astype(F32) + self.land_y[1].astype(F32) + self.land_x[...].astype(F32)
        ).astype(BF16)
        self.swap().start()

    def finish(self):
        self.swap().wait()
        for h in range(2):
            self.to_core(h).wait_send()
            self.to_twin(h).wait_send()
        self.to_side().wait_send()


def project_block(zz, env):
    z, x, c, y = place()
    linear = dot_nt(env.x_line[zz], env.u_qkv[...])
    lane = lax.broadcasted_iota(jnp.int32, (LANES, LANES), 1)
    scale = jnp.where(lane < HEAD, HEAD ** (-0.5), 1.0)
    cosine, sine = env.cosine[zz], env.sine[zz]
    for sl in range(4):
        qk = linear[:, sl * LANES : (sl + 1) * LANES]
        turned = qk * cosine + half_swap(qk) * sine
        env.turned[zz, sl] = turned
        unit = turned * lax.rsqrt(head_means(turned * turned) + EPS)
        out = (unit * env.gain[sl : sl + 1, :]).astype(BF16).astype(F32) * scale
        env.heads_out[zz, sl, 0:LANES, :] = out.astype(BF16)
        pair = linear[:, (4 + sl // 2) * LANES : (5 + sl // 2) * LANES]
        if sl % 2:
            pair = pltpu.roll(pair, HEAD, 1)
        env.heads_out[zz, sl, LANES:, :] = side_by_side(pair).astype(BF16)
    b = zz * 4 + x * 2 + c
    env.heads_in[b] = env.heads_out[zz, x * 2 + c]
    for i, (xx, cc) in enumerate(peers()):
        remote(
            env.heads_out.at[zz, xx * 2 + cc], env.heads_in.at[b], env.hs.at[zz, i], env.hr.at[b],
            dev(z, xx, cc, y),
        ).start()


def attend_block(i, env):
    z, x, c, y = place()
    s = z * 4 + x * 2 + c
    row = lax.broadcasted_iota(jnp.int32, (BLOCK, BLOCK), 0)
    col = lax.broadcasted_iota(jnp.int32, (BLOCK, BLOCK), 1)
    lane = lax.broadcasted_iota(jnp.int32, (BLOCK, LANES), 1)
    rows = pl.ds(i * BLOCK, BLOCK)
    q = env.q_ext[rows, :]
    total = jnp.zeros((BLOCK, LANES), F32)
    for j in range(i + 1):
        keys = pl.ds(j * BLOCK, BLOCK)
        p = jnp.exp(dot_nt(q, env.k_ext[keys, :]))
        if i == j:
            p = jnp.where(row >= col, p, 0.0)
        total = total + dot(p.astype(BF16), env.v_ext[keys, :])
    denom = total[:, HEAD : HEAD + 1]
    out = total / denom
    env.attended[rows, :] = out
    log = -jnp.log(denom)
    high = log.astype(BF16).astype(F32)
    env.q_ext[rows, :] = jnp.where(
        lane == HEAD, high, jnp.where(lane == HEAD + 1, log - high, q.astype(F32))
    ).astype(BF16)
    for k in range(2):
        t = 2 * i + k
        env.att_out[t] = side_by_side(out[k * LANES : (k + 1) * LANES]).astype(BF16)
        send_head(t, s, env.att_out, env.att_in, env.as_, env.ar, y)


def send_head(t, s, src, land, send, recv, y):
    @pl.when(t != s)
    def _():
        remote(src.at[t], land.at[s], send.at[t], recv.at[s], (t, y)).start()

    @pl.when(t == s)
    def _():
        land[t] = src[t]


def wait_heads(s, src, land, send, recv, y):
    @pl.loop(0, 16)
    def _(t):
        @pl.when(t != s)
        def _():
            remote(src.at[t], land.at[t], send.at[t], recv.at[t], (t, y)).wait()


def lay_heads(land, dst):
    lane = lax.broadcasted_iota(jnp.int32, (HEAD, LANES), 1)
    for p in range(8):
        first = land[2 * p].astype(F32)
        second = land[2 * p + 1].astype(F32)
        cols = slice(p * LANES, (p + 1) * LANES)
        dst[0:HEAD, cols] = jnp.where(lane < HEAD, first, pltpu.roll(second, HEAD, 1)).astype(BF16)
        dst[HEAD:, cols] = jnp.where(lane < HEAD, pltpu.roll(first, HEAD, 1), second).astype(BF16)


def mlp_forward(h, env):
    @pl.loop(0, 4)
    def _(n):
        cols = window(n * 256, 256)
        mid = env.h_line[h].reshape(256, 1024)
        up = dot(mid, env.ups[n])
        gate = dot(mid, env.gates[n]) * env.gate_row[:, cols]
        env.up_lin[h, cols, :] = up
        env.gate_val[h, :, cols] = gate
        act = gate * (1.0 / (1.0 + jnp.exp(-gate)))
        env.hidden[h, :, cols] = (up * env.up_row[:, cols] * act).astype(BF16)

    @pl.loop(0, 4)
    def _(n):
        cols = window(n * 256, 256)
        env.part[h, :, :, cols] = dot(env.hidden[h], env.downs[:, :, cols].reshape(1024, 256)).reshape(
            4, 64, 256
        )


def mlp_backward(h, env):
    @pl.loop(0, 4)
    def _(n):
        cols = window(n * 256, 256)
        d_hidden = dot_nt(env.dm_line[h].reshape(256, 1024), env.downs[n])
        up, gate = env.up_lin[h, cols, :], env.gate_val[h, :, cols]
        up_gain, gate_gain = env.up_row[:, cols], env.gate_row[:, cols]
        sig = 1.0 / (1.0 + jnp.exp(-gate))
        d_up = d_hidden * (gate * sig)
        d_gate = d_hidden * (up * up_gain) * (sig * (1.0 + gate * (1.0 - sig)))
        env.gains[0:1, cols] += jnp.sum(d_up * up, axis=0, keepdims=True)
        env.gains[1:2, cols] += jnp.sum(d_gate * gate, axis=0, keepdims=True) / gate_gain
        env.d_up[h, n] = (d_up * up_gain).astype(BF16)
        env.d_gate[h, n] = (d_gate * gate_gain).astype(BF16)

    @pl.loop(0, 4)
    def _(n):
        cols = window(n * 256, 256)
        back = dot_nt(env.d_up[h, 0], env.ups[0, cols, :])
        for m in range(4):
            if m:
                back = back + dot_nt(env.d_up[h, m], env.ups[m, cols, :])
            back = back + dot_nt(env.d_gate[h, m], env.gates[m, cols, :])
        env.part[h, :, :, cols] = back.reshape(4, 64, 256)


def weight_gradient(left, right, store):
    @pl.loop(0, 4)
    def _(n):
        store(n, (dot_tn(left(0), right(0, n)) + dot_tn(left(1), right(1, n))).astype(BF16))


def rows_of(h):
    return slice(64 * h, 64 * (h + 1))


def after_forward(h, reduce, env):
    z, rows = place()[0], rows_of(h)
    reduce.finish(env.total)
    alpha = env.mix_row[1:2, :]
    out, saved = mix(env.mid[rows, :], env.total[...], alpha)
    env.output[rows, :] = out
    d_mid, d_branch, d_alpha = mix_back(env.d_out[rows, :], out, saved, alpha)
    env.d_mid[rows, :] = d_mid
    env.gains[3:4, :] += d_alpha[None, :]
    env.dm_line[h, z] = d_branch.astype(BF16)


def after_backward(h, reduce, env):
    rows = rows_of(h)
    reduce.finish(env.total)
    alpha = env.mix_row[0:1, :]
    mid, saved = mix(env.states[rows, :], env.branch[rows, :], alpha)
    d_state, d_branch, d_alpha = mix_back(env.d_mid[rows, :] + env.total[...], mid, saved, alpha)
    env.d_states[rows, :] = d_state
    env.gains[2:3, :] += d_alpha[None, :]
    env.d_branch[rows, :] = d_branch.astype(BF16)


def spread_grads(b, env):
    rows = window(b * LANES, LANES)
    lane = lax.broadcasted_iota(jnp.int32, (LANES, LANES), 1)
    packed = env.datt_in[b].astype(F32)
    value = jnp.where(lane < HEAD, jnp.concatenate([packed, pltpu.roll(packed, HEAD, 1)], axis=0), 0.0)
    delta = -jnp.sum(value * env.attended[rows, :], axis=1, keepdims=True)
    high = delta.astype(BF16).astype(F32)
    env.do_ext[rows, :] = jnp.where(
        lane == HEAD, high, jnp.where(lane == HEAD + 1, delta - high, value)
    ).astype(BF16)


def attend_back_block(i, env, last):
    z, x, c, y = place()
    row = lax.broadcasted_iota(jnp.int32, (BLOCK, BLOCK), 0)
    col = lax.broadcasted_iota(jnp.int32, (BLOCK, BLOCK), 1)
    lane = lax.broadcasted_iota(jnp.int32, (LANES, LANES), 1)
    rows = pl.ds(i * BLOCK, BLOCK)
    q = env.q_ext[rows, :]
    do = env.do_ext[rows, :]
    dq = jnp.zeros((BLOCK, LANES), F32)
    for j in range(i + 1):
        keys = pl.ds(j * BLOCK, BLOCK)
        k = env.k_ext[keys, :]
        p = jnp.exp(dot_nt(k, q))
        if i == j:
            p = jnp.where(row <= col, p, 0.0)
        ds = (p * dot_nt(env.v_ext[keys, :], do)).astype(BF16)
        dv = dot(p.astype(BF16), do)
        dk = dot(ds, q)
        dq = dq + dot_tn(ds, k)
        if i == last:
            env.dk[keys, :] = dk
            env.dv[keys, :] = dv
        else:
            env.dk[keys, :] += dk
            env.dv[keys, :] += dv
    for n in range(2):
        part = slice(n * LANES, (n + 1) * LANES)
        b = 2 * i + n
        zz, sl = b // 4, b % 4
        tok = pl.ds(b * LANES, LANES)
        env.back_out[zz, sl, 0:LANES, :] = jnp.where(
            lane < HEAD, dq[part] * HEAD ** (-0.5), pltpu.roll(env.dk[tok, :], HEAD, 1)
        ).astype(BF16)
        env.back_out[zz, sl, LANES:, :] = side_by_side(env.dv[tok, :]).astype(BF16)
        mine = 2 * x + c

        @pl.when(sl == mine)
        def _():
            env.back_in[zz * 4 + mine] = env.back_out[zz, sl]

        @pl.when(sl != mine)
        def _():
            back_copy(zz, sl, mine, env).start()


def back_copy(zz, sl, source, env):
    z, x, c, y = place()
    return remote(
        env.back_out.at[zz, sl], env.back_in.at[zz * 4 + source], env.bs.at[zz, sl],
        env.br.at[zz * 4 + source], dev(z, sl // 2, sl % 2, y),
    )


def project_back(zz, env):
    z, x, c, y = place()
    mine = 2 * x + c
    cosine, sine = env.cosine[zz], env.sine[zz]
    lane = lax.broadcasted_iota(jnp.int32, (LANES, LANES), 1)
    values = []
    for sl in range(4):

        @pl.when(sl != mine)
        def _():
            back_copy(zz, sl, sl, env).wait()

        grad = env.back_in[zz * 4 + sl, 0:LANES, :].astype(F32)
        turned = env.turned[zz, sl]
        inverse = lax.rsqrt(head_means(turned * turned) + EPS)
        unit = turned * inverse
        env.gain_sum[sl : sl + 1, :] += jnp.sum(grad * unit, axis=0, keepdims=True)
        d_unit = grad * env.gain[sl : sl + 1, :]
        d_turned = inverse * (d_unit - unit * head_means(d_unit * unit))
        d_lin = d_turned * cosine - half_swap(d_turned) * sine
        env.d_lin[zz, :, sl * LANES : (sl + 1) * LANES] = d_lin.astype(BF16)
        packed = env.back_in[zz * 4 + sl, LANES:, :].astype(F32)
        values.append(jnp.concatenate([packed, pltpu.roll(packed, HEAD, 1)], axis=0))
    for p in range(2):
        pair = jnp.where(lane < HEAD, values[2 * p], pltpu.roll(values[2 * p + 1], HEAD, 1))
        env.d_lin[zz, :, (4 + p) * LANES : (5 + p) * LANES] = pair.astype(BF16)
    d_x = dot(env.d_lin[zz], env.u_qkv[...])
    env.part[0, zz] = d_x[:64]
    env.part[1, zz] = d_x[64:]


def layer(env):
    z, x, c, y = place()
    s = z * 4 + x * 2 + c
    mine = 2 * x + c
    env.back_out, env.back_in = env.heads_out, env.heads_in
    env.g_qkv, env.g_out = env.u_qkv, env.u_out
    tables = []
    for zz in range(4):
        b = zz * 4 + 2 * x + c
        tables.append(pltpu.make_async_copy(env.cosines.at[b], env.cosine.at[zz], env.t_sem.at[zz, 0]))
        tables.append(pltpu.make_async_copy(env.sines.at[b], env.sine.at[zz], env.t_sem.at[zz, 1]))
    each(tables, "start")

    env.x_line[z] = env.states[...].astype(BF16)
    qk_rows, v_rows = qkv_rows(mine)
    env.u_qkv[qk_rows, :] = jnp.concatenate(
        [unit_rows(env.w_query[...]), unit_rows(env.w_key[...])], axis=0
    )
    env.u_qkv[v_rows, :] = unit_rows(env.w_value[...])
    greet_row()
    line = Line(env.x_line, (env.x_send, env.x_recv))
    line.start()
    q_core, q_side, q_relay = qkv_groups(env)
    each(q_side, "start")
    each(q_core, "start")

    lane = lax.broadcasted_iota(jnp.int32, (1, LANES), 1)
    for pair in range(2):
        scale = env.qk_scale[window(z * 256 + pair * LANES, LANES)].reshape(1, LANES)
        turned = pltpu.roll(scale, HEAD, 1)
        env.gain[2 * pair : 2 * pair + 1, :] = jnp.where(lane < HEAD, scale, turned)
        env.gain[2 * pair + 1 : 2 * pair + 2, :] = jnp.where(lane < HEAD, turned, scale)
    env.up_row[...] = env.up_scale[window(z * 1024, 1024)].reshape(1, 1024)
    env.gate_row[...] = env.gate_scale[window(z * 1024, 1024)].reshape(1, 1024)
    env.mix_row[0:1, :] = env.alpha_attn[...].reshape(1, 1024)
    env.mix_row[1:2, :] = env.alpha_mlp[...].reshape(1, 1024)
    env.u_out[s] = unit_rows(env.w_out[...])
    env.ups[mine] = unit_cols(env.w_up[...])
    env.gates[mine] = unit_cols(env.w_gate[...])
    env.downs[mine] = unit_rows(env.w_down[...])
    env.gains[...] = jnp.zeros_like(env.gains)
    env.gain_sum[...] = jnp.zeros_like(env.gain_sum)
    ff = ff_groups(env)
    each(ff[0], "start")
    each(tables, "wait")

    for way in (-1, 1):
        line.arrive(1, way)
    each(q_side, "wait_recv")
    each(q_relay, "start")
    each(q_core, "wait_recv")
    each(q_relay, "wait_recv")
    ff[1][0].start()
    project_block(z, env)

    @pl.loop(1, 4)
    def _(k):
        @pl.when(k < 3)
        def _():
            for way in (-1, 1):
                line.arrive(k + 1, way)

        for i in range(1, 3):

            @pl.when(k == i)
            def _():
                ff[1][i].start()

        for way in (-1, 1):

            @pl.when(inside(z - way * k))
            def _():
                project_block(z - way * k, env)

    line.drain()
    for group in (q_side, q_core, q_relay):
        each(group, "wait_send")
    uo = Row(env.u_out, (env.o_z, env.o_x, env.o_c, env.o_r))
    uo.start()

    @pl.loop(0, 4)
    def _(zz):
        for i, (xx, cc) in enumerate(peers()):
            b = zz * 4 + xx * 2 + cc
            remote(
                env.heads_out.at[zz, xx * 2 + cc], env.heads_in.at[b], env.hs.at[zz, i], env.hr.at[b],
                dev(z, xx, cc, y),
            ).wait()

    @pl.loop(0, 16)
    def _(b):
        spread_heads(b, env)

    uo.arrive(1)
    ff[1][0].wait_recv()
    ff[2][0].start()
    ff[3][0].start()
    for i in range(4):
        attend_block(i, env)
    uo.relay(z)
    for i in range(4, 6):
        attend_block(i, env)
    uo.arrive(2)
    ff[1][1].wait_recv()
    ff[2][1].start()
    ff[3][1].start()
    uo.relay_from(1)
    for i in range(6, 8):
        attend_block(i, env)
    uo.arrive(3)
    ff[1][2].wait_recv()
    ff[2][2].start()
    ff[3][2].start()
    uo.relay_from(2)
    uo.relay_from(3)
    wait_heads(s, env.att_out, env.att_in, env.as_, env.ar, y)
    lay_heads(env.att_in, env.att_low)
    uo.finish()

    branch = dot(env.att_low[...], env.u_out[...].reshape(1024, 1024))
    env.branch[...] = branch
    mid, _ = mix(env.states[...], branch, env.mix_row[0:1, :])
    env.mid[...] = mid
    low = mid.astype(BF16)
    env.h_line[0, z] = low[:64]
    env.h_line[1, z] = low[64:]

    fa = Line(env.h_line.at[0], (env.fa_s, env.fa_r))
    fb = Line(env.h_line.at[1], (env.fb_s, env.fb_r))
    ba = Line(env.dm_line.at[0], (env.ba_s, env.ba_r))
    bb = Line(env.dm_line.at[1], (env.bb_s, env.bb_r))

    def reduce(h, send, recv):
        return Reduce(
            lambda owner: env.part[h, owner], env.passing.at[h], env.landed.at[h], send, recv
        )

    r0, r1 = reduce(0, env.r0_s, env.r0_r), reduce(1, env.r1_s, env.r1_r)

    def arrive(gather, k):
        for way in (-1, 1):
            gather.arrive(k, way)

    fa.start()
    arrive(fa, 1)
    arrive(fa, 2)
    fb.start()
    each(ff[3], "wait_recv")
    each(ff[4], "start")
    each(ff[0], "wait_recv")
    each(ff[2], "wait_recv")
    each(ff[4], "wait_recv")
    arrive(fa, 3)
    mlp_forward(0, env)
    arrive(fb, 1)
    r0.step(3)
    arrive(fb, 2)
    r0.step(2)
    arrive(fb, 3)
    r0.step(1)
    mlp_forward(1, env)
    r1.step(3)
    after_forward(0, r0, env)
    ba.start()
    r1.step(2)
    arrive(ba, 1)
    r1.step(1)
    arrive(ba, 2)
    after_forward(1, r1, env)
    bb.start()
    arrive(ba, 3)
    mlp_backward(0, env)
    arrive(bb, 1)
    r0.step(3)
    arrive(bb, 2)
    r0.step(2)
    arrive(bb, 3)
    r0.step(1)
    mlp_backward(1, env)
    r1.step(3)
    for gather in (fa, fb, ba, bb):
        gather.drain()
    for group in ff:
        each(group, "wait_send")

    def both(ref):
        return lambda h: ref[h].reshape(256, 1024)

    def cols_of(h, n):
        return env.dm_line[h, :, :, window(n * 256, 256)].reshape(256, 256)

    def store_down(n, value):
        env.g_down[:, :, window(n * 256, 256)] = value.reshape(4, 256, 256)

    def store_to(ref):
        def store(n, value):
            ref[n] = value

        return store

    def piece(grad, tag, cut):
        def view(slot, half):
            return grad.at[slot] if half is None else grad.at[slot, window(half * cut, cut), :]

        lc, ly, lx, out, send, recv = tag
        return Piece(view, lc, ly, lx, lambda half: out.at[window(half * cut, cut), :], (send, recv))

    gu = piece(env.g_up, (env.lcu, env.lyu, env.lxu, env.ou, env.us, env.ur), 512)
    gg = piece(env.g_gate, (env.lcg, env.lyg, env.lxg, env.og, env.gs, env.gr), 512)
    gd = piece(env.g_down, (env.lcd, env.lyd, env.lxd, env.od, env.ds, env.dr), 128)
    weight_gradient(lambda h: env.hidden[h], cols_of, store_down)
    gd.start()
    r1.step(2)
    after_backward(0, r0, env)
    weight_gradient(both(env.h_line), lambda h, n: env.d_up[h, n], store_to(env.g_up))
    gu.start()
    gd.pass_twin()
    r1.step(1)
    weight_gradient(both(env.h_line), lambda h, n: env.d_gate[h, n], store_to(env.g_gate))
    gg.start()
    gu.pass_twin()
    after_backward(1, r1, env)

    lane = lax.broadcasted_iota(jnp.int32, (LANES, LANES), 1)
    for p in range(4):
        d_att = dot_nt(env.d_branch[...], env.u_out[4 * p : 4 * p + 4].reshape(256, 1024))
        for k in range(4):
            value = d_att[:, (k // 2) * LANES : (k // 2 + 1) * LANES]
            if k % 2:
                value = pltpu.roll(value, HEAD, 1)
            t = 4 * p + k
            env.datt_out[t] = side_by_side(value).astype(BF16)
            send_head(t, s, env.datt_out, env.datt_in, env.das, env.dar, y)

    @pl.loop(0, 4)
    def _(n):
        cols = window(n * 256, 256)
        grad = dot_tn(env.att_low[...], env.d_branch[:, cols])
        env.g_out[:, :, cols] = grad.reshape(16, 64, 256).astype(BF16)

    out_reduce = RowReduce(env)
    out_reduce.start()
    gg.pass_twin()
    gd.pass_side()
    out_reduce.pass_side()
    wait_heads(s, env.datt_out, env.datt_in, env.das, env.dar, y)

    @pl.loop(0, 16)
    def _(b):
        spread_grads(b, env)

    attend_back_block(7, env, 7)
    gd.pass_back()
    attend_back_block(6, env, 7)
    out_reduce.pass_line()
    out_reduce.step(3)
    gu.pass_side()
    attend_back_block(5, env, 7)
    out_reduce.step(2)
    attend_back_block(4, env, 7)
    out_reduce.step(1)
    gg.pass_side()
    gu.pass_back()
    for i in range(3, -1, -1):
        attend_back_block(i, env, 7)
    project_back(3, env)
    out_reduce.to_twin()
    project_back(2, env)
    gg.pass_back()
    project_back(1, env)
    project_back(0, env)
    for h in range(2):
        (r0, r1)[h].step(3)

    @pl.loop(0, 4)
    def _(n):
        cols = window(n * 256, 256)
        total = dot_tn(env.d_lin[...].reshape(512, 768), env.x_line[:, :, cols].reshape(512, 256))
        env.g_qkv[:, cols] = total.astype(BF16)

    def row_piece(which, tag, cut):
        def view(slot, half):
            start, size = (slot * LANES, LANES) if which == 0 else (4 * LANES + slot * HEAD, HEAD)
            if half is not None:
                start, size = start + half * cut, cut
            return env.g_qkv.at[window(start, size), :]

        lc, ly, lx, out, send, recv = tag
        return Piece(view, lc, ly, lx, lambda half: out.at[window(half * cut, cut), :], (send, recv))

    gq = row_piece(0, (env.lcq, env.lyq, env.lxq, env.oq, env.qqs, env.qqr), 64)
    gv = row_piece(1, (env.lcv, env.lyv, env.lxv, env.ov, env.vvs, env.vvr), 32)
    gq.start()
    gv.start()
    r0.step(2)
    r1.step(2)
    for sl in range(4):
        both_parts = env.gain_sum[sl : sl + 1, 0:HEAD] + env.gain_sum[sl : sl + 1, HEAD:]
        env.gains[4 + sl : 5 + sl, 0:HEAD] = both_parts
    small = [
        remote(env.gains, env.gain_land.at[i], env.sm_s.at[i], env.sm_r.at[i], device)
        for i, device in enumerate((dev(z, x, 1 - c, y), dev(z, 1 - x, c, y), dev(z, x, c, 1 - y)))
    ]
    def tell(k):
        t = (z + k) % 4
        return remote(
            env.gain_line.at[z], env.gain_line.at[z], env.gl_s.at[k], env.gl_r.at[z], dev(t, x, c, y)
        )

    small[0].start()
    gq.pass_twin()
    gv.pass_twin()
    finish_ff(env, gd, 2)
    r0.step(1)
    r1.step(1)
    small[0].wait()
    env.gains[...] += env.gain_land[0]
    small[1].start()
    finish_ff(env, gu, 0)
    gq.pass_side()
    gv.pass_side()
    small[1].wait()
    env.gains[...] += env.gain_land[1]
    small[2].start()
    finish_ff(env, gg, 1)
    gq.pass_back()
    gv.pass_back()
    small[2].wait()
    env.gain_line[z] = env.gains[...] + env.gain_land[2]
    for k in range(1, 4):
        tell(k).start()
    out_reduce.finish()
    unit_out = env.oo[...].astype(F32) + env.yo[...].astype(F32)
    env.gate_val[1, 3 * HEAD :, :] = pull_rows(env.w_out[...], unit_out)
    r0.finish(env.total)
    env.d_states[0:64, :] += env.total[...]
    r1.finish(env.total)
    env.d_states[64:, :] += env.total[...]
    gq.finish()
    gv.finish()
    stage = env.gate_val.at[1]
    stage[0:HEAD, :] = pull_rows(env.w_query[...], env.oq[0:HEAD, :].astype(F32))
    stage[HEAD : 2 * HEAD, :] = pull_rows(env.w_key[...], env.oq[HEAD:, :].astype(F32))
    stage[2 * HEAD : 3 * HEAD, :] = pull_rows(env.w_value[...], env.ov[...].astype(F32))
    results = [
        pltpu.make_async_copy(stage.at[pl.ds(i * HEAD, HEAD), :], ref, env.out_sem.at[3 + i])
        for i, ref in enumerate((env.grad_query, env.grad_key, env.grad_value, env.grad_out))
    ]
    each(results, "start")
    for k in range(1, 4):
        tell(k).wait_send()
        t = (z + k) % 4
        remote(
            env.gain_line.at[t], env.gain_line.at[t], env.gl_s.at[k], env.gl_r.at[t], dev(t, x, c, y)
        ).wait_recv()
    each(results, "wait")
    for i in range(3):
        ff_result(env, i).wait()


def pull_rows(weight, grad):
    wide = weight.astype(F32)
    inverse = lax.rsqrt(jnp.sum(wide * wide, axis=1, keepdims=True) + EPS)
    unit = wide * inverse
    return inverse * (grad - unit * jnp.sum(grad * unit, axis=1, keepdims=True))


def pull_cols(weight, grad):
    wide = weight.astype(F32)
    inverse = lax.rsqrt(jnp.sum(wide * wide, axis=0, keepdims=True) + EPS)
    unit = wide * inverse
    return inverse * (grad - unit * jnp.sum(grad * unit, axis=0, keepdims=True))


def ff_result(env, which):
    stage = (env.up_lin.at[0], env.up_lin.at[1], env.gate_val.at[0])[which]
    out = (env.grad_up, env.grad_gate, env.grad_down)[which]
    return pltpu.make_async_copy(stage, out, env.out_sem.at[which])


def finish_ff(env, piece, which):
    piece.finish()
    if which == 2:
        env.gate_val[0] = pull_rows(env.w_down[...], env.od[...].astype(F32))
    elif which == 0:
        env.up_lin[0] = pull_cols(env.w_up[...], env.ou[...].astype(F32))
    else:
        env.up_lin[1] = pull_cols(env.w_gate[...], env.og[...].astype(F32))
    ff_result(env, which).start()


class RowReduce:
    def __init__(self, env):
        self.env = env
        self.line = Reduce(self.part, env.o_pass, env.o_land, env.ol_s, env.ol_r)

    def part(self, owner):
        z, x, c, y = place()
        return self.env.g_out[owner * 4 + 2 * x + c].astype(F32)

    def to_core(self, zz, xx):
        z, x, c, y = place()
        e = self.env
        return remote(
            e.g_out.at[zz * 4 + 2 * xx + 1 - c], e.o_c_land.at[zz, xx], e.oc_s.at[zz, xx], e.oc_r.at[zz, xx],
            dev(z, x, 1 - c, y),
        )

    def to_side(self, zz):
        z, x, c, y = place()
        e = self.env
        return remote(
            e.g_out.at[zz * 4 + 2 * (1 - x) + c], e.o_x_land.at[zz], e.ox_s.at[zz], e.ox_r.at[zz],
            dev(z, 1 - x, c, y),
        )

    def twin(self):
        z, x, c, y = place()
        e = self.env
        return remote(e.oo, e.yo, e.oy_s, e.oy_r, dev(z, x, c, 1 - y))

    def start(self):
        z, x, c, y = place()

        @pl.loop(0, 4)
        def _(zz):
            self.to_core(zz, 1 - x).start()
            self.to_core(zz, x).start()

    def pass_side(self):
        z, x, c, y = place()
        e = self.env

        @pl.loop(0, 4)
        def _(zz):
            self.to_core(zz, 1 - x).wait_recv()
            b = zz * 4 + 2 * (1 - x) + c
            e.g_out[b] = (e.g_out[b].astype(F32) + e.o_c_land[zz, 1 - x].astype(F32)).astype(BF16)
            self.to_side(zz).start()

    def pass_line(self):
        z, x, c, y = place()
        e = self.env

        @pl.loop(0, 4)
        def _(zz):
            self.to_core(zz, x).wait_recv()
            self.to_side(zz).wait_recv()
            b = zz * 4 + 2 * x + c
            e.g_out[b] = (
                e.g_out[b].astype(F32) + e.o_c_land[zz, x].astype(F32) + e.o_x_land[zz].astype(F32)
            ).astype(BF16)

    def step(self, k):
        self.line.step(k)

    def to_twin(self):
        e = self.env
        self.line.finish(e.total)
        e.oo[...] = e.total[...].astype(BF16)
        self.twin().start()

    def finish(self):
        z, x, c, y = place()
        self.twin().wait()

        @pl.loop(0, 4)
        def _(zz):
            self.to_core(zz, 0).wait_send()
            self.to_core(zz, 1).wait_send()
            self.to_side(zz).wait_send()


DMA = pltpu.SemaphoreType.DMA


def v(shape, dtype=BF16):
    return pltpu.VMEM(shape, dtype)


LAYER_IN = tuple(
    dict(
        states=None,
        w_query=None,
        w_key=None,
        w_value=None,
        w_out=None,
        w_up=None,
        w_gate=None,
        w_down=None,
        qk_scale=None,
        up_scale=None,
        gate_scale=None,
        alpha_attn=None,
        alpha_mlp=None,
        d_out=None,
        cosines=None,
        sines=None,
    )
)
LAYER_OUT = dict(
    output=((128, 1024), F32), d_states=((128, 1024), F32), gain_line=((4, 8, 1024), F32),
    grad_query=((64, 1024), F32), grad_key=((64, 1024), F32), grad_value=((64, 1024), F32),
    grad_out=((64, 1024), F32), grad_up=((1024, 256), F32), grad_gate=((1024, 256), F32),
    grad_down=((256, 1024), F32),
)
IN_VMEM = 3
LAYER_TMP = dict(
    x_line=v((4, 128, 1024)), u_qkv=v((768, 1024)), u_out=v((16, 64, 1024)),
    turned=v((4, 4, 128, 128), F32), cosine=v((4, 128, 128), F32), sine=v((4, 128, 128), F32),
    gain=v((4, 128), F32), up_row=v((1, 1024), F32), gate_row=v((1, 1024), F32), mix_row=v((2, 1024), F32), gain_sum=v((4, 128), F32), gains=v((8, 1024), F32),
    gain_land=v((3, 8, 1024), F32),
    heads_out=v((4, 4, 192, 128)), heads_in=v((16, 192, 128)),
    q_ext=v((2048, 128)), k_ext=v((2048, 128)), v_ext=v((2048, 128)), attended=v((2048, 128), F32),
    att_out=v((16, 64, 128)), att_in=v((16, 64, 128)), att_low=v((128, 1024)),
    ups=v((4, 1024, 256)), gates=v((4, 1024, 256)), downs=v((4, 256, 1024)),
    branch=v((128, 1024), F32), mid=v((128, 1024), F32), d_mid=v((128, 1024), F32),
    total=v((64, 1024), F32), d_branch=v((128, 1024)),
    h_line=v((2, 4, 64, 1024)), dm_line=v((2, 4, 64, 1024)),
    up_lin=v((2, 1024, 256), F32), gate_val=v((2, 256, 1024), F32), hidden=v((2, 256, 1024)),
    d_up=v((2, 4, 256, 256)), d_gate=v((2, 4, 256, 256)),
    part=v((2, 4, 64, 1024), F32), passing=v((2, 4, 64, 1024)), landed=v((2, 5, 64, 1024)),
    g_up=v((4, 1024, 256)), g_gate=v((4, 1024, 256)), g_down=v((4, 256, 1024)),
    lcu=v((2, 1024, 256)), lcg=v((2, 1024, 256)), lcd=v((2, 256, 1024)), lcq=v((2, 128, 1024)),
    lcv=v((2, 64, 1024)),
    lyu=v((2, 512, 256)), lyg=v((2, 512, 256)), lyd=v((2, 128, 1024)), lyq=v((2, 64, 1024)), lyv=v((2, 32, 1024)),
    lxu=v((512, 256)), lxg=v((512, 256)), lxd=v((128, 1024)), lxq=v((64, 1024)), lxv=v((32, 1024)),
    ou=v((1024, 256)), og=v((1024, 256)), od=v((256, 1024)), oq=v((128, 1024)), ov=v((64, 1024)),
    oo=v((64, 1024)), yo=v((64, 1024)), out_sem=DMA((7,)),
    o_c_land=v((4, 2, 64, 1024)), o_x_land=v((4, 64, 1024)), o_pass=v((4, 64, 1024)),
    o_land=v((5, 64, 1024)),
    datt_out=v((16, 64, 128)), datt_in=v((16, 64, 128)), do_ext=v((2048, 128)),
    dk=v((2048, 128), F32), dv=v((2048, 128), F32),
    d_lin=v((4, 128, 768)),
    t_sem=DMA((4, 2)), x_send=DMA((4, 2)), x_recv=DMA((4,)), q_send=DMA((3, 2)), q_recv=DMA((3, 2)),
    w_send=DMA((5, 3)), w_recv=DMA((5, 3)), hs=DMA((4, 3)), hr=DMA((16,)),
    o_z=DMA((4, 2)), o_x=DMA((4,)), o_c=DMA((4, 2)), o_r=DMA((16,)),
    as_=DMA((16,)), ar=DMA((16,)), das=DMA((16,)), dar=DMA((16,)),
    fa_s=DMA((4, 2)), fa_r=DMA((4,)), fb_s=DMA((4, 2)), fb_r=DMA((4,)),
    ba_s=DMA((4, 2)), ba_r=DMA((4,)), bb_s=DMA((4, 2)), bb_r=DMA((4,)),
    r0_s=DMA((4,)), r0_r=DMA((5,)), r1_s=DMA((4,)), r1_r=DMA((5,)),
    us=DMA((6,)), ur=DMA((6,)), gs=DMA((6,)), gr=DMA((6,)), ds=DMA((6,)), dr=DMA((6,)),
    qqs=DMA((6,)), qqr=DMA((6,)), vvs=DMA((6,)), vvr=DMA((6,)),
    oc_s=DMA((4, 2)), oc_r=DMA((4, 2)), ox_s=DMA((4,)), ox_r=DMA((4,)),
    ol_s=DMA((4,)), ol_r=DMA((5,)), oy_s=DMA, oy_r=DMA,
    bs=DMA((4, 4)), br=DMA((16,)), sm_s=DMA((3,)), sm_r=DMA((3,)), gl_s=DMA((4,)), gl_r=DMA((4,)),
)


def run_layer(*args):
    vmem = pl.BlockSpec(memory_space=pltpu.VMEM)
    names = LAYER_IN + tuple(LAYER_OUT) + tuple(LAYER_TMP)

    def kernel(*refs):
        layer(Env(names, refs))

    outs = pl.pallas_call(
        kernel,
        name="layer",
        out_shape=tuple(jax.ShapeDtypeStruct(*o) for o in LAYER_OUT.values()),
        in_specs=[vmem] * (len(LAYER_IN) - 2) + [pl.BlockSpec(memory_space=pl.ANY)] * 2,
        out_specs=(vmem,) * IN_VMEM
        + (pl.BlockSpec(memory_space=pl.ANY),) * (len(LAYER_OUT) - IN_VMEM),
        scratch_shapes=list(LAYER_TMP.values()),
        compiler_params=pltpu.CompilerParams(
            collective_id=1, has_side_effects=True, vmem_limit_bytes=62 * MIB
        ),
    )(*args)
    return dict(zip(LAYER_OUT, outs))


HANDED = tuple(name for name in LAYER_OUT if name != "gain_line")


def hand_over_kernel(*refs):
    count = len(HANDED)
    line = refs[count]
    outs = refs[count + 1 : 2 * count + 6]
    held = refs[2 * count + 6 : 3 * count + 6]
    arrive, leave = refs[3 * count + 6 :]
    loads = [pltpu.make_async_copy(refs[i], held[i], arrive.at[i]) for i in range(count)]
    stores = [pltpu.make_async_copy(held[i], outs[i], leave.at[i]) for i in range(count)]
    each(loads, "start")
    qk, up, gate, attn, mlp = outs[count:]
    lane = lax.broadcasted_iota(jnp.int32, (1, LANES), 1)
    for zz in range(4):
        cols = slice(zz * 1024, (zz + 1) * 1024)
        up[cols] = line[zz, 0:1, :].reshape(1024)
        gate[cols] = line[zz, 1:2, :].reshape(1024)
        for pair in range(2):
            first = line[zz, 4 + 2 * pair : 5 + 2 * pair, 0:LANES]
            second = pltpu.roll(line[zz, 5 + 2 * pair : 6 + 2 * pair, 0:LANES], HEAD, 1)
            both = jnp.where(lane < HEAD, first, second)
            qk[zz * 256 + pair * LANES : zz * 256 + (pair + 1) * LANES] = both.reshape(LANES)
    for row, out in ((2, attn), (3, mlp)):
        parts = [line[zz, row : row + 1, :] for zz in range(4)]
        out[...] = (parts[0] + parts[1] + parts[2] + parts[3]).reshape(1024)
    for load, store in zip(loads, stores):
        load.wait()
        store.start()
    each(stores, "wait")


def hand_over(*arrays):
    vmem, hbm = pl.BlockSpec(memory_space=pltpu.VMEM), pl.BlockSpec(memory_space=pl.ANY)
    count = len(HANDED)
    sizes = (1024, 4096, 4096, 1024, 1024)
    return pl.pallas_call(
        hand_over_kernel,
        name="hand_over",
        out_shape=tuple(jax.ShapeDtypeStruct(a.shape, a.dtype) for a in arrays[:count])
        + tuple(jax.ShapeDtypeStruct((n,), F32) for n in sizes),
        in_specs=[hbm] * count + [vmem],
        out_specs=(hbm,) * count + (vmem,) * len(sizes),
        scratch_shapes=[v(a.shape, a.dtype) for a in arrays[:count]] + [DMA((count,))] * 2,
        compiler_params=pltpu.CompilerParams(vmem_limit_bytes=60 * MIB),
    )(*arrays)


def on_device_heads(
    states,
    lengths,
    w_query,
    w_key,
    w_value,
    w_out,
    w_up,
    w_gate,
    w_down,
    qk_scale,
    up_scale,
    gate_scale,
    alpha_attn,
    alpha_mlp,
    d_out,
):
    tok, width = states.shape[1:]
    cosine, sine = turn_tables(16 * tok)
    got = run_layer(
        states.reshape(tok, width), w_query.T, w_key.T, w_value.T, w_out, w_up, w_gate, w_down,
        qk_scale, up_scale, gate_scale, alpha_attn, alpha_mlp, d_out.reshape(tok, width),
        jnp.asarray(cosine.reshape(16, tok, LANES)), jnp.asarray(sine.reshape(16, tok, LANES)),
    )

    output, d_states, g_query, g_key, g_value, g_out, g_up, g_gate, g_down, *gains = hand_over(
        *(got[name] for name in HANDED), got["gain_line"]
    )
    return (
        output.reshape(states.shape),
        d_states.reshape(states.shape),
        g_query.T,
        g_key.T,
        g_value.T,
        g_out,
        g_up,
        g_gate,
        g_down,
        *gains,
    )


def solution(mesh):
    seq, batch = mesh.shape["seq"], mesh.shape["batch"]
    body = on_device_heads if (seq == HEADS and batch == 2) else on_device_general
    return jax.shard_map(
        body,
        mesh=mesh,
        in_specs=(
            P("batch", "seq", None),
            P("batch", None),
            P(None, "seq"),
            P(None, "seq"),
            P(None, "seq"),
            P("seq", None),
            P(None, "seq"),
            P(None, "seq"),
            P("seq", None),
            P(),
            P(),
            P(),
            P(),
            P(),
            P("batch", "seq", None),
        ),
        out_specs=(
            P("batch", "seq", None),
            P("batch", "seq", None),
            P(None, "seq"),
            P(None, "seq"),
            P(None, "seq"),
            P("seq", None),
            P(None, "seq"),
            P(None, "seq"),
            P("seq", None),
            P(),
            P(),
            P(),
            P(),
            P(),
        ),
        check_vma=False,
    )
```

```python
import jax
import jax.numpy as jnp
import numpy as np
from jax import lax
from jax.experimental import pallas as pl
from jax.experimental.pallas import tpu as pltpu
from jax.sharding import PartitionSpec as P

HEADS = 16
HEAD = 64


EPS = 1e-06


def shifted(value, axis, steps):
    count = lax.axis_size(axis)
    first, last = (max(0, -steps), min(count, count - steps))
    return lax.ppermute(value, axis, [(source, source + steps) for source in range(first, last)])


def shifted_2(block, axis, distance):
    devices = range(lax.axis_size(axis))
    route = [((i - distance) % len(devices), i) for i in devices]
    return lax.ppermute(block, axis, route)


def normalized(weight, axis):
    wide = weight.astype(jnp.float32)
    return wide * lax.rsqrt(jnp.sum(wide * wide, axis=axis, keepdims=True) + EPS)


def rms(values):
    return values * lax.rsqrt(jnp.mean(values * values, axis=-1, keepdims=True) + EPS)


def doc_layout(len_row, tok_index):
    docs = jnp.arange(len_row.shape[0])
    starts = jnp.sum(jnp.where(docs[:, None] < docs[None, :], len_row[:, None], 0), axis=0)
    started = starts[None, :] <= tok_index[:, None]
    doc_ids = jnp.sum(started.astype(jnp.int32), axis=1) - 1
    first_tok = jnp.max(jnp.where(started, starts[None, :], 0), axis=1)
    return (doc_ids, tok_index - first_tok)


def rope(values, position):
    half = values.shape[-1] // 2
    freqs = 10000.0 ** (-jnp.arange(half, dtype=jnp.float32) / half)
    angle = position.astype(jnp.float32)[:, None] * freqs[None, :]
    cosine = jnp.cos(angle)[:, None, :]
    sine = jnp.sin(angle)[:, None, :]
    first = values[..., :half]
    second = values[..., half:]
    return jnp.concatenate(
        [first * cosine - second * sine, first * sine + second * cosine], axis=-1
    )


def prepare(linear, position, gain):
    count = linear.shape[0]
    shaped = linear.reshape(count, HEADS, HEAD)
    turned = rms(rope(shaped, position)) * gain.reshape(HEADS, HEAD)
    return turned.reshape(count, HEADS * HEAD)


def residual_mix(state, branch, alpha):
    return rms(state + alpha * (rms(branch) - state))


def gating(up_lin, gate_lin, up_scale, gate_scale):
    return up_scale * up_lin * jax.nn.silu(gate_scale * gate_lin)


def unit_back(raw_shard, grad_shard, axis):
    primal, pullback = jax.vjp(
        lambda weight: normalized(weight, axis), raw_shard.astype(jnp.float32)
    )
    return pullback(grad_shard)[0]


def on_device_general(
    states,
    lengths,
    w_query,
    w_key,
    w_value,
    w_out,
    w_up,
    w_gate,
    w_down,
    qk_scale,
    up_scale,
    gate_scale,
    alpha_attn,
    alpha_mlp,
    d_out,
):
    seq_count = lax.axis_size("seq")
    my_index = lax.axis_index("seq")
    rows = states.shape[0]
    tok = states.shape[1]
    width = states.shape[2]
    flat = rows * tok
    score_scale = HEAD ** (-0.5)
    row_layout = jax.vmap(doc_layout, in_axes=(0, None))
    unit_query = normalized(w_query, 0).astype(jnp.bfloat16)
    unit_key = normalized(w_key, 0).astype(jnp.bfloat16)
    unit_value = normalized(w_value, 0).astype(jnp.bfloat16)
    unit_out = normalized(w_out, 1).astype(jnp.bfloat16)
    unit_up = normalized(w_up, 0).astype(jnp.bfloat16)
    unit_gate = normalized(w_gate, 0).astype(jnp.bfloat16)
    unit_down = normalized(w_down, 1).astype(jnp.bfloat16)
    full_weights = (
        lax.all_gather(unit_query, "seq", axis=1, tiled=True),
        lax.all_gather(unit_key, "seq", axis=1, tiled=True),
        lax.all_gather(unit_value, "seq", axis=1, tiled=True),
        lax.all_gather(unit_out, "seq", axis=0, tiled=True),
        lax.all_gather(unit_up, "seq", axis=1, tiled=True),
        lax.all_gather(unit_gate, "seq", axis=1, tiled=True),
        lax.all_gather(unit_down, "seq", axis=0, tiled=True),
    )
    full_query, full_key, full_value, full_out, full_up, full_gate, full_down = full_weights
    tok_index = my_index * tok + jnp.arange(tok, dtype=jnp.int32)
    doc_ids, position = row_layout(lengths, tok_index)
    flat_pos = position.reshape(flat)
    state_in = states.reshape(flat, width)
    x_low = state_in.astype(jnp.bfloat16)
    query_lin = jnp.dot(x_low, full_query, preferred_element_type=jnp.float32)
    key_lin = jnp.dot(x_low, full_key, preferred_element_type=jnp.float32)
    value_lin = jnp.dot(x_low, full_value, preferred_element_type=jnp.float32)

    def front(query_part, key_part, gain):
        return (prepare(query_part, flat_pos, gain), prepare(key_part, flat_pos, gain))

    query_f, key_f = front(query_lin, key_lin, qk_scale)
    query_h = query_f.astype(jnp.bfloat16).reshape(rows, tok, HEADS, HEAD)
    key_h = key_f.astype(jnp.bfloat16).reshape(rows, tok, HEADS, HEAD)
    value_h = value_lin.astype(jnp.bfloat16).reshape(rows, tok, HEADS, HEAD)

    def block_scores(key_blk, source):
        key_index = source * tok + jnp.arange(tok, dtype=jnp.int32)
        key_docs, key_pos = row_layout(lengths, key_index)
        scores = (
            jnp.einsum("bqhd,bkhd->bqhk", query_h, key_blk, preferred_element_type=jnp.float32)
            * score_scale
        )
        allowed = (doc_ids[:, :, None] == key_docs[:, None, :]) & (
            key_index[None, None, :] <= tok_index[None, :, None]
        )
        return (scores, allowed[:, :, None, :])

    def is_active(source):
        last_key = jnp.reshape(source * tok + tok - 1, (1,))
        last_doc, last_pos = row_layout(lengths, last_key)
        return (source <= my_index) & jnp.any(last_doc[:, 0] >= doc_ids[:, 0])

    def attend(running, key_blk, value_blk, source):

        def compute(carried):
            best, denom_sum, accum = carried
            scores, allowed = block_scores(key_blk, source)
            new_best = jnp.maximum(best, jnp.max(jnp.where(allowed, scores, -1e30), axis=3))
            weights = jnp.where(allowed, jnp.exp(scores - new_best[:, :, :, None]), 0.0)
            shrink = jnp.exp(best - new_best)
            denom_sum = denom_sum * shrink + jnp.sum(weights, axis=3)
            accum = accum * shrink[:, :, :, None] + jnp.einsum(
                "bqhk,bkhd->bqhd",
                weights.astype(jnp.bfloat16),
                value_blk,
                preferred_element_type=jnp.float32,
            )
            return (new_best, denom_sum, accum)

        return lax.cond(is_active(source), compute, lambda carried: carried, running)

    reach = seq_count - 1
    start_state = (
        jnp.full((rows, tok, HEADS), -1e30, jnp.float32),
        jnp.zeros((rows, tok, HEADS), jnp.float32),
        jnp.zeros((rows, tok, HEADS, HEAD), jnp.float32),
    )
    first_state = attend(start_state, key_h, value_h, my_index)

    def cycle_step(step, loop_carry):
        running, key_blk, value_blk = loop_carry
        key_blk, value_blk = shifted((key_blk, value_blk), "seq", 1)
        source = (my_index - step) % seq_count
        return (attend(running, key_blk, value_blk, source), key_blk, value_blk)

    final_state, spent_key, spent_value = lax.fori_loop(
        1, reach + 1, cycle_step, (first_state, key_h, value_h)
    )
    best, denom_sum, accum = final_state
    attended = accum / denom_sum[:, :, :, None]
    log_sum = best + jnp.log(denom_sum)
    attended_low = attended.astype(jnp.bfloat16).reshape(flat, width)
    attn_branch = jnp.dot(attended_low, full_out, preferred_element_type=jnp.float32)
    state_mid = residual_mix(state_in, attn_branch, alpha_attn)
    mid_low = state_mid.astype(jnp.bfloat16)
    up_lin = jnp.dot(mid_low, full_up, preferred_element_type=jnp.float32)
    gate_lin = jnp.dot(mid_low, full_gate, preferred_element_type=jnp.float32)
    gated_low = gating(up_lin, gate_lin, up_scale, gate_scale).astype(jnp.bfloat16)
    mlp_branch = jnp.dot(gated_low, full_down, preferred_element_type=jnp.float32)
    output = residual_mix(state_mid, mlp_branch, alpha_mlp)
    back_weights = (
        lax.all_gather(unit_query, "seq", axis=1, tiled=True),
        lax.all_gather(unit_key, "seq", axis=1, tiled=True),
        lax.all_gather(unit_value, "seq", axis=1, tiled=True),
        lax.all_gather(unit_out, "seq", axis=0, tiled=True),
        lax.all_gather(unit_up, "seq", axis=1, tiled=True),
        lax.all_gather(unit_gate, "seq", axis=1, tiled=True),
        lax.all_gather(unit_down, "seq", axis=0, tiled=True),
    )
    back_query, back_key, back_value, back_out, back_up, back_gate, back_down = back_weights
    primal, pull_mlp = jax.vjp(residual_mix, state_mid, mlp_branch, alpha_mlp)
    d_mid, d_mlp, g_alpha_mlp = pull_mlp(d_out.reshape(flat, width))
    d_mlp_low = d_mlp.astype(jnp.bfloat16)
    grad_down = jnp.einsum("tf,td->fd", gated_low, d_mlp_low, preferred_element_type=jnp.float32)
    d_gated = jnp.einsum("td,fd->tf", d_mlp_low, back_down, preferred_element_type=jnp.float32)
    primal, pull_gate = jax.vjp(gating, up_lin, gate_lin, up_scale, gate_scale)
    d_up, d_gate, g_up_scale, g_gate_scale = pull_gate(d_gated)
    d_up_low = d_up.astype(jnp.bfloat16)
    d_gate_low = d_gate.astype(jnp.bfloat16)
    grad_up = jnp.einsum("tc,tf->cf", mid_low, d_up_low, preferred_element_type=jnp.float32)
    grad_gate = jnp.einsum("tc,tf->cf", mid_low, d_gate_low, preferred_element_type=jnp.float32)
    d_mid = d_mid + jnp.einsum("tf,cf->tc", d_up_low, back_up, preferred_element_type=jnp.float32)
    d_mid = d_mid + jnp.einsum(
        "tf,cf->tc", d_gate_low, back_gate, preferred_element_type=jnp.float32
    )
    primal, pull_attn = jax.vjp(residual_mix, state_in, attn_branch, alpha_attn)
    d_state, d_attn, g_alpha_attn = pull_attn(d_mid)
    d_attn_low = d_attn.astype(jnp.bfloat16)
    grad_out = jnp.einsum("tc,td->cd", attended_low, d_attn_low, preferred_element_type=jnp.float32)
    d_attended = jnp.einsum("td,cd->tc", d_attn_low, back_out, preferred_element_type=jnp.float32)
    d_att_low = d_attended.astype(jnp.bfloat16).reshape(rows, tok, HEADS, HEAD)
    delta = jnp.sum(d_att_low.astype(jnp.float32) * attended, axis=3)

    def attend_back(d_query, key_blk, value_blk, d_key, d_value, source):

        def compute(carried):
            d_query, d_key, d_value = carried
            scores, allowed = block_scores(key_blk, source)
            probs = jnp.where(allowed, jnp.exp(scores - log_sum[:, :, :, None]), 0.0)
            d_probs = jnp.einsum(
                "bqhd,bkhd->bqhk", d_att_low, value_blk, preferred_element_type=jnp.float32
            )
            d_scores = (probs * (d_probs - delta[:, :, :, None])).astype(jnp.bfloat16)
            d_query = d_query + jnp.einsum(
                "bqhk,bkhd->bqhd", d_scores, key_blk, preferred_element_type=jnp.float32
            )
            d_key = d_key + jnp.einsum(
                "bqhk,bqhd->bkhd", d_scores, query_h, preferred_element_type=jnp.float32
            )
            d_value = d_value + jnp.einsum(
                "bqhk,bqhd->bkhd",
                probs.astype(jnp.bfloat16),
                d_att_low,
                preferred_element_type=jnp.float32,
            )
            return (d_query, d_key, d_value)

        return lax.cond(
            is_active(source), compute, lambda carried: carried, (d_query, d_key, d_value)
        )

    def back_step(step, loop_carry):
        d_query, key_blk, value_blk, d_key, d_value = loop_carry
        source = (my_index - step) % seq_count
        d_query, d_key, d_value = attend_back(d_query, key_blk, value_blk, d_key, d_value, source)
        d_key, d_value = (
            shifted_2(d_key.astype(jnp.bfloat16), "seq", 1).astype(d_key.dtype),
            shifted_2(d_value.astype(jnp.bfloat16), "seq", 1).astype(d_value.dtype),
        )
        key_blk, value_blk = shifted((key_blk, value_blk), "seq", 1)
        return (d_query, key_blk, value_blk, d_key, d_value)

    zero_heads = jnp.zeros((rows, tok, HEADS, HEAD), jnp.float32)
    d_query_h, last_key_blk, last_value_blk, d_key_h, d_value_h = lax.fori_loop(
        0, reach, back_step, (zero_heads, key_h, value_h, zero_heads, zero_heads)
    )
    d_query_h, d_key_h, d_value_h = attend_back(
        d_query_h, last_key_blk, last_value_blk, d_key_h, d_value_h, (my_index - reach) % seq_count
    )
    d_key_h, d_value_h = (
        shifted_2(d_key_h.astype(jnp.bfloat16), "seq", -reach).astype(d_key_h.dtype),
        shifted_2(d_value_h.astype(jnp.bfloat16), "seq", -reach).astype(d_value_h.dtype),
    )
    primal, pull_front = jax.vjp(front, query_lin, key_lin, qk_scale)
    d_query_lin, d_key_lin, g_qk_scale = pull_front(
        (d_query_h.reshape(flat, width) * score_scale, d_key_h.reshape(flat, width) * score_scale)
    )
    d_query_low = d_query_lin.astype(jnp.bfloat16)
    d_key_low = d_key_lin.astype(jnp.bfloat16)
    d_value_low = d_value_h.reshape(flat, width).astype(jnp.bfloat16)
    grad_query = jnp.einsum("tc,tj->cj", x_low, d_query_low, preferred_element_type=jnp.float32)
    grad_key = jnp.einsum("tc,tj->cj", x_low, d_key_low, preferred_element_type=jnp.float32)
    grad_value = jnp.einsum("tc,tj->cj", x_low, d_value_low, preferred_element_type=jnp.float32)
    d_state = d_state + jnp.einsum(
        "tj,cj->tc", d_query_low, back_query, preferred_element_type=jnp.float32
    )
    d_state = d_state + jnp.einsum(
        "tj,cj->tc", d_key_low, back_key, preferred_element_type=jnp.float32
    )
    d_state = d_state + jnp.einsum(
        "tj,cj->tc", d_value_low, back_value, preferred_element_type=jnp.float32
    )
    shards = (
        lax.psum_scatter(
            grad_query.astype(jnp.bfloat16), "seq", scatter_dimension=1, tiled=True
        ).astype(jnp.float32),
        lax.psum_scatter(
            grad_key.astype(jnp.bfloat16), "seq", scatter_dimension=1, tiled=True
        ).astype(jnp.float32),
        lax.psum_scatter(
            grad_value.astype(jnp.bfloat16), "seq", scatter_dimension=1, tiled=True
        ).astype(jnp.float32),
        lax.psum_scatter(
            grad_out.astype(jnp.bfloat16), "seq", scatter_dimension=0, tiled=True
        ).astype(jnp.float32),
        lax.psum_scatter(
            grad_up.astype(jnp.bfloat16), "seq", scatter_dimension=1, tiled=True
        ).astype(jnp.float32),
        lax.psum_scatter(
            grad_gate.astype(jnp.bfloat16), "seq", scatter_dimension=1, tiled=True
        ).astype(jnp.float32),
        lax.psum_scatter(
            grad_down.astype(jnp.bfloat16), "seq", scatter_dimension=0, tiled=True
        ).astype(jnp.float32),
    )
    summed = (
        lax.psum(shards[0].astype(jnp.bfloat16), "batch").astype(jnp.float32),
        lax.psum(shards[1].astype(jnp.bfloat16), "batch").astype(jnp.float32),
        lax.psum(shards[2].astype(jnp.bfloat16), "batch").astype(jnp.float32),
        lax.psum(shards[3].astype(jnp.bfloat16), "batch").astype(jnp.float32),
        lax.psum(shards[4].astype(jnp.bfloat16), "batch").astype(jnp.float32),
        lax.psum(shards[5].astype(jnp.bfloat16), "batch").astype(jnp.float32),
        lax.psum(shards[6].astype(jnp.bfloat16), "batch").astype(jnp.float32),
    )
    gain_grads = lax.psum(
        (g_qk_scale, g_up_scale, g_gate_scale, g_alpha_attn, g_alpha_mlp), ("seq", "batch")
    )
    g_query = unit_back(w_query, summed[0], 0)
    g_key = unit_back(w_key, summed[1], 0)
    g_value = unit_back(w_value, summed[2], 0)
    g_out = unit_back(w_out, summed[3], 1)
    g_up = unit_back(w_up, summed[4], 0)
    g_gate = unit_back(w_gate, summed[5], 0)
    g_down = unit_back(w_down, summed[6], 1)
    return (
        output.reshape(rows, tok, width),
        d_state.reshape(rows, tok, width),
        g_query,
        g_key,
        g_value,
        g_out,
        g_up,
        g_gate,
        g_down,
        gain_grads[0],
        gain_grads[1],
        gain_grads[2],
        gain_grads[3],
        gain_grads[4],
    )


BF16 = jnp.bfloat16
F32 = jnp.float32
LANES = 128
MIB = 1 << 20
NT = (((1,), (1,)), ((), ()))
TN = (((0,), (0,)), ((), ()))


def place():
    s = lax.axis_index("seq")
    return s // 4, (s // 2) % 2, s % 2, lax.axis_index("batch")


def dev(z, x, c, y):
    return (z * 4 + x * 2 + c, y)


def remote(src, dst, send, recv, device):
    return pltpu.make_async_remote_copy(
        src_ref=src,
        dst_ref=dst,
        send_sem=send,
        recv_sem=recv,
        device_id=device,
        device_id_type=pl.DeviceIdType.MESH,
    )


def dot(a, b):
    return jnp.dot(a, b, preferred_element_type=F32)


def dot_nt(a, b):
    return lax.dot_general(a, b, NT, preferred_element_type=F32)


def dot_tn(a, b):
    return lax.dot_general(a, b, TN, preferred_element_type=F32)


BLOCK = 256


def inverse_norm(weight, axis):
    wide = weight.astype(F32)
    return lax.rsqrt(jnp.sum(wide * wide, axis=axis, keepdims=True) + EPS)


def unit_pull(weight, grad, axis):
    inverse = inverse_norm(weight, axis)
    unit = weight.astype(F32) * inverse
    return inverse * (grad - unit * jnp.sum(grad * unit, axis=axis, keepdims=True))


def turn_tables(count):
    half = HEAD // 2
    freqs = (10000.0 ** (-np.arange(half, dtype=np.float32) / half)).astype(np.float32)
    angle = np.arange(count, dtype=np.float32)[:, None] * freqs[None, :]
    cosine = np.cos(angle).astype(np.float32)
    sine = np.sin(angle).astype(np.float32)
    return np.tile(cosine, (1, 4)), np.concatenate([-sine, sine, -sine, sine], axis=1)


def mix(state, branch, alpha):
    inv_b = lax.rsqrt(jnp.mean(branch * branch, axis=-1, keepdims=True) + EPS)
    unit_b = branch * inv_b
    step = unit_b - state
    mixed = state + alpha * step
    inv_m = lax.rsqrt(jnp.mean(mixed * mixed, axis=-1, keepdims=True) + EPS)
    return mixed * inv_m, (unit_b, inv_b, step, inv_m)


def mix_back(grad, out, saved, alpha):
    unit_b, inv_b, step, inv_m = saved
    d_mixed = inv_m * (grad - out * jnp.mean(grad * out, axis=-1, keepdims=True))
    d_alpha = jnp.sum(d_mixed * step, axis=0)
    d_unit = d_mixed * alpha
    d_branch = inv_b * (d_unit - unit_b * jnp.mean(d_unit * unit_b, axis=-1, keepdims=True))
    return d_mixed - d_unit, d_branch, d_alpha


def inside(v):
    return (v >= 0) & (v < 4)


def unit_cols(w):
    wide = w.astype(F32)
    return (wide * lax.rsqrt(jnp.sum(wide * wide, axis=0, keepdims=True) + EPS)).astype(BF16)


def unit_rows(w):
    wide = w.astype(F32)
    return (wide * lax.rsqrt(jnp.sum(wide * wide, axis=1, keepdims=True) + EPS)).astype(BF16)


SUBS = 2


class Line:
    def __init__(self, buf, sems):
        self.buf, (self.send, self.recv) = buf, sems

    def hop(self, zz, way, n):
        z, x, c, y = place()
        size = self.buf.shape[1] // SUBS
        b = self.buf.at[zz, n * size : (n + 1) * size]
        return remote(
            b, b, self.send.at[zz, (way + 1) // 2, n], self.recv.at[zz, n], dev(z + way, x, c, y)
        )

    def start(self):
        z = place()[0]
        for n in range(SUBS):
            for way in (-1, 1):

                @pl.when(inside(z + way))
                def _():
                    self.hop(z, way, n).start()

    def arrive(self, k):
        z = place()[0]
        for n in range(SUBS):
            for way in (-1, 1):
                zz = z - way * k

                @pl.when(inside(zz))
                def _():
                    self.hop(zz, -way, n).wait_recv()

                    @pl.when(inside(z + way))
                    def _():
                        self.hop(zz, way, n).start()

    def drain(self):
        z = place()[0]
        for zz in range(4):
            for way in (-1, 1):

                @pl.when(((zz - z) * way <= 0) & inside(z + way))
                def _():
                    for n in range(SUBS):
                        self.hop(zz, way, n).wait_send()


class Column:
    def __init__(self, buf, sems):
        self.buf, (self.zs, self.cs, self.recv) = buf, sems

    def hop_z(self, zz, way):
        z, x, c, y = place()
        b = 2 * zz + c
        return remote(
            self.buf.at[b], self.buf.at[b], self.zs.at[zz, (way + 1) // 2], self.recv.at[b],
            dev(z + way, x, c, y),
        )

    def hop_c(self, zz):
        z, x, c, y = place()
        b = 2 * zz + c
        return remote(
            self.buf.at[b], self.buf.at[b], self.cs.at[zz], self.recv.at[b], dev(z, x, 1 - c, y)
        )

    def arrived(self, b):
        z, x, c, y = place()
        remote(
            self.buf.at[b], self.buf.at[b], self.cs.at[0], self.recv.at[b], dev(z, x, 1 - c, y)
        ).wait_recv()

    def start(self):
        z = place()[0]
        for way in (-1, 1):

            @pl.when(inside(z + way))
            def _():
                self.hop_z(z, way).start()

        self.hop_c(z).start()

    def arrive(self, k):
        z, x, c, y = place()
        for way in (-1, 1):
            zz = z - way * k

            @pl.when(inside(zz))
            def _():
                self.arrived(2 * zz + c)

                @pl.when(inside(z + way))
                def _():
                    self.hop_z(zz, way).start()

                self.hop_c(zz).start()

    def finish(self):
        z, x, c, y = place()

        @pl.loop(0, 4)
        def _(zz):
            self.arrived(2 * zz + 1 - c)
            for way in (-1, 1):

                @pl.when(((zz - z) * way <= 0) & inside(z + way))
                def _():
                    self.hop_z(zz, way).wait_send()

            self.hop_c(zz).wait_send()


def greet_row():
    z, x, c, y = place()
    s = z * 4 + x * 2 + c
    bar = pltpu.get_barrier_semaphore()

    @pl.loop(1, 16)
    def _(k):
        pl.semaphore_signal(
            bar, inc=1, device_id=((s + k) % 16, y), device_id_type=pl.DeviceIdType.MESH
        )

    pl.semaphore_signal(bar, inc=1, device_id=dev(z, x, c, 1 - y), device_id_type=pl.DeviceIdType.MESH)
    pl.semaphore_wait(bar, 16)


def half_swap(value):
    lane = lax.broadcasted_iota(jnp.int32, value.shape, 1)
    return jnp.where(
        lane % HEAD < HEAD // 2, pltpu.roll(value, LANES - HEAD // 2, 1), pltpu.roll(value, HEAD // 2, 1)
    )


def head_means(value):
    lane = lax.broadcasted_iota(jnp.int32, value.shape, 1)
    first = jnp.sum(jnp.where(lane < HEAD, value, 0.0), axis=1, keepdims=True)
    both = jnp.sum(value, axis=1, keepdims=True)
    return jnp.where(lane < HEAD, first, both - first) * (1.0 / HEAD)


def side_by_side(block):
    half = block.shape[0] // 2
    lane = lax.broadcasted_iota(jnp.int32, (half, LANES), 1)
    return jnp.where(lane < HEAD, block[:half], pltpu.roll(block[half:], HEAD, 1))


def peers():
    z, x, c, y = place()
    return ((x, 1 - c), (1 - x, c), (1 - x, 1 - c))


def spread_heads(b, env):
    rows = pl.ds(pl.multiple_of(b * LANES, LANES), LANES)
    lane = lax.broadcasted_iota(jnp.int32, (LANES, LANES), 1)
    one = jnp.where(lane < HEAD + 2, 1.0, 0.0)
    qk = env.heads_in[b, 0:LANES, :].astype(F32)
    env.q_ext[rows, :] = jnp.where(lane < HEAD, qk, 0.0).astype(BF16)
    env.k_ext[rows, :] = jnp.where(lane < HEAD, pltpu.roll(qk, HEAD, 1), one).astype(BF16)
    packed = env.heads_in[b, LANES:, :].astype(F32)
    value = jnp.concatenate([packed, pltpu.roll(packed, HEAD, 1)], axis=0)
    env.v_ext[rows, :] = jnp.where(lane < HEAD, value, one).astype(BF16)


class Reduce:
    def __init__(self, part, passing, landed, send, recv):
        self.part, self.passing, self.landed, self.send, self.recv = part, passing, landed, send, recv
        self.size = passing.shape[1] // SUBS

    def rows(self, n):
        return slice(n * self.size, (n + 1) * self.size)

    def hop(self, owner, way, n):
        z, x, c, y = place()
        spot = jnp.where((owner == z + way) & (way < 0), 4, owner)
        return remote(
            self.passing.at[owner, self.rows(n)], self.landed.at[spot, self.rows(n)],
            self.send.at[owner, n], self.recv.at[spot, n], dev(z + way, x, c, y),
        )

    def wait_spot(self, spot, n):
        z, x, c, y = place()
        remote(
            self.passing.at[0, self.rows(n)], self.landed.at[spot, self.rows(n)], self.send.at[0, n],
            self.recv.at[spot, n], dev(z, x, 1 - c, y),
        ).wait_recv()

    def step(self, k):
        z = place()[0]
        for n in range(SUBS):
            rows = self.rows(n)
            for way in (-1, 1):
                owner = z + way * k

                @pl.when(inside(owner))
                def _():
                    @pl.when(inside(z - way))
                    def _():
                        self.wait_spot(owner, n)
                        self.passing[owner, rows] = (
                            self.part(owner, rows) + self.landed[owner, rows].astype(F32)
                        ).astype(BF16)

                    @pl.when(jnp.logical_not(inside(z - way)))
                    def _():
                        self.passing[owner, rows] = self.part(owner, rows).astype(BF16)

                    self.hop(owner, way, n).start()

    def finish(self, total):
        z = place()[0]
        everything = slice(0, SUBS * self.size)
        total[...] = self.part(z, everything)
        for edge, spot in ((z > 0, z), (z < 3, 4)):

            @pl.when(edge)
            def _():
                for n in range(SUBS):
                    self.wait_spot(spot, n)
                total[...] += self.landed[spot].astype(F32)

        for owner in range(4):

            @pl.when(owner != z)
            def _():
                for n in range(SUBS):
                    self.hop(owner, jnp.where(owner > z, 1, -1), n).wait_send()


class Env:
    def __init__(self, names, refs):
        for name, ref in zip(names, refs, strict=True):
            setattr(self, name, ref)


def window(start, size):
    return pl.ds(pl.multiple_of(start, size), size)


def qkv_rows(slot):
    return window(slot * LANES, LANES), window(4 * LANES + slot * HEAD, HEAD)


def qkv_copies(env, slot, sems, device):
    (send, recv), spots = sems, qkv_rows(slot)
    return [
        remote(env.u_qkv.at[rows, :], env.u_qkv.at[rows, :], send.at[i], recv.at[i], device)
        for i, rows in enumerate(spots)
    ]


def qkv_groups(env):
    z, x, c, y = place()
    mine, other = 2 * x + c, 2 * (1 - x) + c
    core, side = dev(z, x, 1 - c, y), dev(z, 1 - x, c, y)
    s, r = env.q_send, env.q_recv
    return (
        qkv_copies(env, mine, (s.at[0], r.at[0]), core),
        qkv_copies(env, mine, (s.at[1], r.at[1]), side),
        qkv_copies(env, other, (s.at[2], r.at[2]), core),
    )


def ff_views(env, slot, half=None):
    if half is None:
        return env.ups.at[slot], env.gates.at[slot], env.downs.at[slot]
    upper, lower = window(half * 512, 512), window(half * 128, 128)
    return env.ups.at[slot, upper, :], env.gates.at[slot, upper, :], env.downs.at[slot, lower, :]


def ff_groups(env):
    z, x, c, y = place()
    mine, other = 2 * x + c, 2 * (1 - x) + c
    core, side, twin = dev(z, x, 1 - c, y), dev(z, 1 - x, c, y), dev(z, x, c, 1 - y)

    def group(g, views, device):
        return [
            remote(v, v, env.w_send.at[g, i], env.w_recv.at[g, i], device) for i, v in enumerate(views)
        ]

    return (
        group(0, ff_views(env, mine), core),
        group(1, ff_views(env, mine, y), side),
        group(2, ff_views(env, other, y), core),
        group(3, ff_views(env, other, y), twin),
        group(4, ff_views(env, other, 1 - y), core),
    )


def each(copies, action):
    for copy in copies:
        getattr(copy, action)()


class Piece:
    def __init__(self, view, land_c, land_y, land_x, out, sems, whole):
        self.view, self.land_c, self.land_y, self.land_x, self.out = view, land_c, land_y, land_x, out
        (self.send, self.recv), self.whole = sems, whole

    def total(self):
        return self.whole[...].astype(F32)

    def slot(self, h):
        z, x, c, y = place()
        return 2 * (1 - x if h == 0 else x) + c

    def to_core(self, h):
        z, x, c, y = place()
        xx = 1 - x if h == 0 else x
        return remote(
            self.view(2 * xx + 1 - c, None), self.land_c.at[h], self.send.at[h], self.recv.at[h],
            dev(z, x, 1 - c, y),
        )

    def to_twin(self, h):
        z, x, c, y = place()
        return remote(
            self.view(self.slot(h), 1 - y), self.land_y.at[h], self.send.at[2 + h], self.recv.at[2 + h],
            dev(z, x, c, 1 - y),
        )

    def to_side(self):
        z, x, c, y = place()
        return remote(
            self.view(self.slot(0), y), self.land_x, self.send.at[4], self.recv.at[4], dev(z, 1 - x, c, y)
        )

    def swap(self):
        z, x, c, y = place()
        return remote(self.out(y), self.out(y), self.send.at[5], self.recv.at[5], dev(z, x, c, 1 - y))

    def start(self):
        self.to_core(0).start()
        self.to_core(1).start()

    def pass_twin(self):
        for h in range(2):
            self.to_core(h).wait_recv()
            both = self.view(self.slot(h), None)
            both[...] = (both[...].astype(F32) + self.land_c[h].astype(F32)).astype(BF16)
            self.to_twin(h).start()

    def pass_side(self):
        y = place()[3]
        self.to_twin(0).wait_recv()
        give = self.view(self.slot(0), y)
        give[...] = (give[...].astype(F32) + self.land_y[0].astype(F32)).astype(BF16)
        self.to_side().start()

    def pass_back(self):
        y = place()[3]
        self.to_twin(1).wait_recv()
        self.to_side().wait_recv()
        keep = self.view(self.slot(1), y)
        self.out(y)[...] = (
            keep[...].astype(F32) + self.land_y[1].astype(F32) + self.land_x[...].astype(F32)
        ).astype(BF16)
        self.swap().start()

    def finish(self):
        self.swap().wait()
        for h in range(2):
            self.to_core(h).wait_send()
            self.to_twin(h).wait_send()
        self.to_side().wait_send()


class SidePiece(Piece):
    def total(self):
        return self.whole[...].astype(F32) + self.land_y[0].astype(F32)

    def to_side(self):
        z, x, c, y = place()
        return remote(
            self.view(self.slot(0), None), self.land_x, self.send.at[4], self.recv.at[4], dev(z, 1 - x, c, y)
        )

    def swap(self):
        z, x, c, y = place()
        return remote(
            self.whole, self.land_y.at[0], self.send.at[5], self.recv.at[5], dev(z, x, c, 1 - y)
        )

    def pass_first(self):
        self.to_core(0).wait_recv()
        give = self.view(self.slot(0), None)
        give[...] = (give[...].astype(F32) + self.land_c[0].astype(F32)).astype(BF16)
        self.to_side().start()

    def pass_back(self):
        self.to_core(1).wait_recv()
        self.to_side().wait_recv()
        keep = self.view(self.slot(1), None)
        self.whole[...] = (
            keep[...].astype(F32) + self.land_c[1].astype(F32) + self.land_x[...].astype(F32)
        ).astype(BF16)
        self.swap().start()

    def finish(self):
        self.swap().wait()
        for h in range(2):
            self.to_core(h).wait_send()
        self.to_side().wait_send()


def project_block(zz, env):
    z, x, c, y = place()
    linear = dot_nt(env.x_line[zz], env.u_qkv[...])
    lane = lax.broadcasted_iota(jnp.int32, (LANES, LANES), 1)
    scale = jnp.where(lane < HEAD, HEAD ** (-0.5), 1.0)
    cosine, sine = env.cosine[zz], env.sine[zz]
    for sl in range(4):
        qk = linear[:, sl * LANES : (sl + 1) * LANES]
        turned = qk * cosine + half_swap(qk) * sine
        env.turned[zz, sl] = turned
        unit = turned * lax.rsqrt(head_means(turned * turned) + EPS)
        out = (unit * env.gain[sl : sl + 1, :]).astype(BF16).astype(F32) * scale
        env.heads_out[zz, sl, 0:LANES, :] = out.astype(BF16)
        pair = linear[:, (4 + sl // 2) * LANES : (5 + sl // 2) * LANES]
        if sl % 2:
            pair = pltpu.roll(pair, HEAD, 1)
        env.heads_out[zz, sl, LANES:, :] = side_by_side(pair).astype(BF16)
    b = zz * 4 + x * 2 + c
    env.heads_in[b] = env.heads_out[zz, x * 2 + c]
    for i, (xx, cc) in enumerate(peers()):
        remote(
            env.heads_out.at[zz, xx * 2 + cc], env.heads_in.at[b], env.hs.at[zz, i], env.hr.at[b],
            dev(z, xx, cc, y),
        ).start()


def attend_block(i, env):
    z, x, c, y = place()
    s = z * 4 + x * 2 + c
    row = lax.broadcasted_iota(jnp.int32, (BLOCK, BLOCK), 0)
    col = lax.broadcasted_iota(jnp.int32, (BLOCK, BLOCK), 1)
    lane = lax.broadcasted_iota(jnp.int32, (BLOCK, LANES), 1)
    rows = pl.ds(i * BLOCK, BLOCK)
    q = env.q_ext[rows, :]
    total = jnp.zeros((BLOCK, LANES), F32)
    for j in range(i + 1):
        keys = pl.ds(j * BLOCK, BLOCK)
        p = jnp.exp(dot_nt(q, env.k_ext[keys, :]))
        if i == j:
            p = jnp.where(row >= col, p, 0.0)
        total = total + dot(p.astype(BF16), env.v_ext[keys, :])
    denom = total[:, HEAD : HEAD + 1]
    out = total / denom
    env.attended[rows, :] = out
    log = -jnp.log(denom)
    high = log.astype(BF16).astype(F32)
    env.q_ext[rows, :] = jnp.where(
        lane == HEAD, high, jnp.where(lane == HEAD + 1, log - high, q.astype(F32))
    ).astype(BF16)
    for k in range(2):
        t = 2 * i + k
        env.att_out[t] = side_by_side(out[k * LANES : (k + 1) * LANES]).astype(BF16)
        send_block(t, env.att_out, env.att_in, env.as_, env.ar)


def block_of(b):
    return b // 4, (b // 2) % 2, b % 2


def send_block(b, src, land, send, recv):
    z, x, c, y = place()
    zz, xx, cc = block_of(b)
    own = (zz == z) & (cc == c)
    j = 2 * z + c

    @pl.when(jnp.logical_not(own))
    def _():
        remote(src.at[b], land.at[xx, j], send.at[b], recv.at[xx, j], dev(zz, x, cc, y)).start()

    @pl.when(own)
    def _():
        land[xx, j] = src[b]


def wait_blocks(src, land, send, recv):
    z, x, c, y = place()

    @pl.loop(0, 16)
    def _(b):
        zz, xx, cc = block_of(b)

        @pl.when(jnp.logical_not((zz == z) & (cc == c)))
        def _():
            j = 2 * zz + cc
            remote(src.at[b], land.at[xx, j], send.at[b], recv.at[xx, j], dev(zz, x, cc, y)).wait()


def lay_heads(land, dst):
    lane = lax.broadcasted_iota(jnp.int32, (HEAD, LANES), 1)
    for xx in range(2):
        for p in range(4):
            first = land[xx, 2 * p].astype(F32)
            second = land[xx, 2 * p + 1].astype(F32)
            cols = slice(p * LANES, (p + 1) * LANES)
            dst[xx, 0:HEAD, cols] = jnp.where(lane < HEAD, first, pltpu.roll(second, HEAD, 1)).astype(BF16)
            dst[xx, HEAD:, cols] = jnp.where(lane < HEAD, pltpu.roll(first, HEAD, 1), second).astype(BF16)


def grads_copy(b, target, env):
    x, y = place()[1], place()[3]
    xx = block_of(b)[1]
    j = 2 * target[0] + target[1]
    return remote(
        env.datt_out.at[xx, j], env.datt_in.at[b], env.das.at[xx, j], env.dar.at[b],
        dev(target[0], x, target[1], y),
    )


def send_grads(xx, env):
    z, x, c, y = place()
    b = 4 * z + 2 * xx + c
    for p in range(2):
        d_att = dot_nt(env.d_both[xx], env.u_out[4 * p : 4 * p + 4].reshape(256, 1024))
        for k in range(4):
            value = d_att[:, (k // 2) * LANES : (k // 2 + 1) * LANES]
            if k % 2:
                value = pltpu.roll(value, HEAD, 1)
            j = 4 * p + k
            env.datt_out[xx, j] = side_by_side(value).astype(BF16)
            own = 2 * z + c == j

            @pl.when(own)
            def _():
                env.datt_in[b] = env.datt_out[xx, j]

            @pl.when(jnp.logical_not(own))
            def _():
                grads_copy(b, (j // 2, j % 2), env).start()


def wait_grads(env):
    z, x, c, y = place()

    @pl.loop(0, 16)
    def _(b):
        zz, xx, cc = block_of(b)

        @pl.when(jnp.logical_not((zz == z) & (cc == c)))
        def _():
            grads_copy(b, (zz, cc), env).wait()


def side_rows(h, env):
    z, x, c, y = place()
    rows = env.d_both.at[x, rows_of(h), :]
    return remote(rows, rows, env.db_s.at[h], env.db_r.at[h], dev(z, 1 - x, c, y))


def side_mix(h, env):
    z, x, c, y = place()
    return remote(
        env.mix_out.at[h], env.mix_in.at[h], env.mx_s.at[h], env.mx_r.at[h], dev(z, 1 - x, c, y)
    )


def mlp_forward(h, env):
    @pl.loop(0, 4)
    def _(n):
        cols = window(n * 256, 256)
        mid = env.h_line[h].reshape(256, 1024)
        up = dot(mid, env.ups[n])
        gate = dot(mid, env.gates[n]) * env.gate_row[:, cols]
        env.up_lin[h, cols, :] = up
        env.gate_val[h, :, cols] = gate
        act = gate * (1.0 / (1.0 + jnp.exp(-gate)))
        env.hidden[h, :, cols] = (up * env.up_row[:, cols] * act).astype(BF16)

    @pl.loop(0, 4)
    def _(n):
        cols = window(n * 256, 256)
        env.part[h, :, :, cols] = dot(env.hidden[h], env.downs[:, :, cols].reshape(1024, 256)).reshape(
            4, 64, 256
        )


def mlp_backward(h, env):
    @pl.loop(0, 4)
    def _(n):
        cols = window(n * 256, 256)
        d_hidden = dot_nt(env.dm_line[h].reshape(256, 1024), env.downs[n])
        up, gate = env.up_lin[h, cols, :], env.gate_val[h, :, cols]
        up_gain, gate_gain = env.up_row[:, cols], env.gate_row[:, cols]
        sig = 1.0 / (1.0 + jnp.exp(-gate))
        d_up = d_hidden * (gate * sig)
        d_gate = d_hidden * (up * up_gain) * (sig * (1.0 + gate * (1.0 - sig)))
        env.gains[0:1, cols] += jnp.sum(d_up * up, axis=0, keepdims=True)
        env.gains[1:2, cols] += jnp.sum(d_gate * gate, axis=0, keepdims=True) / gate_gain
        env.d_up[h, n] = (d_up * up_gain).astype(BF16)
        env.d_gate[h, n] = (d_gate * gate_gain).astype(BF16)

    @pl.loop(0, 4)
    def _(n):
        cols = window(n * 256, 256)
        back = dot_nt(env.d_up[h, 0], env.ups[0, cols, :])
        for m in range(4):
            if m:
                back = back + dot_nt(env.d_up[h, m], env.ups[m, cols, :])
            back = back + dot_nt(env.d_gate[h, m], env.gates[m, cols, :])
        env.part[h, :, :, cols] = back.reshape(4, 64, 256)


def weight_gradient(left, right, out, first):
    @pl.loop(0, 4)
    def _(n):
        value = dot_tn(left, right(n))
        ref = out(n)
        if not first:
            value = value + ref[...].astype(F32).reshape(1024, 256)
        ref[...] = value.astype(BF16).reshape(ref.shape)


def grad_down_half(h, env):
    def right(n):
        return env.dm_line[h, :, :, window(n * 256, 256)].reshape(256, 256)

    weight_gradient(
        env.hidden[h], right, lambda n: env.g_down.at[:, :, window(n * 256, 256)], h == 0
    )


def grad_wide_half(h, src, out, env):
    weight_gradient(
        env.h_line[h].reshape(256, 1024), lambda n: src[h, n], lambda n: out.at[n], h == 0
    )


def rows_of(h):
    return slice(64 * h, 64 * (h + 1))


def after_forward(h, reduce, env):
    z, rows = place()[0], rows_of(h)
    reduce.finish(env.total)
    alpha = env.mix_row[1:2, :]
    out, saved = mix(env.mid[rows, :], env.total[...], alpha)
    env.output[rows, :] = out
    d_mid, d_branch, d_alpha = mix_back(env.d_out[rows, :], out, saved, alpha)
    env.d_mid[rows, :] = d_mid
    env.gains[3:4, :] += d_alpha[None, :]
    env.dm_line[h, z] = d_branch.astype(BF16)


def after_backward(h, reduce, env):
    rows = rows_of(h)
    reduce.finish(env.total)
    alpha = env.mix_row[0:1, :]
    mid, saved = mix(env.states[rows, :], env.branch[rows, :], alpha)
    d_state, d_branch, d_alpha = mix_back(env.d_mid[rows, :] + env.total[...], mid, saved, alpha)
    env.d_states[rows, :] = d_state
    env.gains[2:3, :] += d_alpha[None, :]
    env.d_both[place()[1], rows, :] = d_branch.astype(BF16)
    side_rows(h, env).start()


def spread_grads(b, env):
    rows = window(b * LANES, LANES)
    lane = lax.broadcasted_iota(jnp.int32, (LANES, LANES), 1)
    packed = env.datt_in[b].astype(F32)
    value = jnp.where(lane < HEAD, jnp.concatenate([packed, pltpu.roll(packed, HEAD, 1)], axis=0), 0.0)
    delta = -jnp.sum(value * env.attended[rows, :], axis=1, keepdims=True)
    high = delta.astype(BF16).astype(F32)
    env.do_ext[rows, :] = jnp.where(
        lane == HEAD, high, jnp.where(lane == HEAD + 1, delta - high, value)
    ).astype(BF16)


def attend_back_block(i, env, last):
    z, x, c, y = place()
    row = lax.broadcasted_iota(jnp.int32, (BLOCK, BLOCK), 0)
    col = lax.broadcasted_iota(jnp.int32, (BLOCK, BLOCK), 1)
    lane = lax.broadcasted_iota(jnp.int32, (LANES, LANES), 1)
    rows = pl.ds(i * BLOCK, BLOCK)
    q = env.q_ext[rows, :]
    do = env.do_ext[rows, :]
    dq = jnp.zeros((BLOCK, LANES), F32)
    for j in range(i + 1):
        keys = pl.ds(j * BLOCK, BLOCK)
        k = env.k_ext[keys, :]
        p = jnp.exp(dot_nt(k, q))
        if i == j:
            p = jnp.where(row <= col, p, 0.0)
        ds = (p * dot_nt(env.v_ext[keys, :], do)).astype(BF16)
        dv = dot(p.astype(BF16), do)
        dk = dot(ds, q)
        dq = dq + dot_tn(ds, k)
        if i == last:
            env.dk[keys, :] = dk
            env.dv[keys, :] = dv
        else:
            env.dk[keys, :] += dk
            env.dv[keys, :] += dv
    for n in range(2):
        part = slice(n * LANES, (n + 1) * LANES)
        b = 2 * i + n
        zz, sl = b // 4, b % 4
        tok = pl.ds(b * LANES, LANES)
        env.back_out[zz, sl, 0:LANES, :] = jnp.where(
            lane < HEAD, dq[part] * HEAD ** (-0.5), pltpu.roll(env.dk[tok, :], HEAD, 1)
        ).astype(BF16)
        env.back_out[zz, sl, LANES:, :] = side_by_side(env.dv[tok, :]).astype(BF16)
        mine = 2 * x + c

        @pl.when(sl == mine)
        def _():
            env.back_in[zz * 4 + mine] = env.back_out[zz, sl]

        @pl.when(sl != mine)
        def _():
            back_copy(zz, sl, mine, env).start()


def back_copy(zz, sl, source, env):
    z, x, c, y = place()
    return remote(
        env.back_out.at[zz, sl], env.back_in.at[zz * 4 + source], env.bs.at[zz, sl],
        env.br.at[zz * 4 + source], dev(z, sl // 2, sl % 2, y),
    )


def project_back(zz, env):
    z, x, c, y = place()
    mine = 2 * x + c
    cosine, sine = env.cosine[zz], env.sine[zz]
    lane = lax.broadcasted_iota(jnp.int32, (LANES, LANES), 1)
    values = []
    for sl in range(4):

        @pl.when(sl != mine)
        def _():
            back_copy(zz, sl, sl, env).wait()

        grad = env.back_in[zz * 4 + sl, 0:LANES, :].astype(F32)
        turned = env.turned[zz, sl]
        inverse = lax.rsqrt(head_means(turned * turned) + EPS)
        unit = turned * inverse
        env.gain_sum[sl : sl + 1, :] += jnp.sum(grad * unit, axis=0, keepdims=True)
        d_unit = grad * env.gain[sl : sl + 1, :]
        d_turned = inverse * (d_unit - unit * head_means(d_unit * unit))
        d_lin = d_turned * cosine - half_swap(d_turned) * sine
        env.d_lin[zz, :, sl * LANES : (sl + 1) * LANES] = d_lin.astype(BF16)
        packed = env.back_in[zz * 4 + sl, LANES:, :].astype(F32)
        values.append(jnp.concatenate([packed, pltpu.roll(packed, HEAD, 1)], axis=0))
    for p in range(2):
        pair = jnp.where(lane < HEAD, values[2 * p], pltpu.roll(values[2 * p + 1], HEAD, 1))
        env.d_lin[zz, :, (4 + p) * LANES : (5 + p) * LANES] = pair.astype(BF16)


def states_part(zz, env):
    d_x = dot(env.d_lin[zz], env.u_qkv[...])
    env.part[0, zz] = d_x[:64]
    env.part[1, zz] = d_x[64:]


def layer(env):
    z, x, c, y = place()
    s = z * 4 + x * 2 + c
    mine = 2 * x + c
    env.back_out, env.back_in = env.heads_out, env.heads_in
    env.g_out = env.u_out
    tables = []
    for zz in range(4):
        b = zz * 4 + 2 * x + c
        tables.append(pltpu.make_async_copy(env.cosines.at[b], env.cosine.at[zz], env.t_sem.at[zz, 0]))
        tables.append(pltpu.make_async_copy(env.sines.at[b], env.sine.at[zz], env.t_sem.at[zz, 1]))
    each(tables, "start")

    env.x_line[z] = env.states[...].astype(BF16)
    qk_rows, v_rows = qkv_rows(mine)
    env.u_qkv[qk_rows, :] = jnp.concatenate(
        [unit_rows(env.w_query[...]), unit_rows(env.w_key[...])], axis=0
    )
    env.u_qkv[v_rows, :] = unit_rows(env.w_value[...])
    greet_row()
    line = Line(env.x_line, (env.x_send, env.x_recv))
    line.start()
    q_core, q_side, q_relay = qkv_groups(env)
    each(q_side, "start")
    each(q_core, "start")

    lane = lax.broadcasted_iota(jnp.int32, (1, LANES), 1)
    for pair in range(2):
        scale = env.qk_scale[window(z * 256 + pair * LANES, LANES)].reshape(1, LANES)
        turned = pltpu.roll(scale, HEAD, 1)
        env.gain[2 * pair : 2 * pair + 1, :] = jnp.where(lane < HEAD, scale, turned)
        env.gain[2 * pair + 1 : 2 * pair + 2, :] = jnp.where(lane < HEAD, turned, scale)
    env.up_row[...] = env.up_scale[window(z * 1024, 1024)].reshape(1, 1024)
    env.gate_row[...] = env.gate_scale[window(z * 1024, 1024)].reshape(1, 1024)
    env.mix_row[0:1, :] = env.alpha_attn[...].reshape(1, 1024)
    env.mix_row[1:2, :] = env.alpha_mlp[...].reshape(1, 1024)
    env.u_out[2 * z + c] = unit_rows(env.w_out[...])
    env.ups[mine] = unit_cols(env.w_up[...])
    env.gates[mine] = unit_cols(env.w_gate[...])
    env.downs[mine] = unit_rows(env.w_down[...])
    env.gains[...] = jnp.zeros_like(env.gains)
    env.gain_sum[...] = jnp.zeros_like(env.gain_sum)
    ff = ff_groups(env)
    each(ff[0], "start")
    each(tables, "wait")

    line.arrive(1)
    each(q_side, "wait_recv")
    each(q_relay, "start")
    each(q_core, "wait_recv")
    each(q_relay, "wait_recv")
    project_block(z, env)

    @pl.loop(1, 4)
    def _(k):
        @pl.when(k < 3)
        def _():
            line.arrive(k + 1)

        for way in (-1, 1):

            @pl.when(inside(z - way * k))
            def _():
                project_block(z - way * k, env)

    each(ff[1], "start")
    line.drain()
    for group in (q_side, q_core, q_relay):
        each(group, "wait_send")
    uo = Column(env.u_out, (env.o_z, env.o_c, env.o_r))
    uo.start()

    @pl.loop(0, 4)
    def _(zz):
        for i, (xx, cc) in enumerate(peers()):
            b = zz * 4 + xx * 2 + cc
            remote(
                env.heads_out.at[zz, xx * 2 + cc], env.heads_in.at[b], env.hs.at[zz, i], env.hr.at[b],
                dev(z, xx, cc, y),
            ).wait()

    @pl.loop(0, 16)
    def _(b):
        spread_heads(b, env)

    uo.arrive(1)
    for i in range(4):
        attend_block(i, env)
    for i in range(4, 6):
        attend_block(i, env)
    uo.arrive(2)
    for i in range(6, 8):
        attend_block(i, env)
    uo.arrive(3)
    uo.finish()
    ff[1][0].wait_recv()
    ff[2][0].start()
    ff[3][0].start()
    wait_blocks(env.att_out, env.att_in, env.as_, env.ar)
    lay_heads(env.att_in, env.att_low)

    weights = env.u_out[...].reshape(512, 1024)
    for h in range(2):
        env.mix_out[h] = dot(env.att_low[1 - x, rows_of(h), :], weights).astype(BF16)
        side_mix(h, env).start()
    env.branch[...] = dot(env.att_low[x], weights)
    ff[1][1].wait_recv()
    ff[2][1].start()
    ff[3][1].start()

    def mix_half(h):
        rows = rows_of(h)
        side_mix(h, env).wait_recv()
        branch = env.branch[rows, :] + env.mix_in[h].astype(F32)
        env.branch[rows, :] = branch
        mid, _ = mix(env.states[rows, :], branch, env.mix_row[0:1, :])
        env.mid[rows, :] = mid
        env.h_line[h, z] = mid.astype(BF16)

    fa = Line(env.h_line.at[0], (env.fa_s, env.fa_r))
    fb = Line(env.h_line.at[1], (env.fb_s, env.fb_r))
    ba = Line(env.dm_line.at[0], (env.ba_s, env.ba_r))
    bb = Line(env.dm_line.at[1], (env.bb_s, env.bb_r))

    def reduce(h, send, recv):
        return Reduce(
            lambda owner, rows: env.part[h, owner, rows], env.passing.at[h], env.landed.at[h], send, recv
        )

    r0, r1 = reduce(0, env.r0_s, env.r0_r), reduce(1, env.r1_s, env.r1_r)

    def arrive(gather, k):
        gather.arrive(k)

    def piece(grad, tag, cut):
        def view(slot, half):
            return grad.at[slot] if half is None else grad.at[slot, window(half * cut, cut), :]

        lc, ly, lx, out, send, recv = tag
        kind = Piece if ly.shape[1] == cut else SidePiece
        return kind(view, lc, ly, lx, lambda half: out.at[window(half * cut, cut), :], (send, recv), out)

    gu = piece(env.g_up, (env.lcu, env.lyu, env.lxu, env.ou, env.us, env.ur), 512)
    gg = piece(env.g_gate, (env.lcg, env.lyg, env.lxg, env.og, env.gs, env.gr), 512)
    gd = piece(env.g_down, (env.lcd, env.lyd, env.lxd, env.od, env.ds, env.dr), 128)
    mix_half(0)
    fa.start()
    mix_half(1)
    ff[1][2].wait_recv()
    ff[2][2].start()
    ff[3][2].start()
    arrive(fa, 1)
    arrive(fa, 2)
    fb.start()
    each(ff[3], "wait_recv")
    each(ff[4], "start")
    each(ff[0], "wait_recv")
    each(ff[2], "wait_recv")
    each(ff[4], "wait_recv")
    arrive(fa, 3)
    mlp_forward(0, env)
    r0.step(3)
    arrive(fb, 1)
    r0.step(2)
    arrive(fb, 2)
    r0.step(1)
    arrive(fb, 3)
    mlp_forward(1, env)
    r1.step(3)
    after_forward(0, r0, env)
    ba.start()
    r1.step(2)
    arrive(ba, 1)
    r1.step(1)
    arrive(ba, 2)
    after_forward(1, r1, env)
    bb.start()
    arrive(ba, 3)
    mlp_backward(0, env)
    r0.step(3)
    arrive(bb, 1)
    grad_down_half(0, env)
    r0.step(2)
    arrive(bb, 2)
    grad_wide_half(0, env.d_up, env.g_up, env)
    r0.step(1)
    grad_wide_half(0, env.d_gate, env.g_gate, env)
    arrive(bb, 3)
    grad_down_half(1, env)
    gd.start()
    mlp_backward(1, env)
    r1.step(3)
    gd.pass_twin()
    after_backward(0, r0, env)
    grad_wide_half(1, env.d_up, env.g_up, env)
    gu.start()
    r1.step(2)
    for gather in (fa, fb, ba, bb):
        gather.drain()
    for group in ff:
        each(group, "wait_send")
    for h in range(2):
        side_mix(h, env).wait_send()
    gu.pass_first()
    grad_wide_half(1, env.d_gate, env.g_gate, env)
    gg.start()
    r1.step(1)
    after_backward(1, r1, env)

    side_rows(0, env).wait_recv()
    send_grads(x, env)
    side_rows(1, env).wait_recv()
    send_grads(1 - x, env)

    @pl.loop(0, 4)
    def _(n):
        cols = window(n * 256, 256)
        grad = dot_tn(env.att_low[0], env.d_both[0, :, cols]) + dot_tn(env.att_low[1], env.d_both[1, :, cols])
        env.g_out[:, :, cols] = grad.reshape(8, 64, 256).astype(BF16)

    out_reduce = RowReduce(env)
    out_reduce.start()
    gd.pass_side()
    out_reduce.pass_line()
    wait_grads(env)

    @pl.loop(0, 16, unroll=4)
    def _(b):
        spread_grads(b, env)

    gu.pass_back()
    out_reduce.step(3)
    attend_back_block(7, env, 7)
    gd.pass_back()
    out_reduce.step(2)
    attend_back_block(6, env, 7)
    out_reduce.step(1)
    for i in range(5, -1, -1):
        attend_back_block(i, env, 7)
    gg.pass_first()
    for h in range(2):
        side_rows(h, env).wait_send()
    project_back(3, env)
    out_reduce.to_twin()
    project_back(2, env)
    project_back(1, env)
    project_back(0, env)
    @pl.loop(0, 4)
    def _(n):
        cols = window(n * 256, 256)
        total = dot_tn(env.d_lin[...].reshape(512, 768), env.x_line[:, :, cols].reshape(512, 256))
        env.g_qkv[:, cols] = total.astype(BF16)

    def row_piece(which, tag, cut):
        def view(slot, half):
            start, size = (slot * LANES, LANES) if which == 0 else (4 * LANES + slot * HEAD, HEAD)
            if half is not None:
                start, size = start + half * cut, cut
            return env.g_qkv.at[window(start, size), :]

        lc, ly, lx, out, send, recv = tag
        kind = Piece if ly.shape[1] == cut else SidePiece
        return kind(
            view, lc, ly, lx, lambda half: out.at[window(half * cut, cut), :], (send, recv), out
        )

    gq = row_piece(0, (env.lcq, env.lyq, env.lxq, env.oq, env.qqs, env.qqr), 64)
    gv = row_piece(1, (env.lcv, env.lyv, env.lxv, env.ov, env.vvs, env.vvr), 32)
    gq.start()
    gv.start()

    @pl.loop(0, 4)
    def _(zz):
        states_part(zz, env)

    for h in range(2):
        (r0, r1)[h].step(3)
    gq.pass_first()
    gv.pass_twin()
    for sl in range(4):
        both_parts = env.gain_sum[sl : sl + 1, 0:HEAD] + env.gain_sum[sl : sl + 1, HEAD:]
        env.gains[4 + sl : 5 + sl, 0:HEAD] = both_parts
    small = [
        remote(env.gains, env.gain_land.at[i], env.sm_s.at[i], env.sm_r.at[i], device)
        for i, device in enumerate((dev(z, x, 1 - c, y), dev(z, 1 - x, c, y), dev(z, x, c, 1 - y)))
    ]
    def tell(k):
        t = (z + k) % 4
        return remote(
            env.gain_line.at[z], env.gain_line.at[z], env.gl_s.at[k], env.gl_r.at[z], dev(t, x, c, y)
        )

    small[0].start()
    r0.step(2)
    r1.step(2)
    gv.pass_side()
    small[0].wait()
    env.gains[...] += env.gain_land[0]
    small[1].start()
    gg.pass_back()
    finish_ff(env, gd, 2)
    small[1].wait()
    env.gains[...] += env.gain_land[1]
    small[2].start()
    r0.step(1)
    r1.step(1)
    gq.pass_back()
    gv.pass_back()
    finish_ff(env, gu, 0)
    small[2].wait()
    env.gain_line[z] = env.gains[...] + env.gain_land[2]
    for k in range(1, 4):
        tell(k).start()
    finish_ff(env, gg, 1)
    out_reduce.finish()
    unit_out = env.oo[...].astype(F32) + env.yo[...].astype(F32)
    env.gate_val[1, 3 * HEAD :, :] = pull_rows(env.w_out[...], unit_out)
    r0.finish(env.total)
    env.d_states[0:64, :] += env.total[...]
    r1.finish(env.total)
    env.d_states[64:, :] += env.total[...]
    gq.finish()
    gv.finish()
    stage = env.gate_val.at[1]
    total_qk = gq.total()
    stage[0:HEAD, :] = pull_rows(env.w_query[...], total_qk[0:HEAD])
    stage[HEAD : 2 * HEAD, :] = pull_rows(env.w_key[...], total_qk[HEAD:])
    stage[2 * HEAD : 3 * HEAD, :] = pull_rows(env.w_value[...], gv.total())
    results = [
        pltpu.make_async_copy(stage.at[pl.ds(i * HEAD, HEAD), :], ref, env.out_sem.at[3 + i])
        for i, ref in enumerate((env.grad_query, env.grad_key, env.grad_value, env.grad_out))
    ]
    each(results, "start")
    for k in range(1, 4):
        tell(k).wait_send()
        t = (z + k) % 4
        remote(
            env.gain_line.at[t], env.gain_line.at[t], env.gl_s.at[k], env.gl_r.at[t], dev(t, x, c, y)
        ).wait_recv()
    each(results, "wait")
    for i in range(3):
        ff_result(env, i).wait()


def pull_rows(weight, grad):
    wide = weight.astype(F32)
    inverse = lax.rsqrt(jnp.sum(wide * wide, axis=1, keepdims=True) + EPS)
    unit = wide * inverse
    return inverse * (grad - unit * jnp.sum(grad * unit, axis=1, keepdims=True))


def pull_cols(weight, grad):
    wide = weight.astype(F32)
    inverse = lax.rsqrt(jnp.sum(wide * wide, axis=0, keepdims=True) + EPS)
    unit = wide * inverse
    return inverse * (grad - unit * jnp.sum(grad * unit, axis=0, keepdims=True))


def ff_result(env, which):
    stage = (env.up_lin.at[0], env.up_lin.at[1], env.gate_val.at[0])[which]
    out = (env.grad_up, env.grad_gate, env.grad_down)[which]
    return pltpu.make_async_copy(stage, out, env.out_sem.at[which])


def finish_ff(env, piece, which):
    piece.finish()
    if which == 2:
        env.gate_val[0] = pull_rows(env.w_down[...], piece.total())
    elif which == 0:
        env.up_lin[0] = pull_cols(env.w_up[...], piece.total())
    else:
        env.up_lin[1] = pull_cols(env.w_gate[...], piece.total())
    ff_result(env, which).start()


class RowReduce:
    def __init__(self, env):
        self.env = env
        self.line = Reduce(self.part, env.o_pass, env.o_land, env.ol_s, env.ol_r)

    def part(self, owner, rows):
        return self.env.g_out[2 * owner + place()[2], rows].astype(F32)

    def to_core(self, zz):
        z, x, c, y = place()
        e = self.env
        return remote(
            e.g_out.at[2 * zz + 1 - c], e.o_c_land.at[zz], e.oc_s.at[zz], e.oc_r.at[zz], dev(z, x, 1 - c, y)
        )

    def twin(self):
        z, x, c, y = place()
        e = self.env
        return remote(e.oo, e.yo, e.oy_s, e.oy_r, dev(z, x, c, 1 - y))

    def start(self):
        @pl.loop(0, 4)
        def _(zz):
            self.to_core(zz).start()

    def pass_line(self):
        c = place()[2]
        e = self.env

        @pl.loop(0, 4)
        def _(zz):
            self.to_core(zz).wait_recv()
            b = 2 * zz + c
            e.g_out[b] = (e.g_out[b].astype(F32) + e.o_c_land[zz].astype(F32)).astype(BF16)

    def step(self, k):
        self.line.step(k)

    def to_twin(self):
        e = self.env
        self.line.finish(e.total)
        e.oo[...] = e.total[...].astype(BF16)
        self.twin().start()

    def finish(self):
        self.twin().wait()

        @pl.loop(0, 4)
        def _(zz):
            self.to_core(zz).wait_send()


DMA = pltpu.SemaphoreType.DMA


def v(shape, dtype=BF16):
    return pltpu.VMEM(shape, dtype)


LAYER_IN = tuple(
    dict(
        states=None,
        w_query=None,
        w_key=None,
        w_value=None,
        w_out=None,
        w_up=None,
        w_gate=None,
        w_down=None,
        qk_scale=None,
        up_scale=None,
        gate_scale=None,
        alpha_attn=None,
        alpha_mlp=None,
        d_out=None,
        cosines=None,
        sines=None,
    )
)
LAYER_OUT = dict(
    output=((128, 1024), F32), d_states=((128, 1024), F32), gain_line=((4, 8, 1024), F32),
    grad_query=((64, 1024), F32), grad_key=((64, 1024), F32), grad_value=((64, 1024), F32),
    grad_out=((64, 1024), F32), grad_up=((1024, 256), F32), grad_gate=((1024, 256), F32),
    grad_down=((256, 1024), F32),
)
IN_VMEM = 3
LAYER_TMP = dict(
    x_line=v((4, 128, 1024)), u_qkv=v((768, 1024)), u_out=v((8, 64, 1024)), mix_out=v((2, 64, 1024)), mix_in=v((2, 64, 1024)),
    turned=v((4, 4, 128, 128), F32), cosine=v((4, 128, 128), F32), sine=v((4, 128, 128), F32),
    gain=v((4, 128), F32), up_row=v((1, 1024), F32), gate_row=v((1, 1024), F32), mix_row=v((2, 1024), F32), gain_sum=v((4, 128), F32), gains=v((8, 1024), F32),
    gain_land=v((3, 8, 1024), F32),
    heads_out=v((4, 4, 192, 128)), heads_in=v((16, 192, 128)),
    q_ext=v((2048, 128)), k_ext=v((2048, 128)), v_ext=v((2048, 128)), attended=v((2048, 128), F32),
    att_out=v((16, 64, 128)), att_in=v((2, 8, 64, 128)), att_low=v((2, 128, 512)),
    ups=v((4, 1024, 256)), gates=v((4, 1024, 256)), downs=v((4, 256, 1024)),
    branch=v((128, 1024), F32), mid=v((128, 1024), F32), d_mid=v((128, 1024), F32),
    total=v((64, 1024), F32), d_both=v((2, 128, 1024)),
    h_line=v((2, 4, 64, 1024)), dm_line=v((2, 4, 64, 1024)),
    up_lin=v((2, 1024, 256), F32), gate_val=v((2, 256, 1024), F32), hidden=v((2, 256, 1024)),
    d_up=v((2, 4, 256, 256)), d_gate=v((2, 4, 256, 256)),
    part=v((2, 4, 64, 1024), F32), passing=v((2, 4, 64, 1024)), landed=v((2, 5, 64, 1024)),
    g_up=v((4, 1024, 256)), g_gate=v((4, 1024, 256)), g_down=v((4, 256, 1024)), g_qkv=v((768, 1024)),
    lcu=v((2, 1024, 256)), lcg=v((2, 1024, 256)), lcd=v((2, 256, 1024)), lcq=v((2, 128, 1024)),
    lcv=v((2, 64, 1024)),
    lyu=v((1, 1024, 256)), lyg=v((1, 1024, 256)), lyd=v((2, 128, 1024)), lyq=v((1, 128, 1024)), lyv=v((2, 32, 1024)),
    lxu=v((1024, 256)), lxg=v((1024, 256)), lxd=v((128, 1024)), lxq=v((128, 1024)), lxv=v((32, 1024)),
    ou=v((1024, 256)), og=v((1024, 256)), od=v((256, 1024)), oq=v((128, 1024)), ov=v((64, 1024)),
    oo=v((64, 1024)), yo=v((64, 1024)), out_sem=DMA((7,)),
    o_c_land=v((4, 64, 1024)), o_pass=v((4, 64, 1024)),
    o_land=v((5, 64, 1024)),
    datt_out=v((2, 8, 64, 128)), datt_in=v((16, 64, 128)), do_ext=v((2048, 128)),
    dk=v((2048, 128), F32), dv=v((2048, 128), F32),
    d_lin=v((4, 128, 768)),
    t_sem=DMA((4, 2)), x_send=DMA((4, 2, SUBS)), x_recv=DMA((4, SUBS)), q_send=DMA((3, 2)), q_recv=DMA((3, 2)),
    w_send=DMA((5, 3)), w_recv=DMA((5, 3)), hs=DMA((4, 3)), hr=DMA((16,)),
    o_z=DMA((4, 2)), o_c=DMA((4,)), o_r=DMA((8,)),
    as_=DMA((16,)), ar=DMA((2, 8)), das=DMA((2, 8)), dar=DMA((16,)),
    mx_s=DMA((2,)), mx_r=DMA((2,)), db_s=DMA((2,)), db_r=DMA((2,)),
    fa_s=DMA((4, 2, SUBS)), fa_r=DMA((4, SUBS)), fb_s=DMA((4, 2, SUBS)), fb_r=DMA((4, SUBS)),
    ba_s=DMA((4, 2, SUBS)), ba_r=DMA((4, SUBS)), bb_s=DMA((4, 2, SUBS)), bb_r=DMA((4, SUBS)),
    r0_s=DMA((4, SUBS)), r0_r=DMA((5, SUBS)), r1_s=DMA((4, SUBS)), r1_r=DMA((5, SUBS)),
    us=DMA((6,)), ur=DMA((6,)), gs=DMA((6,)), gr=DMA((6,)), ds=DMA((6,)), dr=DMA((6,)),
    qqs=DMA((6,)), qqr=DMA((6,)), vvs=DMA((6,)), vvr=DMA((6,)),
    oc_s=DMA((4,)), oc_r=DMA((4,)),
    ol_s=DMA((4, SUBS)), ol_r=DMA((5, SUBS)), oy_s=DMA, oy_r=DMA,
    bs=DMA((4, 4)), br=DMA((16,)), sm_s=DMA((3,)), sm_r=DMA((3,)), gl_s=DMA((4,)), gl_r=DMA((4,)),
)


def run_layer(*args):
    vmem = pl.BlockSpec(memory_space=pltpu.VMEM)
    names = LAYER_IN + tuple(LAYER_OUT) + tuple(LAYER_TMP)

    def kernel(*refs):
        layer(Env(names, refs))

    outs = pl.pallas_call(
        kernel,
        name="layer",
        out_shape=tuple(jax.ShapeDtypeStruct(*o) for o in LAYER_OUT.values()),
        in_specs=[vmem] * (len(LAYER_IN) - 2) + [pl.BlockSpec(memory_space=pl.ANY)] * 2,
        out_specs=(vmem,) * IN_VMEM
        + (pl.BlockSpec(memory_space=pl.ANY),) * (len(LAYER_OUT) - IN_VMEM),
        scratch_shapes=list(LAYER_TMP.values()),
        compiler_params=pltpu.CompilerParams(
            collective_id=1, has_side_effects=True, vmem_limit_bytes=62 * MIB
        ),
    )(*args)
    return dict(zip(LAYER_OUT, outs))


HANDED = tuple(name for name in LAYER_OUT if name != "gain_line")


def hand_over_kernel(*refs):
    count = len(HANDED)
    line = refs[count]
    outs = refs[count + 1 : 2 * count + 6]
    held = refs[2 * count + 6 : 3 * count + 6]
    arrive, leave = refs[3 * count + 6 :]
    loads = [pltpu.make_async_copy(refs[i], held[i], arrive.at[i]) for i in range(count)]
    stores = [pltpu.make_async_copy(held[i], outs[i], leave.at[i]) for i in range(count)]
    each(loads, "start")
    qk, up, gate, attn, mlp = outs[count:]
    lane = lax.broadcasted_iota(jnp.int32, (1, LANES), 1)
    for zz in range(4):
        cols = slice(zz * 1024, (zz + 1) * 1024)
        up[cols] = line[zz, 0:1, :].reshape(1024)
        gate[cols] = line[zz, 1:2, :].reshape(1024)
        for pair in range(2):
            first = line[zz, 4 + 2 * pair : 5 + 2 * pair, 0:LANES]
            second = pltpu.roll(line[zz, 5 + 2 * pair : 6 + 2 * pair, 0:LANES], HEAD, 1)
            both = jnp.where(lane < HEAD, first, second)
            qk[zz * 256 + pair * LANES : zz * 256 + (pair + 1) * LANES] = both.reshape(LANES)
    for row, out in ((2, attn), (3, mlp)):
        parts = [line[zz, row : row + 1, :] for zz in range(4)]
        out[...] = (parts[0] + parts[1] + parts[2] + parts[3]).reshape(1024)
    for load, store in zip(loads, stores):
        load.wait()
        store.start()
    each(stores, "wait")


def hand_over(*arrays):
    vmem, hbm = pl.BlockSpec(memory_space=pltpu.VMEM), pl.BlockSpec(memory_space=pl.ANY)
    count = len(HANDED)
    sizes = (1024, 4096, 4096, 1024, 1024)
    return pl.pallas_call(
        hand_over_kernel,
        name="hand_over",
        out_shape=tuple(jax.ShapeDtypeStruct(a.shape, a.dtype) for a in arrays[:count])
        + tuple(jax.ShapeDtypeStruct((n,), F32) for n in sizes),
        in_specs=[hbm] * count + [vmem],
        out_specs=(hbm,) * count + (vmem,) * len(sizes),
        scratch_shapes=[v(a.shape, a.dtype) for a in arrays[:count]] + [DMA((count,))] * 2,
        compiler_params=pltpu.CompilerParams(vmem_limit_bytes=60 * MIB),
    )(*arrays)


def on_device_heads(
    states,
    lengths,
    w_query,
    w_key,
    w_value,
    w_out,
    w_up,
    w_gate,
    w_down,
    qk_scale,
    up_scale,
    gate_scale,
    alpha_attn,
    alpha_mlp,
    d_out,
):
    tok, width = states.shape[1:]
    cosine, sine = turn_tables(16 * tok)
    got = run_layer(
        states.reshape(tok, width), w_query.T, w_key.T, w_value.T, w_out, w_up, w_gate, w_down,
        qk_scale, up_scale, gate_scale, alpha_attn, alpha_mlp, d_out.reshape(tok, width),
        jnp.asarray(cosine.reshape(16, tok, LANES)), jnp.asarray(sine.reshape(16, tok, LANES)),
    )

    output, d_states, g_query, g_key, g_value, g_out, g_up, g_gate, g_down, *gains = hand_over(
        *(got[name] for name in HANDED), got["gain_line"]
    )
    return (
        output.reshape(states.shape),
        d_states.reshape(states.shape),
        g_query.T,
        g_key.T,
        g_value.T,
        g_out,
        g_up,
        g_gate,
        g_down,
        *gains,
    )


def solution(mesh):
    seq, batch = mesh.shape["seq"], mesh.shape["batch"]
    body = on_device_heads if (seq == HEADS and batch == 2) else on_device_general
    return jax.shard_map(
        body,
        mesh=mesh,
        in_specs=(
            P("batch", "seq", None),
            P("batch", None),
            P(None, "seq"),
            P(None, "seq"),
            P(None, "seq"),
            P("seq", None),
            P(None, "seq"),
            P(None, "seq"),
            P("seq", None),
            P(),
            P(),
            P(),
            P(),
            P(),
            P("batch", "seq", None),
        ),
        out_specs=(
            P("batch", "seq", None),
            P("batch", "seq", None),
            P(None, "seq"),
            P(None, "seq"),
            P(None, "seq"),
            P("seq", None),
            P(None, "seq"),
            P(None, "seq"),
            P("seq", None),
            P(),
            P(),
            P(),
            P(),
            P(),
        ),
        check_vma=False,
    )
```

```python
import jax
import jax.numpy as jnp
import numpy as np
from jax import lax
from jax.experimental import pallas as pl
from jax.experimental.pallas import tpu as pltpu
from jax.sharding import PartitionSpec as P

HEADS = 16
HEAD = 64


EPS = 1e-06


def shifted(value, axis, steps):
    count = lax.axis_size(axis)
    first, last = (max(0, -steps), min(count, count - steps))
    return lax.ppermute(value, axis, [(source, source + steps) for source in range(first, last)])


def shifted_2(block, axis, distance):
    devices = range(lax.axis_size(axis))
    route = [((i - distance) % len(devices), i) for i in devices]
    return lax.ppermute(block, axis, route)


def normalized(weight, axis):
    wide = weight.astype(jnp.float32)
    return wide * lax.rsqrt(jnp.sum(wide * wide, axis=axis, keepdims=True) + EPS)


def rms(values):
    return values * lax.rsqrt(jnp.mean(values * values, axis=-1, keepdims=True) + EPS)


def doc_layout(len_row, tok_index):
    docs = jnp.arange(len_row.shape[0])
    starts = jnp.sum(jnp.where(docs[:, None] < docs[None, :], len_row[:, None], 0), axis=0)
    started = starts[None, :] <= tok_index[:, None]
    doc_ids = jnp.sum(started.astype(jnp.int32), axis=1) - 1
    first_tok = jnp.max(jnp.where(started, starts[None, :], 0), axis=1)
    return (doc_ids, tok_index - first_tok)


def rope(values, position):
    half = values.shape[-1] // 2
    freqs = 10000.0 ** (-jnp.arange(half, dtype=jnp.float32) / half)
    angle = position.astype(jnp.float32)[:, None] * freqs[None, :]
    cosine = jnp.cos(angle)[:, None, :]
    sine = jnp.sin(angle)[:, None, :]
    first = values[..., :half]
    second = values[..., half:]
    return jnp.concatenate(
        [first * cosine - second * sine, first * sine + second * cosine], axis=-1
    )


def prepare(linear, position, gain):
    count = linear.shape[0]
    shaped = linear.reshape(count, HEADS, HEAD)
    turned = rms(rope(shaped, position)) * gain.reshape(HEADS, HEAD)
    return turned.reshape(count, HEADS * HEAD)


def residual_mix(state, branch, alpha):
    return rms(state + alpha * (rms(branch) - state))


def gating(up_lin, gate_lin, up_scale, gate_scale):
    return up_scale * up_lin * jax.nn.silu(gate_scale * gate_lin)


def unit_back(raw_shard, grad_shard, axis):
    primal, pullback = jax.vjp(
        lambda weight: normalized(weight, axis), raw_shard.astype(jnp.float32)
    )
    return pullback(grad_shard)[0]


def on_device_general(
    states,
    lengths,
    w_query,
    w_key,
    w_value,
    w_out,
    w_up,
    w_gate,
    w_down,
    qk_scale,
    up_scale,
    gate_scale,
    alpha_attn,
    alpha_mlp,
    d_out,
):
    seq_count = lax.axis_size("seq")
    my_index = lax.axis_index("seq")
    rows = states.shape[0]
    tok = states.shape[1]
    width = states.shape[2]
    flat = rows * tok
    score_scale = HEAD ** (-0.5)
    row_layout = jax.vmap(doc_layout, in_axes=(0, None))
    unit_query = normalized(w_query, 0).astype(jnp.bfloat16)
    unit_key = normalized(w_key, 0).astype(jnp.bfloat16)
    unit_value = normalized(w_value, 0).astype(jnp.bfloat16)
    unit_out = normalized(w_out, 1).astype(jnp.bfloat16)
    unit_up = normalized(w_up, 0).astype(jnp.bfloat16)
    unit_gate = normalized(w_gate, 0).astype(jnp.bfloat16)
    unit_down = normalized(w_down, 1).astype(jnp.bfloat16)
    full_weights = (
        lax.all_gather(unit_query, "seq", axis=1, tiled=True),
        lax.all_gather(unit_key, "seq", axis=1, tiled=True),
        lax.all_gather(unit_value, "seq", axis=1, tiled=True),
        lax.all_gather(unit_out, "seq", axis=0, tiled=True),
        lax.all_gather(unit_up, "seq", axis=1, tiled=True),
        lax.all_gather(unit_gate, "seq", axis=1, tiled=True),
        lax.all_gather(unit_down, "seq", axis=0, tiled=True),
    )
    full_query, full_key, full_value, full_out, full_up, full_gate, full_down = full_weights
    tok_index = my_index * tok + jnp.arange(tok, dtype=jnp.int32)
    doc_ids, position = row_layout(lengths, tok_index)
    flat_pos = position.reshape(flat)
    state_in = states.reshape(flat, width)
    x_low = state_in.astype(jnp.bfloat16)
    query_lin = jnp.dot(x_low, full_query, preferred_element_type=jnp.float32)
    key_lin = jnp.dot(x_low, full_key, preferred_element_type=jnp.float32)
    value_lin = jnp.dot(x_low, full_value, preferred_element_type=jnp.float32)

    def front(query_part, key_part, gain):
        return (prepare(query_part, flat_pos, gain), prepare(key_part, flat_pos, gain))

    query_f, key_f = front(query_lin, key_lin, qk_scale)
    query_h = query_f.astype(jnp.bfloat16).reshape(rows, tok, HEADS, HEAD)
    key_h = key_f.astype(jnp.bfloat16).reshape(rows, tok, HEADS, HEAD)
    value_h = value_lin.astype(jnp.bfloat16).reshape(rows, tok, HEADS, HEAD)

    def block_scores(key_blk, source):
        key_index = source * tok + jnp.arange(tok, dtype=jnp.int32)
        key_docs, key_pos = row_layout(lengths, key_index)
        scores = (
            jnp.einsum("bqhd,bkhd->bqhk", query_h, key_blk, preferred_element_type=jnp.float32)
            * score_scale
        )
        allowed = (doc_ids[:, :, None] == key_docs[:, None, :]) & (
            key_index[None, None, :] <= tok_index[None, :, None]
        )
        return (scores, allowed[:, :, None, :])

    def is_active(source):
        last_key = jnp.reshape(source * tok + tok - 1, (1,))
        last_doc, last_pos = row_layout(lengths, last_key)
        return (source <= my_index) & jnp.any(last_doc[:, 0] >= doc_ids[:, 0])

    def attend(running, key_blk, value_blk, source):

        def compute(carried):
            best, denom_sum, accum = carried
            scores, allowed = block_scores(key_blk, source)
            new_best = jnp.maximum(best, jnp.max(jnp.where(allowed, scores, -1e30), axis=3))
            weights = jnp.where(allowed, jnp.exp(scores - new_best[:, :, :, None]), 0.0)
            shrink = jnp.exp(best - new_best)
            denom_sum = denom_sum * shrink + jnp.sum(weights, axis=3)
            accum = accum * shrink[:, :, :, None] + jnp.einsum(
                "bqhk,bkhd->bqhd",
                weights.astype(jnp.bfloat16),
                value_blk,
                preferred_element_type=jnp.float32,
            )
            return (new_best, denom_sum, accum)

        return lax.cond(is_active(source), compute, lambda carried: carried, running)

    reach = seq_count - 1
    start_state = (
        jnp.full((rows, tok, HEADS), -1e30, jnp.float32),
        jnp.zeros((rows, tok, HEADS), jnp.float32),
        jnp.zeros((rows, tok, HEADS, HEAD), jnp.float32),
    )
    first_state = attend(start_state, key_h, value_h, my_index)

    def cycle_step(step, loop_carry):
        running, key_blk, value_blk = loop_carry
        key_blk, value_blk = shifted((key_blk, value_blk), "seq", 1)
        source = (my_index - step) % seq_count
        return (attend(running, key_blk, value_blk, source), key_blk, value_blk)

    final_state, spent_key, spent_value = lax.fori_loop(
        1, reach + 1, cycle_step, (first_state, key_h, value_h)
    )
    best, denom_sum, accum = final_state
    attended = accum / denom_sum[:, :, :, None]
    log_sum = best + jnp.log(denom_sum)
    attended_low = attended.astype(jnp.bfloat16).reshape(flat, width)
    attn_branch = jnp.dot(attended_low, full_out, preferred_element_type=jnp.float32)
    state_mid = residual_mix(state_in, attn_branch, alpha_attn)
    mid_low = state_mid.astype(jnp.bfloat16)
    up_lin = jnp.dot(mid_low, full_up, preferred_element_type=jnp.float32)
    gate_lin = jnp.dot(mid_low, full_gate, preferred_element_type=jnp.float32)
    gated_low = gating(up_lin, gate_lin, up_scale, gate_scale).astype(jnp.bfloat16)
    mlp_branch = jnp.dot(gated_low, full_down, preferred_element_type=jnp.float32)
    output = residual_mix(state_mid, mlp_branch, alpha_mlp)
    back_weights = (
        lax.all_gather(unit_query, "seq", axis=1, tiled=True),
        lax.all_gather(unit_key, "seq", axis=1, tiled=True),
        lax.all_gather(unit_value, "seq", axis=1, tiled=True),
        lax.all_gather(unit_out, "seq", axis=0, tiled=True),
        lax.all_gather(unit_up, "seq", axis=1, tiled=True),
        lax.all_gather(unit_gate, "seq", axis=1, tiled=True),
        lax.all_gather(unit_down, "seq", axis=0, tiled=True),
    )
    back_query, back_key, back_value, back_out, back_up, back_gate, back_down = back_weights
    primal, pull_mlp = jax.vjp(residual_mix, state_mid, mlp_branch, alpha_mlp)
    d_mid, d_mlp, g_alpha_mlp = pull_mlp(d_out.reshape(flat, width))
    d_mlp_low = d_mlp.astype(jnp.bfloat16)
    grad_down = jnp.einsum("tf,td->fd", gated_low, d_mlp_low, preferred_element_type=jnp.float32)
    d_gated = jnp.einsum("td,fd->tf", d_mlp_low, back_down, preferred_element_type=jnp.float32)
    primal, pull_gate = jax.vjp(gating, up_lin, gate_lin, up_scale, gate_scale)
    d_up, d_gate, g_up_scale, g_gate_scale = pull_gate(d_gated)
    d_up_low = d_up.astype(jnp.bfloat16)
    d_gate_low = d_gate.astype(jnp.bfloat16)
    grad_up = jnp.einsum("tc,tf->cf", mid_low, d_up_low, preferred_element_type=jnp.float32)
    grad_gate = jnp.einsum("tc,tf->cf", mid_low, d_gate_low, preferred_element_type=jnp.float32)
    d_mid = d_mid + jnp.einsum("tf,cf->tc", d_up_low, back_up, preferred_element_type=jnp.float32)
    d_mid = d_mid + jnp.einsum(
        "tf,cf->tc", d_gate_low, back_gate, preferred_element_type=jnp.float32
    )
    primal, pull_attn = jax.vjp(residual_mix, state_in, attn_branch, alpha_attn)
    d_state, d_attn, g_alpha_attn = pull_attn(d_mid)
    d_attn_low = d_attn.astype(jnp.bfloat16)
    grad_out = jnp.einsum("tc,td->cd", attended_low, d_attn_low, preferred_element_type=jnp.float32)
    d_attended = jnp.einsum("td,cd->tc", d_attn_low, back_out, preferred_element_type=jnp.float32)
    d_att_low = d_attended.astype(jnp.bfloat16).reshape(rows, tok, HEADS, HEAD)
    delta = jnp.sum(d_att_low.astype(jnp.float32) * attended, axis=3)

    def attend_back(d_query, key_blk, value_blk, d_key, d_value, source):

        def compute(carried):
            d_query, d_key, d_value = carried
            scores, allowed = block_scores(key_blk, source)
            probs = jnp.where(allowed, jnp.exp(scores - log_sum[:, :, :, None]), 0.0)
            d_probs = jnp.einsum(
                "bqhd,bkhd->bqhk", d_att_low, value_blk, preferred_element_type=jnp.float32
            )
            d_scores = (probs * (d_probs - delta[:, :, :, None])).astype(jnp.bfloat16)
            d_query = d_query + jnp.einsum(
                "bqhk,bkhd->bqhd", d_scores, key_blk, preferred_element_type=jnp.float32
            )
            d_key = d_key + jnp.einsum(
                "bqhk,bqhd->bkhd", d_scores, query_h, preferred_element_type=jnp.float32
            )
            d_value = d_value + jnp.einsum(
                "bqhk,bqhd->bkhd",
                probs.astype(jnp.bfloat16),
                d_att_low,
                preferred_element_type=jnp.float32,
            )
            return (d_query, d_key, d_value)

        return lax.cond(
            is_active(source), compute, lambda carried: carried, (d_query, d_key, d_value)
        )

    def back_step(step, loop_carry):
        d_query, key_blk, value_blk, d_key, d_value = loop_carry
        source = (my_index - step) % seq_count
        d_query, d_key, d_value = attend_back(d_query, key_blk, value_blk, d_key, d_value, source)
        d_key, d_value = (
            shifted_2(d_key.astype(jnp.bfloat16), "seq", 1).astype(d_key.dtype),
            shifted_2(d_value.astype(jnp.bfloat16), "seq", 1).astype(d_value.dtype),
        )
        key_blk, value_blk = shifted((key_blk, value_blk), "seq", 1)
        return (d_query, key_blk, value_blk, d_key, d_value)

    zero_heads = jnp.zeros((rows, tok, HEADS, HEAD), jnp.float32)
    d_query_h, last_key_blk, last_value_blk, d_key_h, d_value_h = lax.fori_loop(
        0, reach, back_step, (zero_heads, key_h, value_h, zero_heads, zero_heads)
    )
    d_query_h, d_key_h, d_value_h = attend_back(
        d_query_h, last_key_blk, last_value_blk, d_key_h, d_value_h, (my_index - reach) % seq_count
    )
    d_key_h, d_value_h = (
        shifted_2(d_key_h.astype(jnp.bfloat16), "seq", -reach).astype(d_key_h.dtype),
        shifted_2(d_value_h.astype(jnp.bfloat16), "seq", -reach).astype(d_value_h.dtype),
    )
    primal, pull_front = jax.vjp(front, query_lin, key_lin, qk_scale)
    d_query_lin, d_key_lin, g_qk_scale = pull_front(
        (d_query_h.reshape(flat, width) * score_scale, d_key_h.reshape(flat, width) * score_scale)
    )
    d_query_low = d_query_lin.astype(jnp.bfloat16)
    d_key_low = d_key_lin.astype(jnp.bfloat16)
    d_value_low = d_value_h.reshape(flat, width).astype(jnp.bfloat16)
    grad_query = jnp.einsum("tc,tj->cj", x_low, d_query_low, preferred_element_type=jnp.float32)
    grad_key = jnp.einsum("tc,tj->cj", x_low, d_key_low, preferred_element_type=jnp.float32)
    grad_value = jnp.einsum("tc,tj->cj", x_low, d_value_low, preferred_element_type=jnp.float32)
    d_state = d_state + jnp.einsum(
        "tj,cj->tc", d_query_low, back_query, preferred_element_type=jnp.float32
    )
    d_state = d_state + jnp.einsum(
        "tj,cj->tc", d_key_low, back_key, preferred_element_type=jnp.float32
    )
    d_state = d_state + jnp.einsum(
        "tj,cj->tc", d_value_low, back_value, preferred_element_type=jnp.float32
    )
    shards = (
        lax.psum_scatter(
            grad_query.astype(jnp.bfloat16), "seq", scatter_dimension=1, tiled=True
        ).astype(jnp.float32),
        lax.psum_scatter(
            grad_key.astype(jnp.bfloat16), "seq", scatter_dimension=1, tiled=True
        ).astype(jnp.float32),
        lax.psum_scatter(
            grad_value.astype(jnp.bfloat16), "seq", scatter_dimension=1, tiled=True
        ).astype(jnp.float32),
        lax.psum_scatter(
            grad_out.astype(jnp.bfloat16), "seq", scatter_dimension=0, tiled=True
        ).astype(jnp.float32),
        lax.psum_scatter(
            grad_up.astype(jnp.bfloat16), "seq", scatter_dimension=1, tiled=True
        ).astype(jnp.float32),
        lax.psum_scatter(
            grad_gate.astype(jnp.bfloat16), "seq", scatter_dimension=1, tiled=True
        ).astype(jnp.float32),
        lax.psum_scatter(
            grad_down.astype(jnp.bfloat16), "seq", scatter_dimension=0, tiled=True
        ).astype(jnp.float32),
    )
    summed = (
        lax.psum(shards[0].astype(jnp.bfloat16), "batch").astype(jnp.float32),
        lax.psum(shards[1].astype(jnp.bfloat16), "batch").astype(jnp.float32),
        lax.psum(shards[2].astype(jnp.bfloat16), "batch").astype(jnp.float32),
        lax.psum(shards[3].astype(jnp.bfloat16), "batch").astype(jnp.float32),
        lax.psum(shards[4].astype(jnp.bfloat16), "batch").astype(jnp.float32),
        lax.psum(shards[5].astype(jnp.bfloat16), "batch").astype(jnp.float32),
        lax.psum(shards[6].astype(jnp.bfloat16), "batch").astype(jnp.float32),
    )
    gain_grads = lax.psum(
        (g_qk_scale, g_up_scale, g_gate_scale, g_alpha_attn, g_alpha_mlp), ("seq", "batch")
    )
    g_query = unit_back(w_query, summed[0], 0)
    g_key = unit_back(w_key, summed[1], 0)
    g_value = unit_back(w_value, summed[2], 0)
    g_out = unit_back(w_out, summed[3], 1)
    g_up = unit_back(w_up, summed[4], 0)
    g_gate = unit_back(w_gate, summed[5], 0)
    g_down = unit_back(w_down, summed[6], 1)
    return (
        output.reshape(rows, tok, width),
        d_state.reshape(rows, tok, width),
        g_query,
        g_key,
        g_value,
        g_out,
        g_up,
        g_gate,
        g_down,
        gain_grads[0],
        gain_grads[1],
        gain_grads[2],
        gain_grads[3],
        gain_grads[4],
    )


BF16 = jnp.bfloat16
F32 = jnp.float32
LANES = 128
MIB = 1 << 20
NT = (((1,), (1,)), ((), ()))
TN = (((0,), (0,)), ((), ()))


def place():
    s = lax.axis_index("seq")
    return s // 4, (s // 2) % 2, s % 2, lax.axis_index("batch")


def dev(z, x, c, y):
    return (z * 4 + x * 2 + c, y)


def remote(src, dst, send, recv, device):
    return pltpu.make_async_remote_copy(
        src_ref=src,
        dst_ref=dst,
        send_sem=send,
        recv_sem=recv,
        device_id=device,
        device_id_type=pl.DeviceIdType.MESH,
    )


def dot(a, b):
    return jnp.dot(a, b, preferred_element_type=F32)


def dot_nt(a, b):
    return lax.dot_general(a, b, NT, preferred_element_type=F32)


def dot_tn(a, b):
    return lax.dot_general(a, b, TN, preferred_element_type=F32)


BLOCK = 256


def inverse_norm(weight, axis):
    wide = weight.astype(F32)
    return lax.rsqrt(jnp.sum(wide * wide, axis=axis, keepdims=True) + EPS)


def unit_pull(weight, grad, axis):
    inverse = inverse_norm(weight, axis)
    unit = weight.astype(F32) * inverse
    return inverse * (grad - unit * jnp.sum(grad * unit, axis=axis, keepdims=True))


def turn_tables(count):
    half = HEAD // 2
    freqs = (10000.0 ** (-np.arange(half, dtype=np.float32) / half)).astype(np.float32)
    angle = np.arange(count, dtype=np.float32)[:, None] * freqs[None, :]
    cosine = np.cos(angle).astype(np.float32)
    sine = np.sin(angle).astype(np.float32)
    return np.tile(cosine, (1, 4)), np.concatenate([-sine, sine, -sine, sine], axis=1)


def mix(state, branch, alpha):
    inv_b = lax.rsqrt(jnp.mean(branch * branch, axis=-1, keepdims=True) + EPS)
    unit_b = branch * inv_b
    step = unit_b - state
    mixed = state + alpha * step
    inv_m = lax.rsqrt(jnp.mean(mixed * mixed, axis=-1, keepdims=True) + EPS)
    return mixed * inv_m, (unit_b, inv_b, step, inv_m)


def mix_back(grad, out, saved, alpha):
    unit_b, inv_b, step, inv_m = saved
    d_mixed = inv_m * (grad - out * jnp.mean(grad * out, axis=-1, keepdims=True))
    d_alpha = jnp.sum(d_mixed * step, axis=0)
    d_unit = d_mixed * alpha
    d_branch = inv_b * (d_unit - unit_b * jnp.mean(d_unit * unit_b, axis=-1, keepdims=True))
    return d_mixed - d_unit, d_branch, d_alpha


def inside(v):
    return (v >= 0) & (v < 4)


def unit_cols(w):
    wide = w.astype(F32)
    return (wide * lax.rsqrt(jnp.sum(wide * wide, axis=0, keepdims=True) + EPS)).astype(BF16)


def unit_rows(w):
    wide = w.astype(F32)
    return (wide * lax.rsqrt(jnp.sum(wide * wide, axis=1, keepdims=True) + EPS)).astype(BF16)


SUBS = 2


class Line:
    def __init__(self, buf, sems):
        self.buf, (self.send, self.recv) = buf, sems

    def hop(self, zz, way, n):
        z, x, c, y = place()
        size = self.buf.shape[1] // SUBS
        b = self.buf.at[zz, n * size : (n + 1) * size]
        return remote(
            b, b, self.send.at[zz, (way + 1) // 2, n], self.recv.at[zz, n], dev(z + way, x, c, y)
        )

    def start(self):
        z = place()[0]
        for n in range(SUBS):
            for way in (-1, 1):

                @pl.when(inside(z + way))
                def _():
                    self.hop(z, way, n).start()

    def arrive(self, k):
        z = place()[0]
        for n in range(SUBS):
            for way in (-1, 1):
                zz = z - way * k

                @pl.when(inside(zz))
                def _():
                    self.hop(zz, -way, n).wait_recv()

                    @pl.when(inside(z + way))
                    def _():
                        self.hop(zz, way, n).start()

    def drain(self):
        z = place()[0]
        for zz in range(4):
            for way in (-1, 1):

                @pl.when(((zz - z) * way <= 0) & inside(z + way))
                def _():
                    for n in range(SUBS):
                        self.hop(zz, way, n).wait_send()


class Column:
    def __init__(self, buf, sems):
        self.buf, (self.zs, self.cs, self.recv) = buf, sems

    def hop_z(self, zz, way):
        z, x, c, y = place()
        b = 2 * zz + c
        return remote(
            self.buf.at[b], self.buf.at[b], self.zs.at[zz, (way + 1) // 2], self.recv.at[b],
            dev(z + way, x, c, y),
        )

    def hop_c(self, zz):
        z, x, c, y = place()
        b = 2 * zz + c
        return remote(
            self.buf.at[b], self.buf.at[b], self.cs.at[zz], self.recv.at[b], dev(z, x, 1 - c, y)
        )

    def arrived(self, b):
        z, x, c, y = place()
        remote(
            self.buf.at[b], self.buf.at[b], self.cs.at[0], self.recv.at[b], dev(z, x, 1 - c, y)
        ).wait_recv()

    def start(self):
        z = place()[0]
        for way in (-1, 1):

            @pl.when(inside(z + way))
            def _():
                self.hop_z(z, way).start()

        self.hop_c(z).start()

    def arrive(self, k):
        z, x, c, y = place()
        for way in (-1, 1):
            zz = z - way * k

            @pl.when(inside(zz))
            def _():
                self.arrived(2 * zz + c)

                @pl.when(inside(z + way))
                def _():
                    self.hop_z(zz, way).start()

                self.hop_c(zz).start()

    def finish(self):
        z, x, c, y = place()

        @pl.loop(0, 4)
        def _(zz):
            self.arrived(2 * zz + 1 - c)
            for way in (-1, 1):

                @pl.when(((zz - z) * way <= 0) & inside(z + way))
                def _():
                    self.hop_z(zz, way).wait_send()

            self.hop_c(zz).wait_send()


def greet_row():
    z, x, c, y = place()
    s = z * 4 + x * 2 + c
    bar = pltpu.get_barrier_semaphore()

    @pl.loop(1, 16)
    def _(k):
        pl.semaphore_signal(
            bar, inc=1, device_id=((s + k) % 16, y), device_id_type=pl.DeviceIdType.MESH
        )

    pl.semaphore_signal(bar, inc=1, device_id=dev(z, x, c, 1 - y), device_id_type=pl.DeviceIdType.MESH)


def half_swap(value):
    lane = lax.broadcasted_iota(jnp.int32, value.shape, 1)
    return jnp.where(
        lane % HEAD < HEAD // 2, pltpu.roll(value, LANES - HEAD // 2, 1), pltpu.roll(value, HEAD // 2, 1)
    )


def head_means(value):
    lane = lax.broadcasted_iota(jnp.int32, value.shape, 1)
    first = jnp.sum(jnp.where(lane < HEAD, value, 0.0), axis=1, keepdims=True)
    both = jnp.sum(value, axis=1, keepdims=True)
    return jnp.where(lane < HEAD, first, both - first) * (1.0 / HEAD)


def side_by_side(block):
    half = block.shape[0] // 2
    lane = lax.broadcasted_iota(jnp.int32, (half, LANES), 1)
    return jnp.where(lane < HEAD, block[:half], pltpu.roll(block[half:], HEAD, 1))


def peers():
    z, x, c, y = place()
    return ((x, 1 - c), (1 - x, c), (1 - x, 1 - c))


def spread_heads(b, env):
    rows = pl.ds(pl.multiple_of(b * LANES, LANES), LANES)
    lane = lax.broadcasted_iota(jnp.int32, (LANES, LANES), 1)
    one = jnp.where(lane < HEAD + 2, 1.0, 0.0)
    qk = env.heads_in[b, 0:LANES, :].astype(F32)
    env.q_ext[rows, :] = jnp.where(lane < HEAD, qk, 0.0).astype(BF16)
    env.k_ext[rows, :] = jnp.where(lane < HEAD, pltpu.roll(qk, HEAD, 1), one).astype(BF16)
    packed = env.heads_in[b, LANES:, :].astype(F32)
    value = jnp.concatenate([packed, pltpu.roll(packed, HEAD, 1)], axis=0)
    env.v_ext[rows, :] = jnp.where(lane < HEAD, value, one).astype(BF16)


class Reduce:
    def __init__(self, part, passing, landed, send, recv):
        self.part, self.passing, self.landed, self.send, self.recv = part, passing, landed, send, recv
        self.size = passing.shape[1] // SUBS

    def rows(self, n):
        return slice(n * self.size, (n + 1) * self.size)

    def hop(self, owner, way, n):
        z, x, c, y = place()
        spot = jnp.where((owner == z + way) & (way < 0), 4, owner)
        return remote(
            self.passing.at[owner, self.rows(n)], self.landed.at[spot, self.rows(n)],
            self.send.at[owner, n], self.recv.at[spot, n], dev(z + way, x, c, y),
        )

    def wait_spot(self, spot, n):
        z, x, c, y = place()
        remote(
            self.passing.at[0, self.rows(n)], self.landed.at[spot, self.rows(n)], self.send.at[0, n],
            self.recv.at[spot, n], dev(z, x, 1 - c, y),
        ).wait_recv()

    def step(self, k):
        z = place()[0]
        for n in range(SUBS):
            rows = self.rows(n)
            for way in (-1, 1):
                owner = z + way * k

                @pl.when(inside(owner))
                def _():
                    @pl.when(inside(z - way))
                    def _():
                        self.wait_spot(owner, n)
                        self.passing[owner, rows] = (
                            self.part(owner, rows) + self.landed[owner, rows].astype(F32)
                        ).astype(BF16)

                    @pl.when(jnp.logical_not(inside(z - way)))
                    def _():
                        self.passing[owner, rows] = self.part(owner, rows).astype(BF16)

                    self.hop(owner, way, n).start()

    def finish(self, total):
        z = place()[0]
        everything = slice(0, SUBS * self.size)
        total[...] = self.part(z, everything)
        for edge, spot in ((z > 0, z), (z < 3, 4)):

            @pl.when(edge)
            def _():
                for n in range(SUBS):
                    self.wait_spot(spot, n)
                total[...] += self.landed[spot].astype(F32)

        for owner in range(4):

            @pl.when(owner != z)
            def _():
                for n in range(SUBS):
                    self.hop(owner, jnp.where(owner > z, 1, -1), n).wait_send()


class Env:
    def __init__(self, names, refs):
        for name, ref in zip(names, refs, strict=True):
            setattr(self, name, ref)


def window(start, size):
    return pl.ds(pl.multiple_of(start, size), size)


def qkv_rows(slot):
    return window(slot * LANES, LANES), window(4 * LANES + slot * HEAD, HEAD)


def qkv_copies(env, slot, sems, device):
    (send, recv), spots = sems, qkv_rows(slot)
    return [
        remote(env.u_qkv.at[rows, :], env.u_qkv.at[rows, :], send.at[i], recv.at[i], device)
        for i, rows in enumerate(spots)
    ]


def qkv_groups(env):
    z, x, c, y = place()
    mine, other = 2 * x + c, 2 * (1 - x) + c
    core, side = dev(z, x, 1 - c, y), dev(z, 1 - x, c, y)
    s, r = env.q_send, env.q_recv
    return (
        qkv_copies(env, mine, (s.at[0], r.at[0]), core),
        qkv_copies(env, mine, (s.at[1], r.at[1]), side),
        qkv_copies(env, other, (s.at[2], r.at[2]), core),
    )


def ff_views(env, slot, half=None):
    if half is None:
        return env.ups.at[slot], env.gates.at[slot], env.downs.at[slot]
    upper, lower = window(half * 512, 512), window(half * 128, 128)
    return env.ups.at[slot, upper, :], env.gates.at[slot, upper, :], env.downs.at[slot, lower, :]


def ff_groups(env):
    z, x, c, y = place()
    mine, other = 2 * x + c, 2 * (1 - x) + c
    core, side, twin = dev(z, x, 1 - c, y), dev(z, 1 - x, c, y), dev(z, x, c, 1 - y)

    def group(g, views, device):
        return [
            remote(v, v, env.w_send.at[g, i], env.w_recv.at[g, i], device) for i, v in enumerate(views)
        ]

    return (
        group(0, ff_views(env, mine), core),
        group(1, ff_views(env, mine, y), side),
        group(2, ff_views(env, other, y), core),
        group(3, ff_views(env, other, y), twin),
        group(4, ff_views(env, other, 1 - y), core),
    )


def each(copies, action):
    for copy in copies:
        getattr(copy, action)()


class Piece:
    def __init__(self, view, land_c, land_y, land_x, out, sems, whole):
        self.view, self.land_c, self.land_y, self.land_x, self.out = view, land_c, land_y, land_x, out
        (self.send, self.recv), self.whole = sems, whole

    def total(self):
        return self.whole[...].astype(F32)

    def slot(self, h):
        z, x, c, y = place()
        return 2 * (1 - x if h == 0 else x) + c

    def to_core(self, h):
        z, x, c, y = place()
        xx = 1 - x if h == 0 else x
        return remote(
            self.view(2 * xx + 1 - c, None), self.land_c.at[h], self.send.at[h], self.recv.at[h],
            dev(z, x, 1 - c, y),
        )

    def to_twin(self, h):
        z, x, c, y = place()
        return remote(
            self.view(self.slot(h), 1 - y), self.land_y.at[h], self.send.at[2 + h], self.recv.at[2 + h],
            dev(z, x, c, 1 - y),
        )

    def to_side(self):
        z, x, c, y = place()
        return remote(
            self.view(self.slot(0), y), self.land_x, self.send.at[4], self.recv.at[4], dev(z, 1 - x, c, y)
        )

    def swap(self):
        z, x, c, y = place()
        return remote(self.out(y), self.out(y), self.send.at[5], self.recv.at[5], dev(z, x, c, 1 - y))

    def start(self):
        self.to_core(0).start()
        self.to_core(1).start()

    def pass_twin(self):
        for h in range(2):
            self.to_core(h).wait_recv()
            both = self.view(self.slot(h), None)
            both[...] = (both[...].astype(F32) + self.land_c[h].astype(F32)).astype(BF16)
            self.to_twin(h).start()

    def pass_side(self):
        y = place()[3]
        self.to_twin(0).wait_recv()
        give = self.view(self.slot(0), y)
        give[...] = (give[...].astype(F32) + self.land_y[0].astype(F32)).astype(BF16)
        self.to_side().start()

    def pass_back(self):
        y = place()[3]
        self.to_twin(1).wait_recv()
        self.to_side().wait_recv()
        keep = self.view(self.slot(1), y)
        self.out(y)[...] = (
            keep[...].astype(F32) + self.land_y[1].astype(F32) + self.land_x[...].astype(F32)
        ).astype(BF16)
        self.swap().start()

    def finish(self):
        self.swap().wait()
        for h in range(2):
            self.to_core(h).wait_send()
            self.to_twin(h).wait_send()
        self.to_side().wait_send()


class SidePiece(Piece):
    def total(self):
        return self.whole[...].astype(F32) + self.land_y[0].astype(F32)

    def to_side(self):
        z, x, c, y = place()
        return remote(
            self.view(self.slot(0), None), self.land_x, self.send.at[4], self.recv.at[4], dev(z, 1 - x, c, y)
        )

    def swap(self):
        z, x, c, y = place()
        return remote(
            self.whole, self.land_y.at[0], self.send.at[5], self.recv.at[5], dev(z, x, c, 1 - y)
        )

    def pass_first(self):
        self.to_core(0).wait_recv()
        give = self.view(self.slot(0), None)
        give[...] = (give[...].astype(F32) + self.land_c[0].astype(F32)).astype(BF16)
        self.to_side().start()

    def pass_back(self):
        self.to_core(1).wait_recv()
        self.to_side().wait_recv()
        keep = self.view(self.slot(1), None)
        self.whole[...] = (
            keep[...].astype(F32) + self.land_c[1].astype(F32) + self.land_x[...].astype(F32)
        ).astype(BF16)
        self.swap().start()

    def finish(self):
        self.swap().wait()
        for h in range(2):
            self.to_core(h).wait_send()
        self.to_side().wait_send()


def project_block(zz, env):
    z, x, c, y = place()
    linear = dot_nt(env.x_line[zz], env.u_qkv[...])
    lane = lax.broadcasted_iota(jnp.int32, (LANES, LANES), 1)
    scale = jnp.where(lane < HEAD, HEAD ** (-0.5), 1.0)
    cosine, sine = env.cosine[zz], env.sine[zz]
    for sl in range(4):
        qk = linear[:, sl * LANES : (sl + 1) * LANES]
        turned = qk * cosine + half_swap(qk) * sine
        env.turned[zz, sl] = turned
        unit = turned * lax.rsqrt(head_means(turned * turned) + EPS)
        out = (unit * env.gain[sl : sl + 1, :]).astype(BF16).astype(F32) * scale
        env.heads_out[zz, sl, 0:LANES, :] = out.astype(BF16)
        pair = linear[:, (4 + sl // 2) * LANES : (5 + sl // 2) * LANES]
        if sl % 2:
            pair = pltpu.roll(pair, HEAD, 1)
        env.heads_out[zz, sl, LANES:, :] = side_by_side(pair).astype(BF16)
    b = zz * 4 + x * 2 + c
    env.heads_in[b] = env.heads_out[zz, x * 2 + c]
    for i, (xx, cc) in enumerate(peers()):
        remote(
            env.heads_out.at[zz, xx * 2 + cc], env.heads_in.at[b], env.hs.at[zz, i], env.hr.at[b],
            dev(z, xx, cc, y),
        ).start()


def attend_block(i, env):
    z, x, c, y = place()
    s = z * 4 + x * 2 + c
    row = lax.broadcasted_iota(jnp.int32, (BLOCK, BLOCK), 0)
    col = lax.broadcasted_iota(jnp.int32, (BLOCK, BLOCK), 1)
    lane = lax.broadcasted_iota(jnp.int32, (BLOCK, LANES), 1)
    rows = pl.ds(i * BLOCK, BLOCK)
    q = env.q_ext[rows, :]
    total = jnp.zeros((BLOCK, LANES), F32)
    for j in range(i + 1):
        keys = pl.ds(j * BLOCK, BLOCK)
        p = jnp.exp(dot_nt(q, env.k_ext[keys, :]))
        if i == j:
            p = jnp.where(row >= col, p, 0.0)
        total = total + dot(p.astype(BF16), env.v_ext[keys, :])
    denom = total[:, HEAD : HEAD + 1]
    out = total / denom
    env.attended[rows, :] = out
    log = -jnp.log(denom)
    high = log.astype(BF16).astype(F32)
    env.q_ext[rows, :] = jnp.where(
        lane == HEAD, high, jnp.where(lane == HEAD + 1, log - high, q.astype(F32))
    ).astype(BF16)
    for k in range(2):
        t = 2 * i + k
        env.att_out[t] = side_by_side(out[k * LANES : (k + 1) * LANES]).astype(BF16)
        send_block(t, env.att_out, env.att_in, env.as_, env.ar)


def block_of(b):
    return b // 4, (b // 2) % 2, b % 2


def send_block(b, src, land, send, recv):
    z, x, c, y = place()
    zz, xx, cc = block_of(b)
    own = (zz == z) & (cc == c)
    j = 2 * z + c

    @pl.when(jnp.logical_not(own))
    def _():
        remote(src.at[b], land.at[xx, j], send.at[b], recv.at[xx, j], dev(zz, x, cc, y)).start()

    @pl.when(own)
    def _():
        land[xx, j] = src[b]


def wait_blocks(src, land, send, recv):
    z, x, c, y = place()

    @pl.loop(0, 16)
    def _(b):
        zz, xx, cc = block_of(b)

        @pl.when(jnp.logical_not((zz == z) & (cc == c)))
        def _():
            j = 2 * zz + cc
            remote(src.at[b], land.at[xx, j], send.at[b], recv.at[xx, j], dev(zz, x, cc, y)).wait()


def lay_heads(land, dst):
    lane = lax.broadcasted_iota(jnp.int32, (HEAD, LANES), 1)
    for xx in range(2):
        for p in range(4):
            first = land[xx, 2 * p].astype(F32)
            second = land[xx, 2 * p + 1].astype(F32)
            cols = slice(p * LANES, (p + 1) * LANES)
            dst[xx, 0:HEAD, cols] = jnp.where(lane < HEAD, first, pltpu.roll(second, HEAD, 1)).astype(BF16)
            dst[xx, HEAD:, cols] = jnp.where(lane < HEAD, pltpu.roll(first, HEAD, 1), second).astype(BF16)


def grads_copy(b, target, env):
    x, y = place()[1], place()[3]
    xx = block_of(b)[1]
    j = 2 * target[0] + target[1]
    return remote(
        env.datt_out.at[xx, j], env.datt_in.at[b], env.das.at[xx, j], env.dar.at[b],
        dev(target[0], x, target[1], y),
    )


def send_grads(xx, env):
    z, x, c, y = place()
    b = 4 * z + 2 * xx + c
    for p in range(2):
        d_att = dot_nt(env.d_both[xx], env.u_out[4 * p : 4 * p + 4].reshape(256, 1024))
        for k in range(4):
            value = d_att[:, (k // 2) * LANES : (k // 2 + 1) * LANES]
            if k % 2:
                value = pltpu.roll(value, HEAD, 1)
            j = 4 * p + k
            env.datt_out[xx, j] = side_by_side(value).astype(BF16)
            own = 2 * z + c == j

            @pl.when(own)
            def _():
                env.datt_in[b] = env.datt_out[xx, j]

            @pl.when(jnp.logical_not(own))
            def _():
                grads_copy(b, (j // 2, j % 2), env).start()


def wait_grads(env):
    z, x, c, y = place()

    @pl.loop(0, 16)
    def _(b):
        zz, xx, cc = block_of(b)

        @pl.when(jnp.logical_not((zz == z) & (cc == c)))
        def _():
            grads_copy(b, (zz, cc), env).wait()


def side_rows(h, env):
    z, x, c, y = place()
    rows = env.d_both.at[x, rows_of(h), :]
    return remote(rows, rows, env.db_s.at[h], env.db_r.at[h], dev(z, 1 - x, c, y))


def side_mix(h, env):
    z, x, c, y = place()
    return remote(
        env.mix_out.at[h], env.mix_in.at[h], env.mx_s.at[h], env.mx_r.at[h], dev(z, 1 - x, c, y)
    )


def mlp_forward(h, env):
    @pl.loop(0, 4)
    def _(n):
        cols = window(n * 256, 256)
        mid = env.h_line[h].reshape(256, 1024)
        up = dot(mid, env.ups[n])
        gate = dot(mid, env.gates[n]) * env.gate_row[:, cols]
        env.up_lin[h, cols, :] = up
        env.gate_val[h, :, cols] = gate
        act = gate * (1.0 / (1.0 + jnp.exp(-gate)))
        env.hidden[h, :, cols] = (up * env.up_row[:, cols] * act).astype(BF16)

    @pl.loop(0, 4)
    def _(n):
        cols = window(n * 256, 256)
        env.part[h, :, :, cols] = dot(env.hidden[h], env.downs[:, :, cols].reshape(1024, 256)).reshape(
            4, 64, 256
        )


def mlp_backward(h, env):
    @pl.loop(0, 4)
    def _(n):
        cols = window(n * 256, 256)
        d_hidden = dot_nt(env.dm_line[h].reshape(256, 1024), env.downs[n])
        up, gate = env.up_lin[h, cols, :], env.gate_val[h, :, cols]
        up_gain, gate_gain = env.up_row[:, cols], env.gate_row[:, cols]
        sig = 1.0 / (1.0 + jnp.exp(-gate))
        d_up = d_hidden * (gate * sig)
        d_gate = d_hidden * (up * up_gain) * (sig * (1.0 + gate * (1.0 - sig)))
        env.gains[0:1, cols] += jnp.sum(d_up * up, axis=0, keepdims=True)
        env.gains[1:2, cols] += jnp.sum(d_gate * gate, axis=0, keepdims=True) / gate_gain
        env.d_up[h, n] = (d_up * up_gain).astype(BF16)
        env.d_gate[h, n] = (d_gate * gate_gain).astype(BF16)

    @pl.loop(0, 4)
    def _(n):
        cols = window(n * 256, 256)
        back = dot_nt(env.d_up[h, 0], env.ups[0, cols, :])
        for m in range(4):
            if m:
                back = back + dot_nt(env.d_up[h, m], env.ups[m, cols, :])
            back = back + dot_nt(env.d_gate[h, m], env.gates[m, cols, :])
        env.part[h, :, :, cols] = back.reshape(4, 64, 256)


def weight_gradient(left, right, out, first):
    @pl.loop(0, 4)
    def _(n):
        value = dot_tn(left, right(n))
        ref = out(n)
        if not first:
            value = value + ref[...].astype(F32).reshape(1024, 256)
        ref[...] = value.astype(BF16).reshape(ref.shape)


def grad_down_half(h, env):
    def right(n):
        return env.dm_line[h, :, :, window(n * 256, 256)].reshape(256, 256)

    weight_gradient(
        env.hidden[h], right, lambda n: env.g_down.at[:, :, window(n * 256, 256)], h == 0
    )


def grad_wide_half(h, src, out, env):
    weight_gradient(
        env.h_line[h].reshape(256, 1024), lambda n: src[h, n], lambda n: out.at[n], h == 0
    )


def rows_of(h):
    return slice(64 * h, 64 * (h + 1))


def after_forward(h, reduce, env):
    z, rows = place()[0], rows_of(h)
    reduce.finish(env.total)
    alpha = env.mix_row[1:2, :]
    out, saved = mix(env.mid[rows, :], env.total[...], alpha)
    env.output[rows, :] = out
    d_mid, d_branch, d_alpha = mix_back(env.d_out[rows, :], out, saved, alpha)
    env.d_mid[rows, :] = d_mid
    env.gains[3:4, :] += d_alpha[None, :]
    env.dm_line[h, z] = d_branch.astype(BF16)


def after_backward(h, reduce, env):
    rows = rows_of(h)
    reduce.finish(env.total)
    alpha = env.mix_row[0:1, :]
    mid, saved = mix(env.states[rows, :], env.branch[rows, :], alpha)
    d_state, d_branch, d_alpha = mix_back(env.d_mid[rows, :] + env.total[...], mid, saved, alpha)
    env.d_states[rows, :] = d_state
    env.gains[2:3, :] += d_alpha[None, :]
    env.d_both[place()[1], rows, :] = d_branch.astype(BF16)
    side_rows(h, env).start()


def spread_grads(b, env):
    rows = window(b * LANES, LANES)
    lane = lax.broadcasted_iota(jnp.int32, (LANES, LANES), 1)
    packed = env.datt_in[b].astype(F32)
    value = jnp.where(lane < HEAD, jnp.concatenate([packed, pltpu.roll(packed, HEAD, 1)], axis=0), 0.0)
    delta = -jnp.sum(value * env.attended[rows, :], axis=1, keepdims=True)
    high = delta.astype(BF16).astype(F32)
    env.do_ext[rows, :] = jnp.where(
        lane == HEAD, high, jnp.where(lane == HEAD + 1, delta - high, value)
    ).astype(BF16)


def attend_back_block(i, env, last):
    z, x, c, y = place()
    row = lax.broadcasted_iota(jnp.int32, (BLOCK, BLOCK), 0)
    col = lax.broadcasted_iota(jnp.int32, (BLOCK, BLOCK), 1)
    lane = lax.broadcasted_iota(jnp.int32, (LANES, LANES), 1)
    rows = pl.ds(i * BLOCK, BLOCK)
    q = env.q_ext[rows, :]
    do = env.do_ext[rows, :]
    dq = jnp.zeros((BLOCK, LANES), F32)
    for j in range(i + 1):
        keys = pl.ds(j * BLOCK, BLOCK)
        k = env.k_ext[keys, :]
        p = jnp.exp(dot_nt(k, q))
        if i == j:
            p = jnp.where(row <= col, p, 0.0)
        ds = (p * dot_nt(env.v_ext[keys, :], do)).astype(BF16)
        dv = dot(p.astype(BF16), do)
        dk = dot(ds, q)
        dq = dq + dot_tn(ds, k)
        if i == last:
            env.dk[keys, :] = dk
            env.dv[keys, :] = dv
        else:
            env.dk[keys, :] += dk
            env.dv[keys, :] += dv
    for n in range(2):
        part = slice(n * LANES, (n + 1) * LANES)
        b = 2 * i + n
        zz, sl = b // 4, b % 4
        tok = pl.ds(b * LANES, LANES)
        env.back_out[zz, sl, 0:LANES, :] = jnp.where(
            lane < HEAD, dq[part] * HEAD ** (-0.5), pltpu.roll(env.dk[tok, :], HEAD, 1)
        ).astype(BF16)
        env.back_out[zz, sl, LANES:, :] = side_by_side(env.dv[tok, :]).astype(BF16)
        mine = 2 * x + c

        @pl.when(sl == mine)
        def _():
            env.back_in[zz * 4 + mine] = env.back_out[zz, sl]

        @pl.when(sl != mine)
        def _():
            back_copy(zz, sl, mine, env).start()


def back_copy(zz, sl, source, env):
    z, x, c, y = place()
    return remote(
        env.back_out.at[zz, sl], env.back_in.at[zz * 4 + source], env.bs.at[zz, sl],
        env.br.at[zz * 4 + source], dev(z, sl // 2, sl % 2, y),
    )


def project_back(zz, env):
    z, x, c, y = place()
    mine = 2 * x + c
    cosine, sine = env.cosine[zz], env.sine[zz]
    lane = lax.broadcasted_iota(jnp.int32, (LANES, LANES), 1)
    values = []
    for sl in range(4):

        @pl.when(sl != mine)
        def _():
            back_copy(zz, sl, sl, env).wait()

        grad = env.back_in[zz * 4 + sl, 0:LANES, :].astype(F32)
        turned = env.turned[zz, sl]
        inverse = lax.rsqrt(head_means(turned * turned) + EPS)
        unit = turned * inverse
        env.gain_sum[sl : sl + 1, :] += jnp.sum(grad * unit, axis=0, keepdims=True)
        d_unit = grad * env.gain[sl : sl + 1, :]
        d_turned = inverse * (d_unit - unit * head_means(d_unit * unit))
        d_lin = d_turned * cosine - half_swap(d_turned) * sine
        env.d_lin[zz, :, sl * LANES : (sl + 1) * LANES] = d_lin.astype(BF16)
        packed = env.back_in[zz * 4 + sl, LANES:, :].astype(F32)
        values.append(jnp.concatenate([packed, pltpu.roll(packed, HEAD, 1)], axis=0))
    for p in range(2):
        pair = jnp.where(lane < HEAD, values[2 * p], pltpu.roll(values[2 * p + 1], HEAD, 1))
        env.d_lin[zz, :, (4 + p) * LANES : (5 + p) * LANES] = pair.astype(BF16)


def states_part(zz, env):
    d_x = dot(env.d_lin[zz], env.u_qkv[...])
    env.part[0, zz] = d_x[:64]
    env.part[1, zz] = d_x[64:]


def layer(env):
    z, x, c, y = place()
    s = z * 4 + x * 2 + c
    mine = 2 * x + c
    env.back_out, env.back_in = env.heads_out, env.heads_in
    env.g_out = env.u_out
    tables = []
    for zz in range(4):
        b = zz * 4 + 2 * x + c
        tables.append(pltpu.make_async_copy(env.cosines.at[b], env.cosine.at[zz], env.t_sem.at[zz, 0]))
        tables.append(pltpu.make_async_copy(env.sines.at[b], env.sine.at[zz], env.t_sem.at[zz, 1]))
    each(tables, "start")

    greet_row()
    env.x_line[z] = env.states[...].astype(BF16)
    qk_rows, v_rows = qkv_rows(mine)
    env.u_qkv[qk_rows, :] = jnp.concatenate(
        [unit_rows(env.w_query[...]), unit_rows(env.w_key[...])], axis=0
    )
    env.u_qkv[v_rows, :] = unit_rows(env.w_value[...])
    pl.semaphore_wait(pltpu.get_barrier_semaphore(), 16)
    line = Line(env.x_line, (env.x_send, env.x_recv))
    line.start()
    q_core, q_side, q_relay = qkv_groups(env)
    each(q_side, "start")
    each(q_core, "start")

    lane = lax.broadcasted_iota(jnp.int32, (1, LANES), 1)
    for pair in range(2):
        scale = env.qk_scale[window(z * 256 + pair * LANES, LANES)].reshape(1, LANES)
        turned = pltpu.roll(scale, HEAD, 1)
        env.gain[2 * pair : 2 * pair + 1, :] = jnp.where(lane < HEAD, scale, turned)
        env.gain[2 * pair + 1 : 2 * pair + 2, :] = jnp.where(lane < HEAD, turned, scale)
    env.up_row[...] = env.up_scale[window(z * 1024, 1024)].reshape(1, 1024)
    env.gate_row[...] = env.gate_scale[window(z * 1024, 1024)].reshape(1, 1024)
    env.mix_row[0:1, :] = env.alpha_attn[...].reshape(1, 1024)
    env.mix_row[1:2, :] = env.alpha_mlp[...].reshape(1, 1024)
    env.u_out[2 * z + c] = unit_rows(env.w_out[...])
    env.ups[mine] = unit_cols(env.w_up[...])
    env.gates[mine] = unit_cols(env.w_gate[...])
    env.downs[mine] = unit_rows(env.w_down[...])
    env.gains[...] = jnp.zeros_like(env.gains)
    env.gain_sum[...] = jnp.zeros_like(env.gain_sum)
    ff = ff_groups(env)
    each(ff[0], "start")
    each(tables, "wait")

    line.arrive(1)
    each(q_side, "wait_recv")
    each(q_relay, "start")
    each(q_core, "wait_recv")
    each(q_relay, "wait_recv")
    project_block(z, env)

    @pl.loop(1, 4)
    def _(k):
        @pl.when(k < 3)
        def _():
            line.arrive(k + 1)

        for way in (-1, 1):

            @pl.when(inside(z - way * k))
            def _():
                project_block(z - way * k, env)

    each(ff[1], "start")
    line.drain()
    for group in (q_side, q_core, q_relay):
        each(group, "wait_send")
    uo = Column(env.u_out, (env.o_z, env.o_c, env.o_r))
    uo.start()

    @pl.loop(0, 4)
    def _(zz):
        for i, (xx, cc) in enumerate(peers()):
            b = zz * 4 + xx * 2 + cc
            remote(
                env.heads_out.at[zz, xx * 2 + cc], env.heads_in.at[b], env.hs.at[zz, i], env.hr.at[b],
                dev(z, xx, cc, y),
            ).wait()

    @pl.loop(0, 16)
    def _(b):
        spread_heads(b, env)

    uo.arrive(1)
    for i in range(4):
        attend_block(i, env)
    for i in range(4, 6):
        attend_block(i, env)
    uo.arrive(2)
    for i in range(6, 8):
        attend_block(i, env)
    uo.arrive(3)
    uo.finish()
    ff[1][0].wait_recv()
    ff[2][0].start()
    ff[3][0].start()
    wait_blocks(env.att_out, env.att_in, env.as_, env.ar)
    lay_heads(env.att_in, env.att_low)

    weights = env.u_out[...].reshape(512, 1024)
    for h in range(2):
        env.mix_out[h] = dot(env.att_low[1 - x, rows_of(h), :], weights).astype(BF16)
        side_mix(h, env).start()
    env.branch[...] = dot(env.att_low[x], weights)
    ff[1][1].wait_recv()
    ff[2][1].start()
    ff[3][1].start()

    def mix_half(h):
        rows = rows_of(h)
        side_mix(h, env).wait_recv()
        branch = env.branch[rows, :] + env.mix_in[h].astype(F32)
        env.branch[rows, :] = branch
        mid, _ = mix(env.states[rows, :], branch, env.mix_row[0:1, :])
        env.mid[rows, :] = mid
        env.h_line[h, z] = mid.astype(BF16)

    fa = Line(env.h_line.at[0], (env.fa_s, env.fa_r))
    fb = Line(env.h_line.at[1], (env.fb_s, env.fb_r))
    ba = Line(env.dm_line.at[0], (env.ba_s, env.ba_r))
    bb = Line(env.dm_line.at[1], (env.bb_s, env.bb_r))

    def reduce(h, send, recv):
        return Reduce(
            lambda owner, rows: env.part[h, owner, rows], env.passing.at[h], env.landed.at[h], send, recv
        )

    r0, r1 = reduce(0, env.r0_s, env.r0_r), reduce(1, env.r1_s, env.r1_r)

    def arrive(gather, k):
        gather.arrive(k)

    def piece(grad, tag, cut):
        def view(slot, half):
            return grad.at[slot] if half is None else grad.at[slot, window(half * cut, cut), :]

        lc, ly, lx, out, send, recv = tag
        kind = Piece if ly.shape[1] == cut else SidePiece
        return kind(view, lc, ly, lx, lambda half: out.at[window(half * cut, cut), :], (send, recv), out)

    gu = piece(env.g_up, (env.lcu, env.lyu, env.lxu, env.ou, env.us, env.ur), 512)
    gg = piece(env.g_gate, (env.lcg, env.lyg, env.lxg, env.og, env.gs, env.gr), 512)
    gd = piece(env.g_down, (env.lcd, env.lyd, env.lxd, env.od, env.ds, env.dr), 128)
    mix_half(0)
    fa.start()
    mix_half(1)
    ff[1][2].wait_recv()
    ff[2][2].start()
    ff[3][2].start()
    arrive(fa, 1)
    arrive(fa, 2)
    fb.start()
    each(ff[3], "wait_recv")
    each(ff[4], "start")
    each(ff[0], "wait_recv")
    each(ff[2], "wait_recv")
    each(ff[4], "wait_recv")
    arrive(fa, 3)
    mlp_forward(0, env)
    r0.step(3)
    arrive(fb, 1)
    r0.step(2)
    arrive(fb, 2)
    r0.step(1)
    arrive(fb, 3)
    mlp_forward(1, env)
    r1.step(3)
    after_forward(0, r0, env)
    ba.start()
    r1.step(2)
    arrive(ba, 1)
    r1.step(1)
    arrive(ba, 2)
    after_forward(1, r1, env)
    bb.start()
    arrive(ba, 3)
    mlp_backward(0, env)
    r0.step(3)
    arrive(bb, 1)
    grad_down_half(0, env)
    r0.step(2)
    arrive(bb, 2)
    grad_wide_half(0, env.d_up, env.g_up, env)
    r0.step(1)
    grad_wide_half(0, env.d_gate, env.g_gate, env)
    arrive(bb, 3)
    grad_down_half(1, env)
    gd.start()
    mlp_backward(1, env)
    r1.step(3)
    gd.pass_twin()
    after_backward(0, r0, env)
    grad_wide_half(1, env.d_up, env.g_up, env)
    gu.start()
    r1.step(2)
    for gather in (fa, fb, ba, bb):
        gather.drain()
    for group in ff:
        each(group, "wait_send")
    for h in range(2):
        side_mix(h, env).wait_send()
    gu.pass_first()
    grad_wide_half(1, env.d_gate, env.g_gate, env)
    gg.start()
    r1.step(1)
    after_backward(1, r1, env)

    side_rows(0, env).wait_recv()
    send_grads(x, env)
    side_rows(1, env).wait_recv()
    send_grads(1 - x, env)
    gg.pass_twin()

    @pl.loop(0, 4)
    def _(n):
        cols = window(n * 256, 256)
        grad = dot_tn(env.att_low[0], env.d_both[0, :, cols]) + dot_tn(env.att_low[1], env.d_both[1, :, cols])
        env.g_out[:, :, cols] = grad.reshape(8, 64, 256).astype(BF16)

    out_reduce = RowReduce(env)
    out_reduce.start()
    gd.pass_side()
    out_reduce.pass_line()
    wait_grads(env)

    @pl.loop(0, 16, unroll=4)
    def _(b):
        spread_grads(b, env)

    gu.pass_back()
    out_reduce.step(3)
    attend_back_block(7, env, 7)
    gd.pass_back()
    out_reduce.step(2)
    attend_back_block(6, env, 7)
    out_reduce.step(1)
    for i in range(5, -1, -1):
        attend_back_block(i, env, 7)
    gg.pass_side()
    for h in range(2):
        side_rows(h, env).wait_send()
    project_back(3, env)
    out_reduce.to_twin()
    project_back(2, env)
    project_back(1, env)
    project_back(0, env)
    @pl.loop(0, 4)
    def _(n):
        cols = window(n * 256, 256)
        total = dot_tn(env.d_lin[...].reshape(512, 768), env.x_line[:, :, cols].reshape(512, 256))
        env.g_qkv[:, cols] = total.astype(BF16)

    def row_piece(which, tag, cut):
        def view(slot, half):
            start, size = (slot * LANES, LANES) if which == 0 else (4 * LANES + slot * HEAD, HEAD)
            if half is not None:
                start, size = start + half * cut, cut
            return env.g_qkv.at[window(start, size), :]

        lc, ly, lx, out, send, recv = tag
        kind = Piece if ly.shape[1] == cut else SidePiece
        return kind(
            view, lc, ly, lx, lambda half: out.at[window(half * cut, cut), :], (send, recv), out
        )

    gq = row_piece(0, (env.lcq, env.lyq, env.lxq, env.oq, env.qqs, env.qqr), 64)
    gv = row_piece(1, (env.lcv, env.lyv, env.lxv, env.ov, env.vvs, env.vvr), 32)
    gq.start()
    gv.start()

    @pl.loop(0, 4)
    def _(zz):
        states_part(zz, env)

    for h in range(2):
        (r0, r1)[h].step(3)
    gq.pass_first()
    gv.pass_twin()
    for sl in range(4):
        both_parts = env.gain_sum[sl : sl + 1, 0:HEAD] + env.gain_sum[sl : sl + 1, HEAD:]
        env.gains[4 + sl : 5 + sl, 0:HEAD] = both_parts
    small = [
        remote(env.gains, env.gain_land.at[i], env.sm_s.at[i], env.sm_r.at[i], device)
        for i, device in enumerate((dev(z, x, 1 - c, y), dev(z, 1 - x, c, y), dev(z, x, c, 1 - y)))
    ]
    def tell(k):
        t = (z + k) % 4
        return remote(
            env.gain_line.at[z], env.gain_line.at[z], env.gl_s.at[k], env.gl_r.at[z], dev(t, x, c, y)
        )

    small[0].start()
    r0.step(2)
    r1.step(2)
    gv.pass_side()
    small[0].wait()
    env.gains[...] += env.gain_land[0]
    small[1].start()
    gg.pass_back()
    finish_ff(env, gd, 2)
    small[1].wait()
    env.gains[...] += env.gain_land[1]
    small[2].start()
    r0.step(1)
    r1.step(1)
    gq.pass_back()
    gv.pass_back()
    finish_ff(env, gu, 0)
    small[2].wait()
    env.gain_line[z] = env.gains[...] + env.gain_land[2]
    for k in range(1, 4):
        tell(k).start()
    finish_ff(env, gg, 1)
    out_reduce.finish()
    unit_out = env.oo[...].astype(F32) + env.yo[...].astype(F32)
    env.gate_val[1, 3 * HEAD :, :] = pull_rows(env.w_out[...], unit_out)
    r0.finish(env.total)
    env.d_states[0:64, :] += env.total[...]
    r1.finish(env.total)
    env.d_states[64:, :] += env.total[...]
    gq.finish()
    gv.finish()
    stage = env.gate_val.at[1]
    total_qk = gq.total()
    stage[0:HEAD, :] = pull_rows(env.w_query[...], total_qk[0:HEAD])
    stage[HEAD : 2 * HEAD, :] = pull_rows(env.w_key[...], total_qk[HEAD:])
    stage[2 * HEAD : 3 * HEAD, :] = pull_rows(env.w_value[...], gv.total())
    results = [
        pltpu.make_async_copy(stage.at[pl.ds(i * HEAD, HEAD), :], ref, env.out_sem.at[3 + i])
        for i, ref in enumerate((env.grad_query, env.grad_key, env.grad_value, env.grad_out))
    ]
    each(results, "start")
    for k in range(1, 4):
        tell(k).wait_send()
        t = (z + k) % 4
        remote(
            env.gain_line.at[t], env.gain_line.at[t], env.gl_s.at[k], env.gl_r.at[t], dev(t, x, c, y)
        ).wait_recv()
    each(results, "wait")
    for i in range(3):
        ff_result(env, i).wait()


def pull_rows(weight, grad):
    wide = weight.astype(F32)
    inverse = lax.rsqrt(jnp.sum(wide * wide, axis=1, keepdims=True) + EPS)
    unit = wide * inverse
    return inverse * (grad - unit * jnp.sum(grad * unit, axis=1, keepdims=True))


def pull_cols(weight, grad):
    wide = weight.astype(F32)
    inverse = lax.rsqrt(jnp.sum(wide * wide, axis=0, keepdims=True) + EPS)
    unit = wide * inverse
    return inverse * (grad - unit * jnp.sum(grad * unit, axis=0, keepdims=True))


def ff_result(env, which):
    stage = (env.up_lin.at[0], env.up_lin.at[1], env.gate_val.at[0])[which]
    out = (env.grad_up, env.grad_gate, env.grad_down)[which]
    return pltpu.make_async_copy(stage, out, env.out_sem.at[which])


def finish_ff(env, piece, which):
    piece.finish()
    if which == 2:
        env.gate_val[0] = pull_rows(env.w_down[...], piece.total())
    elif which == 0:
        env.up_lin[0] = pull_cols(env.w_up[...], piece.total())
    else:
        env.up_lin[1] = pull_cols(env.w_gate[...], piece.total())
    ff_result(env, which).start()


class RowReduce:
    def __init__(self, env):
        self.env = env
        self.line = Reduce(self.part, env.o_pass, env.o_land, env.ol_s, env.ol_r)

    def part(self, owner, rows):
        return self.env.g_out[2 * owner + place()[2], rows].astype(F32)

    def to_core(self, zz):
        z, x, c, y = place()
        e = self.env
        return remote(
            e.g_out.at[2 * zz + 1 - c], e.o_c_land.at[zz], e.oc_s.at[zz], e.oc_r.at[zz], dev(z, x, 1 - c, y)
        )

    def twin(self):
        z, x, c, y = place()
        e = self.env
        return remote(e.oo, e.yo, e.oy_s, e.oy_r, dev(z, x, c, 1 - y))

    def start(self):
        @pl.loop(0, 4)
        def _(zz):
            self.to_core(zz).start()

    def pass_line(self):
        c = place()[2]
        e = self.env

        @pl.loop(0, 4)
        def _(zz):
            self.to_core(zz).wait_recv()
            b = 2 * zz + c
            e.g_out[b] = (e.g_out[b].astype(F32) + e.o_c_land[zz].astype(F32)).astype(BF16)

    def step(self, k):
        self.line.step(k)

    def to_twin(self):
        e = self.env
        self.line.finish(e.total)
        e.oo[...] = e.total[...].astype(BF16)
        self.twin().start()

    def finish(self):
        self.twin().wait()

        @pl.loop(0, 4)
        def _(zz):
            self.to_core(zz).wait_send()


DMA = pltpu.SemaphoreType.DMA


def v(shape, dtype=BF16):
    return pltpu.VMEM(shape, dtype)


LAYER_IN = tuple(
    dict(
        states=None,
        w_query=None,
        w_key=None,
        w_value=None,
        w_out=None,
        w_up=None,
        w_gate=None,
        w_down=None,
        qk_scale=None,
        up_scale=None,
        gate_scale=None,
        alpha_attn=None,
        alpha_mlp=None,
        d_out=None,
        cosines=None,
        sines=None,
    )
)
LAYER_OUT = dict(
    output=((128, 1024), F32), d_states=((128, 1024), F32), gain_line=((4, 8, 1024), F32),
    grad_query=((64, 1024), F32), grad_key=((64, 1024), F32), grad_value=((64, 1024), F32),
    grad_out=((64, 1024), F32), grad_up=((1024, 256), F32), grad_gate=((1024, 256), F32),
    grad_down=((256, 1024), F32),
)
IN_VMEM = 3
LAYER_TMP = dict(
    x_line=v((4, 128, 1024)), u_qkv=v((768, 1024)), u_out=v((8, 64, 1024)), mix_out=v((2, 64, 1024)), mix_in=v((2, 64, 1024)),
    turned=v((4, 4, 128, 128), F32), cosine=v((4, 128, 128), F32), sine=v((4, 128, 128), F32),
    gain=v((4, 128), F32), up_row=v((1, 1024), F32), gate_row=v((1, 1024), F32), mix_row=v((2, 1024), F32), gain_sum=v((4, 128), F32), gains=v((8, 1024), F32),
    gain_land=v((3, 8, 1024), F32),
    heads_out=v((4, 4, 192, 128)), heads_in=v((16, 192, 128)),
    q_ext=v((2048, 128)), k_ext=v((2048, 128)), v_ext=v((2048, 128)), attended=v((2048, 128), F32),
    att_out=v((16, 64, 128)), att_in=v((2, 8, 64, 128)), att_low=v((2, 128, 512)),
    ups=v((4, 1024, 256)), gates=v((4, 1024, 256)), downs=v((4, 256, 1024)),
    branch=v((128, 1024), F32), mid=v((128, 1024), F32), d_mid=v((128, 1024), F32),
    total=v((64, 1024), F32), d_both=v((2, 128, 1024)),
    h_line=v((2, 4, 64, 1024)), dm_line=v((2, 4, 64, 1024)),
    up_lin=v((2, 1024, 256), F32), gate_val=v((2, 256, 1024), F32), hidden=v((2, 256, 1024)),
    d_up=v((2, 4, 256, 256)), d_gate=v((2, 4, 256, 256)),
    part=v((2, 4, 64, 1024), F32), passing=v((2, 4, 64, 1024)), landed=v((2, 5, 64, 1024)),
    g_up=v((4, 1024, 256)), g_gate=v((4, 1024, 256)), g_down=v((4, 256, 1024)), g_qkv=v((768, 1024)),
    lcu=v((2, 1024, 256)), lcg=v((2, 1024, 256)), lcd=v((2, 256, 1024)), lcq=v((2, 128, 1024)),
    lcv=v((2, 64, 1024)),
    lyu=v((1, 1024, 256)), lyg=v((2, 512, 256)), lyd=v((2, 128, 1024)), lyq=v((1, 128, 1024)), lyv=v((2, 32, 1024)),
    lxu=v((1024, 256)), lxg=v((512, 256)), lxd=v((128, 1024)), lxq=v((128, 1024)), lxv=v((32, 1024)),
    ou=v((1024, 256)), og=v((1024, 256)), od=v((256, 1024)), oq=v((128, 1024)), ov=v((64, 1024)),
    oo=v((64, 1024)), yo=v((64, 1024)), out_sem=DMA((7,)),
    o_c_land=v((4, 64, 1024)), o_pass=v((4, 64, 1024)),
    o_land=v((5, 64, 1024)),
    datt_out=v((2, 8, 64, 128)), datt_in=v((16, 64, 128)), do_ext=v((2048, 128)),
    dk=v((2048, 128), F32), dv=v((2048, 128), F32),
    d_lin=v((4, 128, 768)),
    t_sem=DMA((4, 2)), x_send=DMA((4, 2, SUBS)), x_recv=DMA((4, SUBS)), q_send=DMA((3, 2)), q_recv=DMA((3, 2)),
    w_send=DMA((5, 3)), w_recv=DMA((5, 3)), hs=DMA((4, 3)), hr=DMA((16,)),
    o_z=DMA((4, 2)), o_c=DMA((4,)), o_r=DMA((8,)),
    as_=DMA((16,)), ar=DMA((2, 8)), das=DMA((2, 8)), dar=DMA((16,)),
    mx_s=DMA((2,)), mx_r=DMA((2,)), db_s=DMA((2,)), db_r=DMA((2,)),
    fa_s=DMA((4, 2, SUBS)), fa_r=DMA((4, SUBS)), fb_s=DMA((4, 2, SUBS)), fb_r=DMA((4, SUBS)),
    ba_s=DMA((4, 2, SUBS)), ba_r=DMA((4, SUBS)), bb_s=DMA((4, 2, SUBS)), bb_r=DMA((4, SUBS)),
    r0_s=DMA((4, SUBS)), r0_r=DMA((5, SUBS)), r1_s=DMA((4, SUBS)), r1_r=DMA((5, SUBS)),
    us=DMA((6,)), ur=DMA((6,)), gs=DMA((6,)), gr=DMA((6,)), ds=DMA((6,)), dr=DMA((6,)),
    qqs=DMA((6,)), qqr=DMA((6,)), vvs=DMA((6,)), vvr=DMA((6,)),
    oc_s=DMA((4,)), oc_r=DMA((4,)),
    ol_s=DMA((4, SUBS)), ol_r=DMA((5, SUBS)), oy_s=DMA, oy_r=DMA,
    bs=DMA((4, 4)), br=DMA((16,)), sm_s=DMA((3,)), sm_r=DMA((3,)), gl_s=DMA((4,)), gl_r=DMA((4,)),
)


def run_layer(*args):
    vmem = pl.BlockSpec(memory_space=pltpu.VMEM)
    names = LAYER_IN + tuple(LAYER_OUT) + tuple(LAYER_TMP)

    def kernel(*refs):
        layer(Env(names, refs))

    outs = pl.pallas_call(
        kernel,
        name="layer",
        out_shape=tuple(jax.ShapeDtypeStruct(*o) for o in LAYER_OUT.values()),
        in_specs=[vmem] * (len(LAYER_IN) - 2) + [pl.BlockSpec(memory_space=pl.ANY)] * 2,
        out_specs=(vmem,) * IN_VMEM
        + (pl.BlockSpec(memory_space=pl.ANY),) * (len(LAYER_OUT) - IN_VMEM),
        scratch_shapes=list(LAYER_TMP.values()),
        compiler_params=pltpu.CompilerParams(
            collective_id=1, has_side_effects=True, vmem_limit_bytes=62 * MIB
        ),
    )(*args)
    return dict(zip(LAYER_OUT, outs))


HANDED = tuple(name for name in LAYER_OUT if name != "gain_line")


def hand_over_kernel(*refs):
    count = len(HANDED)
    line = refs[count]
    outs = refs[count + 1 : 2 * count + 6]
    held = refs[2 * count + 6 : 3 * count + 6]
    arrive, leave = refs[3 * count + 6 :]
    loads = [pltpu.make_async_copy(refs[i], held[i], arrive.at[i]) for i in range(count)]
    stores = [pltpu.make_async_copy(held[i], outs[i], leave.at[i]) for i in range(count)]
    each(loads, "start")
    qk, up, gate, attn, mlp = outs[count:]
    lane = lax.broadcasted_iota(jnp.int32, (1, LANES), 1)
    for zz in range(4):
        cols = slice(zz * 1024, (zz + 1) * 1024)
        up[cols] = line[zz, 0:1, :].reshape(1024)
        gate[cols] = line[zz, 1:2, :].reshape(1024)
        for pair in range(2):
            first = line[zz, 4 + 2 * pair : 5 + 2 * pair, 0:LANES]
            second = pltpu.roll(line[zz, 5 + 2 * pair : 6 + 2 * pair, 0:LANES], HEAD, 1)
            both = jnp.where(lane < HEAD, first, second)
            qk[zz * 256 + pair * LANES : zz * 256 + (pair + 1) * LANES] = both.reshape(LANES)
    for row, out in ((2, attn), (3, mlp)):
        parts = [line[zz, row : row + 1, :] for zz in range(4)]
        out[...] = (parts[0] + parts[1] + parts[2] + parts[3]).reshape(1024)
    for load, store in zip(loads, stores):
        load.wait()
        store.start()
    each(stores, "wait")


def hand_over(*arrays):
    vmem, hbm = pl.BlockSpec(memory_space=pltpu.VMEM), pl.BlockSpec(memory_space=pl.ANY)
    count = len(HANDED)
    sizes = (1024, 4096, 4096, 1024, 1024)
    return pl.pallas_call(
        hand_over_kernel,
        name="hand_over",
        out_shape=tuple(jax.ShapeDtypeStruct(a.shape, a.dtype) for a in arrays[:count])
        + tuple(jax.ShapeDtypeStruct((n,), F32) for n in sizes),
        in_specs=[hbm] * count + [vmem],
        out_specs=(hbm,) * count + (vmem,) * len(sizes),
        scratch_shapes=[v(a.shape, a.dtype) for a in arrays[:count]] + [DMA((count,))] * 2,
        compiler_params=pltpu.CompilerParams(vmem_limit_bytes=60 * MIB),
    )(*arrays)


def on_device_heads(
    states,
    lengths,
    w_query,
    w_key,
    w_value,
    w_out,
    w_up,
    w_gate,
    w_down,
    qk_scale,
    up_scale,
    gate_scale,
    alpha_attn,
    alpha_mlp,
    d_out,
):
    tok, width = states.shape[1:]
    cosine, sine = turn_tables(16 * tok)
    got = run_layer(
        states.reshape(tok, width), w_query.T, w_key.T, w_value.T, w_out, w_up, w_gate, w_down,
        qk_scale, up_scale, gate_scale, alpha_attn, alpha_mlp, d_out.reshape(tok, width),
        jnp.asarray(cosine.reshape(16, tok, LANES)), jnp.asarray(sine.reshape(16, tok, LANES)),
    )

    output, d_states, g_query, g_key, g_value, g_out, g_up, g_gate, g_down, *gains = hand_over(
        *(got[name] for name in HANDED), got["gain_line"]
    )
    return (
        output.reshape(states.shape),
        d_states.reshape(states.shape),
        g_query.T,
        g_key.T,
        g_value.T,
        g_out,
        g_up,
        g_gate,
        g_down,
        *gains,
    )


def solution(mesh):
    seq, batch = mesh.shape["seq"], mesh.shape["batch"]
    body = on_device_heads if (seq == HEADS and batch == 2) else on_device_general
    return jax.shard_map(
        body,
        mesh=mesh,
        in_specs=(
            P("batch", "seq", None),
            P("batch", None),
            P(None, "seq"),
            P(None, "seq"),
            P(None, "seq"),
            P("seq", None),
            P(None, "seq"),
            P(None, "seq"),
            P("seq", None),
            P(),
            P(),
            P(),
            P(),
            P(),
            P("batch", "seq", None),
        ),
        out_specs=(
            P("batch", "seq", None),
            P("batch", "seq", None),
            P(None, "seq"),
            P(None, "seq"),
            P(None, "seq"),
            P("seq", None),
            P(None, "seq"),
            P(None, "seq"),
            P("seq", None),
            P(),
            P(),
            P(),
            P(),
            P(),
        ),
        check_vma=False,
    )
```

```python
import jax
import jax.numpy as jnp
import numpy as np
from jax import lax
from jax.experimental import pallas as pl
from jax.experimental.pallas import tpu as pltpu
from jax.sharding import PartitionSpec as P

HEADS = 16
HEAD = 64


EPS = 1e-06


def shifted(value, axis, steps):
    count = lax.axis_size(axis)
    first, last = (max(0, -steps), min(count, count - steps))
    return lax.ppermute(value, axis, [(source, source + steps) for source in range(first, last)])


def shifted_2(block, axis, distance):
    devices = range(lax.axis_size(axis))
    route = [((i - distance) % len(devices), i) for i in devices]
    return lax.ppermute(block, axis, route)


def normalized(weight, axis):
    wide = weight.astype(jnp.float32)
    return wide * lax.rsqrt(jnp.sum(wide * wide, axis=axis, keepdims=True) + EPS)


def rms(values):
    return values * lax.rsqrt(jnp.mean(values * values, axis=-1, keepdims=True) + EPS)


def doc_layout(len_row, tok_index):
    docs = jnp.arange(len_row.shape[0])
    starts = jnp.sum(jnp.where(docs[:, None] < docs[None, :], len_row[:, None], 0), axis=0)
    started = starts[None, :] <= tok_index[:, None]
    doc_ids = jnp.sum(started.astype(jnp.int32), axis=1) - 1
    first_tok = jnp.max(jnp.where(started, starts[None, :], 0), axis=1)
    return (doc_ids, tok_index - first_tok)


def rope(values, position):
    half = values.shape[-1] // 2
    freqs = 10000.0 ** (-jnp.arange(half, dtype=jnp.float32) / half)
    angle = position.astype(jnp.float32)[:, None] * freqs[None, :]
    cosine = jnp.cos(angle)[:, None, :]
    sine = jnp.sin(angle)[:, None, :]
    first = values[..., :half]
    second = values[..., half:]
    return jnp.concatenate(
        [first * cosine - second * sine, first * sine + second * cosine], axis=-1
    )


def prepare(linear, position, gain):
    count = linear.shape[0]
    shaped = linear.reshape(count, HEADS, HEAD)
    turned = rms(rope(shaped, position)) * gain.reshape(HEADS, HEAD)
    return turned.reshape(count, HEADS * HEAD)


def residual_mix(state, branch, alpha):
    return rms(state + alpha * (rms(branch) - state))


def gating(up_lin, gate_lin, up_scale, gate_scale):
    return up_scale * up_lin * jax.nn.silu(gate_scale * gate_lin)


def unit_back(raw_shard, grad_shard, axis):
    primal, pullback = jax.vjp(
        lambda weight: normalized(weight, axis), raw_shard.astype(jnp.float32)
    )
    return pullback(grad_shard)[0]


def on_device_general(
    states,
    lengths,
    w_query,
    w_key,
    w_value,
    w_out,
    w_up,
    w_gate,
    w_down,
    qk_scale,
    up_scale,
    gate_scale,
    alpha_attn,
    alpha_mlp,
    d_out,
):
    seq_count = lax.axis_size("seq")
    my_index = lax.axis_index("seq")
    rows = states.shape[0]
    tok = states.shape[1]
    width = states.shape[2]
    flat = rows * tok
    score_scale = HEAD ** (-0.5)
    row_layout = jax.vmap(doc_layout, in_axes=(0, None))
    unit_query = normalized(w_query, 0).astype(jnp.bfloat16)
    unit_key = normalized(w_key, 0).astype(jnp.bfloat16)
    unit_value = normalized(w_value, 0).astype(jnp.bfloat16)
    unit_out = normalized(w_out, 1).astype(jnp.bfloat16)
    unit_up = normalized(w_up, 0).astype(jnp.bfloat16)
    unit_gate = normalized(w_gate, 0).astype(jnp.bfloat16)
    unit_down = normalized(w_down, 1).astype(jnp.bfloat16)
    full_weights = (
        lax.all_gather(unit_query, "seq", axis=1, tiled=True),
        lax.all_gather(unit_key, "seq", axis=1, tiled=True),
        lax.all_gather(unit_value, "seq", axis=1, tiled=True),
        lax.all_gather(unit_out, "seq", axis=0, tiled=True),
        lax.all_gather(unit_up, "seq", axis=1, tiled=True),
        lax.all_gather(unit_gate, "seq", axis=1, tiled=True),
        lax.all_gather(unit_down, "seq", axis=0, tiled=True),
    )
    full_query, full_key, full_value, full_out, full_up, full_gate, full_down = full_weights
    tok_index = my_index * tok + jnp.arange(tok, dtype=jnp.int32)
    doc_ids, position = row_layout(lengths, tok_index)
    flat_pos = position.reshape(flat)
    state_in = states.reshape(flat, width)
    x_low = state_in.astype(jnp.bfloat16)
    query_lin = jnp.dot(x_low, full_query, preferred_element_type=jnp.float32)
    key_lin = jnp.dot(x_low, full_key, preferred_element_type=jnp.float32)
    value_lin = jnp.dot(x_low, full_value, preferred_element_type=jnp.float32)

    def front(query_part, key_part, gain):
        return (prepare(query_part, flat_pos, gain), prepare(key_part, flat_pos, gain))

    query_f, key_f = front(query_lin, key_lin, qk_scale)
    query_h = query_f.astype(jnp.bfloat16).reshape(rows, tok, HEADS, HEAD)
    key_h = key_f.astype(jnp.bfloat16).reshape(rows, tok, HEADS, HEAD)
    value_h = value_lin.astype(jnp.bfloat16).reshape(rows, tok, HEADS, HEAD)

    def block_scores(key_blk, source):
        key_index = source * tok + jnp.arange(tok, dtype=jnp.int32)
        key_docs, key_pos = row_layout(lengths, key_index)
        scores = (
            jnp.einsum("bqhd,bkhd->bqhk", query_h, key_blk, preferred_element_type=jnp.float32)
            * score_scale
        )
        allowed = (doc_ids[:, :, None] == key_docs[:, None, :]) & (
            key_index[None, None, :] <= tok_index[None, :, None]
        )
        return (scores, allowed[:, :, None, :])

    def is_active(source):
        last_key = jnp.reshape(source * tok + tok - 1, (1,))
        last_doc, last_pos = row_layout(lengths, last_key)
        return (source <= my_index) & jnp.any(last_doc[:, 0] >= doc_ids[:, 0])

    def attend(running, key_blk, value_blk, source):

        def compute(carried):
            best, denom_sum, accum = carried
            scores, allowed = block_scores(key_blk, source)
            new_best = jnp.maximum(best, jnp.max(jnp.where(allowed, scores, -1e30), axis=3))
            weights = jnp.where(allowed, jnp.exp(scores - new_best[:, :, :, None]), 0.0)
            shrink = jnp.exp(best - new_best)
            denom_sum = denom_sum * shrink + jnp.sum(weights, axis=3)
            accum = accum * shrink[:, :, :, None] + jnp.einsum(
                "bqhk,bkhd->bqhd",
                weights.astype(jnp.bfloat16),
                value_blk,
                preferred_element_type=jnp.float32,
            )
            return (new_best, denom_sum, accum)

        return lax.cond(is_active(source), compute, lambda carried: carried, running)

    reach = seq_count - 1
    start_state = (
        jnp.full((rows, tok, HEADS), -1e30, jnp.float32),
        jnp.zeros((rows, tok, HEADS), jnp.float32),
        jnp.zeros((rows, tok, HEADS, HEAD), jnp.float32),
    )
    first_state = attend(start_state, key_h, value_h, my_index)

    def cycle_step(step, loop_carry):
        running, key_blk, value_blk = loop_carry
        key_blk, value_blk = shifted((key_blk, value_blk), "seq", 1)
        source = (my_index - step) % seq_count
        return (attend(running, key_blk, value_blk, source), key_blk, value_blk)

    final_state, spent_key, spent_value = lax.fori_loop(
        1, reach + 1, cycle_step, (first_state, key_h, value_h)
    )
    best, denom_sum, accum = final_state
    attended = accum / denom_sum[:, :, :, None]
    log_sum = best + jnp.log(denom_sum)
    attended_low = attended.astype(jnp.bfloat16).reshape(flat, width)
    attn_branch = jnp.dot(attended_low, full_out, preferred_element_type=jnp.float32)
    state_mid = residual_mix(state_in, attn_branch, alpha_attn)
    mid_low = state_mid.astype(jnp.bfloat16)
    up_lin = jnp.dot(mid_low, full_up, preferred_element_type=jnp.float32)
    gate_lin = jnp.dot(mid_low, full_gate, preferred_element_type=jnp.float32)
    gated_low = gating(up_lin, gate_lin, up_scale, gate_scale).astype(jnp.bfloat16)
    mlp_branch = jnp.dot(gated_low, full_down, preferred_element_type=jnp.float32)
    output = residual_mix(state_mid, mlp_branch, alpha_mlp)
    back_weights = (
        lax.all_gather(unit_query, "seq", axis=1, tiled=True),
        lax.all_gather(unit_key, "seq", axis=1, tiled=True),
        lax.all_gather(unit_value, "seq", axis=1, tiled=True),
        lax.all_gather(unit_out, "seq", axis=0, tiled=True),
        lax.all_gather(unit_up, "seq", axis=1, tiled=True),
        lax.all_gather(unit_gate, "seq", axis=1, tiled=True),
        lax.all_gather(unit_down, "seq", axis=0, tiled=True),
    )
    back_query, back_key, back_value, back_out, back_up, back_gate, back_down = back_weights
    primal, pull_mlp = jax.vjp(residual_mix, state_mid, mlp_branch, alpha_mlp)
    d_mid, d_mlp, g_alpha_mlp = pull_mlp(d_out.reshape(flat, width))
    d_mlp_low = d_mlp.astype(jnp.bfloat16)
    grad_down = jnp.einsum("tf,td->fd", gated_low, d_mlp_low, preferred_element_type=jnp.float32)
    d_gated = jnp.einsum("td,fd->tf", d_mlp_low, back_down, preferred_element_type=jnp.float32)
    primal, pull_gate = jax.vjp(gating, up_lin, gate_lin, up_scale, gate_scale)
    d_up, d_gate, g_up_scale, g_gate_scale = pull_gate(d_gated)
    d_up_low = d_up.astype(jnp.bfloat16)
    d_gate_low = d_gate.astype(jnp.bfloat16)
    grad_up = jnp.einsum("tc,tf->cf", mid_low, d_up_low, preferred_element_type=jnp.float32)
    grad_gate = jnp.einsum("tc,tf->cf", mid_low, d_gate_low, preferred_element_type=jnp.float32)
    d_mid = d_mid + jnp.einsum("tf,cf->tc", d_up_low, back_up, preferred_element_type=jnp.float32)
    d_mid = d_mid + jnp.einsum(
        "tf,cf->tc", d_gate_low, back_gate, preferred_element_type=jnp.float32
    )
    primal, pull_attn = jax.vjp(residual_mix, state_in, attn_branch, alpha_attn)
    d_state, d_attn, g_alpha_attn = pull_attn(d_mid)
    d_attn_low = d_attn.astype(jnp.bfloat16)
    grad_out = jnp.einsum("tc,td->cd", attended_low, d_attn_low, preferred_element_type=jnp.float32)
    d_attended = jnp.einsum("td,cd->tc", d_attn_low, back_out, preferred_element_type=jnp.float32)
    d_att_low = d_attended.astype(jnp.bfloat16).reshape(rows, tok, HEADS, HEAD)
    delta = jnp.sum(d_att_low.astype(jnp.float32) * attended, axis=3)

    def attend_back(d_query, key_blk, value_blk, d_key, d_value, source):

        def compute(carried):
            d_query, d_key, d_value = carried
            scores, allowed = block_scores(key_blk, source)
            probs = jnp.where(allowed, jnp.exp(scores - log_sum[:, :, :, None]), 0.0)
            d_probs = jnp.einsum(
                "bqhd,bkhd->bqhk", d_att_low, value_blk, preferred_element_type=jnp.float32
            )
            d_scores = (probs * (d_probs - delta[:, :, :, None])).astype(jnp.bfloat16)
            d_query = d_query + jnp.einsum(
                "bqhk,bkhd->bqhd", d_scores, key_blk, preferred_element_type=jnp.float32
            )
            d_key = d_key + jnp.einsum(
                "bqhk,bqhd->bkhd", d_scores, query_h, preferred_element_type=jnp.float32
            )
            d_value = d_value + jnp.einsum(
                "bqhk,bqhd->bkhd",
                probs.astype(jnp.bfloat16),
                d_att_low,
                preferred_element_type=jnp.float32,
            )
            return (d_query, d_key, d_value)

        return lax.cond(
            is_active(source), compute, lambda carried: carried, (d_query, d_key, d_value)
        )

    def back_step(step, loop_carry):
        d_query, key_blk, value_blk, d_key, d_value = loop_carry
        source = (my_index - step) % seq_count
        d_query, d_key, d_value = attend_back(d_query, key_blk, value_blk, d_key, d_value, source)
        d_key, d_value = (
            shifted_2(d_key.astype(jnp.bfloat16), "seq", 1).astype(d_key.dtype),
            shifted_2(d_value.astype(jnp.bfloat16), "seq", 1).astype(d_value.dtype),
        )
        key_blk, value_blk = shifted((key_blk, value_blk), "seq", 1)
        return (d_query, key_blk, value_blk, d_key, d_value)

    zero_heads = jnp.zeros((rows, tok, HEADS, HEAD), jnp.float32)
    d_query_h, last_key_blk, last_value_blk, d_key_h, d_value_h = lax.fori_loop(
        0, reach, back_step, (zero_heads, key_h, value_h, zero_heads, zero_heads)
    )
    d_query_h, d_key_h, d_value_h = attend_back(
        d_query_h, last_key_blk, last_value_blk, d_key_h, d_value_h, (my_index - reach) % seq_count
    )
    d_key_h, d_value_h = (
        shifted_2(d_key_h.astype(jnp.bfloat16), "seq", -reach).astype(d_key_h.dtype),
        shifted_2(d_value_h.astype(jnp.bfloat16), "seq", -reach).astype(d_value_h.dtype),
    )
    primal, pull_front = jax.vjp(front, query_lin, key_lin, qk_scale)
    d_query_lin, d_key_lin, g_qk_scale = pull_front(
        (d_query_h.reshape(flat, width) * score_scale, d_key_h.reshape(flat, width) * score_scale)
    )
    d_query_low = d_query_lin.astype(jnp.bfloat16)
    d_key_low = d_key_lin.astype(jnp.bfloat16)
    d_value_low = d_value_h.reshape(flat, width).astype(jnp.bfloat16)
    grad_query = jnp.einsum("tc,tj->cj", x_low, d_query_low, preferred_element_type=jnp.float32)
    grad_key = jnp.einsum("tc,tj->cj", x_low, d_key_low, preferred_element_type=jnp.float32)
    grad_value = jnp.einsum("tc,tj->cj", x_low, d_value_low, preferred_element_type=jnp.float32)
    d_state = d_state + jnp.einsum(
        "tj,cj->tc", d_query_low, back_query, preferred_element_type=jnp.float32
    )
    d_state = d_state + jnp.einsum(
        "tj,cj->tc", d_key_low, back_key, preferred_element_type=jnp.float32
    )
    d_state = d_state + jnp.einsum(
        "tj,cj->tc", d_value_low, back_value, preferred_element_type=jnp.float32
    )
    shards = (
        lax.psum_scatter(
            grad_query.astype(jnp.bfloat16), "seq", scatter_dimension=1, tiled=True
        ).astype(jnp.float32),
        lax.psum_scatter(
            grad_key.astype(jnp.bfloat16), "seq", scatter_dimension=1, tiled=True
        ).astype(jnp.float32),
        lax.psum_scatter(
            grad_value.astype(jnp.bfloat16), "seq", scatter_dimension=1, tiled=True
        ).astype(jnp.float32),
        lax.psum_scatter(
            grad_out.astype(jnp.bfloat16), "seq", scatter_dimension=0, tiled=True
        ).astype(jnp.float32),
        lax.psum_scatter(
            grad_up.astype(jnp.bfloat16), "seq", scatter_dimension=1, tiled=True
        ).astype(jnp.float32),
        lax.psum_scatter(
            grad_gate.astype(jnp.bfloat16), "seq", scatter_dimension=1, tiled=True
        ).astype(jnp.float32),
        lax.psum_scatter(
            grad_down.astype(jnp.bfloat16), "seq", scatter_dimension=0, tiled=True
        ).astype(jnp.float32),
    )
    summed = (
        lax.psum(shards[0].astype(jnp.bfloat16), "batch").astype(jnp.float32),
        lax.psum(shards[1].astype(jnp.bfloat16), "batch").astype(jnp.float32),
        lax.psum(shards[2].astype(jnp.bfloat16), "batch").astype(jnp.float32),
        lax.psum(shards[3].astype(jnp.bfloat16), "batch").astype(jnp.float32),
        lax.psum(shards[4].astype(jnp.bfloat16), "batch").astype(jnp.float32),
        lax.psum(shards[5].astype(jnp.bfloat16), "batch").astype(jnp.float32),
        lax.psum(shards[6].astype(jnp.bfloat16), "batch").astype(jnp.float32),
    )
    gain_grads = lax.psum(
        (g_qk_scale, g_up_scale, g_gate_scale, g_alpha_attn, g_alpha_mlp), ("seq", "batch")
    )
    g_query = unit_back(w_query, summed[0], 0)
    g_key = unit_back(w_key, summed[1], 0)
    g_value = unit_back(w_value, summed[2], 0)
    g_out = unit_back(w_out, summed[3], 1)
    g_up = unit_back(w_up, summed[4], 0)
    g_gate = unit_back(w_gate, summed[5], 0)
    g_down = unit_back(w_down, summed[6], 1)
    return (
        output.reshape(rows, tok, width),
        d_state.reshape(rows, tok, width),
        g_query,
        g_key,
        g_value,
        g_out,
        g_up,
        g_gate,
        g_down,
        gain_grads[0],
        gain_grads[1],
        gain_grads[2],
        gain_grads[3],
        gain_grads[4],
    )


BF16 = jnp.bfloat16
F32 = jnp.float32
LANES = 128
MIB = 1 << 20
NT = (((1,), (1,)), ((), ()))
TN = (((0,), (0,)), ((), ()))


def place():
    s = lax.axis_index("seq")
    return s // 4, (s // 2) % 2, s % 2, lax.axis_index("batch")


def dev(z, x, c, y):
    return (z * 4 + x * 2 + c, y)


def remote(src, dst, send, recv, device):
    return pltpu.make_async_remote_copy(
        src_ref=src,
        dst_ref=dst,
        send_sem=send,
        recv_sem=recv,
        device_id=device,
        device_id_type=pl.DeviceIdType.MESH,
    )


def dot(a, b):
    return jnp.dot(a, b, preferred_element_type=F32)


def dot_nt(a, b):
    return lax.dot_general(a, b, NT, preferred_element_type=F32)


def dot_tn(a, b):
    return lax.dot_general(a, b, TN, preferred_element_type=F32)


BLOCK = 256


def inverse_norm(weight, axis):
    wide = weight.astype(F32)
    return lax.rsqrt(jnp.sum(wide * wide, axis=axis, keepdims=True) + EPS)


def unit_pull(weight, grad, axis):
    inverse = inverse_norm(weight, axis)
    unit = weight.astype(F32) * inverse
    return inverse * (grad - unit * jnp.sum(grad * unit, axis=axis, keepdims=True))


def turn_tables(count):
    half = HEAD // 2
    freqs = (10000.0 ** (-np.arange(half, dtype=np.float32) / half)).astype(np.float32)
    angle = np.arange(count, dtype=np.float32)[:, None] * freqs[None, :]
    cosine = np.cos(angle).astype(np.float32)
    sine = np.sin(angle).astype(np.float32)
    return np.tile(cosine, (1, 4)), np.concatenate([-sine, sine, -sine, sine], axis=1)


def mix(state, branch, alpha):
    inv_b = lax.rsqrt(jnp.mean(branch * branch, axis=-1, keepdims=True) + EPS)
    unit_b = branch * inv_b
    step = unit_b - state
    mixed = state + alpha * step
    inv_m = lax.rsqrt(jnp.mean(mixed * mixed, axis=-1, keepdims=True) + EPS)
    return mixed * inv_m, (unit_b, inv_b, step, inv_m)


def mix_back(grad, out, saved, alpha):
    unit_b, inv_b, step, inv_m = saved
    d_mixed = inv_m * (grad - out * jnp.mean(grad * out, axis=-1, keepdims=True))
    d_alpha = jnp.sum(d_mixed * step, axis=0)
    d_unit = d_mixed * alpha
    d_branch = inv_b * (d_unit - unit_b * jnp.mean(d_unit * unit_b, axis=-1, keepdims=True))
    return d_mixed - d_unit, d_branch, d_alpha


def inside(v):
    return (v >= 0) & (v < 4)


def unit_cols(w):
    wide = w.astype(F32)
    return (wide * lax.rsqrt(jnp.sum(wide * wide, axis=0, keepdims=True) + EPS)).astype(BF16)


def unit_rows(w):
    wide = w.astype(F32)
    return (wide * lax.rsqrt(jnp.sum(wide * wide, axis=1, keepdims=True) + EPS)).astype(BF16)


SUBS = 2


class Line:
    def __init__(self, buf, sems):
        self.buf, (self.send, self.recv) = buf, sems

    def hop(self, zz, way, n):
        z, x, c, y = place()
        size = self.buf.shape[1] // SUBS
        b = self.buf.at[zz, n * size : (n + 1) * size]
        return remote(
            b, b, self.send.at[zz, (way + 1) // 2, n], self.recv.at[zz, n], dev(z + way, x, c, y)
        )

    def start(self):
        z = place()[0]
        for n in range(SUBS):
            for way in (-1, 1):

                @pl.when(inside(z + way))
                def _():
                    self.hop(z, way, n).start()

    def arrive(self, k):
        z = place()[0]
        for n in range(SUBS):
            for way in (-1, 1):
                zz = z - way * k

                @pl.when(inside(zz))
                def _():
                    self.hop(zz, -way, n).wait_recv()

                    @pl.when(inside(z + way))
                    def _():
                        self.hop(zz, way, n).start()

    def drain(self):
        z = place()[0]
        for zz in range(4):
            for way in (-1, 1):

                @pl.when(((zz - z) * way <= 0) & inside(z + way))
                def _():
                    for n in range(SUBS):
                        self.hop(zz, way, n).wait_send()


class Column:
    def __init__(self, buf, sems):
        self.buf, (self.zs, self.cs, self.recv) = buf, sems

    def hop_z(self, zz, way):
        z, x, c, y = place()
        b = 2 * zz + c
        return remote(
            self.buf.at[b], self.buf.at[b], self.zs.at[zz, (way + 1) // 2], self.recv.at[b],
            dev(z + way, x, c, y),
        )

    def hop_c(self, zz):
        z, x, c, y = place()
        b = 2 * zz + c
        return remote(
            self.buf.at[b], self.buf.at[b], self.cs.at[zz], self.recv.at[b], dev(z, x, 1 - c, y)
        )

    def arrived(self, b):
        z, x, c, y = place()
        remote(
            self.buf.at[b], self.buf.at[b], self.cs.at[0], self.recv.at[b], dev(z, x, 1 - c, y)
        ).wait_recv()

    def start(self):
        z = place()[0]
        for way in (-1, 1):

            @pl.when(inside(z + way))
            def _():
                self.hop_z(z, way).start()

        self.hop_c(z).start()

    def arrive(self, k):
        z, x, c, y = place()
        for way in (-1, 1):
            zz = z - way * k

            @pl.when(inside(zz))
            def _():
                self.arrived(2 * zz + c)

                @pl.when(inside(z + way))
                def _():
                    self.hop_z(zz, way).start()

                self.hop_c(zz).start()

    def finish(self):
        z, x, c, y = place()

        @pl.loop(0, 4)
        def _(zz):
            self.arrived(2 * zz + 1 - c)
            for way in (-1, 1):

                @pl.when(((zz - z) * way <= 0) & inside(z + way))
                def _():
                    self.hop_z(zz, way).wait_send()

            self.hop_c(zz).wait_send()


def greet_row():
    z, x, c, y = place()
    s = z * 4 + x * 2 + c
    bar = pltpu.get_barrier_semaphore()

    @pl.loop(1, 16)
    def _(k):
        pl.semaphore_signal(
            bar, inc=1, device_id=((s + k) % 16, y), device_id_type=pl.DeviceIdType.MESH
        )

    pl.semaphore_signal(bar, inc=1, device_id=dev(z, x, c, 1 - y), device_id_type=pl.DeviceIdType.MESH)


def half_swap(value):
    lane = lax.broadcasted_iota(jnp.int32, value.shape, 1)
    return jnp.where(
        lane % HEAD < HEAD // 2, pltpu.roll(value, LANES - HEAD // 2, 1), pltpu.roll(value, HEAD // 2, 1)
    )


def head_means(value):
    lane = lax.broadcasted_iota(jnp.int32, value.shape, 1)
    first = jnp.sum(jnp.where(lane < HEAD, value, 0.0), axis=1, keepdims=True)
    both = jnp.sum(value, axis=1, keepdims=True)
    return jnp.where(lane < HEAD, first, both - first) * (1.0 / HEAD)


def side_by_side(block):
    half = block.shape[0] // 2
    lane = lax.broadcasted_iota(jnp.int32, (half, LANES), 1)
    return jnp.where(lane < HEAD, block[:half], pltpu.roll(block[half:], HEAD, 1))


def peers():
    z, x, c, y = place()
    return ((x, 1 - c), (1 - x, c), (1 - x, 1 - c))


def spread_heads(b, env):
    rows = pl.ds(pl.multiple_of(b * LANES, LANES), LANES)
    lane = lax.broadcasted_iota(jnp.int32, (LANES, LANES), 1)
    one = jnp.where(lane < HEAD + 2, 1.0, 0.0)
    qk = env.heads_in[b, 0:LANES, :].astype(F32)
    env.q_ext[rows, :] = jnp.where(lane < HEAD, qk, 0.0).astype(BF16)
    env.k_ext[rows, :] = jnp.where(lane < HEAD, pltpu.roll(qk, HEAD, 1), one).astype(BF16)
    packed = env.heads_in[b, LANES:, :].astype(F32)
    value = jnp.concatenate([packed, pltpu.roll(packed, HEAD, 1)], axis=0)
    env.v_ext[rows, :] = jnp.where(lane < HEAD, value, one).astype(BF16)


class Reduce:
    def __init__(self, part, passing, landed, send, recv):
        self.part, self.passing, self.landed, self.send, self.recv = part, passing, landed, send, recv
        self.size = passing.shape[1] // SUBS

    def rows(self, n):
        return slice(n * self.size, (n + 1) * self.size)

    def hop(self, owner, way, n):
        z, x, c, y = place()
        spot = jnp.where((owner == z + way) & (way < 0), 4, owner)
        return remote(
            self.passing.at[owner, self.rows(n)], self.landed.at[spot, self.rows(n)],
            self.send.at[owner, n], self.recv.at[spot, n], dev(z + way, x, c, y),
        )

    def wait_spot(self, spot, n):
        z, x, c, y = place()
        remote(
            self.passing.at[0, self.rows(n)], self.landed.at[spot, self.rows(n)], self.send.at[0, n],
            self.recv.at[spot, n], dev(z, x, 1 - c, y),
        ).wait_recv()

    def step(self, k):
        z = place()[0]
        for n in range(SUBS):
            rows = self.rows(n)
            for way in (-1, 1):
                owner = z + way * k

                @pl.when(inside(owner))
                def _():
                    @pl.when(inside(z - way))
                    def _():
                        self.wait_spot(owner, n)
                        self.passing[owner, rows] = (
                            self.part(owner, rows) + self.landed[owner, rows].astype(F32)
                        ).astype(BF16)

                    @pl.when(jnp.logical_not(inside(z - way)))
                    def _():
                        self.passing[owner, rows] = self.part(owner, rows).astype(BF16)

                    self.hop(owner, way, n).start()

    def finish(self, total):
        z = place()[0]
        everything = slice(0, SUBS * self.size)
        total[...] = self.part(z, everything)
        for edge, spot in ((z > 0, z), (z < 3, 4)):

            @pl.when(edge)
            def _():
                for n in range(SUBS):
                    self.wait_spot(spot, n)
                total[...] += self.landed[spot].astype(F32)

        for owner in range(4):

            @pl.when(owner != z)
            def _():
                for n in range(SUBS):
                    self.hop(owner, jnp.where(owner > z, 1, -1), n).wait_send()


class Env:
    def __init__(self, names, refs):
        for name, ref in zip(names, refs, strict=True):
            setattr(self, name, ref)


def window(start, size):
    return pl.ds(pl.multiple_of(start, size), size)


def qkv_rows(slot):
    return window(slot * LANES, LANES), window(4 * LANES + slot * HEAD, HEAD)


def qkv_copies(env, slot, sems, device):
    (send, recv), spots = sems, qkv_rows(slot)
    return [
        remote(env.u_qkv.at[rows, :], env.u_qkv.at[rows, :], send.at[i], recv.at[i], device)
        for i, rows in enumerate(spots)
    ]


def qkv_groups(env):
    z, x, c, y = place()
    mine, other = 2 * x + c, 2 * (1 - x) + c
    core, side = dev(z, x, 1 - c, y), dev(z, 1 - x, c, y)
    s, r = env.q_send, env.q_recv
    return (
        qkv_copies(env, mine, (s.at[0], r.at[0]), core),
        qkv_copies(env, mine, (s.at[1], r.at[1]), side),
        qkv_copies(env, other, (s.at[2], r.at[2]), core),
    )


def ff_views(env, slot, half=None):
    if half is None:
        return env.ups.at[slot], env.gates.at[slot], env.downs.at[slot]
    upper, lower = window(half * 512, 512), window(half * 128, 128)
    return env.ups.at[slot, upper, :], env.gates.at[slot, upper, :], env.downs.at[slot, lower, :]


def ff_groups(env):
    z, x, c, y = place()
    mine, other = 2 * x + c, 2 * (1 - x) + c
    core, side, twin = dev(z, x, 1 - c, y), dev(z, 1 - x, c, y), dev(z, x, c, 1 - y)

    def group(g, views, device):
        return [
            remote(v, v, env.w_send.at[g, i], env.w_recv.at[g, i], device) for i, v in enumerate(views)
        ]

    return (
        group(0, ff_views(env, mine), core),
        group(1, ff_views(env, mine, y), side),
        group(2, ff_views(env, other, y), core),
        group(3, ff_views(env, other, y), twin),
        group(4, ff_views(env, other, 1 - y), core),
    )


def each(copies, action):
    for copy in copies:
        getattr(copy, action)()


class Piece:
    def __init__(self, view, land_c, land_y, land_x, out, sems, whole):
        self.view, self.land_c, self.land_y, self.land_x, self.out = view, land_c, land_y, land_x, out
        (self.send, self.recv), self.whole = sems, whole

    def total(self):
        return self.whole[...].astype(F32)

    def slot(self, h):
        z, x, c, y = place()
        return 2 * (1 - x if h == 0 else x) + c

    def to_core(self, h):
        z, x, c, y = place()
        xx = 1 - x if h == 0 else x
        return remote(
            self.view(2 * xx + 1 - c, None), self.land_c.at[h], self.send.at[h], self.recv.at[h],
            dev(z, x, 1 - c, y),
        )

    def to_twin(self, h):
        z, x, c, y = place()
        return remote(
            self.view(self.slot(h), 1 - y), self.land_y.at[h], self.send.at[2 + h], self.recv.at[2 + h],
            dev(z, x, c, 1 - y),
        )

    def to_side(self):
        z, x, c, y = place()
        return remote(
            self.view(self.slot(0), y), self.land_x, self.send.at[4], self.recv.at[4], dev(z, 1 - x, c, y)
        )

    def swap(self):
        z, x, c, y = place()
        return remote(self.out(y), self.out(y), self.send.at[5], self.recv.at[5], dev(z, x, c, 1 - y))

    def start(self):
        self.to_core(0).start()
        self.to_core(1).start()

    def pass_twin(self):
        for h in range(2):
            self.to_core(h).wait_recv()
            both = self.view(self.slot(h), None)
            both[...] = (both[...].astype(F32) + self.land_c[h].astype(F32)).astype(BF16)
            self.to_twin(h).start()

    def pass_side(self):
        y = place()[3]
        self.to_twin(0).wait_recv()
        give = self.view(self.slot(0), y)
        give[...] = (give[...].astype(F32) + self.land_y[0].astype(F32)).astype(BF16)
        self.to_side().start()

    def pass_back(self):
        y = place()[3]
        self.to_twin(1).wait_recv()
        self.to_side().wait_recv()
        keep = self.view(self.slot(1), y)
        self.out(y)[...] = (
            keep[...].astype(F32) + self.land_y[1].astype(F32) + self.land_x[...].astype(F32)
        ).astype(BF16)
        self.swap().start()

    def finish(self):
        self.swap().wait()
        for h in range(2):
            self.to_core(h).wait_send()
            self.to_twin(h).wait_send()
        self.to_side().wait_send()


class SidePiece(Piece):
    def total(self):
        return self.whole[...].astype(F32) + self.land_y[0].astype(F32)

    def to_side(self):
        z, x, c, y = place()
        return remote(
            self.view(self.slot(0), None), self.land_x, self.send.at[4], self.recv.at[4], dev(z, 1 - x, c, y)
        )

    def swap(self):
        z, x, c, y = place()
        return remote(
            self.whole, self.land_y.at[0], self.send.at[5], self.recv.at[5], dev(z, x, c, 1 - y)
        )

    def pass_first(self):
        self.to_core(0).wait_recv()
        give = self.view(self.slot(0), None)
        give[...] = (give[...].astype(F32) + self.land_c[0].astype(F32)).astype(BF16)
        self.to_side().start()

    def pass_back(self):
        self.to_core(1).wait_recv()
        self.to_side().wait_recv()
        keep = self.view(self.slot(1), None)
        self.whole[...] = (
            keep[...].astype(F32) + self.land_c[1].astype(F32) + self.land_x[...].astype(F32)
        ).astype(BF16)
        self.swap().start()

    def finish(self):
        self.swap().wait()
        for h in range(2):
            self.to_core(h).wait_send()
        self.to_side().wait_send()


def project_block(zz, env):
    z, x, c, y = place()
    linear = dot_nt(env.x_line[zz], env.u_qkv[...])
    lane = lax.broadcasted_iota(jnp.int32, (LANES, LANES), 1)
    scale = jnp.where(lane < HEAD, HEAD ** (-0.5), 1.0)
    cosine, sine = env.cosine[zz], env.sine[zz]
    for sl in range(4):
        qk = linear[:, sl * LANES : (sl + 1) * LANES]
        turned = qk * cosine + half_swap(qk) * sine
        env.turned[zz, sl] = turned
        unit = turned * lax.rsqrt(head_means(turned * turned) + EPS)
        out = (unit * env.gain[sl : sl + 1, :]).astype(BF16).astype(F32) * scale
        env.heads_out[zz, sl, 0:LANES, :] = out.astype(BF16)
        pair = linear[:, (4 + sl // 2) * LANES : (5 + sl // 2) * LANES]
        if sl % 2:
            pair = pltpu.roll(pair, HEAD, 1)
        env.heads_out[zz, sl, LANES:, :] = side_by_side(pair).astype(BF16)
    b = zz * 4 + x * 2 + c
    env.heads_in[b] = env.heads_out[zz, x * 2 + c]
    for i, (xx, cc) in enumerate(peers()):
        remote(
            env.heads_out.at[zz, xx * 2 + cc], env.heads_in.at[b], env.hs.at[zz, i], env.hr.at[b],
            dev(z, xx, cc, y),
        ).start()


def attend_block(i, env):
    z, x, c, y = place()
    s = z * 4 + x * 2 + c
    row = lax.broadcasted_iota(jnp.int32, (BLOCK, BLOCK), 0)
    col = lax.broadcasted_iota(jnp.int32, (BLOCK, BLOCK), 1)
    lane = lax.broadcasted_iota(jnp.int32, (BLOCK, LANES), 1)
    rows = pl.ds(i * BLOCK, BLOCK)
    q = env.q_ext[rows, :]
    total = jnp.zeros((BLOCK, LANES), F32)
    for j in range(i + 1):
        keys = pl.ds(j * BLOCK, BLOCK)
        p = jnp.exp(dot_nt(q, env.k_ext[keys, :]))
        if i == j:
            p = jnp.where(row >= col, p, 0.0)
        total = total + dot(p.astype(BF16), env.v_ext[keys, :])
    denom = total[:, HEAD : HEAD + 1]
    out = total / denom
    env.attended[rows, :] = out
    log = -jnp.log(denom)
    high = log.astype(BF16).astype(F32)
    env.q_ext[rows, :] = jnp.where(
        lane == HEAD, high, jnp.where(lane == HEAD + 1, log - high, q.astype(F32))
    ).astype(BF16)
    for k in range(2):
        t = 2 * i + k
        env.att_out[t] = side_by_side(out[k * LANES : (k + 1) * LANES]).astype(BF16)
        send_block(t, env.att_out, env.att_in, env.as_, env.ar)


def block_of(b):
    return b // 4, (b // 2) % 2, b % 2


def send_block(b, src, land, send, recv):
    z, x, c, y = place()
    zz, xx, cc = block_of(b)
    own = (zz == z) & (cc == c)
    j = 2 * z + c

    @pl.when(jnp.logical_not(own))
    def _():
        remote(src.at[b], land.at[xx, j], send.at[b], recv.at[xx, j], dev(zz, x, cc, y)).start()

    @pl.when(own)
    def _():
        land[xx, j] = src[b]


def wait_blocks(src, land, send, recv):
    z, x, c, y = place()

    @pl.loop(0, 16)
    def _(b):
        zz, xx, cc = block_of(b)

        @pl.when(jnp.logical_not((zz == z) & (cc == c)))
        def _():
            j = 2 * zz + cc
            remote(src.at[b], land.at[xx, j], send.at[b], recv.at[xx, j], dev(zz, x, cc, y)).wait()


def lay_heads(land, dst):
    lane = lax.broadcasted_iota(jnp.int32, (HEAD, LANES), 1)
    for xx in range(2):
        for p in range(4):
            first = land[xx, 2 * p].astype(F32)
            second = land[xx, 2 * p + 1].astype(F32)
            cols = slice(p * LANES, (p + 1) * LANES)
            dst[xx, 0:HEAD, cols] = jnp.where(lane < HEAD, first, pltpu.roll(second, HEAD, 1)).astype(BF16)
            dst[xx, HEAD:, cols] = jnp.where(lane < HEAD, pltpu.roll(first, HEAD, 1), second).astype(BF16)


def grads_copy(b, target, env):
    x, y = place()[1], place()[3]
    xx = block_of(b)[1]
    j = 2 * target[0] + target[1]
    return remote(
        env.datt_out.at[xx, j], env.datt_in.at[b], env.das.at[xx, j], env.dar.at[b],
        dev(target[0], x, target[1], y),
    )


def send_grads(xx, env):
    z, x, c, y = place()
    b = 4 * z + 2 * xx + c
    for p in range(2):
        d_att = dot_nt(env.d_both[xx], env.u_out[4 * p : 4 * p + 4].reshape(256, 1024))
        for k in range(4):
            value = d_att[:, (k // 2) * LANES : (k // 2 + 1) * LANES]
            if k % 2:
                value = pltpu.roll(value, HEAD, 1)
            j = 4 * p + k
            env.datt_out[xx, j] = side_by_side(value).astype(BF16)
            own = 2 * z + c == j

            @pl.when(own)
            def _():
                env.datt_in[b] = env.datt_out[xx, j]

            @pl.when(jnp.logical_not(own))
            def _():
                grads_copy(b, (j // 2, j % 2), env).start()


def wait_grads(b, env):
    z, x, c, y = place()
    zz, xx, cc = block_of(b)

    @pl.when(jnp.logical_not((zz == z) & (cc == c)))
    def _():
        grads_copy(b, (zz, cc), env).wait()


def side_rows(h, env):
    z, x, c, y = place()
    rows = env.d_both.at[x, rows_of(h), :]
    return remote(rows, rows, env.db_s.at[h], env.db_r.at[h], dev(z, 1 - x, c, y))


def side_mix(h, env):
    z, x, c, y = place()
    return remote(
        env.mix_out.at[h], env.mix_in.at[h], env.mx_s.at[h], env.mx_r.at[h], dev(z, 1 - x, c, y)
    )


def mlp_forward(h, env):
    @pl.loop(0, 4)
    def _(n):
        cols = window(n * 256, 256)
        mid = env.h_line[h].reshape(256, 1024)
        up = dot(mid, env.ups[n])
        gate = dot(mid, env.gates[n]) * env.gate_row[:, cols]
        env.up_lin[h, cols, :] = up
        env.gate_val[h, :, cols] = gate
        act = gate * (1.0 / (1.0 + jnp.exp(-gate)))
        env.hidden[h, :, cols] = (up * env.up_row[:, cols] * act).astype(BF16)

    @pl.loop(0, 4)
    def _(n):
        cols = window(n * 256, 256)
        env.part[h, :, :, cols] = dot(env.hidden[h], env.downs[:, :, cols].reshape(1024, 256)).reshape(
            4, 64, 256
        )


def mlp_backward(h, env):
    @pl.loop(0, 4)
    def _(n):
        cols = window(n * 256, 256)
        d_hidden = dot_nt(env.dm_line[h].reshape(256, 1024), env.downs[n])
        up, gate = env.up_lin[h, cols, :], env.gate_val[h, :, cols]
        up_gain, gate_gain = env.up_row[:, cols], env.gate_row[:, cols]
        sig = 1.0 / (1.0 + jnp.exp(-gate))
        d_up = d_hidden * (gate * sig)
        d_gate = d_hidden * (up * up_gain) * (sig * (1.0 + gate * (1.0 - sig)))
        env.gains[0:1, cols] += jnp.sum(d_up * up, axis=0, keepdims=True)
        env.gains[1:2, cols] += jnp.sum(d_gate * gate, axis=0, keepdims=True) / gate_gain
        env.d_up[h, n] = (d_up * up_gain).astype(BF16)
        env.d_gate[h, n] = (d_gate * gate_gain).astype(BF16)

    @pl.loop(0, 4)
    def _(n):
        cols = window(n * 256, 256)
        back = dot_nt(env.d_up[h, 0], env.ups[0, cols, :])
        for m in range(4):
            if m:
                back = back + dot_nt(env.d_up[h, m], env.ups[m, cols, :])
            back = back + dot_nt(env.d_gate[h, m], env.gates[m, cols, :])
        env.part[h, :, :, cols] = back.reshape(4, 64, 256)


def weight_gradient(left, right, out, first):
    @pl.loop(0, 4)
    def _(n):
        value = dot_tn(left, right(n))
        ref = out(n)
        if not first:
            value = value + ref[...].astype(F32).reshape(1024, 256)
        ref[...] = value.astype(BF16).reshape(ref.shape)


def grad_down_half(h, env):
    def right(n):
        return env.dm_line[h, :, :, window(n * 256, 256)].reshape(256, 256)

    weight_gradient(
        env.hidden[h], right, lambda n: env.g_down.at[:, :, window(n * 256, 256)], h == 0
    )


def grad_wide_half(h, src, out, env):
    weight_gradient(
        env.h_line[h].reshape(256, 1024), lambda n: src[h, n], lambda n: out.at[n], h == 0
    )


def rows_of(h):
    return slice(64 * h, 64 * (h + 1))


def after_forward(h, reduce, env):
    z, rows = place()[0], rows_of(h)
    reduce.finish(env.total)
    alpha = env.mix_row[1:2, :]
    out, saved = mix(env.mid[rows, :], env.total[...], alpha)
    env.output[rows, :] = out
    d_mid, d_branch, d_alpha = mix_back(env.d_out[rows, :], out, saved, alpha)
    env.d_mid[rows, :] = d_mid
    env.gains[3:4, :] += d_alpha[None, :]
    env.dm_line[h, z] = d_branch.astype(BF16)


def after_backward(h, reduce, env):
    rows = rows_of(h)
    reduce.finish(env.total)
    alpha = env.mix_row[0:1, :]
    mid, saved = mix(env.states[rows, :], env.branch[rows, :], alpha)
    d_state, d_branch, d_alpha = mix_back(env.d_mid[rows, :] + env.total[...], mid, saved, alpha)
    env.d_states[rows, :] = d_state
    env.gains[2:3, :] += d_alpha[None, :]
    env.d_both[place()[1], rows, :] = d_branch.astype(BF16)
    side_rows(h, env).start()


def spread_grads(b, env):
    rows = pl.ds(b * LANES, LANES)
    lane = lax.broadcasted_iota(jnp.int32, (LANES, LANES), 1)
    packed = env.datt_in[b].astype(F32)
    value = jnp.where(lane < HEAD, jnp.concatenate([packed, pltpu.roll(packed, HEAD, 1)], axis=0), 0.0)
    delta = -jnp.sum(value * env.attended[rows, :], axis=1, keepdims=True)
    high = delta.astype(BF16).astype(F32)
    env.do_ext[rows, :] = jnp.where(
        lane == HEAD, high, jnp.where(lane == HEAD + 1, delta - high, value)
    ).astype(BF16)


def attend_back_block(i, env, last):
    z, x, c, y = place()
    row = lax.broadcasted_iota(jnp.int32, (BLOCK, BLOCK), 0)
    col = lax.broadcasted_iota(jnp.int32, (BLOCK, BLOCK), 1)
    lane = lax.broadcasted_iota(jnp.int32, (LANES, LANES), 1)
    rows = pl.ds(i * BLOCK, BLOCK)
    q = env.q_ext[rows, :]
    do = env.do_ext[rows, :]
    dq = jnp.zeros((BLOCK, LANES), F32)
    for j in range(i + 1):
        keys = pl.ds(j * BLOCK, BLOCK)
        k = env.k_ext[keys, :]
        p = jnp.exp(dot_nt(k, q))
        if i == j:
            p = jnp.where(row <= col, p, 0.0)
        ds = (p * dot_nt(env.v_ext[keys, :], do)).astype(BF16)
        dv = dot(p.astype(BF16), do)
        dk = dot(ds, q)
        dq = dq + dot_tn(ds, k)
        if i == last:
            env.dk[keys, :] = dk
            env.dv[keys, :] = dv
        else:
            env.dk[keys, :] += dk
            env.dv[keys, :] += dv
    for n in range(2):
        part = slice(n * LANES, (n + 1) * LANES)
        b = 2 * i + n
        zz, sl = b // 4, b % 4
        tok = pl.ds(b * LANES, LANES)
        env.back_out[zz, sl, 0:LANES, :] = jnp.where(
            lane < HEAD, dq[part] * HEAD ** (-0.5), pltpu.roll(env.dk[tok, :], HEAD, 1)
        ).astype(BF16)
        env.back_out[zz, sl, LANES:, :] = side_by_side(env.dv[tok, :]).astype(BF16)
        mine = 2 * x + c

        @pl.when(sl == mine)
        def _():
            env.back_in[zz * 4 + mine] = env.back_out[zz, sl]

        @pl.when(sl != mine)
        def _():
            back_copy(zz, sl, mine, env).start()


def back_copy(zz, sl, source, env):
    z, x, c, y = place()
    return remote(
        env.back_out.at[zz, sl], env.back_in.at[zz * 4 + source], env.bs.at[zz, sl],
        env.br.at[zz * 4 + source], dev(z, sl // 2, sl % 2, y),
    )


def project_back(zz, env):
    z, x, c, y = place()
    mine = 2 * x + c
    cosine, sine = env.cosine[zz], env.sine[zz]
    lane = lax.broadcasted_iota(jnp.int32, (LANES, LANES), 1)
    values = []
    for sl in range(4):

        @pl.when(sl != mine)
        def _():
            back_copy(zz, sl, sl, env).wait()

        grad = env.back_in[zz * 4 + sl, 0:LANES, :].astype(F32)
        turned = env.turned[zz, sl]
        inverse = lax.rsqrt(head_means(turned * turned) + EPS)
        unit = turned * inverse
        env.gain_sum[sl : sl + 1, :] += jnp.sum(grad * unit, axis=0, keepdims=True)
        d_unit = grad * env.gain[sl : sl + 1, :]
        d_turned = inverse * (d_unit - unit * head_means(d_unit * unit))
        d_lin = d_turned * cosine - half_swap(d_turned) * sine
        env.d_lin[zz, :, sl * LANES : (sl + 1) * LANES] = d_lin.astype(BF16)
        packed = env.back_in[zz * 4 + sl, LANES:, :].astype(F32)
        values.append(jnp.concatenate([packed, pltpu.roll(packed, HEAD, 1)], axis=0))
    for p in range(2):
        pair = jnp.where(lane < HEAD, values[2 * p], pltpu.roll(values[2 * p + 1], HEAD, 1))
        env.d_lin[zz, :, (4 + p) * LANES : (5 + p) * LANES] = pair.astype(BF16)


def states_part(zz, env):
    d_x = dot(env.d_lin[zz], env.u_qkv[...])
    env.part[0, zz] = d_x[:64]
    env.part[1, zz] = d_x[64:]


def layer(env):
    z, x, c, y = place()
    s = z * 4 + x * 2 + c
    mine = 2 * x + c
    env.back_out, env.back_in = env.heads_out, env.heads_in
    env.g_out = env.u_out
    tables = []
    for zz in range(4):
        b = zz * 4 + 2 * x + c
        tables.append(pltpu.make_async_copy(env.cosines.at[b], env.cosine.at[zz], env.t_sem.at[zz, 0]))
        tables.append(pltpu.make_async_copy(env.sines.at[b], env.sine.at[zz], env.t_sem.at[zz, 1]))
    each(tables, "start")

    greet_row()
    env.x_line[z] = env.states[...].astype(BF16)
    qk_rows, v_rows = qkv_rows(mine)
    env.u_qkv[qk_rows, :] = jnp.concatenate(
        [unit_rows(env.w_query[...]), unit_rows(env.w_key[...])], axis=0
    )
    env.u_qkv[v_rows, :] = unit_rows(env.w_value[...])
    pl.semaphore_wait(pltpu.get_barrier_semaphore(), 16)
    line = Line(env.x_line, (env.x_send, env.x_recv))
    line.start()
    q_core, q_side, q_relay = qkv_groups(env)
    each(q_side, "start")
    each(q_core, "start")

    lane = lax.broadcasted_iota(jnp.int32, (1, LANES), 1)
    for pair in range(2):
        scale = env.qk_scale[window(z * 256 + pair * LANES, LANES)].reshape(1, LANES)
        turned = pltpu.roll(scale, HEAD, 1)
        env.gain[2 * pair : 2 * pair + 1, :] = jnp.where(lane < HEAD, scale, turned)
        env.gain[2 * pair + 1 : 2 * pair + 2, :] = jnp.where(lane < HEAD, turned, scale)
    env.up_row[...] = env.up_scale[window(z * 1024, 1024)].reshape(1, 1024)
    env.gate_row[...] = env.gate_scale[window(z * 1024, 1024)].reshape(1, 1024)
    env.mix_row[0:1, :] = env.alpha_attn[...].reshape(1, 1024)
    env.mix_row[1:2, :] = env.alpha_mlp[...].reshape(1, 1024)
    env.u_out[2 * z + c] = unit_rows(env.w_out[...])
    env.ups[mine] = unit_cols(env.w_up[...])
    env.gates[mine] = unit_cols(env.w_gate[...])
    env.downs[mine] = unit_rows(env.w_down[...])
    env.gains[...] = jnp.zeros_like(env.gains)
    env.gain_sum[...] = jnp.zeros_like(env.gain_sum)
    ff = ff_groups(env)
    each(ff[0], "start")
    each(tables, "wait")

    line.arrive(1)
    each(q_side, "wait_recv")
    each(q_relay, "start")
    each(q_core, "wait_recv")
    each(q_relay, "wait_recv")
    project_block(z, env)

    @pl.loop(1, 4)
    def _(k):
        @pl.when(k < 3)
        def _():
            line.arrive(k + 1)

        for way in (-1, 1):

            @pl.when(inside(z - way * k))
            def _():
                project_block(z - way * k, env)

    each(ff[1], "start")
    line.drain()
    for group in (q_side, q_core, q_relay):
        each(group, "wait_send")
    uo = Column(env.u_out, (env.o_z, env.o_c, env.o_r))
    uo.start()

    @pl.loop(0, 4)
    def _(zz):
        for i, (xx, cc) in enumerate(peers()):
            b = zz * 4 + xx * 2 + cc
            remote(
                env.heads_out.at[zz, xx * 2 + cc], env.heads_in.at[b], env.hs.at[zz, i], env.hr.at[b],
                dev(z, xx, cc, y),
            ).wait()

    @pl.loop(0, 16)
    def _(b):
        spread_heads(b, env)

    uo.arrive(1)
    for i in range(4):
        attend_block(i, env)
    for i in range(4, 6):
        attend_block(i, env)
    uo.arrive(2)
    for i in range(6, 8):
        attend_block(i, env)
    uo.arrive(3)
    uo.finish()
    ff[1][0].wait_recv()
    ff[2][0].start()
    ff[3][0].start()
    wait_blocks(env.att_out, env.att_in, env.as_, env.ar)
    lay_heads(env.att_in, env.att_low)

    weights = env.u_out[...].reshape(512, 1024)
    for h in range(2):
        env.mix_out[h] = dot(env.att_low[1 - x, rows_of(h), :], weights).astype(BF16)
        side_mix(h, env).start()
    env.branch[...] = dot(env.att_low[x], weights)
    ff[1][1].wait_recv()
    ff[2][1].start()
    ff[3][1].start()

    def mix_half(h):
        rows = rows_of(h)
        side_mix(h, env).wait_recv()
        branch = env.branch[rows, :] + env.mix_in[h].astype(F32)
        env.branch[rows, :] = branch
        mid, _ = mix(env.states[rows, :], branch, env.mix_row[0:1, :])
        env.mid[rows, :] = mid
        env.h_line[h, z] = mid.astype(BF16)

    fa = Line(env.h_line.at[0], (env.fa_s, env.fa_r))
    fb = Line(env.h_line.at[1], (env.fb_s, env.fb_r))
    ba = Line(env.dm_line.at[0], (env.ba_s, env.ba_r))
    bb = Line(env.dm_line.at[1], (env.bb_s, env.bb_r))

    def reduce(h, send, recv):
        return Reduce(
            lambda owner, rows: env.part[h, owner, rows], env.passing.at[h], env.landed.at[h], send, recv
        )

    r0, r1 = reduce(0, env.r0_s, env.r0_r), reduce(1, env.r1_s, env.r1_r)

    def arrive(gather, k):
        gather.arrive(k)

    def piece(grad, tag, cut):
        def view(slot, half):
            return grad.at[slot] if half is None else grad.at[slot, window(half * cut, cut), :]

        lc, ly, lx, out, send, recv = tag
        kind = Piece if ly.shape[1] == cut else SidePiece
        return kind(view, lc, ly, lx, lambda half: out.at[window(half * cut, cut), :], (send, recv), out)

    gu = piece(env.g_up, (env.lcu, env.lyu, env.lxu, env.ou, env.us, env.ur), 512)
    gg = piece(env.g_gate, (env.lcg, env.lyg, env.lxg, env.og, env.gs, env.gr), 512)
    gd = piece(env.g_down, (env.lcd, env.lyd, env.lxd, env.od, env.ds, env.dr), 128)
    mix_half(0)
    fa.start()
    mix_half(1)
    ff[1][2].wait_recv()
    ff[2][2].start()
    ff[3][2].start()
    arrive(fa, 1)
    arrive(fa, 2)
    fb.start()
    each(ff[3], "wait_recv")
    each(ff[4], "start")
    each(ff[0], "wait_recv")
    each(ff[2], "wait_recv")
    each(ff[4], "wait_recv")
    arrive(fa, 3)
    mlp_forward(0, env)
    r0.step(3)
    arrive(fb, 1)
    r0.step(2)
    arrive(fb, 2)
    r0.step(1)
    arrive(fb, 3)
    mlp_forward(1, env)
    r1.step(3)
    after_forward(0, r0, env)
    ba.start()
    r1.step(2)
    arrive(ba, 1)
    r1.step(1)
    arrive(ba, 2)
    after_forward(1, r1, env)
    bb.start()
    arrive(ba, 3)
    mlp_backward(0, env)
    r0.step(3)
    arrive(bb, 1)
    grad_down_half(0, env)
    r0.step(2)
    arrive(bb, 2)
    grad_wide_half(0, env.d_up, env.g_up, env)
    r0.step(1)
    grad_wide_half(0, env.d_gate, env.g_gate, env)
    arrive(bb, 3)
    grad_down_half(1, env)
    gd.start()
    mlp_backward(1, env)
    r1.step(3)
    gd.pass_twin()
    after_backward(0, r0, env)
    grad_wide_half(1, env.d_up, env.g_up, env)
    gu.start()
    r1.step(2)
    for gather in (fa, fb, ba, bb):
        gather.drain()
    for group in ff:
        each(group, "wait_send")
    for h in range(2):
        side_mix(h, env).wait_send()
    gu.pass_first()
    grad_wide_half(1, env.d_gate, env.g_gate, env)
    gg.start()
    r1.step(1)
    after_backward(1, r1, env)

    side_rows(0, env).wait_recv()
    send_grads(x, env)
    side_rows(1, env).wait_recv()
    send_grads(1 - x, env)
    gg.pass_twin()

    @pl.loop(0, 4)
    def _(n):
        cols = window(n * 256, 256)
        grad = dot_tn(env.att_low[0], env.d_both[0, :, cols]) + dot_tn(env.att_low[1], env.d_both[1, :, cols])
        env.g_out[:, :, cols] = grad.reshape(8, 64, 256).astype(BF16)

    out_reduce = RowReduce(env)
    out_reduce.start()
    gd.pass_side()
    out_reduce.pass_line()
    for i in range(7, -1, -1):
        wait_grads(2 * i, env)
        wait_grads(2 * i + 1, env)
        spread_grads(2 * i, env)
        spread_grads(2 * i + 1, env)
        attend_back_block(i, env, 7)
        if i == 7:
            gu.pass_back()
            out_reduce.step(3)
        elif i == 6:
            gd.pass_back()
            out_reduce.step(2)
        elif i == 5:
            out_reduce.step(1)
    gg.pass_side()
    for h in range(2):
        side_rows(h, env).wait_send()
    project_back(3, env)
    out_reduce.to_twin()
    project_back(2, env)
    project_back(1, env)
    project_back(0, env)
    @pl.loop(0, 4)
    def _(n):
        cols = window(n * 256, 256)
        total = dot_tn(env.d_lin[...].reshape(512, 768), env.x_line[:, :, cols].reshape(512, 256))
        env.g_qkv[:, cols] = total.astype(BF16)

    def row_piece(which, tag, cut):
        def view(slot, half):
            start, size = (slot * LANES, LANES) if which == 0 else (4 * LANES + slot * HEAD, HEAD)
            if half is not None:
                start, size = start + half * cut, cut
            return env.g_qkv.at[window(start, size), :]

        lc, ly, lx, out, send, recv = tag
        kind = Piece if ly.shape[1] == cut else SidePiece
        return kind(
            view, lc, ly, lx, lambda half: out.at[window(half * cut, cut), :], (send, recv), out
        )

    gq = row_piece(0, (env.lcq, env.lyq, env.lxq, env.oq, env.qqs, env.qqr), 64)
    gv = row_piece(1, (env.lcv, env.lyv, env.lxv, env.ov, env.vvs, env.vvr), 32)
    gq.start()
    gv.start()

    @pl.loop(0, 4)
    def _(zz):
        states_part(zz, env)

    for h in range(2):
        (r0, r1)[h].step(3)
    gq.pass_first()
    gv.pass_twin()
    for sl in range(4):
        both_parts = env.gain_sum[sl : sl + 1, 0:HEAD] + env.gain_sum[sl : sl + 1, HEAD:]
        env.gains[4 + sl : 5 + sl, 0:HEAD] = both_parts
    small = [
        remote(env.gains, env.gain_land.at[i], env.sm_s.at[i], env.sm_r.at[i], device)
        for i, device in enumerate((dev(z, x, 1 - c, y), dev(z, 1 - x, c, y), dev(z, x, c, 1 - y)))
    ]
    def tell(k):
        t = (z + k) % 4
        return remote(
            env.gain_line.at[z], env.gain_line.at[z], env.gl_s.at[k], env.gl_r.at[z], dev(t, x, c, y)
        )

    small[0].start()
    r0.step(2)
    r1.step(2)
    gv.pass_side()
    small[0].wait()
    env.gains[...] += env.gain_land[0]
    small[1].start()
    gg.pass_back()
    finish_ff(env, gd, 2)
    small[1].wait()
    env.gains[...] += env.gain_land[1]
    small[2].start()
    r0.step(1)
    r1.step(1)
    gq.pass_back()
    gv.pass_back()
    finish_ff(env, gu, 0)
    small[2].wait()
    env.gain_line[z] = env.gains[...] + env.gain_land[2]
    for k in range(1, 4):
        tell(k).start()
    finish_ff(env, gg, 1)
    out_reduce.finish()
    unit_out = env.oo[...].astype(F32) + env.yo[...].astype(F32)
    env.gate_val[1, 3 * HEAD :, :] = pull_rows(env.w_out[...], unit_out)
    r0.finish(env.total)
    env.d_states[0:64, :] += env.total[...]
    r1.finish(env.total)
    env.d_states[64:, :] += env.total[...]
    gq.finish()
    gv.finish()
    stage = env.gate_val.at[1]
    total_qk = gq.total()
    stage[0:HEAD, :] = pull_rows(env.w_query[...], total_qk[0:HEAD])
    stage[HEAD : 2 * HEAD, :] = pull_rows(env.w_key[...], total_qk[HEAD:])
    stage[2 * HEAD : 3 * HEAD, :] = pull_rows(env.w_value[...], gv.total())
    results = [
        pltpu.make_async_copy(stage.at[pl.ds(i * HEAD, HEAD), :], ref, env.out_sem.at[3 + i])
        for i, ref in enumerate((env.grad_query, env.grad_key, env.grad_value, env.grad_out))
    ]
    each(results, "start")
    for k in range(1, 4):
        tell(k).wait_send()
        t = (z + k) % 4
        remote(
            env.gain_line.at[t], env.gain_line.at[t], env.gl_s.at[k], env.gl_r.at[t], dev(t, x, c, y)
        ).wait_recv()
    each(results, "wait")
    for i in range(3):
        ff_result(env, i).wait()


def pull_rows(weight, grad):
    wide = weight.astype(F32)
    inverse = lax.rsqrt(jnp.sum(wide * wide, axis=1, keepdims=True) + EPS)
    unit = wide * inverse
    return inverse * (grad - unit * jnp.sum(grad * unit, axis=1, keepdims=True))


def pull_cols(weight, grad):
    wide = weight.astype(F32)
    inverse = lax.rsqrt(jnp.sum(wide * wide, axis=0, keepdims=True) + EPS)
    unit = wide * inverse
    return inverse * (grad - unit * jnp.sum(grad * unit, axis=0, keepdims=True))


def ff_result(env, which):
    stage = (env.up_lin.at[0], env.up_lin.at[1], env.gate_val.at[0])[which]
    out = (env.grad_up, env.grad_gate, env.grad_down)[which]
    return pltpu.make_async_copy(stage, out, env.out_sem.at[which])


def finish_ff(env, piece, which):
    piece.finish()
    if which == 2:
        env.gate_val[0] = pull_rows(env.w_down[...], piece.total())
    elif which == 0:
        env.up_lin[0] = pull_cols(env.w_up[...], piece.total())
    else:
        env.up_lin[1] = pull_cols(env.w_gate[...], piece.total())
    ff_result(env, which).start()


class RowReduce:
    def __init__(self, env):
        self.env = env
        self.line = Reduce(self.part, env.o_pass, env.o_land, env.ol_s, env.ol_r)

    def part(self, owner, rows):
        return self.env.g_out[2 * owner + place()[2], rows].astype(F32)

    def to_core(self, zz):
        z, x, c, y = place()
        e = self.env
        return remote(
            e.g_out.at[2 * zz + 1 - c], e.o_c_land.at[zz], e.oc_s.at[zz], e.oc_r.at[zz], dev(z, x, 1 - c, y)
        )

    def twin(self):
        z, x, c, y = place()
        e = self.env
        return remote(e.oo, e.yo, e.oy_s, e.oy_r, dev(z, x, c, 1 - y))

    def start(self):
        @pl.loop(0, 4)
        def _(zz):
            self.to_core(zz).start()

    def pass_line(self):
        c = place()[2]
        e = self.env

        @pl.loop(0, 4)
        def _(zz):
            self.to_core(zz).wait_recv()
            b = 2 * zz + c
            e.g_out[b] = (e.g_out[b].astype(F32) + e.o_c_land[zz].astype(F32)).astype(BF16)

    def step(self, k):
        self.line.step(k)

    def to_twin(self):
        e = self.env
        self.line.finish(e.total)
        e.oo[...] = e.total[...].astype(BF16)
        self.twin().start()

    def finish(self):
        self.twin().wait()

        @pl.loop(0, 4)
        def _(zz):
            self.to_core(zz).wait_send()


DMA = pltpu.SemaphoreType.DMA


def v(shape, dtype=BF16):
    return pltpu.VMEM(shape, dtype)


LAYER_IN = tuple(
    dict(
        states=None,
        w_query=None,
        w_key=None,
        w_value=None,
        w_out=None,
        w_up=None,
        w_gate=None,
        w_down=None,
        qk_scale=None,
        up_scale=None,
        gate_scale=None,
        alpha_attn=None,
        alpha_mlp=None,
        d_out=None,
        cosines=None,
        sines=None,
    )
)
LAYER_OUT = dict(
    output=((128, 1024), F32), d_states=((128, 1024), F32), gain_line=((4, 8, 1024), F32),
    grad_query=((64, 1024), F32), grad_key=((64, 1024), F32), grad_value=((64, 1024), F32),
    grad_out=((64, 1024), F32), grad_up=((1024, 256), F32), grad_gate=((1024, 256), F32),
    grad_down=((256, 1024), F32),
)
IN_VMEM = 3
LAYER_TMP = dict(
    x_line=v((4, 128, 1024)), u_qkv=v((768, 1024)), u_out=v((8, 64, 1024)), mix_out=v((2, 64, 1024)), mix_in=v((2, 64, 1024)),
    turned=v((4, 4, 128, 128), F32), cosine=v((4, 128, 128), F32), sine=v((4, 128, 128), F32),
    gain=v((4, 128), F32), up_row=v((1, 1024), F32), gate_row=v((1, 1024), F32), mix_row=v((2, 1024), F32), gain_sum=v((4, 128), F32), gains=v((8, 1024), F32),
    gain_land=v((3, 8, 1024), F32),
    heads_out=v((4, 4, 192, 128)), heads_in=v((16, 192, 128)),
    q_ext=v((2048, 128)), k_ext=v((2048, 128)), v_ext=v((2048, 128)), attended=v((2048, 128), F32),
    att_out=v((16, 64, 128)), att_in=v((2, 8, 64, 128)), att_low=v((2, 128, 512)),
    ups=v((4, 1024, 256)), gates=v((4, 1024, 256)), downs=v((4, 256, 1024)),
    branch=v((128, 1024), F32), mid=v((128, 1024), F32), d_mid=v((128, 1024), F32),
    total=v((64, 1024), F32), d_both=v((2, 128, 1024)),
    h_line=v((2, 4, 64, 1024)), dm_line=v((2, 4, 64, 1024)),
    up_lin=v((2, 1024, 256), F32), gate_val=v((2, 256, 1024), F32), hidden=v((2, 256, 1024)),
    d_up=v((2, 4, 256, 256)), d_gate=v((2, 4, 256, 256)),
    part=v((2, 4, 64, 1024), F32), passing=v((2, 4, 64, 1024)), landed=v((2, 5, 64, 1024)),
    g_up=v((4, 1024, 256)), g_gate=v((4, 1024, 256)), g_down=v((4, 256, 1024)), g_qkv=v((768, 1024)),
    lcu=v((2, 1024, 256)), lcg=v((2, 1024, 256)), lcd=v((2, 256, 1024)), lcq=v((2, 128, 1024)),
    lcv=v((2, 64, 1024)),
    lyu=v((1, 1024, 256)), lyg=v((2, 512, 256)), lyd=v((2, 128, 1024)), lyq=v((1, 128, 1024)), lyv=v((2, 32, 1024)),
    lxu=v((1024, 256)), lxg=v((512, 256)), lxd=v((128, 1024)), lxq=v((128, 1024)), lxv=v((32, 1024)),
    ou=v((1024, 256)), og=v((1024, 256)), od=v((256, 1024)), oq=v((128, 1024)), ov=v((64, 1024)),
    oo=v((64, 1024)), yo=v((64, 1024)), out_sem=DMA((7,)),
    o_c_land=v((4, 64, 1024)), o_pass=v((4, 64, 1024)),
    o_land=v((5, 64, 1024)),
    datt_out=v((2, 8, 64, 128)), datt_in=v((16, 64, 128)), do_ext=v((2048, 128)),
    dk=v((2048, 128), F32), dv=v((2048, 128), F32),
    d_lin=v((4, 128, 768)),
    t_sem=DMA((4, 2)), x_send=DMA((4, 2, SUBS)), x_recv=DMA((4, SUBS)), q_send=DMA((3, 2)), q_recv=DMA((3, 2)),
    w_send=DMA((5, 3)), w_recv=DMA((5, 3)), hs=DMA((4, 3)), hr=DMA((16,)),
    o_z=DMA((4, 2)), o_c=DMA((4,)), o_r=DMA((8,)),
    as_=DMA((16,)), ar=DMA((2, 8)), das=DMA((2, 8)), dar=DMA((16,)),
    mx_s=DMA((2,)), mx_r=DMA((2,)), db_s=DMA((2,)), db_r=DMA((2,)),
    fa_s=DMA((4, 2, SUBS)), fa_r=DMA((4, SUBS)), fb_s=DMA((4, 2, SUBS)), fb_r=DMA((4, SUBS)),
    ba_s=DMA((4, 2, SUBS)), ba_r=DMA((4, SUBS)), bb_s=DMA((4, 2, SUBS)), bb_r=DMA((4, SUBS)),
    r0_s=DMA((4, SUBS)), r0_r=DMA((5, SUBS)), r1_s=DMA((4, SUBS)), r1_r=DMA((5, SUBS)),
    us=DMA((6,)), ur=DMA((6,)), gs=DMA((6,)), gr=DMA((6,)), ds=DMA((6,)), dr=DMA((6,)),
    qqs=DMA((6,)), qqr=DMA((6,)), vvs=DMA((6,)), vvr=DMA((6,)),
    oc_s=DMA((4,)), oc_r=DMA((4,)),
    ol_s=DMA((4, SUBS)), ol_r=DMA((5, SUBS)), oy_s=DMA, oy_r=DMA,
    bs=DMA((4, 4)), br=DMA((16,)), sm_s=DMA((3,)), sm_r=DMA((3,)), gl_s=DMA((4,)), gl_r=DMA((4,)),
)


def run_layer(*args):
    vmem = pl.BlockSpec(memory_space=pltpu.VMEM)
    names = LAYER_IN + tuple(LAYER_OUT) + tuple(LAYER_TMP)

    def kernel(*refs):
        layer(Env(names, refs))

    outs = pl.pallas_call(
        kernel,
        name="layer",
        out_shape=tuple(jax.ShapeDtypeStruct(*o) for o in LAYER_OUT.values()),
        in_specs=[vmem] * (len(LAYER_IN) - 2) + [pl.BlockSpec(memory_space=pl.ANY)] * 2,
        out_specs=(vmem,) * IN_VMEM
        + (pl.BlockSpec(memory_space=pl.ANY),) * (len(LAYER_OUT) - IN_VMEM),
        scratch_shapes=list(LAYER_TMP.values()),
        compiler_params=pltpu.CompilerParams(
            collective_id=1, has_side_effects=True, vmem_limit_bytes=62 * MIB
        ),
    )(*args)
    return dict(zip(LAYER_OUT, outs))


HANDED = tuple(name for name in LAYER_OUT if name != "gain_line")


def hand_over_kernel(*refs):
    count = len(HANDED)
    line = refs[count]
    outs = refs[count + 1 : 2 * count + 6]
    held = refs[2 * count + 6 : 3 * count + 6]
    arrive, leave = refs[3 * count + 6 :]
    loads = [pltpu.make_async_copy(refs[i], held[i], arrive.at[i]) for i in range(count)]
    stores = [pltpu.make_async_copy(held[i], outs[i], leave.at[i]) for i in range(count)]
    each(loads, "start")
    qk, up, gate, attn, mlp = outs[count:]
    lane = lax.broadcasted_iota(jnp.int32, (1, LANES), 1)
    for zz in range(4):
        cols = slice(zz * 1024, (zz + 1) * 1024)
        up[cols] = line[zz, 0:1, :].reshape(1024)
        gate[cols] = line[zz, 1:2, :].reshape(1024)
        for pair in range(2):
            first = line[zz, 4 + 2 * pair : 5 + 2 * pair, 0:LANES]
            second = pltpu.roll(line[zz, 5 + 2 * pair : 6 + 2 * pair, 0:LANES], HEAD, 1)
            both = jnp.where(lane < HEAD, first, second)
            qk[zz * 256 + pair * LANES : zz * 256 + (pair + 1) * LANES] = both.reshape(LANES)
    for row, out in ((2, attn), (3, mlp)):
        parts = [line[zz, row : row + 1, :] for zz in range(4)]
        out[...] = (parts[0] + parts[1] + parts[2] + parts[3]).reshape(1024)
    for load, store in zip(loads, stores):
        load.wait()
        store.start()
    each(stores, "wait")


def hand_over(*arrays):
    vmem, hbm = pl.BlockSpec(memory_space=pltpu.VMEM), pl.BlockSpec(memory_space=pl.ANY)
    count = len(HANDED)
    sizes = (1024, 4096, 4096, 1024, 1024)
    return pl.pallas_call(
        hand_over_kernel,
        name="hand_over",
        out_shape=tuple(jax.ShapeDtypeStruct(a.shape, a.dtype) for a in arrays[:count])
        + tuple(jax.ShapeDtypeStruct((n,), F32) for n in sizes),
        in_specs=[hbm] * count + [vmem],
        out_specs=(hbm,) * count + (vmem,) * len(sizes),
        scratch_shapes=[v(a.shape, a.dtype) for a in arrays[:count]] + [DMA((count,))] * 2,
        compiler_params=pltpu.CompilerParams(vmem_limit_bytes=60 * MIB),
    )(*arrays)


def on_device_heads(
    states,
    lengths,
    w_query,
    w_key,
    w_value,
    w_out,
    w_up,
    w_gate,
    w_down,
    qk_scale,
    up_scale,
    gate_scale,
    alpha_attn,
    alpha_mlp,
    d_out,
):
    tok, width = states.shape[1:]
    cosine, sine = turn_tables(16 * tok)
    got = run_layer(
        states.reshape(tok, width), w_query.T, w_key.T, w_value.T, w_out, w_up, w_gate, w_down,
        qk_scale, up_scale, gate_scale, alpha_attn, alpha_mlp, d_out.reshape(tok, width),
        jnp.asarray(cosine.reshape(16, tok, LANES)), jnp.asarray(sine.reshape(16, tok, LANES)),
    )

    output, d_states, g_query, g_key, g_value, g_out, g_up, g_gate, g_down, *gains = hand_over(
        *(got[name] for name in HANDED), got["gain_line"]
    )
    return (
        output.reshape(states.shape),
        d_states.reshape(states.shape),
        g_query.T,
        g_key.T,
        g_value.T,
        g_out,
        g_up,
        g_gate,
        g_down,
        *gains,
    )


def solution(mesh):
    seq, batch = mesh.shape["seq"], mesh.shape["batch"]
    body = on_device_heads if (seq == HEADS and batch == 2) else on_device_general
    return jax.shard_map(
        body,
        mesh=mesh,
        in_specs=(
            P("batch", "seq", None),
            P("batch", None),
            P(None, "seq"),
            P(None, "seq"),
            P(None, "seq"),
            P("seq", None),
            P(None, "seq"),
            P(None, "seq"),
            P("seq", None),
            P(),
            P(),
            P(),
            P(),
            P(),
            P("batch", "seq", None),
        ),
        out_specs=(
            P("batch", "seq", None),
            P("batch", "seq", None),
            P(None, "seq"),
            P(None, "seq"),
            P(None, "seq"),
            P("seq", None),
            P(None, "seq"),
            P(None, "seq"),
            P("seq", None),
            P(),
            P(),
            P(),
            P(),
            P(),
        ),
        check_vma=False,
    )
```

```python
import jax
import jax.numpy as jnp
import numpy as np
from jax import lax
from jax.experimental import pallas as pl
from jax.experimental.pallas import tpu as pltpu
from jax.sharding import PartitionSpec as P

HEADS = 16
HEAD = 64


EPS = 1e-06


def shifted(value, axis, steps):
    count = lax.axis_size(axis)
    first, last = (max(0, -steps), min(count, count - steps))
    return lax.ppermute(value, axis, [(source, source + steps) for source in range(first, last)])


def shifted_2(block, axis, distance):
    devices = range(lax.axis_size(axis))
    route = [((i - distance) % len(devices), i) for i in devices]
    return lax.ppermute(block, axis, route)


def normalized(weight, axis):
    wide = weight.astype(jnp.float32)
    return wide * lax.rsqrt(jnp.sum(wide * wide, axis=axis, keepdims=True) + EPS)


def rms(values):
    return values * lax.rsqrt(jnp.mean(values * values, axis=-1, keepdims=True) + EPS)


def doc_layout(len_row, tok_index):
    docs = jnp.arange(len_row.shape[0])
    starts = jnp.sum(jnp.where(docs[:, None] < docs[None, :], len_row[:, None], 0), axis=0)
    started = starts[None, :] <= tok_index[:, None]
    doc_ids = jnp.sum(started.astype(jnp.int32), axis=1) - 1
    first_tok = jnp.max(jnp.where(started, starts[None, :], 0), axis=1)
    return (doc_ids, tok_index - first_tok)


def rope(values, position):
    half = values.shape[-1] // 2
    freqs = 10000.0 ** (-jnp.arange(half, dtype=jnp.float32) / half)
    angle = position.astype(jnp.float32)[:, None] * freqs[None, :]
    cosine = jnp.cos(angle)[:, None, :]
    sine = jnp.sin(angle)[:, None, :]
    first = values[..., :half]
    second = values[..., half:]
    return jnp.concatenate(
        [first * cosine - second * sine, first * sine + second * cosine], axis=-1
    )


def prepare(linear, position, gain):
    count = linear.shape[0]
    shaped = linear.reshape(count, HEADS, HEAD)
    turned = rms(rope(shaped, position)) * gain.reshape(HEADS, HEAD)
    return turned.reshape(count, HEADS * HEAD)


def residual_mix(state, branch, alpha):
    return rms(state + alpha * (rms(branch) - state))


def gating(up_lin, gate_lin, up_scale, gate_scale):
    return up_scale * up_lin * jax.nn.silu(gate_scale * gate_lin)


def unit_back(raw_shard, grad_shard, axis):
    primal, pullback = jax.vjp(
        lambda weight: normalized(weight, axis), raw_shard.astype(jnp.float32)
    )
    return pullback(grad_shard)[0]


def on_device_general(
    states,
    lengths,
    w_query,
    w_key,
    w_value,
    w_out,
    w_up,
    w_gate,
    w_down,
    qk_scale,
    up_scale,
    gate_scale,
    alpha_attn,
    alpha_mlp,
    d_out,
):
    seq_count = lax.axis_size("seq")
    my_index = lax.axis_index("seq")
    rows = states.shape[0]
    tok = states.shape[1]
    width = states.shape[2]
    flat = rows * tok
    score_scale = HEAD ** (-0.5)
    row_layout = jax.vmap(doc_layout, in_axes=(0, None))
    unit_query = normalized(w_query, 0).astype(jnp.bfloat16)
    unit_key = normalized(w_key, 0).astype(jnp.bfloat16)
    unit_value = normalized(w_value, 0).astype(jnp.bfloat16)
    unit_out = normalized(w_out, 1).astype(jnp.bfloat16)
    unit_up = normalized(w_up, 0).astype(jnp.bfloat16)
    unit_gate = normalized(w_gate, 0).astype(jnp.bfloat16)
    unit_down = normalized(w_down, 1).astype(jnp.bfloat16)
    full_weights = (
        lax.all_gather(unit_query, "seq", axis=1, tiled=True),
        lax.all_gather(unit_key, "seq", axis=1, tiled=True),
        lax.all_gather(unit_value, "seq", axis=1, tiled=True),
        lax.all_gather(unit_out, "seq", axis=0, tiled=True),
        lax.all_gather(unit_up, "seq", axis=1, tiled=True),
        lax.all_gather(unit_gate, "seq", axis=1, tiled=True),
        lax.all_gather(unit_down, "seq", axis=0, tiled=True),
    )
    full_query, full_key, full_value, full_out, full_up, full_gate, full_down = full_weights
    tok_index = my_index * tok + jnp.arange(tok, dtype=jnp.int32)
    doc_ids, position = row_layout(lengths, tok_index)
    flat_pos = position.reshape(flat)
    state_in = states.reshape(flat, width)
    x_low = state_in.astype(jnp.bfloat16)
    query_lin = jnp.dot(x_low, full_query, preferred_element_type=jnp.float32)
    key_lin = jnp.dot(x_low, full_key, preferred_element_type=jnp.float32)
    value_lin = jnp.dot(x_low, full_value, preferred_element_type=jnp.float32)

    def front(query_part, key_part, gain):
        return (prepare(query_part, flat_pos, gain), prepare(key_part, flat_pos, gain))

    query_f, key_f = front(query_lin, key_lin, qk_scale)
    query_h = query_f.astype(jnp.bfloat16).reshape(rows, tok, HEADS, HEAD)
    key_h = key_f.astype(jnp.bfloat16).reshape(rows, tok, HEADS, HEAD)
    value_h = value_lin.astype(jnp.bfloat16).reshape(rows, tok, HEADS, HEAD)

    def block_scores(key_blk, source):
        key_index = source * tok + jnp.arange(tok, dtype=jnp.int32)
        key_docs, key_pos = row_layout(lengths, key_index)
        scores = (
            jnp.einsum("bqhd,bkhd->bqhk", query_h, key_blk, preferred_element_type=jnp.float32)
            * score_scale
        )
        allowed = (doc_ids[:, :, None] == key_docs[:, None, :]) & (
            key_index[None, None, :] <= tok_index[None, :, None]
        )
        return (scores, allowed[:, :, None, :])

    def is_active(source):
        last_key = jnp.reshape(source * tok + tok - 1, (1,))
        last_doc, last_pos = row_layout(lengths, last_key)
        return (source <= my_index) & jnp.any(last_doc[:, 0] >= doc_ids[:, 0])

    def attend(running, key_blk, value_blk, source):

        def compute(carried):
            best, denom_sum, accum = carried
            scores, allowed = block_scores(key_blk, source)
            new_best = jnp.maximum(best, jnp.max(jnp.where(allowed, scores, -1e30), axis=3))
            weights = jnp.where(allowed, jnp.exp(scores - new_best[:, :, :, None]), 0.0)
            shrink = jnp.exp(best - new_best)
            denom_sum = denom_sum * shrink + jnp.sum(weights, axis=3)
            accum = accum * shrink[:, :, :, None] + jnp.einsum(
                "bqhk,bkhd->bqhd",
                weights.astype(jnp.bfloat16),
                value_blk,
                preferred_element_type=jnp.float32,
            )
            return (new_best, denom_sum, accum)

        return lax.cond(is_active(source), compute, lambda carried: carried, running)

    reach = seq_count - 1
    start_state = (
        jnp.full((rows, tok, HEADS), -1e30, jnp.float32),
        jnp.zeros((rows, tok, HEADS), jnp.float32),
        jnp.zeros((rows, tok, HEADS, HEAD), jnp.float32),
    )
    first_state = attend(start_state, key_h, value_h, my_index)

    def cycle_step(step, loop_carry):
        running, key_blk, value_blk = loop_carry
        key_blk, value_blk = shifted((key_blk, value_blk), "seq", 1)
        source = (my_index - step) % seq_count
        return (attend(running, key_blk, value_blk, source), key_blk, value_blk)

    final_state, spent_key, spent_value = lax.fori_loop(
        1, reach + 1, cycle_step, (first_state, key_h, value_h)
    )
    best, denom_sum, accum = final_state
    attended = accum / denom_sum[:, :, :, None]
    log_sum = best + jnp.log(denom_sum)
    attended_low = attended.astype(jnp.bfloat16).reshape(flat, width)
    attn_branch = jnp.dot(attended_low, full_out, preferred_element_type=jnp.float32)
    state_mid = residual_mix(state_in, attn_branch, alpha_attn)
    mid_low = state_mid.astype(jnp.bfloat16)
    up_lin = jnp.dot(mid_low, full_up, preferred_element_type=jnp.float32)
    gate_lin = jnp.dot(mid_low, full_gate, preferred_element_type=jnp.float32)
    gated_low = gating(up_lin, gate_lin, up_scale, gate_scale).astype(jnp.bfloat16)
    mlp_branch = jnp.dot(gated_low, full_down, preferred_element_type=jnp.float32)
    output = residual_mix(state_mid, mlp_branch, alpha_mlp)
    back_weights = (
        lax.all_gather(unit_query, "seq", axis=1, tiled=True),
        lax.all_gather(unit_key, "seq", axis=1, tiled=True),
        lax.all_gather(unit_value, "seq", axis=1, tiled=True),
        lax.all_gather(unit_out, "seq", axis=0, tiled=True),
        lax.all_gather(unit_up, "seq", axis=1, tiled=True),
        lax.all_gather(unit_gate, "seq", axis=1, tiled=True),
        lax.all_gather(unit_down, "seq", axis=0, tiled=True),
    )
    back_query, back_key, back_value, back_out, back_up, back_gate, back_down = back_weights
    primal, pull_mlp = jax.vjp(residual_mix, state_mid, mlp_branch, alpha_mlp)
    d_mid, d_mlp, g_alpha_mlp = pull_mlp(d_out.reshape(flat, width))
    d_mlp_low = d_mlp.astype(jnp.bfloat16)
    grad_down = jnp.einsum("tf,td->fd", gated_low, d_mlp_low, preferred_element_type=jnp.float32)
    d_gated = jnp.einsum("td,fd->tf", d_mlp_low, back_down, preferred_element_type=jnp.float32)
    primal, pull_gate = jax.vjp(gating, up_lin, gate_lin, up_scale, gate_scale)
    d_up, d_gate, g_up_scale, g_gate_scale = pull_gate(d_gated)
    d_up_low = d_up.astype(jnp.bfloat16)
    d_gate_low = d_gate.astype(jnp.bfloat16)
    grad_up = jnp.einsum("tc,tf->cf", mid_low, d_up_low, preferred_element_type=jnp.float32)
    grad_gate = jnp.einsum("tc,tf->cf", mid_low, d_gate_low, preferred_element_type=jnp.float32)
    d_mid = d_mid + jnp.einsum("tf,cf->tc", d_up_low, back_up, preferred_element_type=jnp.float32)
    d_mid = d_mid + jnp.einsum(
        "tf,cf->tc", d_gate_low, back_gate, preferred_element_type=jnp.float32
    )
    primal, pull_attn = jax.vjp(residual_mix, state_in, attn_branch, alpha_attn)
    d_state, d_attn, g_alpha_attn = pull_attn(d_mid)
    d_attn_low = d_attn.astype(jnp.bfloat16)
    grad_out = jnp.einsum("tc,td->cd", attended_low, d_attn_low, preferred_element_type=jnp.float32)
    d_attended = jnp.einsum("td,cd->tc", d_attn_low, back_out, preferred_element_type=jnp.float32)
    d_att_low = d_attended.astype(jnp.bfloat16).reshape(rows, tok, HEADS, HEAD)
    delta = jnp.sum(d_att_low.astype(jnp.float32) * attended, axis=3)

    def attend_back(d_query, key_blk, value_blk, d_key, d_value, source):

        def compute(carried):
            d_query, d_key, d_value = carried
            scores, allowed = block_scores(key_blk, source)
            probs = jnp.where(allowed, jnp.exp(scores - log_sum[:, :, :, None]), 0.0)
            d_probs = jnp.einsum(
                "bqhd,bkhd->bqhk", d_att_low, value_blk, preferred_element_type=jnp.float32
            )
            d_scores = (probs * (d_probs - delta[:, :, :, None])).astype(jnp.bfloat16)
            d_query = d_query + jnp.einsum(
                "bqhk,bkhd->bqhd", d_scores, key_blk, preferred_element_type=jnp.float32
            )
            d_key = d_key + jnp.einsum(
                "bqhk,bqhd->bkhd", d_scores, query_h, preferred_element_type=jnp.float32
            )
            d_value = d_value + jnp.einsum(
                "bqhk,bqhd->bkhd",
                probs.astype(jnp.bfloat16),
                d_att_low,
                preferred_element_type=jnp.float32,
            )
            return (d_query, d_key, d_value)

        return lax.cond(
            is_active(source), compute, lambda carried: carried, (d_query, d_key, d_value)
        )

    def back_step(step, loop_carry):
        d_query, key_blk, value_blk, d_key, d_value = loop_carry
        source = (my_index - step) % seq_count
        d_query, d_key, d_value = attend_back(d_query, key_blk, value_blk, d_key, d_value, source)
        d_key, d_value = (
            shifted_2(d_key.astype(jnp.bfloat16), "seq", 1).astype(d_key.dtype),
            shifted_2(d_value.astype(jnp.bfloat16), "seq", 1).astype(d_value.dtype),
        )
        key_blk, value_blk = shifted((key_blk, value_blk), "seq", 1)
        return (d_query, key_blk, value_blk, d_key, d_value)

    zero_heads = jnp.zeros((rows, tok, HEADS, HEAD), jnp.float32)
    d_query_h, last_key_blk, last_value_blk, d_key_h, d_value_h = lax.fori_loop(
        0, reach, back_step, (zero_heads, key_h, value_h, zero_heads, zero_heads)
    )
    d_query_h, d_key_h, d_value_h = attend_back(
        d_query_h, last_key_blk, last_value_blk, d_key_h, d_value_h, (my_index - reach) % seq_count
    )
    d_key_h, d_value_h = (
        shifted_2(d_key_h.astype(jnp.bfloat16), "seq", -reach).astype(d_key_h.dtype),
        shifted_2(d_value_h.astype(jnp.bfloat16), "seq", -reach).astype(d_value_h.dtype),
    )
    primal, pull_front = jax.vjp(front, query_lin, key_lin, qk_scale)
    d_query_lin, d_key_lin, g_qk_scale = pull_front(
        (d_query_h.reshape(flat, width) * score_scale, d_key_h.reshape(flat, width) * score_scale)
    )
    d_query_low = d_query_lin.astype(jnp.bfloat16)
    d_key_low = d_key_lin.astype(jnp.bfloat16)
    d_value_low = d_value_h.reshape(flat, width).astype(jnp.bfloat16)
    grad_query = jnp.einsum("tc,tj->cj", x_low, d_query_low, preferred_element_type=jnp.float32)
    grad_key = jnp.einsum("tc,tj->cj", x_low, d_key_low, preferred_element_type=jnp.float32)
    grad_value = jnp.einsum("tc,tj->cj", x_low, d_value_low, preferred_element_type=jnp.float32)
    d_state = d_state + jnp.einsum(
        "tj,cj->tc", d_query_low, back_query, preferred_element_type=jnp.float32
    )
    d_state = d_state + jnp.einsum(
        "tj,cj->tc", d_key_low, back_key, preferred_element_type=jnp.float32
    )
    d_state = d_state + jnp.einsum(
        "tj,cj->tc", d_value_low, back_value, preferred_element_type=jnp.float32
    )
    shards = (
        lax.psum_scatter(
            grad_query.astype(jnp.bfloat16), "seq", scatter_dimension=1, tiled=True
        ).astype(jnp.float32),
        lax.psum_scatter(
            grad_key.astype(jnp.bfloat16), "seq", scatter_dimension=1, tiled=True
        ).astype(jnp.float32),
        lax.psum_scatter(
            grad_value.astype(jnp.bfloat16), "seq", scatter_dimension=1, tiled=True
        ).astype(jnp.float32),
        lax.psum_scatter(
            grad_out.astype(jnp.bfloat16), "seq", scatter_dimension=0, tiled=True
        ).astype(jnp.float32),
        lax.psum_scatter(
            grad_up.astype(jnp.bfloat16), "seq", scatter_dimension=1, tiled=True
        ).astype(jnp.float32),
        lax.psum_scatter(
            grad_gate.astype(jnp.bfloat16), "seq", scatter_dimension=1, tiled=True
        ).astype(jnp.float32),
        lax.psum_scatter(
            grad_down.astype(jnp.bfloat16), "seq", scatter_dimension=0, tiled=True
        ).astype(jnp.float32),
    )
    summed = (
        lax.psum(shards[0].astype(jnp.bfloat16), "batch").astype(jnp.float32),
        lax.psum(shards[1].astype(jnp.bfloat16), "batch").astype(jnp.float32),
        lax.psum(shards[2].astype(jnp.bfloat16), "batch").astype(jnp.float32),
        lax.psum(shards[3].astype(jnp.bfloat16), "batch").astype(jnp.float32),
        lax.psum(shards[4].astype(jnp.bfloat16), "batch").astype(jnp.float32),
        lax.psum(shards[5].astype(jnp.bfloat16), "batch").astype(jnp.float32),
        lax.psum(shards[6].astype(jnp.bfloat16), "batch").astype(jnp.float32),
    )
    gain_grads = lax.psum(
        (g_qk_scale, g_up_scale, g_gate_scale, g_alpha_attn, g_alpha_mlp), ("seq", "batch")
    )
    g_query = unit_back(w_query, summed[0], 0)
    g_key = unit_back(w_key, summed[1], 0)
    g_value = unit_back(w_value, summed[2], 0)
    g_out = unit_back(w_out, summed[3], 1)
    g_up = unit_back(w_up, summed[4], 0)
    g_gate = unit_back(w_gate, summed[5], 0)
    g_down = unit_back(w_down, summed[6], 1)
    return (
        output.reshape(rows, tok, width),
        d_state.reshape(rows, tok, width),
        g_query,
        g_key,
        g_value,
        g_out,
        g_up,
        g_gate,
        g_down,
        gain_grads[0],
        gain_grads[1],
        gain_grads[2],
        gain_grads[3],
        gain_grads[4],
    )


BF16 = jnp.bfloat16
F32 = jnp.float32
LANES = 128
MIB = 1 << 20
NT = (((1,), (1,)), ((), ()))
TN = (((0,), (0,)), ((), ()))


def place():
    s = lax.axis_index("seq")
    return s // 4, (s // 2) % 2, s % 2, lax.axis_index("batch")


def dev(z, x, c, y):
    return (z * 4 + x * 2 + c, y)


def remote(src, dst, send, recv, device):
    return pltpu.make_async_remote_copy(
        src_ref=src,
        dst_ref=dst,
        send_sem=send,
        recv_sem=recv,
        device_id=device,
        device_id_type=pl.DeviceIdType.MESH,
    )


def dot(a, b):
    return jnp.dot(a, b, preferred_element_type=F32)


def dot_nt(a, b):
    return lax.dot_general(a, b, NT, preferred_element_type=F32)


def dot_tn(a, b):
    return lax.dot_general(a, b, TN, preferred_element_type=F32)


BLOCK = 256


def inverse_norm(weight, axis):
    wide = weight.astype(F32)
    return lax.rsqrt(jnp.sum(wide * wide, axis=axis, keepdims=True) + EPS)


def unit_pull(weight, grad, axis):
    inverse = inverse_norm(weight, axis)
    unit = weight.astype(F32) * inverse
    return inverse * (grad - unit * jnp.sum(grad * unit, axis=axis, keepdims=True))


def turn_tables(count):
    half = HEAD // 2
    freqs = (10000.0 ** (-np.arange(half, dtype=np.float32) / half)).astype(np.float32)
    angle = np.arange(count, dtype=np.float32)[:, None] * freqs[None, :]
    cosine = np.cos(angle).astype(np.float32)
    sine = np.sin(angle).astype(np.float32)
    return np.tile(cosine, (1, 4)), np.concatenate([-sine, sine, -sine, sine], axis=1)


def mix(state, branch, alpha):
    inv_b = lax.rsqrt(jnp.mean(branch * branch, axis=-1, keepdims=True) + EPS)
    unit_b = branch * inv_b
    step = unit_b - state
    mixed = state + alpha * step
    inv_m = lax.rsqrt(jnp.mean(mixed * mixed, axis=-1, keepdims=True) + EPS)
    return mixed * inv_m, (unit_b, inv_b, step, inv_m)


def mix_back(grad, out, saved, alpha):
    unit_b, inv_b, step, inv_m = saved
    d_mixed = inv_m * (grad - out * jnp.mean(grad * out, axis=-1, keepdims=True))
    d_alpha = jnp.sum(d_mixed * step, axis=0)
    d_unit = d_mixed * alpha
    d_branch = inv_b * (d_unit - unit_b * jnp.mean(d_unit * unit_b, axis=-1, keepdims=True))
    return d_mixed - d_unit, d_branch, d_alpha


def inside(v):
    return (v >= 0) & (v < 4)


def unit_cols(w):
    wide = w.astype(F32)
    return (wide * lax.rsqrt(jnp.sum(wide * wide, axis=0, keepdims=True) + EPS)).astype(BF16)


def unit_rows(w):
    wide = w.astype(F32)
    return (wide * lax.rsqrt(jnp.sum(wide * wide, axis=1, keepdims=True) + EPS)).astype(BF16)


SUBS = 2


class Line:
    def __init__(self, buf, sems):
        self.buf, (self.send, self.recv) = buf, sems

    def hop(self, zz, way, n):
        z, x, c, y = place()
        size = self.buf.shape[1] // SUBS
        b = self.buf.at[zz, n * size : (n + 1) * size]
        return remote(
            b, b, self.send.at[zz, (way + 1) // 2, n], self.recv.at[zz, n], dev(z + way, x, c, y)
        )

    def start(self):
        z = place()[0]
        for n in range(SUBS):
            for way in (-1, 1):

                @pl.when(inside(z + way))
                def _():
                    self.hop(z, way, n).start()

    def arrive(self, k):
        z = place()[0]
        for n in range(SUBS):
            for way in (-1, 1):
                zz = z - way * k

                @pl.when(inside(zz))
                def _():
                    self.hop(zz, -way, n).wait_recv()

                    @pl.when(inside(z + way))
                    def _():
                        self.hop(zz, way, n).start()

    def drain(self):
        z = place()[0]
        for zz in range(4):
            for way in (-1, 1):

                @pl.when(((zz - z) * way <= 0) & inside(z + way))
                def _():
                    for n in range(SUBS):
                        self.hop(zz, way, n).wait_send()


class Column:
    def __init__(self, buf, sems):
        self.buf, (self.zs, self.cs, self.recv) = buf, sems

    def hop_z(self, zz, way):
        z, x, c, y = place()
        b = 2 * zz + c
        return remote(
            self.buf.at[b], self.buf.at[b], self.zs.at[zz, (way + 1) // 2], self.recv.at[b],
            dev(z + way, x, c, y),
        )

    def hop_c(self, zz):
        z, x, c, y = place()
        b = 2 * zz + c
        return remote(
            self.buf.at[b], self.buf.at[b], self.cs.at[zz], self.recv.at[b], dev(z, x, 1 - c, y)
        )

    def arrived(self, b):
        z, x, c, y = place()
        remote(
            self.buf.at[b], self.buf.at[b], self.cs.at[0], self.recv.at[b], dev(z, x, 1 - c, y)
        ).wait_recv()

    def start(self):
        z = place()[0]
        for way in (-1, 1):

            @pl.when(inside(z + way))
            def _():
                self.hop_z(z, way).start()

        self.hop_c(z).start()

    def arrive(self, k):
        z, x, c, y = place()
        for way in (-1, 1):
            zz = z - way * k

            @pl.when(inside(zz))
            def _():
                self.arrived(2 * zz + c)

                @pl.when(inside(z + way))
                def _():
                    self.hop_z(zz, way).start()

                self.hop_c(zz).start()

    def finish(self):
        z, x, c, y = place()

        @pl.loop(0, 4)
        def _(zz):
            self.arrived(2 * zz + 1 - c)
            for way in (-1, 1):

                @pl.when(((zz - z) * way <= 0) & inside(z + way))
                def _():
                    self.hop_z(zz, way).wait_send()

            self.hop_c(zz).wait_send()


def greet_row():
    z, x, c, y = place()
    s = z * 4 + x * 2 + c
    bar = pltpu.get_barrier_semaphore()

    @pl.loop(1, 16)
    def _(k):
        pl.semaphore_signal(
            bar, inc=1, device_id=((s + k) % 16, y), device_id_type=pl.DeviceIdType.MESH
        )

    pl.semaphore_signal(bar, inc=1, device_id=dev(z, x, c, 1 - y), device_id_type=pl.DeviceIdType.MESH)


def half_swap(value):
    lane = lax.broadcasted_iota(jnp.int32, value.shape, 1)
    return jnp.where(
        lane % HEAD < HEAD // 2, pltpu.roll(value, LANES - HEAD // 2, 1), pltpu.roll(value, HEAD // 2, 1)
    )


def head_means(value):
    lane = lax.broadcasted_iota(jnp.int32, value.shape, 1)
    first = jnp.sum(jnp.where(lane < HEAD, value, 0.0), axis=1, keepdims=True)
    both = jnp.sum(value, axis=1, keepdims=True)
    return jnp.where(lane < HEAD, first, both - first) * (1.0 / HEAD)


def side_by_side(block):
    half = block.shape[0] // 2
    lane = lax.broadcasted_iota(jnp.int32, (half, LANES), 1)
    return jnp.where(lane < HEAD, block[:half], pltpu.roll(block[half:], HEAD, 1))


def peers():
    z, x, c, y = place()
    return ((x, 1 - c), (1 - x, c), (1 - x, 1 - c))


def spread_heads(b, env):
    rows = pl.ds(pl.multiple_of(b * LANES, LANES), LANES)
    lane = lax.broadcasted_iota(jnp.int32, (LANES, LANES), 1)
    one = jnp.where(lane < HEAD + 2, 1.0, 0.0)
    qk = env.heads_in[b, 0:LANES, :].astype(F32)
    env.q_ext[rows, :] = jnp.where(lane < HEAD, qk, 0.0).astype(BF16)
    env.k_ext[rows, :] = jnp.where(lane < HEAD, pltpu.roll(qk, HEAD, 1), one).astype(BF16)
    packed = env.heads_in[b, LANES:, :].astype(F32)
    value = jnp.concatenate([packed, pltpu.roll(packed, HEAD, 1)], axis=0)
    env.v_ext[rows, :] = jnp.where(lane < HEAD, value, one).astype(BF16)


class Reduce:
    def __init__(self, part, passing, landed, send, recv):
        self.part, self.passing, self.landed, self.send, self.recv = part, passing, landed, send, recv
        self.size = passing.shape[1] // SUBS

    def rows(self, n):
        return slice(n * self.size, (n + 1) * self.size)

    def hop(self, owner, way, n):
        z, x, c, y = place()
        spot = jnp.where((owner == z + way) & (way < 0), 4, owner)
        return remote(
            self.passing.at[owner, self.rows(n)], self.landed.at[spot, self.rows(n)],
            self.send.at[owner, n], self.recv.at[spot, n], dev(z + way, x, c, y),
        )

    def wait_spot(self, spot, n):
        z, x, c, y = place()
        remote(
            self.passing.at[0, self.rows(n)], self.landed.at[spot, self.rows(n)], self.send.at[0, n],
            self.recv.at[spot, n], dev(z, x, 1 - c, y),
        ).wait_recv()

    def step(self, k):
        z = place()[0]
        for n in range(SUBS):
            rows = self.rows(n)
            for way in (-1, 1):
                owner = z + way * k

                @pl.when(inside(owner))
                def _():
                    @pl.when(inside(z - way))
                    def _():
                        self.wait_spot(owner, n)
                        self.passing[owner, rows] = (
                            self.part(owner, rows) + self.landed[owner, rows].astype(F32)
                        ).astype(BF16)

                    @pl.when(jnp.logical_not(inside(z - way)))
                    def _():
                        self.passing[owner, rows] = self.part(owner, rows).astype(BF16)

                    self.hop(owner, way, n).start()

    def finish(self, total):
        z = place()[0]
        everything = slice(0, SUBS * self.size)
        total[...] = self.part(z, everything)
        for edge, spot in ((z > 0, z), (z < 3, 4)):

            @pl.when(edge)
            def _():
                for n in range(SUBS):
                    self.wait_spot(spot, n)
                total[...] += self.landed[spot].astype(F32)

        for owner in range(4):

            @pl.when(owner != z)
            def _():
                for n in range(SUBS):
                    self.hop(owner, jnp.where(owner > z, 1, -1), n).wait_send()


class Env:
    def __init__(self, names, refs):
        for name, ref in zip(names, refs, strict=True):
            setattr(self, name, ref)


def window(start, size):
    return pl.ds(pl.multiple_of(start, size), size)


def qkv_rows(slot):
    return window(slot * LANES, LANES), window(4 * LANES + slot * HEAD, HEAD)


def qkv_copies(env, slot, sems, device):
    (send, recv), spots = sems, qkv_rows(slot)
    return [
        remote(env.u_qkv.at[rows, :], env.u_qkv.at[rows, :], send.at[i], recv.at[i], device)
        for i, rows in enumerate(spots)
    ]


def qkv_groups(env):
    z, x, c, y = place()
    mine, other = 2 * x + c, 2 * (1 - x) + c
    core, side = dev(z, x, 1 - c, y), dev(z, 1 - x, c, y)
    s, r = env.q_send, env.q_recv
    return (
        qkv_copies(env, mine, (s.at[0], r.at[0]), core),
        qkv_copies(env, mine, (s.at[1], r.at[1]), side),
        qkv_copies(env, other, (s.at[2], r.at[2]), core),
    )


def ff_views(env, slot, half=None):
    if half is None:
        return env.ups.at[slot], env.gates.at[slot], env.downs.at[slot]
    upper, lower = window(half * 512, 512), window(half * 128, 128)
    return env.ups.at[slot, upper, :], env.gates.at[slot, upper, :], env.downs.at[slot, lower, :]


def ff_groups(env):
    z, x, c, y = place()
    mine, other = 2 * x + c, 2 * (1 - x) + c
    core, side, twin = dev(z, x, 1 - c, y), dev(z, 1 - x, c, y), dev(z, x, c, 1 - y)

    def group(g, views, device):
        return [
            remote(v, v, env.w_send.at[g, i], env.w_recv.at[g, i], device) for i, v in enumerate(views)
        ]

    return (
        group(0, ff_views(env, mine), core),
        group(1, ff_views(env, mine, y), side),
        group(2, ff_views(env, other, y), core),
        group(3, ff_views(env, other, y), twin),
        group(4, ff_views(env, other, 1 - y), core),
    )


def each(copies, action):
    for copy in copies:
        getattr(copy, action)()


class Piece:
    def __init__(self, view, land_c, land_y, land_x, out, sems, whole):
        self.view, self.land_c, self.land_y, self.land_x, self.out = view, land_c, land_y, land_x, out
        (self.send, self.recv), self.whole = sems, whole

    def total(self):
        return self.whole[...].astype(F32)

    def slot(self, h):
        z, x, c, y = place()
        return 2 * (1 - x if h == 0 else x) + c

    def to_core(self, h):
        z, x, c, y = place()
        xx = 1 - x if h == 0 else x
        return remote(
            self.view(2 * xx + 1 - c, None), self.land_c.at[h], self.send.at[h], self.recv.at[h],
            dev(z, x, 1 - c, y),
        )

    def to_twin(self, h):
        z, x, c, y = place()
        return remote(
            self.view(self.slot(h), 1 - y), self.land_y.at[h], self.send.at[2 + h], self.recv.at[2 + h],
            dev(z, x, c, 1 - y),
        )

    def to_side(self):
        z, x, c, y = place()
        return remote(
            self.view(self.slot(0), y), self.land_x, self.send.at[4], self.recv.at[4], dev(z, 1 - x, c, y)
        )

    def swap(self):
        z, x, c, y = place()
        return remote(self.out(y), self.out(y), self.send.at[5], self.recv.at[5], dev(z, x, c, 1 - y))

    def start(self):
        self.to_core(0).start()
        self.to_core(1).start()

    def pass_twin(self):
        for h in range(2):
            self.to_core(h).wait_recv()
            both = self.view(self.slot(h), None)
            both[...] = (both[...].astype(F32) + self.land_c[h].astype(F32)).astype(BF16)
            self.to_twin(h).start()

    def pass_side(self):
        y = place()[3]
        self.to_twin(0).wait_recv()
        give = self.view(self.slot(0), y)
        give[...] = (give[...].astype(F32) + self.land_y[0].astype(F32)).astype(BF16)
        self.to_side().start()

    def pass_back(self):
        y = place()[3]
        self.to_twin(1).wait_recv()
        self.to_side().wait_recv()
        keep = self.view(self.slot(1), y)
        self.out(y)[...] = (
            keep[...].astype(F32) + self.land_y[1].astype(F32) + self.land_x[...].astype(F32)
        ).astype(BF16)
        self.swap().start()

    def finish(self):
        self.swap().wait()
        for h in range(2):
            self.to_core(h).wait_send()
            self.to_twin(h).wait_send()
        self.to_side().wait_send()


class SidePiece(Piece):
    def total(self):
        return self.whole[...].astype(F32) + self.land_y[0].astype(F32)

    def to_side(self):
        z, x, c, y = place()
        return remote(
            self.view(self.slot(0), None), self.land_x, self.send.at[4], self.recv.at[4], dev(z, 1 - x, c, y)
        )

    def swap(self):
        z, x, c, y = place()
        return remote(
            self.whole, self.land_y.at[0], self.send.at[5], self.recv.at[5], dev(z, x, c, 1 - y)
        )

    def pass_first(self):
        self.to_core(0).wait_recv()
        give = self.view(self.slot(0), None)
        give[...] = (give[...].astype(F32) + self.land_c[0].astype(F32)).astype(BF16)
        self.to_side().start()

    def pass_back(self):
        self.to_core(1).wait_recv()
        self.to_side().wait_recv()
        keep = self.view(self.slot(1), None)
        self.whole[...] = (
            keep[...].astype(F32) + self.land_c[1].astype(F32) + self.land_x[...].astype(F32)
        ).astype(BF16)
        self.swap().start()

    def finish(self):
        self.swap().wait()
        for h in range(2):
            self.to_core(h).wait_send()
        self.to_side().wait_send()


def project_block(zz, env):
    z, x, c, y = place()
    linear = dot_nt(env.x_line[zz], env.u_qkv[...])
    lane = lax.broadcasted_iota(jnp.int32, (LANES, LANES), 1)
    scale = jnp.where(lane < HEAD, HEAD ** (-0.5), 1.0)
    cosine, sine = env.cosine[zz], env.sine[zz]
    for sl in range(4):
        qk = linear[:, sl * LANES : (sl + 1) * LANES]
        turned = qk * cosine + half_swap(qk) * sine
        env.turned[zz, sl] = turned
        unit = turned * lax.rsqrt(head_means(turned * turned) + EPS)
        out = (unit * env.gain[sl : sl + 1, :]).astype(BF16).astype(F32) * scale
        env.heads_out[zz, sl, 0:LANES, :] = out.astype(BF16)
        pair = linear[:, (4 + sl // 2) * LANES : (5 + sl // 2) * LANES]
        if sl % 2:
            pair = pltpu.roll(pair, HEAD, 1)
        env.heads_out[zz, sl, LANES:, :] = side_by_side(pair).astype(BF16)
    b = zz * 4 + x * 2 + c
    env.heads_in[b] = env.heads_out[zz, x * 2 + c]
    for i, (xx, cc) in enumerate(peers()):
        remote(
            env.heads_out.at[zz, xx * 2 + cc], env.heads_in.at[b], env.hs.at[zz, i], env.hr.at[b],
            dev(z, xx, cc, y),
        ).start()


def attend_block(i, env):
    z, x, c, y = place()
    s = z * 4 + x * 2 + c
    row = lax.broadcasted_iota(jnp.int32, (BLOCK, BLOCK), 0)
    col = lax.broadcasted_iota(jnp.int32, (BLOCK, BLOCK), 1)
    lane = lax.broadcasted_iota(jnp.int32, (BLOCK, LANES), 1)
    rows = pl.ds(i * BLOCK, BLOCK)
    q = env.q_ext[rows, :]
    total = jnp.zeros((BLOCK, LANES), F32)
    for j in range(i + 1):
        keys = pl.ds(j * BLOCK, BLOCK)
        p = jnp.exp(dot_nt(q, env.k_ext[keys, :]))
        if i == j:
            p = jnp.where(row >= col, p, 0.0)
        total = total + dot(p.astype(BF16), env.v_ext[keys, :])
    denom = total[:, HEAD : HEAD + 1]
    out = total / denom
    env.attended[rows, :] = out
    log = -jnp.log(denom)
    high = log.astype(BF16).astype(F32)
    env.q_ext[rows, :] = jnp.where(
        lane == HEAD, high, jnp.where(lane == HEAD + 1, log - high, q.astype(F32))
    ).astype(BF16)
    for k in range(2):
        t = 2 * i + k
        env.att_out[t] = side_by_side(out[k * LANES : (k + 1) * LANES]).astype(BF16)
        send_block(t, env.att_out, env.att_in, env.as_, env.ar)


def block_of(b):
    return b // 4, (b // 2) % 2, b % 2


def send_block(b, src, land, send, recv):
    z, x, c, y = place()
    zz, xx, cc = block_of(b)
    own = (zz == z) & (cc == c)
    j = 2 * z + c

    @pl.when(jnp.logical_not(own))
    def _():
        remote(src.at[b], land.at[xx, j], send.at[b], recv.at[xx, j], dev(zz, x, cc, y)).start()

    @pl.when(own)
    def _():
        land[xx, j] = src[b]


def wait_blocks(src, land, send, recv):
    z, x, c, y = place()

    @pl.loop(0, 16)
    def _(b):
        zz, xx, cc = block_of(b)

        @pl.when(jnp.logical_not((zz == z) & (cc == c)))
        def _():
            j = 2 * zz + cc
            remote(src.at[b], land.at[xx, j], send.at[b], recv.at[xx, j], dev(zz, x, cc, y)).wait()


def lay_heads(land, dst):
    lane = lax.broadcasted_iota(jnp.int32, (HEAD, LANES), 1)
    for xx in range(2):
        for p in range(4):
            first = land[xx, 2 * p].astype(F32)
            second = land[xx, 2 * p + 1].astype(F32)
            cols = slice(p * LANES, (p + 1) * LANES)
            dst[xx, 0:HEAD, cols] = jnp.where(lane < HEAD, first, pltpu.roll(second, HEAD, 1)).astype(BF16)
            dst[xx, HEAD:, cols] = jnp.where(lane < HEAD, pltpu.roll(first, HEAD, 1), second).astype(BF16)


def grads_copy(b, target, env):
    x, y = place()[1], place()[3]
    xx = block_of(b)[1]
    j = 2 * target[0] + target[1]
    return remote(
        env.datt_out.at[xx, j], env.datt_in.at[b], env.das.at[xx, j], env.dar.at[b],
        dev(target[0], x, target[1], y),
    )


def send_grads(xx, env):
    z, x, c, y = place()
    b = 4 * z + 2 * xx + c
    for p in range(2):
        d_att = dot_nt(env.d_both[xx], env.u_out[4 * p : 4 * p + 4].reshape(256, 1024))
        for k in range(4):
            value = d_att[:, (k // 2) * LANES : (k // 2 + 1) * LANES]
            if k % 2:
                value = pltpu.roll(value, HEAD, 1)
            j = 4 * p + k
            env.datt_out[xx, j] = side_by_side(value).astype(BF16)
            own = 2 * z + c == j

            @pl.when(own)
            def _():
                env.datt_in[b] = env.datt_out[xx, j]

            @pl.when(jnp.logical_not(own))
            def _():
                grads_copy(b, (j // 2, j % 2), env).start()


def wait_grads(b, env):
    z, x, c, y = place()
    zz, xx, cc = block_of(b)

    @pl.when(jnp.logical_not((zz == z) & (cc == c)))
    def _():
        grads_copy(b, (zz, cc), env).wait()


def side_rows(h, env):
    z, x, c, y = place()
    rows = env.d_both.at[x, rows_of(h), :]
    return remote(rows, rows, env.db_s.at[h], env.db_r.at[h], dev(z, 1 - x, c, y))


def side_mix(h, env):
    z, x, c, y = place()
    return remote(
        env.mix_out.at[h], env.mix_in.at[h], env.mx_s.at[h], env.mx_r.at[h], dev(z, 1 - x, c, y)
    )


def mlp_forward(h, env):
    @pl.loop(0, 4)
    def _(n):
        cols = window(n * 256, 256)
        mid = env.h_line[h].reshape(256, 1024)
        up = dot(mid, env.ups[n])
        gate = dot(mid, env.gates[n]) * env.gate_row[:, cols]
        env.up_lin[h, cols, :] = up
        env.gate_val[h, :, cols] = gate
        act = gate * (1.0 / (1.0 + jnp.exp(-gate)))
        env.hidden[h, :, cols] = (up * env.up_row[:, cols] * act).astype(BF16)

    @pl.loop(0, 4)
    def _(n):
        cols = window(n * 256, 256)
        env.part[h, :, :, cols] = dot(env.hidden[h], env.downs[:, :, cols].reshape(1024, 256)).reshape(
            4, 64, 256
        )


def mlp_backward(h, env):
    @pl.loop(0, 4)
    def _(n):
        cols = window(n * 256, 256)
        d_hidden = dot_nt(env.dm_line[h].reshape(256, 1024), env.downs[n])
        up, gate = env.up_lin[h, cols, :], env.gate_val[h, :, cols]
        up_gain, gate_gain = env.up_row[:, cols], env.gate_row[:, cols]
        sig = 1.0 / (1.0 + jnp.exp(-gate))
        d_up = d_hidden * (gate * sig)
        d_gate = d_hidden * (up * up_gain) * (sig * (1.0 + gate * (1.0 - sig)))
        env.gains[0:1, cols] += jnp.sum(d_up * up, axis=0, keepdims=True)
        env.gains[1:2, cols] += jnp.sum(d_gate * gate, axis=0, keepdims=True) / gate_gain
        env.d_up[h, n] = (d_up * up_gain).astype(BF16)
        env.d_gate[h, n] = (d_gate * gate_gain).astype(BF16)

    @pl.loop(0, 4)
    def _(n):
        cols = window(n * 256, 256)
        back = dot_nt(env.d_up[h, 0], env.ups[0, cols, :])
        for m in range(4):
            if m:
                back = back + dot_nt(env.d_up[h, m], env.ups[m, cols, :])
            back = back + dot_nt(env.d_gate[h, m], env.gates[m, cols, :])
        env.part[h, :, :, cols] = back.reshape(4, 64, 256)


def weight_gradient(left, right, out, first):
    @pl.loop(0, 4)
    def _(n):
        value = dot_tn(left, right(n))
        ref = out(n)
        if not first:
            value = value + ref[...].astype(F32).reshape(1024, 256)
        ref[...] = value.astype(BF16).reshape(ref.shape)


def grad_down_half(h, env):
    def right(n):
        return env.dm_line[h, :, :, window(n * 256, 256)].reshape(256, 256)

    weight_gradient(
        env.hidden[h], right, lambda n: env.g_down.at[:, :, window(n * 256, 256)], h == 0
    )


def grad_wide_half(h, src, out, env):
    weight_gradient(
        env.h_line[h].reshape(256, 1024), lambda n: src[h, n], lambda n: out.at[n], h == 0
    )


def rows_of(h):
    return slice(64 * h, 64 * (h + 1))


def after_forward(h, reduce, env):
    z, rows = place()[0], rows_of(h)
    reduce.finish(env.total)
    alpha = env.mix_row[1:2, :]
    out, saved = mix(env.mid[rows, :], env.total[...], alpha)
    env.output[rows, :] = out
    d_mid, d_branch, d_alpha = mix_back(env.d_out[rows, :], out, saved, alpha)
    env.d_mid[rows, :] = d_mid
    env.gains[3:4, :] += d_alpha[None, :]
    env.dm_line[h, z] = d_branch.astype(BF16)


def after_backward(h, reduce, env):
    rows = rows_of(h)
    reduce.finish(env.total)
    alpha = env.mix_row[0:1, :]
    mid, saved = mix(env.states[rows, :], env.branch[rows, :], alpha)
    d_state, d_branch, d_alpha = mix_back(env.d_mid[rows, :] + env.total[...], mid, saved, alpha)
    env.d_states[rows, :] = d_state
    env.gains[2:3, :] += d_alpha[None, :]
    env.d_both[place()[1], rows, :] = d_branch.astype(BF16)
    side_rows(h, env).start()


def spread_grads(b, env):
    rows = pl.ds(b * LANES, LANES)
    lane = lax.broadcasted_iota(jnp.int32, (LANES, LANES), 1)
    packed = env.datt_in[b].astype(F32)
    value = jnp.where(lane < HEAD, jnp.concatenate([packed, pltpu.roll(packed, HEAD, 1)], axis=0), 0.0)
    delta = -jnp.sum(value * env.attended[rows, :], axis=1, keepdims=True)
    high = delta.astype(BF16).astype(F32)
    env.do_ext[rows, :] = jnp.where(
        lane == HEAD, high, jnp.where(lane == HEAD + 1, delta - high, value)
    ).astype(BF16)


def attend_back_block(i, env, last):
    z, x, c, y = place()
    row = lax.broadcasted_iota(jnp.int32, (BLOCK, BLOCK), 0)
    col = lax.broadcasted_iota(jnp.int32, (BLOCK, BLOCK), 1)
    lane = lax.broadcasted_iota(jnp.int32, (LANES, LANES), 1)
    rows = pl.ds(i * BLOCK, BLOCK)
    q = env.q_ext[rows, :]
    do = env.do_ext[rows, :]
    dq = jnp.zeros((BLOCK, LANES), F32)
    for j in range(i + 1):
        keys = pl.ds(j * BLOCK, BLOCK)
        k = env.k_ext[keys, :]
        p = jnp.exp(dot_nt(k, q))
        if i == j:
            p = jnp.where(row <= col, p, 0.0)
        ds = (p * dot_nt(env.v_ext[keys, :], do)).astype(BF16)
        dv = dot(p.astype(BF16), do)
        dk = dot(ds, q)
        dq = dq + dot_tn(ds, k)
        if i == last:
            env.dk[keys, :] = dk
            env.dv[keys, :] = dv
        else:
            env.dk[keys, :] += dk
            env.dv[keys, :] += dv
    for n in range(2):
        part = slice(n * LANES, (n + 1) * LANES)
        b = 2 * i + n
        zz, sl = b // 4, b % 4
        tok = pl.ds(b * LANES, LANES)
        env.back_out[zz, sl, 0:LANES, :] = jnp.where(
            lane < HEAD, dq[part] * HEAD ** (-0.5), pltpu.roll(env.dk[tok, :], HEAD, 1)
        ).astype(BF16)
        env.back_out[zz, sl, LANES:, :] = side_by_side(env.dv[tok, :]).astype(BF16)
        mine = 2 * x + c

        @pl.when(sl == mine)
        def _():
            env.back_in[zz * 4 + mine] = env.back_out[zz, sl]

        @pl.when(sl != mine)
        def _():
            back_copy(zz, sl, mine, env).start()


def back_copy(zz, sl, source, env):
    z, x, c, y = place()
    return remote(
        env.back_out.at[zz, sl], env.back_in.at[zz * 4 + source], env.bs.at[zz, sl],
        env.br.at[zz * 4 + source], dev(z, sl // 2, sl % 2, y),
    )


def project_back(zz, env):
    z, x, c, y = place()
    mine = 2 * x + c
    cosine, sine = env.cosine[zz], env.sine[zz]
    lane = lax.broadcasted_iota(jnp.int32, (LANES, LANES), 1)
    values = []
    for sl in range(4):

        @pl.when(sl != mine)
        def _():
            back_copy(zz, sl, sl, env).wait()

        grad = env.back_in[zz * 4 + sl, 0:LANES, :].astype(F32)
        turned = env.turned[zz, sl]
        inverse = lax.rsqrt(head_means(turned * turned) + EPS)
        unit = turned * inverse
        env.gain_sum[sl : sl + 1, :] += jnp.sum(grad * unit, axis=0, keepdims=True)
        d_unit = grad * env.gain[sl : sl + 1, :]
        d_turned = inverse * (d_unit - unit * head_means(d_unit * unit))
        d_lin = d_turned * cosine - half_swap(d_turned) * sine
        env.d_lin[zz, :, sl * LANES : (sl + 1) * LANES] = d_lin.astype(BF16)
        packed = env.back_in[zz * 4 + sl, LANES:, :].astype(F32)
        values.append(jnp.concatenate([packed, pltpu.roll(packed, HEAD, 1)], axis=0))
    for p in range(2):
        pair = jnp.where(lane < HEAD, values[2 * p], pltpu.roll(values[2 * p + 1], HEAD, 1))
        env.d_lin[zz, :, (4 + p) * LANES : (5 + p) * LANES] = pair.astype(BF16)


def states_part(zz, env):
    d_x = dot(env.d_lin[zz], env.u_qkv[...])
    env.part[0, zz] = d_x[:64]
    env.part[1, zz] = d_x[64:]


def layer(env):
    z, x, c, y = place()
    s = z * 4 + x * 2 + c
    mine = 2 * x + c
    env.back_out, env.back_in = env.heads_out, env.heads_in
    env.g_out = env.u_out
    tables = []
    for zz in range(4):
        b = zz * 4 + 2 * x + c
        tables.append(pltpu.make_async_copy(env.cosines.at[b], env.cosine.at[zz], env.t_sem.at[zz, 0]))
        tables.append(pltpu.make_async_copy(env.sines.at[b], env.sine.at[zz], env.t_sem.at[zz, 1]))
    each(tables, "start")

    greet_row()
    env.x_line[z] = env.states[...].astype(BF16)
    qk_rows, v_rows = qkv_rows(mine)
    env.u_qkv[qk_rows, :] = jnp.concatenate(
        [unit_rows(env.w_query[...]), unit_rows(env.w_key[...])], axis=0
    )
    env.u_qkv[v_rows, :] = unit_rows(env.w_value[...])
    pl.semaphore_wait(pltpu.get_barrier_semaphore(), 16)
    line = Line(env.x_line, (env.x_send, env.x_recv))
    line.start()
    q_core, q_side, q_relay = qkv_groups(env)
    each(q_side, "start")
    each(q_core, "start")

    lane = lax.broadcasted_iota(jnp.int32, (1, LANES), 1)
    for pair in range(2):
        scale = env.qk_scale[window(z * 256 + pair * LANES, LANES)].reshape(1, LANES)
        turned = pltpu.roll(scale, HEAD, 1)
        env.gain[2 * pair : 2 * pair + 1, :] = jnp.where(lane < HEAD, scale, turned)
        env.gain[2 * pair + 1 : 2 * pair + 2, :] = jnp.where(lane < HEAD, turned, scale)
    env.up_row[...] = env.up_scale[window(z * 1024, 1024)].reshape(1, 1024)
    env.gate_row[...] = env.gate_scale[window(z * 1024, 1024)].reshape(1, 1024)
    env.mix_row[0:1, :] = env.alpha_attn[...].reshape(1, 1024)
    env.mix_row[1:2, :] = env.alpha_mlp[...].reshape(1, 1024)
    env.u_out[2 * z + c] = unit_rows(env.w_out[...])
    env.ups[mine] = unit_cols(env.w_up[...])
    env.gates[mine] = unit_cols(env.w_gate[...])
    env.downs[mine] = unit_rows(env.w_down[...])
    env.gains[...] = jnp.zeros_like(env.gains)
    env.gain_sum[...] = jnp.zeros_like(env.gain_sum)
    ff = ff_groups(env)
    each(ff[0], "start")
    each(tables, "wait")

    line.arrive(1)
    each(q_side, "wait_recv")
    each(q_relay, "start")
    each(q_core, "wait_recv")
    each(q_relay, "wait_recv")
    project_block(z, env)

    @pl.loop(1, 4)
    def _(k):
        @pl.when(k < 3)
        def _():
            line.arrive(k + 1)

        for way in (-1, 1):

            @pl.when(inside(z - way * k))
            def _():
                project_block(z - way * k, env)

    each(ff[1], "start")
    line.drain()
    for group in (q_side, q_core, q_relay):
        each(group, "wait_send")
    uo = Column(env.u_out, (env.o_z, env.o_c, env.o_r))
    uo.start()

    @pl.loop(0, 4)
    def _(zz):
        for i, (xx, cc) in enumerate(peers()):
            b = zz * 4 + xx * 2 + cc
            remote(
                env.heads_out.at[zz, xx * 2 + cc], env.heads_in.at[b], env.hs.at[zz, i], env.hr.at[b],
                dev(z, xx, cc, y),
            ).wait()

    @pl.loop(0, 16)
    def _(b):
        spread_heads(b, env)

    uo.arrive(1)
    for i in range(4):
        attend_block(i, env)
    for i in range(4, 6):
        attend_block(i, env)
    uo.arrive(2)
    for i in range(6, 8):
        attend_block(i, env)
    uo.arrive(3)
    uo.finish()
    ff[1][0].wait_recv()
    ff[2][0].start()
    ff[3][0].start()
    wait_blocks(env.att_out, env.att_in, env.as_, env.ar)
    lay_heads(env.att_in, env.att_low)

    weights = env.u_out[...].reshape(512, 1024)
    for h in range(2):
        env.mix_out[h] = dot(env.att_low[1 - x, rows_of(h), :], weights).astype(BF16)
        side_mix(h, env).start()
    env.branch[...] = dot(env.att_low[x], weights)
    ff[1][1].wait_recv()
    ff[2][1].start()
    ff[3][1].start()

    def mix_half(h):
        rows = rows_of(h)
        side_mix(h, env).wait_recv()
        branch = env.branch[rows, :] + env.mix_in[h].astype(F32)
        env.branch[rows, :] = branch
        mid, _ = mix(env.states[rows, :], branch, env.mix_row[0:1, :])
        env.mid[rows, :] = mid
        env.h_line[h, z] = mid.astype(BF16)

    fa = Line(env.h_line.at[0], (env.fa_s, env.fa_r))
    fb = Line(env.h_line.at[1], (env.fb_s, env.fb_r))
    ba = Line(env.dm_line.at[0], (env.ba_s, env.ba_r))
    bb = Line(env.dm_line.at[1], (env.bb_s, env.bb_r))

    def reduce(h, send, recv):
        return Reduce(
            lambda owner, rows: env.part[h, owner, rows], env.passing.at[h], env.landed.at[h], send, recv
        )

    r0, r1 = reduce(0, env.r0_s, env.r0_r), reduce(1, env.r1_s, env.r1_r)

    def arrive(gather, k):
        gather.arrive(k)

    def piece(grad, tag, cut):
        def view(slot, half):
            return grad.at[slot] if half is None else grad.at[slot, window(half * cut, cut), :]

        lc, ly, lx, out, send, recv = tag
        kind = Piece if ly.shape[1] == cut else SidePiece
        return kind(view, lc, ly, lx, lambda half: out.at[window(half * cut, cut), :], (send, recv), out)

    gu = piece(env.g_up, (env.lcu, env.lyu, env.lxu, env.ou, env.us, env.ur), 512)
    gg = piece(env.g_gate, (env.lcg, env.lyg, env.lxg, env.og, env.gs, env.gr), 512)
    gd = piece(env.g_down, (env.lcd, env.lyd, env.lxd, env.od, env.ds, env.dr), 128)
    mix_half(0)
    fa.start()
    mix_half(1)
    ff[1][2].wait_recv()
    ff[2][2].start()
    ff[3][2].start()
    arrive(fa, 1)
    arrive(fa, 2)
    fb.start()
    each(ff[3], "wait_recv")
    each(ff[4], "start")
    each(ff[0], "wait_recv")
    each(ff[2], "wait_recv")
    each(ff[4], "wait_recv")
    arrive(fa, 3)
    mlp_forward(0, env)
    r0.step(3)
    arrive(fb, 1)
    r0.step(2)
    arrive(fb, 2)
    r0.step(1)
    arrive(fb, 3)
    mlp_forward(1, env)
    r1.step(3)
    after_forward(0, r0, env)
    ba.start()
    r1.step(2)
    arrive(ba, 1)
    r1.step(1)
    arrive(ba, 2)
    after_forward(1, r1, env)
    bb.start()
    arrive(ba, 3)
    mlp_backward(0, env)
    r0.step(3)
    arrive(bb, 1)
    grad_down_half(0, env)
    r0.step(2)
    arrive(bb, 2)
    grad_wide_half(0, env.d_up, env.g_up, env)
    r0.step(1)
    grad_wide_half(0, env.d_gate, env.g_gate, env)
    arrive(bb, 3)
    grad_down_half(1, env)
    gd.start()
    mlp_backward(1, env)
    r1.step(3)
    gd.pass_twin()
    after_backward(0, r0, env)
    grad_wide_half(1, env.d_up, env.g_up, env)
    gu.start()
    r1.step(2)
    for gather in (fa, fb, ba, bb):
        gather.drain()
    for group in ff:
        each(group, "wait_send")
    for h in range(2):
        side_mix(h, env).wait_send()
    gu.pass_first()
    grad_wide_half(1, env.d_gate, env.g_gate, env)
    gg.start()
    r1.step(1)
    after_backward(1, r1, env)

    side_rows(0, env).wait_recv()
    send_grads(x, env)
    side_rows(1, env).wait_recv()
    send_grads(1 - x, env)
    gg.pass_twin()

    @pl.loop(0, 4)
    def _(n):
        cols = window(n * 256, 256)
        grad = dot_tn(env.att_low[0], env.d_both[0, :, cols]) + dot_tn(env.att_low[1], env.d_both[1, :, cols])
        env.g_out[:, :, cols] = grad.reshape(8, 64, 256).astype(BF16)

    out_reduce = RowReduce(env)
    out_reduce.start()
    gd.pass_side()
    out_reduce.pass_line()
    for i in range(7, -1, -1):
        wait_grads(2 * i, env)
        wait_grads(2 * i + 1, env)
        spread_grads(2 * i, env)
        spread_grads(2 * i + 1, env)
        attend_back_block(i, env, 7)
        if i == 7:
            gu.pass_back()
            out_reduce.step(3)
        elif i == 6:
            gd.pass_back()
            out_reduce.step(2)
        elif i == 5:
            out_reduce.step(1)
    gg.pass_side()
    for h in range(2):
        side_rows(h, env).wait_send()
    project_back(3, env)
    out_reduce.to_twin()
    project_back(2, env)
    project_back(1, env)
    project_back(0, env)
    @pl.loop(0, 4)
    def _(n):
        cols = window(n * 256, 256)
        total = dot_tn(env.d_lin[...].reshape(512, 768), env.x_line[:, :, cols].reshape(512, 256))
        env.g_qkv[:, cols] = total.astype(BF16)

    def row_piece(which, tag, cut):
        def view(slot, half):
            start, size = (slot * LANES, LANES) if which == 0 else (4 * LANES + slot * HEAD, HEAD)
            if half is not None:
                start, size = start + half * cut, cut
            return env.g_qkv.at[window(start, size), :]

        lc, ly, lx, out, send, recv = tag
        kind = Piece if ly.shape[1] == cut else SidePiece
        return kind(
            view, lc, ly, lx, lambda half: out.at[window(half * cut, cut), :], (send, recv), out
        )

    gq = row_piece(0, (env.lcq, env.lyq, env.lxq, env.oq, env.qqs, env.qqr), 64)
    gv = row_piece(1, (env.lcv, env.lyv, env.lxv, env.ov, env.vvs, env.vvr), 32)
    gq.start()
    gv.start()

    @pl.loop(0, 4)
    def _(zz):
        states_part(zz, env)

    for h in range(2):
        (r0, r1)[h].step(3)
    gq.pass_first()
    gv.pass_first()
    for sl in range(4):
        both_parts = env.gain_sum[sl : sl + 1, 0:HEAD] + env.gain_sum[sl : sl + 1, HEAD:]
        env.gains[4 + sl : 5 + sl, 0:HEAD] = both_parts
    small = [
        remote(env.gains, env.gain_land.at[i], env.sm_s.at[i], env.sm_r.at[i], device)
        for i, device in enumerate((dev(z, x, 1 - c, y), dev(z, 1 - x, c, y), dev(z, x, c, 1 - y)))
    ]
    def tell(k):
        t = (z + k) % 4
        return remote(
            env.gain_line.at[z], env.gain_line.at[z], env.gl_s.at[k], env.gl_r.at[z], dev(t, x, c, y)
        )

    small[0].start()
    r0.step(2)
    r1.step(2)
    small[0].wait()
    env.gains[...] += env.gain_land[0]
    small[1].start()
    gg.pass_back()
    finish_ff(env, gd, 2)
    small[1].wait()
    env.gains[...] += env.gain_land[1]
    small[2].start()
    r0.step(1)
    r1.step(1)
    gq.pass_back()
    gv.pass_back()
    finish_ff(env, gu, 0)
    small[2].wait()
    env.gain_line[z] = env.gains[...] + env.gain_land[2]
    for k in range(1, 4):
        tell(k).start()
    finish_ff(env, gg, 1)
    out_reduce.finish()
    unit_out = env.oo[...].astype(F32) + env.yo[...].astype(F32)
    env.gate_val[1, 3 * HEAD :, :] = pull_rows(env.w_out[...], unit_out)
    r0.finish(env.total)
    env.d_states[0:64, :] += env.total[...]
    r1.finish(env.total)
    env.d_states[64:, :] += env.total[...]
    gq.finish()
    gv.finish()
    stage = env.gate_val.at[1]
    total_qk = gq.total()
    stage[0:HEAD, :] = pull_rows(env.w_query[...], total_qk[0:HEAD])
    stage[HEAD : 2 * HEAD, :] = pull_rows(env.w_key[...], total_qk[HEAD:])
    stage[2 * HEAD : 3 * HEAD, :] = pull_rows(env.w_value[...], gv.total())
    results = [
        pltpu.make_async_copy(stage.at[pl.ds(i * HEAD, HEAD), :], ref, env.out_sem.at[3 + i])
        for i, ref in enumerate((env.grad_query, env.grad_key, env.grad_value, env.grad_out))
    ]
    each(results, "start")
    for k in range(1, 4):
        tell(k).wait_send()
        t = (z + k) % 4
        remote(
            env.gain_line.at[t], env.gain_line.at[t], env.gl_s.at[k], env.gl_r.at[t], dev(t, x, c, y)
        ).wait_recv()
    each(results, "wait")
    for i in range(3):
        ff_result(env, i).wait()


def pull_rows(weight, grad):
    wide = weight.astype(F32)
    inverse = lax.rsqrt(jnp.sum(wide * wide, axis=1, keepdims=True) + EPS)
    unit = wide * inverse
    return inverse * (grad - unit * jnp.sum(grad * unit, axis=1, keepdims=True))


def pull_cols(weight, grad):
    wide = weight.astype(F32)
    inverse = lax.rsqrt(jnp.sum(wide * wide, axis=0, keepdims=True) + EPS)
    unit = wide * inverse
    return inverse * (grad - unit * jnp.sum(grad * unit, axis=0, keepdims=True))


def ff_result(env, which):
    stage = (env.up_lin.at[0], env.up_lin.at[1], env.gate_val.at[0])[which]
    out = (env.grad_up, env.grad_gate, env.grad_down)[which]
    return pltpu.make_async_copy(stage, out, env.out_sem.at[which])


def finish_ff(env, piece, which):
    piece.finish()
    if which == 2:
        env.gate_val[0] = pull_rows(env.w_down[...], piece.total())
    elif which == 0:
        env.up_lin[0] = pull_cols(env.w_up[...], piece.total())
    else:
        env.up_lin[1] = pull_cols(env.w_gate[...], piece.total())
    ff_result(env, which).start()


class RowReduce:
    def __init__(self, env):
        self.env = env
        self.line = Reduce(self.part, env.o_pass, env.o_land, env.ol_s, env.ol_r)

    def part(self, owner, rows):
        return self.env.g_out[2 * owner + place()[2], rows].astype(F32)

    def to_core(self, zz):
        z, x, c, y = place()
        e = self.env
        return remote(
            e.g_out.at[2 * zz + 1 - c], e.o_c_land.at[zz], e.oc_s.at[zz], e.oc_r.at[zz], dev(z, x, 1 - c, y)
        )

    def twin(self):
        z, x, c, y = place()
        e = self.env
        return remote(e.oo, e.yo, e.oy_s, e.oy_r, dev(z, x, c, 1 - y))

    def start(self):
        @pl.loop(0, 4)
        def _(zz):
            self.to_core(zz).start()

    def pass_line(self):
        c = place()[2]
        e = self.env

        @pl.loop(0, 4)
        def _(zz):
            self.to_core(zz).wait_recv()
            b = 2 * zz + c
            e.g_out[b] = (e.g_out[b].astype(F32) + e.o_c_land[zz].astype(F32)).astype(BF16)

    def step(self, k):
        self.line.step(k)

    def to_twin(self):
        e = self.env
        self.line.finish(e.total)
        e.oo[...] = e.total[...].astype(BF16)
        self.twin().start()

    def finish(self):
        self.twin().wait()

        @pl.loop(0, 4)
        def _(zz):
            self.to_core(zz).wait_send()


DMA = pltpu.SemaphoreType.DMA


def v(shape, dtype=BF16):
    return pltpu.VMEM(shape, dtype)


LAYER_IN = tuple(
    dict(
        states=None,
        w_query=None,
        w_key=None,
        w_value=None,
        w_out=None,
        w_up=None,
        w_gate=None,
        w_down=None,
        qk_scale=None,
        up_scale=None,
        gate_scale=None,
        alpha_attn=None,
        alpha_mlp=None,
        d_out=None,
        cosines=None,
        sines=None,
    )
)
LAYER_OUT = dict(
    output=((128, 1024), F32), d_states=((128, 1024), F32), gain_line=((4, 8, 1024), F32),
    grad_query=((64, 1024), F32), grad_key=((64, 1024), F32), grad_value=((64, 1024), F32),
    grad_out=((64, 1024), F32), grad_up=((1024, 256), F32), grad_gate=((1024, 256), F32),
    grad_down=((256, 1024), F32),
)
IN_VMEM = 3
LAYER_TMP = dict(
    x_line=v((4, 128, 1024)), u_qkv=v((768, 1024)), u_out=v((8, 64, 1024)), mix_out=v((2, 64, 1024)), mix_in=v((2, 64, 1024)),
    turned=v((4, 4, 128, 128), F32), cosine=v((4, 128, 128), F32), sine=v((4, 128, 128), F32),
    gain=v((4, 128), F32), up_row=v((1, 1024), F32), gate_row=v((1, 1024), F32), mix_row=v((2, 1024), F32), gain_sum=v((4, 128), F32), gains=v((8, 1024), F32),
    gain_land=v((3, 8, 1024), F32),
    heads_out=v((4, 4, 192, 128)), heads_in=v((16, 192, 128)),
    q_ext=v((2048, 128)), k_ext=v((2048, 128)), v_ext=v((2048, 128)), attended=v((2048, 128), F32),
    att_out=v((16, 64, 128)), att_in=v((2, 8, 64, 128)), att_low=v((2, 128, 512)),
    ups=v((4, 1024, 256)), gates=v((4, 1024, 256)), downs=v((4, 256, 1024)),
    branch=v((128, 1024), F32), mid=v((128, 1024), F32), d_mid=v((128, 1024), F32),
    total=v((64, 1024), F32), d_both=v((2, 128, 1024)),
    h_line=v((2, 4, 64, 1024)), dm_line=v((2, 4, 64, 1024)),
    up_lin=v((2, 1024, 256), F32), gate_val=v((2, 256, 1024), F32), hidden=v((2, 256, 1024)),
    d_up=v((2, 4, 256, 256)), d_gate=v((2, 4, 256, 256)),
    part=v((2, 4, 64, 1024), F32), passing=v((2, 4, 64, 1024)), landed=v((2, 5, 64, 1024)),
    g_up=v((4, 1024, 256)), g_gate=v((4, 1024, 256)), g_down=v((4, 256, 1024)), g_qkv=v((768, 1024)),
    lcu=v((2, 1024, 256)), lcg=v((2, 1024, 256)), lcd=v((2, 256, 1024)), lcq=v((2, 128, 1024)),
    lcv=v((2, 64, 1024)),
    lyu=v((1, 1024, 256)), lyg=v((2, 512, 256)), lyd=v((2, 128, 1024)), lyq=v((1, 128, 1024)), lyv=v((1, 64, 1024)),
    lxu=v((1024, 256)), lxg=v((512, 256)), lxd=v((128, 1024)), lxq=v((128, 1024)), lxv=v((64, 1024)),
    ou=v((1024, 256)), og=v((1024, 256)), od=v((256, 1024)), oq=v((128, 1024)), ov=v((64, 1024)),
    oo=v((64, 1024)), yo=v((64, 1024)), out_sem=DMA((7,)),
    o_c_land=v((4, 64, 1024)), o_pass=v((4, 64, 1024)),
    o_land=v((5, 64, 1024)),
    datt_out=v((2, 8, 64, 128)), datt_in=v((16, 64, 128)), do_ext=v((2048, 128)),
    dk=v((2048, 128), F32), dv=v((2048, 128), F32),
    d_lin=v((4, 128, 768)),
    t_sem=DMA((4, 2)), x_send=DMA((4, 2, SUBS)), x_recv=DMA((4, SUBS)), q_send=DMA((3, 2)), q_recv=DMA((3, 2)),
    w_send=DMA((5, 3)), w_recv=DMA((5, 3)), hs=DMA((4, 3)), hr=DMA((16,)),
    o_z=DMA((4, 2)), o_c=DMA((4,)), o_r=DMA((8,)),
    as_=DMA((16,)), ar=DMA((2, 8)), das=DMA((2, 8)), dar=DMA((16,)),
    mx_s=DMA((2,)), mx_r=DMA((2,)), db_s=DMA((2,)), db_r=DMA((2,)),
    fa_s=DMA((4, 2, SUBS)), fa_r=DMA((4, SUBS)), fb_s=DMA((4, 2, SUBS)), fb_r=DMA((4, SUBS)),
    ba_s=DMA((4, 2, SUBS)), ba_r=DMA((4, SUBS)), bb_s=DMA((4, 2, SUBS)), bb_r=DMA((4, SUBS)),
    r0_s=DMA((4, SUBS)), r0_r=DMA((5, SUBS)), r1_s=DMA((4, SUBS)), r1_r=DMA((5, SUBS)),
    us=DMA((6,)), ur=DMA((6,)), gs=DMA((6,)), gr=DMA((6,)), ds=DMA((6,)), dr=DMA((6,)),
    qqs=DMA((6,)), qqr=DMA((6,)), vvs=DMA((6,)), vvr=DMA((6,)),
    oc_s=DMA((4,)), oc_r=DMA((4,)),
    ol_s=DMA((4, SUBS)), ol_r=DMA((5, SUBS)), oy_s=DMA, oy_r=DMA,
    bs=DMA((4, 4)), br=DMA((16,)), sm_s=DMA((3,)), sm_r=DMA((3,)), gl_s=DMA((4,)), gl_r=DMA((4,)),
)


def run_layer(*args):
    vmem = pl.BlockSpec(memory_space=pltpu.VMEM)
    names = LAYER_IN + tuple(LAYER_OUT) + tuple(LAYER_TMP)

    def kernel(*refs):
        layer(Env(names, refs))

    outs = pl.pallas_call(
        kernel,
        name="layer",
        out_shape=tuple(jax.ShapeDtypeStruct(*o) for o in LAYER_OUT.values()),
        in_specs=[vmem] * (len(LAYER_IN) - 2) + [pl.BlockSpec(memory_space=pl.ANY)] * 2,
        out_specs=(vmem,) * IN_VMEM
        + (pl.BlockSpec(memory_space=pl.ANY),) * (len(LAYER_OUT) - IN_VMEM),
        scratch_shapes=list(LAYER_TMP.values()),
        compiler_params=pltpu.CompilerParams(
            collective_id=1, has_side_effects=True, vmem_limit_bytes=62 * MIB
        ),
    )(*args)
    return dict(zip(LAYER_OUT, outs))


HANDED = tuple(name for name in LAYER_OUT if name != "gain_line")


def hand_over_kernel(*refs):
    count = len(HANDED)
    line = refs[count]
    outs = refs[count + 1 : 2 * count + 6]
    held = refs[2 * count + 6 : 3 * count + 6]
    arrive, leave = refs[3 * count + 6 :]
    loads = [pltpu.make_async_copy(refs[i], held[i], arrive.at[i]) for i in range(count)]
    stores = [pltpu.make_async_copy(held[i], outs[i], leave.at[i]) for i in range(count)]
    each(loads, "start")
    qk, up, gate, attn, mlp = outs[count:]
    lane = lax.broadcasted_iota(jnp.int32, (1, LANES), 1)
    for zz in range(4):
        cols = slice(zz * 1024, (zz + 1) * 1024)
        up[cols] = line[zz, 0:1, :].reshape(1024)
        gate[cols] = line[zz, 1:2, :].reshape(1024)
        for pair in range(2):
            first = line[zz, 4 + 2 * pair : 5 + 2 * pair, 0:LANES]
            second = pltpu.roll(line[zz, 5 + 2 * pair : 6 + 2 * pair, 0:LANES], HEAD, 1)
            both = jnp.where(lane < HEAD, first, second)
            qk[zz * 256 + pair * LANES : zz * 256 + (pair + 1) * LANES] = both.reshape(LANES)
    for row, out in ((2, attn), (3, mlp)):
        parts = [line[zz, row : row + 1, :] for zz in range(4)]
        out[...] = (parts[0] + parts[1] + parts[2] + parts[3]).reshape(1024)
    for load, store in zip(loads, stores):
        load.wait()
        store.start()
    each(stores, "wait")


def hand_over(*arrays):
    vmem, hbm = pl.BlockSpec(memory_space=pltpu.VMEM), pl.BlockSpec(memory_space=pl.ANY)
    count = len(HANDED)
    sizes = (1024, 4096, 4096, 1024, 1024)
    return pl.pallas_call(
        hand_over_kernel,
        name="hand_over",
        out_shape=tuple(jax.ShapeDtypeStruct(a.shape, a.dtype) for a in arrays[:count])
        + tuple(jax.ShapeDtypeStruct((n,), F32) for n in sizes),
        in_specs=[hbm] * count + [vmem],
        out_specs=(hbm,) * count + (vmem,) * len(sizes),
        scratch_shapes=[v(a.shape, a.dtype) for a in arrays[:count]] + [DMA((count,))] * 2,
        compiler_params=pltpu.CompilerParams(vmem_limit_bytes=60 * MIB),
    )(*arrays)


def on_device_heads(
    states,
    lengths,
    w_query,
    w_key,
    w_value,
    w_out,
    w_up,
    w_gate,
    w_down,
    qk_scale,
    up_scale,
    gate_scale,
    alpha_attn,
    alpha_mlp,
    d_out,
):
    tok, width = states.shape[1:]
    cosine, sine = turn_tables(16 * tok)
    got = run_layer(
        states.reshape(tok, width), w_query.T, w_key.T, w_value.T, w_out, w_up, w_gate, w_down,
        qk_scale, up_scale, gate_scale, alpha_attn, alpha_mlp, d_out.reshape(tok, width),
        jnp.asarray(cosine.reshape(16, tok, LANES)), jnp.asarray(sine.reshape(16, tok, LANES)),
    )

    output, d_states, g_query, g_key, g_value, g_out, g_up, g_gate, g_down, *gains = hand_over(
        *(got[name] for name in HANDED), got["gain_line"]
    )
    return (
        output.reshape(states.shape),
        d_states.reshape(states.shape),
        g_query.T,
        g_key.T,
        g_value.T,
        g_out,
        g_up,
        g_gate,
        g_down,
        *gains,
    )


def solution(mesh):
    seq, batch = mesh.shape["seq"], mesh.shape["batch"]
    body = on_device_heads if (seq == HEADS and batch == 2) else on_device_general
    return jax.shard_map(
        body,
        mesh=mesh,
        in_specs=(
            P("batch", "seq", None),
            P("batch", None),
            P(None, "seq"),
            P(None, "seq"),
            P(None, "seq"),
            P("seq", None),
            P(None, "seq"),
            P(None, "seq"),
            P("seq", None),
            P(),
            P(),
            P(),
            P(),
            P(),
            P("batch", "seq", None),
        ),
        out_specs=(
            P("batch", "seq", None),
            P("batch", "seq", None),
            P(None, "seq"),
            P(None, "seq"),
            P(None, "seq"),
            P("seq", None),
            P(None, "seq"),
            P(None, "seq"),
            P("seq", None),
            P(),
            P(),
            P(),
            P(),
            P(),
        ),
        check_vma=False,
    )
```
